32 devices in a mesh: seg: 4 (over x, core), clip: 8 (over z, y).
Axes of the slice: x: 2, y: 2, z: 4, core: 2. Of those that a mesh axis runs over, the one named last changes fastest.
Arguments:
- tokens: bfloat16 [64, 8, 49, 2048], P('clip', 'seg'), may hold values from -6 to 6
- segment_index: int32 [64, 8], P('clip'), may hold values from 0 to 28, as said below
- crop_video: int32 [64], P('clip'), may hold values from 0 to 31, as said below
- stem_down: bfloat16 [2048, 512], replicated, may hold values from -0.125 to 0.125
- stem_up: bfloat16 [512, 2048], replicated, may hold values from -0.25 to 0.25
- reduce_weight: bfloat16 [2048, 512], replicated, may hold values from -0.125 to 0.125
- conv_weight: bfloat16 [9, 512, 512], replicated, may hold values from -0.09375 to 0.09375
- expand_weight: bfloat16 [512, 2048], replicated, may hold values from -0.25 to 0.25
- depth_near: float32 [9, 512], replicated, may hold values from -2.5 to 2.5
- depth_far: float32 [9, 512], replicated, may hold values from -2.5 to 2.5
- gate_bias: float32 [512], replicated, may hold values from -3 to 3
- gains_mid: float32 [3, 512], replicated, may hold values from 0.25 to 1.75
- biases_mid: float32 [3, 512], replicated, may hold values from -2.5 to 2.5
- gains_wide: float32 [2, 2048], replicated, may hold values from 0.25 to 1.75
- biases_wide: float32 [2, 2048], replicated, may hold values from -2.5 to 2.5
- cotangent: bfloat16 [64, 8, 49, 2048], P('clip', 'seg'), may hold values from -6 to 6
Outputs:
- activations: bfloat16 [64, 8, 49, 2048], P('clip', 'seg')
- video_means: float32 [32, 2048], replicated
- tokens_grad: float32 [64, 8, 49, 2048], P('clip', 'seg')
- stem_down_grad: float32 [2048, 512], P('clip')
- stem_up_grad: float32 [512, 2048], P('clip')
- reduce_grad: float32 [2048, 512], P('clip')
- conv_grad: float32 [9, 512, 512], P(None, 'clip')
- expand_grad: float32 [512, 2048], P('clip')
- near_grad: float32 [9, 512], replicated
- far_grad: float32 [9, 512], replicated
- gate_bias_grad: float32 [512], replicated
- gains_mid_grad: float32 [3, 512], replicated
- biases_mid_grad: float32 [3, 512], replicated
- gains_wide_grad: float32 [2, 2048], replicated
- biases_wide_grad: float32 [2, 2048], replicated
The draws below stay inside these ranges and needn't reach their ends.
Inputs may be any that keep to these rules, and one draw needn't show every extreme that they name: `segment_index`: every clip starts at frame 0 and each later segment's frame index exceeds the one before by 1 to 4. `crop_video`: every video has at least one crop; videos have different numbers of crops.
All inputs are finite; a program needn't handle non-finite values.
Results may differ from the reference program's by a relative error of at most 0.02.
Values may be sent and summed in bfloat16 or wider, within the bound.
A program may use at most 192 MiB of HBM per device.

```python
from functools import partial
import jax
import jax.numpy as jnp
from jax import lax

D = 2048
MID = 512
HEIGHT = 7
WIDTH = 7
SEGS = 8
PIX = 49
CLIPS = 64
NVID = 32


def draw_segment_index(key, part):
    key = jax.random.fold_in(key, 11)
    increments = jax.random.randint(jax.random.fold_in(key, 1), (CLIPS, SEGS - 1), 1, 5)
    chosen = jax.random.randint(jax.random.fold_in(key, 2), (), 0, CLIPS)
    clip_rows = jnp.arange(CLIPS)[:, None]
    increments = jnp.where(clip_rows == chosen, 4, increments).astype(jnp.int32)
    starts = jnp.zeros((CLIPS, 1), jnp.int32)
    return jnp.concatenate([starts, jnp.cumsum(increments, axis=1).astype(jnp.int32)], axis=1)


def draw_crop_video(key, part):
    key = jax.random.fold_in(key, 23)
    additional = jax.random.randint(jax.random.fold_in(key, 1), (CLIPS - NVID,), 0, NVID).astype(jnp.int32)
    video_ids = jnp.concatenate([jnp.arange(NVID, dtype=jnp.int32), additional])
    shuffle = jax.random.permutation(jax.random.fold_in(key, 2), CLIPS)
    return video_ids[shuffle]


def shard_levels(key, shape, cuts, low, high):
    factor_of, own = 1.0, jax.random.fold_in(key, 6)
    for axis_at, shards_of in cuts:
        draws = jnp.exp(jax.random.uniform(jax.random.fold_in(own, axis_at), (shards_of,), jnp.float32, low / len(cuts), high / len(cuts)))
        factor_of = factor_of * jnp.repeat(draws, shape[axis_at] // shards_of).reshape([-1 if axis == axis_at else 1 for axis in range(len(shape))])
    return factor_of


def gaussian(own_key, extent, width, most, cuts=(), kind=jnp.bfloat16):
    values = jax.random.normal(own_key, extent, jnp.float32) * width
    if len(cuts) > 0:
        values = shard_levels(own_key, extent, cuts, -0.22, 0.18) * values
    return jnp.clip(values, min=-most, max=most).astype(kind)


def setup_inputs(seed: int = 0) -> dict:
    key_of = jax.random.split(jax.random.key(seed), 17)
    return {
        "tokens": gaussian(key_of[0], (CLIPS, SEGS, PIX, D), 1.0, 6.0, ((0, 8), (1, 4))),
        "segment_index": draw_segment_index(jax.random.fold_in(key_of[16], 71), 0),
        "crop_video": draw_crop_video(jax.random.fold_in(key_of[16], 71), 0),
        "stem_down": gaussian(key_of[3], (D, MID), D ** -0.5, 0.125),
        "stem_up": gaussian(key_of[4], (MID, D), MID ** -0.5, 0.25),
        "reduce_weight": gaussian(key_of[5], (D, MID), D ** -0.5, 0.125),
        "conv_weight": gaussian(key_of[6], (9, MID, MID), (9 * MID) ** -0.5, 0.09375),
        "expand_weight": gaussian(key_of[7], (MID, D), MID ** -0.5, 0.25),
        "depth_near": gaussian(key_of[8], (9, MID), 0.4, 2.5, (), jnp.float32),
        "depth_far": gaussian(key_of[9], (9, MID), 0.4, 2.5, (), jnp.float32),
        "gate_bias": gaussian(key_of[10], (MID,), 0.5, 3.0, (), jnp.float32),
        "gains_mid": jnp.clip(1.0 + 0.15 * jax.random.normal(key_of[11], (3, MID), jnp.float32), 0.25, 1.75),
        "biases_mid": gaussian(key_of[12], (3, MID), 0.3, 2.5, (), jnp.float32),
        "gains_wide": jnp.clip(1.0 + 0.15 * jax.random.normal(key_of[13], (2, D), jnp.float32), 0.25, 1.75),
        "biases_wide": gaussian(key_of[14], (2, D), 0.3, 2.5, (), jnp.float32),
        "cotangent": gaussian(key_of[15], (CLIPS, SEGS, PIX, D), 1.0, 6.0, ((0, 8), (1, 4))),
    }


NORM_EPSILON = 1e-05
FULL_PRECISION = lax.Precision.HIGHEST

@jax.custom_vjp
def low(v):
    return lax.optimization_barrier(v.astype(jnp.bfloat16)).astype(jnp.float32)

@jax.custom_vjp
def low_back(v):
    return v

def low_keep(v):
    return (low(v), None)

def low_pass(kept, grad):
    return (grad,)

def back_keep(v):
    return (v, None)

def back_low(kept, grad):
    return (low(grad),)
low.defvjp(low_keep, low_pass)
low_back.defvjp(back_keep, back_low)

def step_weight(segment_index):
    spacing = (segment_index[:, 1:] - segment_index[:, :-1]).astype(jnp.float32)
    return jnp.concatenate([1.0 / spacing, jnp.zeros((spacing.shape[0], 1), jnp.float32)], axis=1)

def temporal_change(values, weights):
    later = jnp.concatenate([values[:, 1:], jnp.zeros_like(values[:, :1])], axis=1)
    return (later - values) * weights[:, :, None, None]

def normalize(values, scales, shifts):
    amount = values.shape[0] * values.shape[1] * values.shape[2]
    first_sum = lax.optimization_barrier(jnp.sum(values, axis=(0, 1, 2)))
    second_sum = lax.optimization_barrier(jnp.sum(values * values, axis=(0, 1, 2)))
    center = first_sum / amount
    spread = second_sum / amount - center * center
    return (values - center) * lax.rsqrt(spread + NORM_EPSILON) * scales + shifts

def smooth(values):
    return jax.nn.gelu(values, approximate=True)

def depth_conv(field, kernel, reach):
    leading = field.shape[:2]
    planes = field.reshape(leading + (HEIGHT, WIDTH, field.shape[3]))
    padded = jnp.pad(planes, ((0, 0), (0, 0), (reach, reach), (reach, reach), (0, 0)))
    result = jnp.zeros_like(planes)
    for position in range(9):
        down = position // 3 * reach
        across = position % 3 * reach
        result = result + padded[:, :, down:down + HEIGHT, across:across + WIDTH, :] * kernel[position]
    return result.reshape(field.shape)

def gate_apply(active, change, near_kernel, far_kernel, offsets):
    mixed = depth_conv(change, near_kernel, 1) + depth_conv(change, far_kernel, 2) + offsets
    return active * (1.0 + jax.nn.sigmoid(mixed))

def project(field, weight):
    return jnp.einsum('cspk,ko->cspo', field, weight, precision=FULL_PRECISION)

def frame_conv(field, weight):
    leading = field.shape[:2]
    planes = field.reshape(leading + (HEIGHT, WIDTH, field.shape[3]))
    padded = jnp.pad(planes, ((0, 0), (0, 0), (1, 1), (1, 1), (0, 0)))
    result = jnp.zeros(leading + (HEIGHT, WIDTH, weight.shape[2]), jnp.float32)
    for position in range(9):
        down = position // 3
        across = position % 3
        window = padded[:, :, down:down + HEIGHT, across:across + WIDTH, :]
        result = result + jnp.einsum('csijk,ko->csijo', window, weight[position], precision=FULL_PRECISION)
    return result.reshape(field.shape[:3] + (weight.shape[2],))

def forward(weights, frames, stem_down, stem_up, reduce_weight, conv_weight, expand_weight, depth_near, depth_far, gate_bias, gains_mid, biases_mid, gains_wide, biases_wide):
    frame_change = low(temporal_change(frames, weights))
    stem_inner = low_back(project(frame_change, stem_down))
    stem_active = low(smooth(normalize(stem_inner, gains_mid[0], biases_mid[0])))
    stem_outer = low_back(project(stem_active, stem_up))
    block_input = low(frames + normalize(stem_outer, gains_wide[0], biases_wide[0]))
    reduced = low_back(project(block_input, reduce_weight))
    reduced_act = low_back(low(smooth(normalize(reduced, gains_mid[1], biases_mid[1]))))
    act_change = temporal_change(reduced_act, weights)
    gated = low_back(low(gate_apply(reduced_act, act_change, depth_near, depth_far, gate_bias)))
    convolved = low_back(frame_conv(gated, conv_weight))
    conv_act = low(smooth(normalize(convolved, gains_mid[2], biases_mid[2])))
    expanded = low_back(project(conv_act, expand_weight))
    return smooth(block_input + normalize(expanded, gains_wide[1], biases_wide[1]))

def reference(tokens, segment_index, crop_video, stem_down, stem_up, reduce_weight, conv_weight, expand_weight, depth_near, depth_far, gate_bias, gains_mid, biases_mid, gains_wide, biases_wide, cotangent):
    weights = step_weight(segment_index)
    primals = tuple((member.astype(jnp.float32) for member in (tokens, stem_down, stem_up, reduce_weight, conv_weight, expand_weight, depth_near, depth_far, gate_bias, gains_mid, biases_mid, gains_wide, biases_wide)))
    block_output, pull = jax.vjp(partial(forward, weights), *primals)
    grads = pull(cotangent.astype(jnp.float32))
    pooled = lax.optimization_barrier(jnp.mean(block_output, axis=(1, 2)))
    video_sums = jax.ops.segment_sum(pooled, crop_video, num_segments=NVID)
    counts = jax.ops.segment_sum(jnp.ones_like(pooled[:, 0]), crop_video, num_segments=NVID)
    video_means = video_sums / counts[:, None]
    return (block_output.astype(jnp.bfloat16), video_means, grads[0], grads[1], grads[2], grads[3], grads[4], grads[5], grads[6], grads[7], grads[8], grads[9], grads[10], grads[11], grads[12])
```

```python
import functools

import jax
import jax.numpy as jnp
from jax import lax
from jax.experimental import pallas as pl
from jax.experimental.pallas import tpu as pltpu
from jax.sharding import PartitionSpec as P

HEIGHT = 7
WIDTH = 7
SEGS = 8
PIX = 49


NORM_EPSILON = 1e-05


MESH = pl.DeviceIdType.MESH


def exchange(source, landing, send_sem, recv_sem, axis, count):
    here = lax.axis_index(axis)
    for step in range(1, count):
        pltpu.make_async_remote_copy(
            source,
            landing.at[here],
            send_sem,
            recv_sem,
            device_id={axis: lax.rem(here + step, count)},
            device_id_type=MESH,
        ).start()
    landing[pl.ds(here, 1)] = source[...][None]
    arrived = landing.at[pl.ds(0, count - 1)]
    pltpu.make_async_copy(arrived, arrived, recv_sem).wait()
    total = landing[0]
    for rank in range(1, count):
        total = total + landing[rank]
    pltpu.make_async_copy(arrived, arrived, send_sem).wait()
    return total


def sum_kernel(segs, clips, values, result, middle, seg_land, clip_land, sems):
    barrier = pltpu.get_barrier_semaphore()
    for axis, count in (("seg", segs), ("clip", clips)):
        here = lax.axis_index(axis)
        for step in range(1, count):
            pl.semaphore_signal(
                barrier,
                inc=1,
                device_id={axis: lax.rem(here + step, count)},
                device_id_type=MESH,
            )
    pl.semaphore_wait(barrier, segs + clips - 2)
    middle[...] = exchange(values, seg_land, sems.at[0], sems.at[1], "seg", segs)
    result[...] = exchange(middle, clip_land, sems.at[2], sems.at[3], "clip", clips)


def sum_everywhere(first, second):
    segs, clips = lax.axis_size("seg"), lax.axis_size("clip")
    width = first.shape[0]
    summed = pl.pallas_call(
        functools.partial(sum_kernel, segs, clips),
        out_shape=jax.ShapeDtypeStruct((2, width), jnp.float32),
        in_specs=[pl.BlockSpec(memory_space=pltpu.VMEM)],
        out_specs=pl.BlockSpec(memory_space=pltpu.VMEM),
        scratch_shapes=[
            pltpu.VMEM((2, width), jnp.float32),
            pltpu.VMEM((segs, 2, width), jnp.float32),
            pltpu.VMEM((clips, 2, width), jnp.float32),
            pltpu.SemaphoreType.DMA((4,)),
        ],
        compiler_params=pltpu.CompilerParams(
            collective_id=0 if width < 1024 else 1, has_side_effects=True
        ),
    )(jnp.stack([first, second]))
    return summed[0], summed[1]


def shifted(block, axis, distance):
    devices = range(lax.axis_size(axis))
    route = [(i - distance, i) for i in devices if i - distance in devices]
    return lax.ppermute(block, axis, route)


def row_product(left_side, weight):
    return lax.dot_general(
        left_side,
        weight,
        (((left_side.ndim - 1,), (0,)), ((), ())),
        preferred_element_type=jnp.float32,
    )


def back_product(gradient, weight):
    return lax.dot_general(
        gradient,
        weight,
        (((gradient.ndim - 1,), (1,)), ((), ())),
        preferred_element_type=jnp.float32,
    )


def weight_gradient(left_side, gradient):
    return jnp.einsum("cspk,cspo->ko", left_side, gradient, preferred_element_type=jnp.float32)


def smooth(values):
    return jax.nn.gelu(values, approximate=True)


def depth_conv(field, kernel, reach):
    leading = field.shape[:2]
    planes = field.reshape(leading + (HEIGHT, WIDTH, field.shape[3]))
    padded = jnp.pad(planes, ((0, 0), (0, 0), (reach, reach), (reach, reach), (0, 0)))
    result = jnp.zeros_like(planes)
    for position in range(9):
        down = position // 3 * reach
        across = position % 3 * reach
        result = (
            result
            + padded[:, :, down : down + HEIGHT, across : across + WIDTH, :] * kernel[position]
        )
    return result.reshape(field.shape)


def gate_apply(active, change, near_kernel, far_kernel, offsets):
    mixed = depth_conv(change, near_kernel, 1) + depth_conv(change, far_kernel, 2) + offsets
    return active * (1.0 + jax.nn.sigmoid(mixed))


def frame_planes(field):
    planes = field.reshape(field.shape[:2] + (HEIGHT, WIDTH, field.shape[3]))
    return jnp.pad(planes, ((0, 0), (0, 0), (1, 1), (1, 1), (0, 0)))


def frame_conv(field, weight):
    padded = frame_planes(field)
    result = jnp.zeros(field.shape[:2] + (HEIGHT, WIDTH, weight.shape[2]), jnp.float32)
    for position in range(9):
        down = position // 3
        across = position % 3
        result = result + row_product(
            padded[:, :, down : down + HEIGHT, across : across + WIDTH, :], weight[position]
        )
    return result.reshape(field.shape[:3] + (weight.shape[2],))


def frame_conv_back(field, weight, gradient):
    padded = frame_planes(field)
    planes = gradient.reshape(gradient.shape[:2] + (HEIGHT, WIDTH, gradient.shape[3]))
    field_grad = jnp.zeros(padded.shape, jnp.float32)
    kernel_grads = []
    for position in range(9):
        down = position // 3
        across = position % 3
        window = padded[:, :, down : down + HEIGHT, across : across + WIDTH, :]
        kernel_grads.append(
            jnp.einsum("csijk,csijo->ko", window, planes, preferred_element_type=jnp.float32)
        )
        field_grad = field_grad.at[:, :, down : down + HEIGHT, across : across + WIDTH, :].add(
            back_product(planes, weight[position])
        )
    inner = field_grad[:, :, 1 : 1 + HEIGHT, 1 : 1 + WIDTH, :]
    return (inner.reshape(field.shape), jnp.stack(kernel_grads))


def body(
    tokens,
    segment_index,
    crop_video,
    stem_down,
    stem_up,
    reduce_weight,
    conv_weight,
    expand_weight,
    depth_near,
    depth_far,
    gate_bias,
    gains_mid,
    biases_mid,
    gains_wide,
    biases_wide,
    cotangent,
):
    seg_count = lax.axis_size("seg")
    clip_count = lax.axis_size("clip")
    seg_here = lax.axis_index("seg")
    local_segs = tokens.shape[1]
    amount = tokens.shape[0] * local_segs * tokens.shape[2] * seg_count * clip_count
    spacing = (segment_index[:, 1:] - segment_index[:, :-1]).astype(jnp.float32)
    full_weight = jnp.concatenate(
        [1.0 / spacing, jnp.zeros((spacing.shape[0], 1), jnp.float32)], axis=1
    )
    local_weight = lax.dynamic_slice_in_dim(full_weight, seg_here * local_segs, local_segs, 1)

    def gather_stats(values):
        return sum_everywhere(
            jnp.sum(values, axis=(0, 1, 2)), jnp.sum(values * values, axis=(0, 1, 2))
        )

    def normalize(values, first_sum, second_sum, scales, shifts):
        center = first_sum / amount
        spread = second_sum / amount - center * center
        return (values - center) * lax.rsqrt(spread + NORM_EPSILON) * scales + shifts

    def norm_smooth(values, first_sum, second_sum, scales, shifts):
        return smooth(normalize(values, first_sum, second_sum, scales, shifts))

    def block_finish(values, first_sum, second_sum, scales, shifts, skipped):
        return smooth(skipped + normalize(values, first_sum, second_sum, scales, shifts))

    def norm_back(piece, primals, gradient):
        unused, pull = jax.vjp(piece, *primals)
        pulled = pull(gradient)
        first_grad, second_grad = sum_everywhere(pulled[1], pulled[2])
        values = primals[0]
        return (pulled[0] + first_grad + 2.0 * values * second_grad,) + tuple(pulled[3:])

    frames = tokens.astype(jnp.float32)
    following = shifted(tokens[:, :1], "seg", -1).astype(jnp.float32)
    later = jnp.concatenate([frames[:, 1:], following], axis=1)
    frame_change = ((later - frames) * local_weight[:, :, None, None]).astype(jnp.bfloat16)
    stem_inner = row_product(frame_change, stem_down)
    inner_sums = gather_stats(stem_inner)
    stem_active = norm_smooth(
        stem_inner, inner_sums[0], inner_sums[1], gains_mid[0], biases_mid[0]
    ).astype(jnp.bfloat16)
    stem_outer = row_product(stem_active, stem_up)
    outer_sums = gather_stats(stem_outer)
    block_input = (
        frames + normalize(stem_outer, outer_sums[0], outer_sums[1], gains_wide[0], biases_wide[0])
    ).astype(jnp.bfloat16)
    reduced = row_product(block_input, reduce_weight)
    reduced_sums = gather_stats(reduced)
    reduced_act = norm_smooth(
        reduced, reduced_sums[0], reduced_sums[1], gains_mid[1], biases_mid[1]
    ).astype(jnp.bfloat16)
    channel_act = lax.all_to_all(
        reduced_act, "seg", split_axis=3, concat_axis=1, tiled=True
    ).astype(jnp.float32)
    narrow = channel_act.shape[3]
    near_local = lax.dynamic_slice_in_dim(depth_near, seg_here * narrow, narrow, 1)
    far_local = lax.dynamic_slice_in_dim(depth_far, seg_here * narrow, narrow, 1)
    offset_local = lax.dynamic_slice_in_dim(gate_bias, seg_here * narrow, narrow, 0)
    shifted_act = jnp.concatenate([channel_act[:, 1:], jnp.zeros_like(channel_act[:, :1])], axis=1)
    act_change = (shifted_act - channel_act) * full_weight[:, :, None, None]
    gated_channels = gate_apply(
        channel_act, act_change, near_local, far_local, offset_local
    ).astype(jnp.bfloat16)
    gated = lax.all_to_all(gated_channels, "seg", split_axis=1, concat_axis=3, tiled=True)
    convolved = frame_conv(gated, conv_weight)
    conv_sums = gather_stats(convolved)
    conv_act = norm_smooth(
        convolved, conv_sums[0], conv_sums[1], gains_mid[2], biases_mid[2]
    ).astype(jnp.bfloat16)
    expanded = row_product(conv_act, expand_weight)
    expanded_sums = gather_stats(expanded)
    residual = block_input.astype(jnp.float32)
    block_output = block_finish(
        expanded, expanded_sums[0], expanded_sums[1], gains_wide[1], biases_wide[1], residual
    )
    activations = block_output.astype(jnp.bfloat16)
    video_total = tokens.shape[0] * clip_count // 2
    pooled = jnp.sum(block_output, axis=(1, 2)) / (SEGS * PIX)
    membership = (crop_video[:, None] == jnp.arange(video_total, dtype=jnp.int32)[None, :]).astype(
        jnp.float32
    )
    video_part = jnp.dot(membership.T, pooled, precision=lax.Precision.HIGHEST)
    count_part = jnp.sum(membership, axis=0) * (seg_here == 0).astype(jnp.float32)
    video_sums, video_counts = lax.psum((video_part, count_part), ("seg", "clip"))
    video_means = video_sums / video_counts[:, None]
    grad_output = cotangent.astype(jnp.float32)
    grad_expanded, wide_gain_one, wide_bias_one, grad_skip = norm_back(
        block_finish,
        (expanded, expanded_sums[0], expanded_sums[1], gains_wide[1], biases_wide[1], residual),
        grad_output,
    )
    grad_expanded = grad_expanded.astype(jnp.bfloat16)
    expand_grad = weight_gradient(conv_act, grad_expanded)
    grad_conv_act = back_product(grad_expanded, expand_weight)
    grad_convolved, mid_gain_two, mid_bias_two = norm_back(
        norm_smooth,
        (convolved, conv_sums[0], conv_sums[1], gains_mid[2], biases_mid[2]),
        grad_conv_act,
    )
    grad_convolved = grad_convolved.astype(jnp.bfloat16)
    grad_gated, conv_grad = frame_conv_back(gated, conv_weight, grad_convolved)
    grad_gated = grad_gated.astype(jnp.bfloat16)
    grad_gated_channels = lax.all_to_all(
        grad_gated, "seg", split_axis=3, concat_axis=1, tiled=True
    ).astype(jnp.float32)
    unused_gate, gate_pull = jax.vjp(
        gate_apply, channel_act, act_change, near_local, far_local, offset_local
    )
    grad_direct, grad_change, near_part, far_part, offset_part = gate_pull(grad_gated_channels)
    weighted = grad_change * full_weight[:, :, None, None]
    grad_act_channels = (
        grad_direct
        + jnp.concatenate([jnp.zeros_like(weighted[:, :1]), weighted[:, :-1]], axis=1)
        - weighted
    ).astype(jnp.bfloat16)
    grad_reduced_act = lax.all_to_all(
        grad_act_channels, "seg", split_axis=1, concat_axis=3, tiled=True
    ).astype(jnp.float32)
    near_grad = lax.dynamic_update_slice_in_dim(
        jnp.zeros_like(depth_near), near_part, seg_here * narrow, 1
    )
    far_grad = lax.dynamic_update_slice_in_dim(
        jnp.zeros_like(depth_far), far_part, seg_here * narrow, 1
    )
    gate_bias_grad = lax.dynamic_update_slice_in_dim(
        jnp.zeros_like(gate_bias), offset_part, seg_here * narrow, 0
    )
    grad_reduced, mid_gain_one, mid_bias_one = norm_back(
        norm_smooth,
        (reduced, reduced_sums[0], reduced_sums[1], gains_mid[1], biases_mid[1]),
        grad_reduced_act,
    )
    grad_reduced = grad_reduced.astype(jnp.bfloat16)
    reduce_grad = weight_gradient(block_input, grad_reduced)
    grad_block_input = back_product(grad_reduced, reduce_weight) + grad_skip
    grad_stem_outer, wide_gain_zero, wide_bias_zero = norm_back(
        normalize,
        (stem_outer, outer_sums[0], outer_sums[1], gains_wide[0], biases_wide[0]),
        grad_block_input,
    )
    grad_stem_outer = grad_stem_outer.astype(jnp.bfloat16)
    stem_up_grad = weight_gradient(stem_active, grad_stem_outer)
    grad_stem_active = back_product(grad_stem_outer, stem_up)
    grad_stem_inner, mid_gain_zero, mid_bias_zero = norm_back(
        norm_smooth,
        (stem_inner, inner_sums[0], inner_sums[1], gains_mid[0], biases_mid[0]),
        grad_stem_active,
    )
    grad_stem_inner = grad_stem_inner.astype(jnp.bfloat16)
    stem_down_grad = weight_gradient(frame_change, grad_stem_inner)
    grad_change_in = back_product(grad_stem_inner, stem_down)
    weighted_in = grad_change_in * local_weight[:, :, None, None]
    earlier = shifted(weighted_in[:, -1:].astype(jnp.bfloat16), "seg", 1).astype(jnp.float32)
    tokens_grad = (
        grad_block_input + jnp.concatenate([earlier, weighted_in[:, :-1]], axis=1) - weighted_in
    )
    members = (
        near_grad,
        far_grad,
        gate_bias_grad,
        jnp.stack([mid_gain_zero, mid_gain_one, mid_gain_two]),
        jnp.stack([mid_bias_zero, mid_bias_one, mid_bias_two]),
        jnp.stack([wide_gain_zero, wide_gain_one]),
        jnp.stack([wide_bias_zero, wide_bias_one]),
    )
    flat_grads = jnp.concatenate([member.reshape(-1) for member in members])
    summed_small = lax.psum(flat_grads, ("seg", "clip"))
    unpacked = []
    cursor = 0
    for member in members:
        unpacked.append(summed_small[cursor : cursor + member.size].reshape(member.shape))
        cursor = cursor + member.size
    shares = (
        lax.psum_scatter(
            stem_down_grad.astype(jnp.bfloat16), "clip", scatter_dimension=0, tiled=True
        ).astype(jnp.float32),
        lax.psum_scatter(
            stem_up_grad.astype(jnp.bfloat16), "clip", scatter_dimension=0, tiled=True
        ).astype(jnp.float32),
        lax.psum_scatter(
            reduce_grad.astype(jnp.bfloat16), "clip", scatter_dimension=0, tiled=True
        ).astype(jnp.float32),
        lax.psum_scatter(
            conv_grad.astype(jnp.bfloat16), "clip", scatter_dimension=1, tiled=True
        ).astype(jnp.float32),
        lax.psum_scatter(
            expand_grad.astype(jnp.bfloat16), "clip", scatter_dimension=0, tiled=True
        ).astype(jnp.float32),
    )
    big = (
        lax.psum(shares[0].astype(jnp.bfloat16), "seg").astype(jnp.float32),
        lax.psum(shares[1].astype(jnp.bfloat16), "seg").astype(jnp.float32),
        lax.psum(shares[2].astype(jnp.bfloat16), "seg").astype(jnp.float32),
        lax.psum(shares[3].astype(jnp.bfloat16), "seg").astype(jnp.float32),
        lax.psum(shares[4].astype(jnp.bfloat16), "seg").astype(jnp.float32),
    )
    return (
        activations,
        video_means,
        tokens_grad,
        big[0],
        big[1],
        big[2],
        big[3],
        big[4],
        unpacked[0],
        unpacked[1],
        unpacked[2],
        unpacked[3],
        unpacked[4],
        unpacked[5],
        unpacked[6],
    )


def solution(mesh):
    return jax.shard_map(
        body,
        mesh=mesh,
        in_specs=(
            P("clip", "seg", None, None),
            P("clip", None),
            P("clip"),
            P(),
            P(),
            P(),
            P(),
            P(),
            P(),
            P(),
            P(),
            P(),
            P(),
            P(),
            P(),
            P("clip", "seg", None, None),
        ),
        out_specs=(
            P("clip", "seg", None, None),
            P(),
            P("clip", "seg", None, None),
            P("clip", None),
            P("clip", None),
            P("clip", None),
            P(None, "clip", None),
            P("clip", None),
            P(),
            P(),
            P(),
            P(),
            P(),
            P(),
            P(),
        ),
        check_vma=False,
    )
```

```python
import functools

import jax
import jax.numpy as jnp
from jax import lax
from jax.experimental import pallas as pl
from jax.experimental.pallas import tpu as pltpu
from jax.sharding import PartitionSpec as P

HEIGHT = 7
WIDTH = 7
SEGS = 8
PIX = 49


NORM_EPSILON = 1e-05


MESH = pl.DeviceIdType.MESH


def exchange(source, landing, send_sem, recv_sem, axis, count):
    here = lax.axis_index(axis)
    for step in range(1, count):
        pltpu.make_async_remote_copy(
            source,
            landing.at[here],
            send_sem,
            recv_sem,
            device_id={axis: lax.rem(here + step, count)},
            device_id_type=MESH,
        ).start()
    landing[pl.ds(here, 1)] = source[...][None]
    arrived = landing.at[pl.ds(0, count - 1)]
    pltpu.make_async_copy(arrived, arrived, recv_sem).wait()
    total = landing[0]
    for rank in range(1, count):
        total = total + landing[rank]
    pltpu.make_async_copy(arrived, arrived, send_sem).wait()
    return total


def sum_kernel(segs, clips, values, result, middle, seg_land, clip_land, sems):
    barrier = pltpu.get_barrier_semaphore()
    for axis, count in (("seg", segs), ("clip", clips)):
        here = lax.axis_index(axis)
        for step in range(1, count):
            pl.semaphore_signal(
                barrier,
                inc=1,
                device_id={axis: lax.rem(here + step, count)},
                device_id_type=MESH,
            )
    pl.semaphore_wait(barrier, segs + clips - 2)
    middle[...] = exchange(values, seg_land, sems.at[0], sems.at[1], "seg", segs)
    result[...] = exchange(middle, clip_land, sems.at[2], sems.at[3], "clip", clips)


def sum_everywhere(first, second):
    segs, clips = lax.axis_size("seg"), lax.axis_size("clip")
    width = first.shape[0]
    summed = pl.pallas_call(
        functools.partial(sum_kernel, segs, clips),
        out_shape=jax.ShapeDtypeStruct((2, width), jnp.float32),
        in_specs=[pl.BlockSpec(memory_space=pltpu.VMEM)],
        out_specs=pl.BlockSpec(memory_space=pltpu.VMEM),
        scratch_shapes=[
            pltpu.VMEM((2, width), jnp.float32),
            pltpu.VMEM((segs, 2, width), jnp.float32),
            pltpu.VMEM((clips, 2, width), jnp.float32),
            pltpu.SemaphoreType.DMA((4,)),
        ],
        compiler_params=pltpu.CompilerParams(
            collective_id=0 if width < 1024 else 1, has_side_effects=True
        ),
    )(jnp.stack([first, second]))
    return summed[0], summed[1]


def shifted(block, axis, distance):
    devices = range(lax.axis_size(axis))
    route = [(i - distance, i) for i in devices if i - distance in devices]
    return lax.ppermute(block, axis, route)


def row_product(left_side, weight):
    return lax.dot_general(
        left_side,
        weight,
        (((left_side.ndim - 1,), (0,)), ((), ())),
        preferred_element_type=jnp.float32,
    )


def back_product(gradient, weight):
    return lax.dot_general(
        gradient,
        weight,
        (((gradient.ndim - 1,), (1,)), ((), ())),
        preferred_element_type=jnp.float32,
    )


def weight_gradient(left_side, gradient):
    return jnp.einsum("cspk,cspo->ko", left_side, gradient, preferred_element_type=jnp.float32)


def smooth(values):
    return jax.nn.gelu(values, approximate=True)


def depth_conv(field, kernel, reach):
    leading = field.shape[:2]
    planes = field.reshape(leading + (HEIGHT, WIDTH, field.shape[3]))
    padded = jnp.pad(planes, ((0, 0), (0, 0), (reach, reach), (reach, reach), (0, 0)))
    result = jnp.zeros_like(planes)
    for position in range(9):
        down = position // 3 * reach
        across = position % 3 * reach
        result = (
            result
            + padded[:, :, down : down + HEIGHT, across : across + WIDTH, :] * kernel[position]
        )
    return result.reshape(field.shape)


def gate_apply(active, change, near_kernel, far_kernel, offsets):
    mixed = depth_conv(change, near_kernel, 1) + depth_conv(change, far_kernel, 2) + offsets
    return active * (1.0 + jax.nn.sigmoid(mixed))


def frame_planes(field):
    planes = field.reshape(field.shape[:2] + (HEIGHT, WIDTH, field.shape[3]))
    return jnp.pad(planes, ((0, 0), (0, 0), (1, 1), (1, 1), (0, 0)))


def frame_conv(field, weight):
    padded = frame_planes(field)
    result = jnp.zeros(field.shape[:2] + (HEIGHT, WIDTH, weight.shape[2]), jnp.float32)
    for position in range(9):
        down = position // 3
        across = position % 3
        result = result + row_product(
            padded[:, :, down : down + HEIGHT, across : across + WIDTH, :], weight[position]
        )
    return result.reshape(field.shape[:3] + (weight.shape[2],))


def frame_conv_back(field, weight, gradient):
    padded = frame_planes(field)
    planes = gradient.reshape(gradient.shape[:2] + (HEIGHT, WIDTH, gradient.shape[3]))
    field_grad = jnp.zeros(padded.shape, jnp.float32)
    kernel_grads = []
    for position in range(9):
        down = position // 3
        across = position % 3
        window = padded[:, :, down : down + HEIGHT, across : across + WIDTH, :]
        kernel_grads.append(
            jnp.einsum("csijk,csijo->ko", window, planes, preferred_element_type=jnp.float32)
        )
        field_grad = field_grad.at[:, :, down : down + HEIGHT, across : across + WIDTH, :].add(
            back_product(planes, weight[position])
        )
    inner = field_grad[:, :, 1 : 1 + HEIGHT, 1 : 1 + WIDTH, :]
    return (inner.reshape(field.shape), jnp.stack(kernel_grads))


def body(
    tokens,
    segment_index,
    crop_video,
    stem_down,
    stem_up,
    reduce_weight,
    conv_weight,
    expand_weight,
    depth_near,
    depth_far,
    gate_bias,
    gains_mid,
    biases_mid,
    gains_wide,
    biases_wide,
    cotangent,
):
    seg_count = lax.axis_size("seg")
    clip_count = lax.axis_size("clip")
    seg_here = lax.axis_index("seg")
    local_segs = tokens.shape[1]
    amount = tokens.shape[0] * local_segs * tokens.shape[2] * seg_count * clip_count
    spacing = (segment_index[:, 1:] - segment_index[:, :-1]).astype(jnp.float32)
    full_weight = jnp.concatenate(
        [1.0 / spacing, jnp.zeros((spacing.shape[0], 1), jnp.float32)], axis=1
    )
    local_weight = lax.dynamic_slice_in_dim(full_weight, seg_here * local_segs, local_segs, 1)

    def gather_stats(values):
        return sum_everywhere(
            jnp.sum(values, axis=(0, 1, 2)), jnp.sum(values * values, axis=(0, 1, 2))
        )

    def normalize(values, first_sum, second_sum, scales, shifts):
        center = first_sum / amount
        spread = second_sum / amount - center * center
        return (values - center) * lax.rsqrt(spread + NORM_EPSILON) * scales + shifts

    def norm_smooth(values, first_sum, second_sum, scales, shifts):
        return smooth(normalize(values, first_sum, second_sum, scales, shifts))

    def block_finish(values, first_sum, second_sum, scales, shifts, skipped):
        return smooth(skipped + normalize(values, first_sum, second_sum, scales, shifts))

    def norm_back(piece, primals, gradient):
        unused, pull = jax.vjp(piece, *primals)
        pulled = pull(gradient)
        first_grad, second_grad = sum_everywhere(pulled[1], pulled[2])
        values = primals[0]
        return (pulled[0] + first_grad + 2.0 * values * second_grad,) + tuple(pulled[3:])

    frames = tokens.astype(jnp.float32)
    following = shifted(tokens[:, :1], "seg", -1).astype(jnp.float32)
    later = jnp.concatenate([frames[:, 1:], following], axis=1)
    frame_change = ((later - frames) * local_weight[:, :, None, None]).astype(jnp.bfloat16)
    stem_inner = row_product(frame_change, stem_down)
    inner_sums = gather_stats(stem_inner)
    stem_active = norm_smooth(
        stem_inner, inner_sums[0], inner_sums[1], gains_mid[0], biases_mid[0]
    ).astype(jnp.bfloat16)
    stem_outer = row_product(stem_active, stem_up)
    outer_sums = gather_stats(stem_outer)
    block_input = (
        frames + normalize(stem_outer, outer_sums[0], outer_sums[1], gains_wide[0], biases_wide[0])
    ).astype(jnp.bfloat16)
    reduced = row_product(block_input, reduce_weight)
    reduced_sums = gather_stats(reduced)
    reduced_act = norm_smooth(
        reduced, reduced_sums[0], reduced_sums[1], gains_mid[1], biases_mid[1]
    ).astype(jnp.bfloat16)
    channel_act = lax.all_to_all(
        reduced_act, "seg", split_axis=3, concat_axis=1, tiled=True
    ).astype(jnp.float32)
    narrow = channel_act.shape[3]
    near_local = lax.dynamic_slice_in_dim(depth_near, seg_here * narrow, narrow, 1)
    far_local = lax.dynamic_slice_in_dim(depth_far, seg_here * narrow, narrow, 1)
    offset_local = lax.dynamic_slice_in_dim(gate_bias, seg_here * narrow, narrow, 0)
    shifted_act = jnp.concatenate([channel_act[:, 1:], jnp.zeros_like(channel_act[:, :1])], axis=1)
    act_change = (shifted_act - channel_act) * full_weight[:, :, None, None]
    gated_channels = gate_apply(
        channel_act, act_change, near_local, far_local, offset_local
    ).astype(jnp.bfloat16)
    gated = lax.all_to_all(gated_channels, "seg", split_axis=1, concat_axis=3, tiled=True)
    convolved = frame_conv(gated, conv_weight)
    conv_sums = gather_stats(convolved)
    conv_act = norm_smooth(
        convolved, conv_sums[0], conv_sums[1], gains_mid[2], biases_mid[2]
    ).astype(jnp.bfloat16)
    expanded = row_product(conv_act, expand_weight)
    expanded_sums = gather_stats(expanded)
    residual = block_input.astype(jnp.float32)
    block_output = block_finish(
        expanded, expanded_sums[0], expanded_sums[1], gains_wide[1], biases_wide[1], residual
    )
    activations = block_output.astype(jnp.bfloat16)
    video_total = tokens.shape[0] * clip_count // 2
    pooled = jnp.sum(block_output, axis=(1, 2)) / (SEGS * PIX)
    membership = (crop_video[:, None] == jnp.arange(video_total, dtype=jnp.int32)[None, :]).astype(
        jnp.float32
    )
    video_part = jnp.dot(membership.T, pooled, precision=lax.Precision.HIGHEST)
    count_part = jnp.sum(membership, axis=0) * (seg_here == 0).astype(jnp.float32)
    video_sums, video_counts = lax.psum((video_part, count_part), ("seg", "clip"))
    video_means = video_sums / video_counts[:, None]
    grad_output = cotangent.astype(jnp.float32)
    grad_expanded, wide_gain_one, wide_bias_one, grad_skip = norm_back(
        block_finish,
        (expanded, expanded_sums[0], expanded_sums[1], gains_wide[1], biases_wide[1], residual),
        grad_output,
    )
    grad_expanded = grad_expanded.astype(jnp.bfloat16)
    expand_grad = weight_gradient(conv_act, grad_expanded)
    grad_conv_act = back_product(grad_expanded, expand_weight)
    grad_convolved, mid_gain_two, mid_bias_two = norm_back(
        norm_smooth,
        (convolved, conv_sums[0], conv_sums[1], gains_mid[2], biases_mid[2]),
        grad_conv_act,
    )
    grad_convolved = grad_convolved.astype(jnp.bfloat16)
    grad_gated, conv_grad = frame_conv_back(gated, conv_weight, grad_convolved)
    grad_gated = grad_gated.astype(jnp.bfloat16)
    grad_gated_channels = lax.all_to_all(
        grad_gated, "seg", split_axis=3, concat_axis=1, tiled=True
    ).astype(jnp.float32)
    unused_gate, gate_pull = jax.vjp(
        gate_apply, channel_act, act_change, near_local, far_local, offset_local
    )
    grad_direct, grad_change, near_part, far_part, offset_part = gate_pull(grad_gated_channels)
    weighted = grad_change * full_weight[:, :, None, None]
    grad_act_channels = (
        grad_direct
        + jnp.concatenate([jnp.zeros_like(weighted[:, :1]), weighted[:, :-1]], axis=1)
        - weighted
    ).astype(jnp.bfloat16)
    grad_reduced_act = lax.all_to_all(
        grad_act_channels, "seg", split_axis=1, concat_axis=3, tiled=True
    ).astype(jnp.float32)
    near_grad = lax.dynamic_update_slice_in_dim(
        jnp.zeros_like(depth_near), near_part, seg_here * narrow, 1
    )
    far_grad = lax.dynamic_update_slice_in_dim(
        jnp.zeros_like(depth_far), far_part, seg_here * narrow, 1
    )
    gate_bias_grad = lax.dynamic_update_slice_in_dim(
        jnp.zeros_like(gate_bias), offset_part, seg_here * narrow, 0
    )
    grad_reduced, mid_gain_one, mid_bias_one = norm_back(
        norm_smooth,
        (reduced, reduced_sums[0], reduced_sums[1], gains_mid[1], biases_mid[1]),
        grad_reduced_act,
    )
    grad_reduced = grad_reduced.astype(jnp.bfloat16)
    reduce_grad = weight_gradient(block_input, grad_reduced)
    grad_block_input = back_product(grad_reduced, reduce_weight) + grad_skip
    grad_stem_outer, wide_gain_zero, wide_bias_zero = norm_back(
        normalize,
        (stem_outer, outer_sums[0], outer_sums[1], gains_wide[0], biases_wide[0]),
        grad_block_input,
    )
    grad_stem_outer = grad_stem_outer.astype(jnp.bfloat16)
    stem_up_grad = weight_gradient(stem_active, grad_stem_outer)
    grad_stem_active = back_product(grad_stem_outer, stem_up)
    grad_stem_inner, mid_gain_zero, mid_bias_zero = norm_back(
        norm_smooth,
        (stem_inner, inner_sums[0], inner_sums[1], gains_mid[0], biases_mid[0]),
        grad_stem_active,
    )
    grad_stem_inner = grad_stem_inner.astype(jnp.bfloat16)
    stem_down_grad = weight_gradient(frame_change, grad_stem_inner)
    grad_change_in = back_product(grad_stem_inner, stem_down)
    weighted_in = grad_change_in * local_weight[:, :, None, None]
    earlier = shifted(weighted_in[:, -1:].astype(jnp.bfloat16), "seg", 1).astype(jnp.float32)
    tokens_grad = (
        grad_block_input + jnp.concatenate([earlier, weighted_in[:, :-1]], axis=1) - weighted_in
    )
    members = (
        near_grad,
        far_grad,
        gate_bias_grad,
        jnp.stack([mid_gain_zero, mid_gain_one, mid_gain_two]),
        jnp.stack([mid_bias_zero, mid_bias_one, mid_bias_two]),
        jnp.stack([wide_gain_zero, wide_gain_one]),
        jnp.stack([wide_bias_zero, wide_bias_one]),
    )
    flat_grads = jnp.concatenate([member.reshape(-1) for member in members])
    summed_small = lax.psum(flat_grads, ("seg", "clip"))
    unpacked = []
    cursor = 0
    for member in members:
        unpacked.append(summed_small[cursor : cursor + member.size].reshape(member.shape))
        cursor = cursor + member.size
    shares = (
        lax.psum_scatter(
            stem_down_grad.astype(jnp.bfloat16), "clip", scatter_dimension=0, tiled=True
        ).astype(jnp.float32),
        lax.psum_scatter(
            stem_up_grad.astype(jnp.bfloat16), "clip", scatter_dimension=0, tiled=True
        ).astype(jnp.float32),
        lax.psum_scatter(
            reduce_grad.astype(jnp.bfloat16), "clip", scatter_dimension=0, tiled=True
        ).astype(jnp.float32),
        lax.psum_scatter(
            conv_grad.astype(jnp.bfloat16), "clip", scatter_dimension=1, tiled=True
        ).astype(jnp.float32),
        lax.psum_scatter(
            expand_grad.astype(jnp.bfloat16), "clip", scatter_dimension=0, tiled=True
        ).astype(jnp.float32),
    )
    big = (
        lax.psum(shares[0].astype(jnp.bfloat16), "seg").astype(jnp.float32),
        lax.psum(shares[1].astype(jnp.bfloat16), "seg").astype(jnp.float32),
        lax.psum(shares[2].astype(jnp.bfloat16), "seg").astype(jnp.float32),
        lax.psum(shares[3].astype(jnp.bfloat16), "seg").astype(jnp.float32),
        lax.psum(shares[4].astype(jnp.bfloat16), "seg").astype(jnp.float32),
    )
    return (
        activations,
        video_means,
        tokens_grad,
        big[0],
        big[1],
        big[2],
        big[3],
        big[4],
        unpacked[0],
        unpacked[1],
        unpacked[2],
        unpacked[3],
        unpacked[4],
        unpacked[5],
        unpacked[6],
    )


ROOT_TWO_OVER_PI = 0.7978845608
CUBIC = 0.044715


def smooth_pair(values):
    square = values * values
    bent = jnp.tanh(values * (ROOT_TWO_OVER_PI + ROOT_TWO_OVER_PI * CUBIC * square))
    half = 0.5 + 0.5 * bent
    slope = half * (
        1.0
        + values * (1.0 - bent) * (ROOT_TWO_OVER_PI + 3.0 * ROOT_TWO_OVER_PI * CUBIC * square)
    )
    return values * half, slope


def smooth_value(values):
    square = values * values
    bent = jnp.tanh(values * (ROOT_TWO_OVER_PI + ROOT_TWO_OVER_PI * CUBIC * square))
    return values * (0.5 + 0.5 * bent)


def rows_sum(values):
    return jnp.sum(values, axis=0, keepdims=True)


def flat(values):
    return values.reshape(-1, values.shape[-1])


def dot(left, right):
    return jnp.dot(left, right, preferred_element_type=jnp.float32)


def dot_back(left, right):
    return lax.dot_general(left, right, (((1,), (1,)), ((), ())), preferred_element_type=jnp.float32)


def dot_rows(left, right):
    return lax.dot_general(left, right, (((0,), (0,)), ((), ())), preferred_element_type=jnp.float32)


BF = jnp.bfloat16
F32 = jnp.float32
WIDE_TILE = 256
COLUMNS = 512


def near_taps():
    return [(a - 1, b - 1) for a in range(3) for b in range(3)]


def far_taps():
    return [(2 * (a - 1), 2 * (b - 1)) for a in range(3) for b in range(3)]


def block_kernel(segs, clips, amount, *refs):
    (
        tokens_hbm, cot_hbm, down_hbm, up_hbm, reduce_hbm, conv_hbm, expand_hbm,
        depth, gate_bias, gains_mid, biases_mid, gains_wide, biases_wide, step_weight, past_weight,
        act_hbm, tokens_grad_hbm, down_grad, up_grad, reduce_grad, conv_grad, expand_grad, spill,
        pooled, depth_grad, gains_mid_grad, biases_mid_grad, gains_wide_grad, biases_wide_grad,
        tok, frame, outer, skip, cot, wide,
        inner, active, reduced, acts, change, gates, conv, conv_act, gated, back_pad, temp, back,
        halo_out, halo_in,
        down, up, reduce_w, conv_w, expand_w,
        slim_src, slim_land, wide_src, wide_mid, wide_seg, wide_clip,
        slim_norm, wide_norm, depth_part,
        load_sem, store_sem, halo_sem, slim_sem, wide_sem,
    ) = refs
    seg = lax.axis_index("seg")
    clip = lax.axis_index("clip")
    devices = segs * clips
    me = seg * clips + clip
    scale = 1.0 / amount

    def peer_of(step):
        peer = lax.rem(me + step, devices)
        return (peer // clips, lax.rem(peer, clips))

    barrier = pltpu.get_barrier_semaphore()

    def greet(step, carry):
        pl.semaphore_signal(barrier, inc=1, device_id=peer_of(step), device_id_type=MESH)
        return carry

    lax.fori_loop(1, devices, greet, 0)

    loads = {}
    for at, (name, source, target) in enumerate(
        (
            ("tok", tokens_hbm, tok),
            ("down", down_hbm, down),
            ("up", up_hbm, up),
            ("reduce", reduce_hbm, reduce_w),
            ("conv", conv_hbm, conv_w),
            ("expand", expand_hbm, expand_w),
            ("cot", cot_hbm, cot),
        )
    ):
        loads[name] = pltpu.make_async_copy(source, target, load_sem.at[at])
        loads[name].start()

    def slim_start(at):
        def one(step, carry):
            pltpu.make_async_remote_copy(
                slim_src.at[at], slim_land.at[at, me], slim_sem.at[0, at], slim_sem.at[1, at],
                device_id=peer_of(step), device_id_type=MESH,
            ).start()
            return carry

        lax.fori_loop(1, devices, one, 0)
        slim_land[at, pl.ds(me, 1)] = slim_src[at][None]

    def gather_wait(landing, count, sem):
        arrived = landing.at[pl.ds(0, count - 1)]
        pltpu.make_async_copy(arrived, arrived, sem).wait()

    def slot_total(landing, count):
        total = landing[0]
        for rank in range(1, count):
            total = total + landing[rank]
        return total

    def slim_finish(at):
        land = slim_land.at[at]
        gather_wait(land, devices, slim_sem.at[1, at])
        total = slot_total(land, devices)
        gather_wait(land, devices, slim_sem.at[0, at])
        return total

    def axis_start(source, landing, axis, count, send, recv):
        here = lax.axis_index(axis)
        for step in range(1, count):
            pltpu.make_async_remote_copy(
                source, landing.at[here], send, recv,
                device_id={axis: lax.rem(here + step, count)}, device_id_type=MESH,
            ).start()
        landing[pl.ds(here, 1)] = source[...][None]

    def wide_start(at):
        axis_start(wide_src.at[at], wide_seg.at[at], "seg", segs, wide_sem.at[0, at], wide_sem.at[1, at])
        gather_wait(wide_seg.at[at], segs, wide_sem.at[1, at])
        wide_mid[at] = slot_total(wide_seg.at[at], segs)
        gather_wait(wide_seg.at[at], segs, wide_sem.at[0, at])
        axis_start(wide_mid.at[at], wide_clip.at[at], "clip", clips, wide_sem.at[2, at], wide_sem.at[3, at])

    def wide_finish(at):
        gather_wait(wide_clip.at[at], clips, wide_sem.at[3, at])
        total = slot_total(wide_clip.at[at], clips)
        gather_wait(wide_clip.at[at], clips, wide_sem.at[2, at])
        return total

    def keep_norm(total, kept):
        center = total[0:1] * scale
        spread = total[1:2] * scale - center * center
        kept[0:1] = center
        kept[1:2] = lax.rsqrt(spread + NORM_EPSILON)

    def pixels(body, start):
        def line(row, carry):
            for across in range(WIDTH):
                carry = body(row * WIDTH + across, row, across, carry)
            return carry

        return lax.fori_loop(0, HEIGHT, line, start)

    def halves(values):
        return values[0:8], values[8:16]

    def fold(values):
        return values[0:8] + values[8:16]

    slim_zero = jnp.zeros((8, COLUMNS), F32)

    def spread_row(row):
        return jnp.broadcast_to(row, (8, row.shape[-1]))

    def both(values):
        return jnp.concatenate([values, values], axis=0)

    def row16(row):
        return jnp.broadcast_to(row, (16, row.shape[-1]))

    def halo_start(source, target, at, ahead):
        copy = pltpu.make_async_remote_copy(
            source, target, halo_sem.at[0, at], halo_sem.at[1, at],
            device_id={"seg": jnp.clip(seg + ahead, 0, segs - 1)}, device_id_type=MESH,
        )
        can = seg < segs - 1 if ahead > 0 else seg > 0

        @pl.when(can)
        def _():
            copy.start()

    def halo_finish(source, target, at, ahead):
        copy = pltpu.make_async_remote_copy(
            source, target, halo_sem.at[0, at], halo_sem.at[1, at],
            device_id={"seg": jnp.clip(seg + ahead, 0, segs - 1)}, device_id_type=MESH,
        )
        sends = seg < segs - 1 if ahead > 0 else seg > 0
        takes = seg > 0 if ahead > 0 else seg < segs - 1

        @pl.when(takes)
        def _():
            copy.wait_recv()

        @pl.when(jnp.logical_not(takes))
        def _():
            target[...] = jnp.zeros_like(target)

        @pl.when(sends)
        def _():
            copy.wait_send()

    product, product_next = change, conv
    loads["tok"].wait()
    loads["down"].wait()
    for tile in range(2):
        at = pl.ds(tile * WIDE_TILE, WIDE_TILE)
        value = dot(flat(tok[...]), down[:, at])
        product[:, :, :, at] = value.reshape(PIX, 2, 8, WIDE_TILE)
        if tile == 0:
            pl.semaphore_wait(barrier, devices - 1)
        halo_start(product.at[:, 0, :, at], product_next.at[:, 0, :, at], tile, -1)
    for tile in range(2):
        at = pl.ds(tile * WIDE_TILE, WIDE_TILE)
        halo_finish(product.at[:, 0, :, at], product_next.at[:, 0, :, at], tile, -1)

    def inner_body(pixel, row, across, carry):
        first, second = carry
        zero, one, after = product[pixel, 0], product[pixel, 1], product_next[pixel, 0]
        early = (one - zero) * step_weight[0:8]
        late = (after - one) * step_weight[8:16]
        inner[pixel] = jnp.concatenate([early, late], axis=0)
        return first + early + late, second + early * early + late * late

    first, second = pixels(inner_body, (slim_zero, slim_zero))
    slim_src[0, 0:1] = rows_sum(first)
    slim_src[0, 1:2] = rows_sum(second)
    slim_start(0)

    token_out, token_in = wide.at[:, :, pl.ds(0, 1024)], wide.at[:, :, pl.ds(1024, 1024)]

    def token_pack(pixel, row, across, carry):
        value = tok[pixel].astype(F32)[0:8]
        wide[pixel, :, pl.ds(0, 1024)] = jnp.concatenate(
            [value[:, 0:1024], value[:, 1024:2048]], axis=0
        ).astype(BF)
        return carry

    pixels(token_pack, 0)
    halo_start(token_out, token_in, 2, -1)

    keep_norm(slim_finish(0), slim_norm.at[0])

    def activate(source, target, at):
        center, rate = row16(slim_norm[at, 0:1]), row16(slim_norm[at, 1:2] * gains_mid[at : at + 1])
        bias = row16(biases_mid[at : at + 1])

        def body(pixel, row, across, carry):
            target[pixel] = smooth_value((source[pixel] - center) * rate + bias).astype(BF)
            return carry

        pixels(body, 0)

    activate(inner, active, 0)

    loads["up"].wait()

    def widen(source, weight, sums):
        def body(tile, carry):
            at = pl.ds(pl.multiple_of(tile * WIDE_TILE, WIDE_TILE), WIDE_TILE)
            value = dot(flat(source[...]), weight[:, at])
            outer[:, :, at] = value.reshape(PIX, 16, WIDE_TILE)
            wide_src[sums, 0:1, at] = rows_sum(value)
            wide_src[sums, 1:2, at] = rows_sum(value * value)
            return carry

        lax.fori_loop(0, 2048 // WIDE_TILE, body, 0)

    widen(active, up, 0)
    wide_start(0)

    def frame_start(pixel, row, across, carry):
        for part in range(4):
            at = pl.ds(part * COLUMNS, COLUMNS)
            zero, one = halves(tok[pixel, :, at].astype(F32))
            frame[pixel, :, at] = jnp.concatenate(
                [(one - zero) * step_weight[0:8], one], axis=0
            ).astype(BF)
        return carry

    pixels(frame_start, 0)
    keep_norm(wide_finish(0), wide_norm.at[0])

    def wide_pixels(body, parts=4):
        def part(at, carry):
            columns = pl.ds(pl.multiple_of(at * COLUMNS, COLUMNS), COLUMNS)
            body(columns)
            return carry

        lax.fori_loop(0, parts, part, 0)

    def input_part(columns):
        center = row16(wide_norm[0, 0:1, columns])
        rate = row16(wide_norm[0, 1:2, columns] * gains_wide[0:1, columns])
        bias = row16(biases_wide[0:1, columns])

        def body(pixel, row, across, carry):
            value = (outer[pixel, :, columns] - center) * rate + bias
            tok[pixel, :, columns] = (tok[pixel, :, columns].astype(F32) + value).astype(BF)
            return carry

        pixels(body, 0)

    wide_pixels(input_part)
    block_input = tok
    spill_out = pltpu.make_async_copy(outer, spill, store_sem.at[0])
    spill_out.start()

    loads["reduce"].wait()
    for tile in range(2):
        at = pl.ds(tile * WIDE_TILE, WIDE_TILE)
        value = dot(flat(block_input[...]), reduce_w[:, at])
        reduced[:, :, at] = value.reshape(PIX, 16, WIDE_TILE)
        slim_src[1, 0:1, at] = rows_sum(value)
        slim_src[1, 1:2, at] = rows_sum(value * value)
    slim_start(1)
    halo_finish(token_out, token_in, 2, -1)

    def frame_finish(pixel, row, across, carry):
        ahead = wide[pixel, :, pl.ds(1024, 1024)].astype(F32)
        for part in range(4):
            at = pl.ds(part * COLUMNS, COLUMNS)
            zero, one = halves(frame[pixel, :, at].astype(F32))
            half, low = (0, part) if part < 2 else (8, part - 2)
            after = ahead[half : half + 8, low * COLUMNS : (low + 1) * COLUMNS]
            frame[pixel, :, at] = jnp.concatenate(
                [zero, (after - one) * step_weight[8:16]], axis=0
            ).astype(BF)
        return carry

    pixels(frame_finish, 0)
    keep_norm(slim_finish(1), slim_norm.at[1])

    def act_parts():
        center, rate = row16(slim_norm[1, 0:1]), row16(slim_norm[1, 1:2] * gains_mid[1:2])
        bias = row16(biases_mid[1:2])

        def body(pixel, row, across, carry):
            value = smooth_value((reduced[pixel] - center) * rate + bias).astype(BF)
            acts[pixel] = value
            lead = value.astype(F32)[0:8]
            halo_out[pixel] = jnp.concatenate([lead[:, 0:256], lead[:, 256:512]], axis=0).astype(BF)
            return carry

        pixels(body, 0)

    act_parts()
    halo_start(halo_out.at[pl.ds(0, PIX)], halo_in.at[pl.ds(0, PIX)], 3, -1)

    def change_early(pixel, row, across, carry):
        zero, one = halves(acts[pixel].astype(F32))
        change[pixel, 0] = (one - zero) * step_weight[0:8]
        change[pixel, 1] = one
        return carry

    pixels(change_early, 0)

    def lanes_of(tile):
        return pl.ds(pl.multiple_of(tile * 128, 128), 128)

    def inside(row, column):
        return 0 <= row < HEIGHT and 0 <= column < WIDTH

    def gate_tile(which):
        def body(tile, carry):
            lanes = lanes_of(tile)
            kernels = [depth[k, :, lanes] for k in range(18)]
            middle = kernels[4] + kernels[13]
            offsets = jnp.broadcast_to(gate_bias[0:1, lanes], (8, 128))
            field = [change[p, which, :, lanes] for p in range(PIX)]
            for i in range(HEIGHT):
                for j in range(WIDTH):
                    mixed = offsets + middle * field[i * WIDTH + j]
                    for base, taps in ((0, near_taps()), (9, far_taps())):
                        for k, (di, dj) in enumerate(taps):
                            if (di or dj) and inside(i + di, j + dj):
                                mixed = mixed + kernels[base + k] * field[(i + di) * WIDTH + j + dj]
                    gates[i * WIDTH + j, which, :, lanes] = 0.5 + 0.5 * jnp.tanh(0.5 * mixed)
            return carry

        lax.fori_loop(0, 4, body, 0)

    gate_tile(0)
    halo_finish(halo_out.at[pl.ds(0, PIX)], halo_in.at[pl.ds(0, PIX)], 3, -1)

    def change_late(pixel, row, across, carry):
        ahead = halo_in[pixel].astype(F32)
        after = jnp.concatenate([ahead[0:8], ahead[8:16]], axis=1)
        change[pixel, 1] = (after - change[pixel, 1]) * step_weight[8:16]
        return carry

    pixels(change_late, 0)
    gate_tile(1)

    for side in range(9):
        edge = jnp.zeros((16, COLUMNS), BF)
        for pad in (gated, back_pad):
            pad[0, side] = edge
            pad[8, side] = edge
            pad[side, 0] = edge
            pad[side, 8] = edge

    def gated_body(pixel, row, across, carry):
        both_gates = jnp.concatenate([gates[pixel, 0], gates[pixel, 1]], axis=0)
        gated[row + 1, across + 1] = (acts[pixel].astype(F32) * (1.0 + both_gates)).astype(BF)
        return carry

    pixels(gated_body, 0)

    loads["conv"].wait()

    def window(pad, a, b):
        return flat(pad[a : a + HEIGHT, b : b + WIDTH])

    for tile in range(2):
        at = pl.ds(tile * WIDE_TILE, WIDE_TILE)
        value = dot(window(gated, 0, 0), conv_w[0, :, at])
        for tap in range(1, 9):
            value = value + dot(window(gated, tap // 3, tap % 3), conv_w[tap, :, at])
        conv[:, :, :, at] = value.reshape(PIX, 2, 8, WIDE_TILE)
        slim_src[2, 0:1, at] = rows_sum(value)
        slim_src[2, 1:2, at] = rows_sum(value * value)
    slim_start(2)
    spill_out.wait()
    loads["expand"].wait()
    loads["cot"].wait()
    keep_norm(slim_finish(2), slim_norm.at[2])

    def conv_rows(pixel):
        return conv[pixel].reshape(16, COLUMNS)

    def conv_act_part():
        center, rate = row16(slim_norm[2, 0:1]), row16(slim_norm[2, 1:2] * gains_mid[2:3])
        bias = row16(biases_mid[2:3])

        def body(pixel, row, across, carry):
            conv_act[pixel] = smooth_value((conv_rows(pixel) - center) * rate + bias).astype(BF)
            return carry

        pixels(body, 0)

    conv_act_part()
    widen(conv_act, expand_w, 1)
    wide_start(1)
    keep_norm(wide_finish(1), wide_norm.at[1])

    def output_part(columns):
        center = row16(wide_norm[1, 0:1, columns])
        rate = row16(wide_norm[1, 1:2, columns])
        gain = row16(gains_wide[1:2, columns])
        bias = row16(biases_wide[1:2, columns])

        def body(pixel, row, across, carry):
            pool, shift, stretch = carry
            unit = (outer[pixel, :, columns] - center) * rate
            value, slope = smooth_pair(block_input[pixel, :, columns].astype(F32) + unit * gain + bias)
            incoming = cot[pixel, :, columns].astype(F32) * slope
            cot[pixel, :, columns] = value.astype(BF)
            skip[pixel, :, columns] = incoming
            return pool + fold(value), shift + fold(incoming), stretch + fold(incoming * unit)

        pool, shift, stretch = pixels(body, (slim_zero, slim_zero, slim_zero))
        pooled[:, columns] = pool
        wide_src[2, 0:1, columns] = rows_sum(shift)
        wide_src[2, 1:2, columns] = rows_sum(stretch)

    wide_pixels(output_part)
    wide_start(2)
    act_out = pltpu.make_async_copy(cot, act_hbm, store_sem.at[1])
    act_out.start()
    total = wide_finish(2)
    biases_wide_grad[1:2] = total[0:1]
    gains_wide_grad[1:2] = total[1:2]

    def wide_back(at, columns):
        center = row16(wide_norm[at, 0:1, columns])
        rate = row16(wide_norm[at, 1:2, columns])
        factor = rate * row16(gains_wide[at : at + 1, columns])
        shift = row16(biases_wide_grad[at : at + 1, columns] * scale)
        stretch = row16(gains_wide_grad[at : at + 1, columns] * scale) * rate

        def body(pixel, row, across, carry):
            value = skip[pixel, :, columns] - shift - (outer[pixel, :, columns] - center) * stretch
            wide[pixel, :, columns] = (value * factor).astype(BF)
            return carry

        pixels(body, 0)

    wide_pixels(functools.partial(wide_back, 1))
    spill_in = pltpu.make_async_copy(spill, outer, store_sem.at[0])
    spill_in.start()

    def narrow(weight):
        for tile in range(2):
            at = pl.ds(tile * WIDE_TILE, WIDE_TILE)
            value = dot_back(flat(wide[...]), weight[at, :])
            temp[:, :, at] = value.reshape(PIX, 16, WIDE_TILE)

    narrow(expand_w)

    def slope_sums(source, norm, sums):
        center, rate = row16(slim_norm[norm, 0:1]), row16(slim_norm[norm, 1:2])
        gain, bias = row16(gains_mid[norm : norm + 1]), row16(biases_mid[norm : norm + 1])

        def body(pixel, row, across, carry):
            shift, stretch = carry
            unit = (source(pixel) - center) * rate
            unused, slope = smooth_pair(unit * gain + bias)
            value = temp[pixel] * slope
            temp[pixel] = value
            return shift + fold(value), stretch + fold(value * unit)

        shift, stretch = pixels(body, (slim_zero, slim_zero))
        slim_src[sums, 0:1] = rows_sum(shift)
        slim_src[sums, 1:2] = rows_sum(stretch)
        slim_start(sums)

    def slope_finish(source, norm, sums, store):
        total = slim_finish(sums)
        biases_mid_grad[norm : norm + 1] = total[0:1]
        gains_mid_grad[norm : norm + 1] = total[1:2]
        center, rate = row16(slim_norm[norm, 0:1]), row16(slim_norm[norm, 1:2])
        factor = rate * row16(gains_mid[norm : norm + 1])
        shift = row16(total[0:1] * scale)
        stretch = row16(total[1:2] * scale) * rate

        def body(pixel, row, across, carry):
            value = temp[pixel] - shift - (source(pixel) - center) * stretch
            store(pixel, row, across, (value * factor).astype(BF))
            return carry

        pixels(body, 0)

    slope_sums(conv_rows, 2, 3)
    act_out.wait()

    def wide_weight_grad(left, target, at):
        def body(tile, carry):
            columns = pl.ds(pl.multiple_of(tile * WIDE_TILE, WIDE_TILE), WIDE_TILE)
            value = dot_rows(flat(left[...]), flat(wide[:, :, columns])).astype(BF)
            cot[0:32, :, columns] = value.reshape(32, 16, WIDE_TILE)
            return carry

        lax.fori_loop(0, 2048 // WIDE_TILE, body, 0)
        pltpu.make_async_copy(cot.at[0:32], target, store_sem.at[at]).start()

    def wide_weight_wait(target, at):
        pltpu.make_async_copy(cot.at[0:32], target, store_sem.at[at]).wait()

    wide_weight_grad(conv_act, expand_grad, 2)

    def store_conv(pixel, row, across, value):
        back_pad[row + 1, across + 1] = value

    slope_finish(conv_rows, 2, 3, store_conv)

    grad_gated = conv_act
    for tile in range(2):
        at = pl.ds(tile * WIDE_TILE, WIDE_TILE)
        value = dot_back(window(back_pad, 2, 2), conv_w[0, at, :])
        for tap in range(1, 9):
            value = value + dot_back(window(back_pad, 2 - tap // 3, 2 - tap % 3), conv_w[tap, at, :])
        grad_gated[:, :, at] = value.astype(BF).reshape(PIX, 16, WIDE_TILE)

    grad_mixed = conv

    def mixed_body(pixel, row, across, carry):
        incoming = grad_gated[pixel].astype(F32)
        both_gates = jnp.concatenate([gates[pixel, 0], gates[pixel, 1]], axis=0)
        value = incoming * acts[pixel].astype(F32) * both_gates * (1.0 - both_gates)
        grad_mixed[pixel] = value.reshape(2, 8, COLUMNS)
        temp[pixel] = incoming * (1.0 + both_gates)
        return carry

    pixels(mixed_body, 0)
    weighted = gates

    def gate_back_tile(which):
        def body(tile, carry):
            lanes = lanes_of(tile)
            kernels = [depth[k, :, lanes] for k in range(18)]
            middle = kernels[4] + kernels[13]
            weight = step_weight[which * 8 : which * 8 + 8, 0:128]
            field = [grad_mixed[p, which, :, lanes] for p in range(PIX)]
            for i in range(HEIGHT):
                for j in range(WIDTH):
                    value = middle * field[i * WIDTH + j]
                    for base, taps in ((0, near_taps()), (9, far_taps())):
                        for k, (di, dj) in enumerate(taps):
                            if (di or dj) and inside(i - di, j - dj):
                                value = value + kernels[base + k] * field[(i - di) * WIDTH + j - dj]
                    weighted[i * WIDTH + j, which, :, lanes] = value * weight
            return carry

        lax.fori_loop(0, 4, body, 0)

    def depth_grad_tile(which):
        def body(tile, carry):
            lanes = lanes_of(tile)
            field = [grad_mixed[p, which, :, lanes] for p in range(PIX)]
            bias_sum = field[0]
            for p in range(1, PIX):
                bias_sum = bias_sum + field[p]
            depth_part[18, which, :, lanes] = bias_sum
            for base, taps in ((0, near_taps()), (9, far_taps())):
                for k, (di, dj) in enumerate(taps):
                    value = None
                    for i in range(HEIGHT):
                        for j in range(WIDTH):
                            if inside(i + di, j + dj):
                                term = field[i * WIDTH + j] * change[
                                    (i + di) * WIDTH + j + dj, which, :, lanes
                                ]
                                value = term if value is None else value + term
                    depth_part[base + k, which, :, lanes] = value
            return carry

        lax.fori_loop(0, 4, body, 0)

    gate_back_tile(1)

    def weighted_pack(pixel, row, across, carry):
        last = weighted[pixel, 1]
        halo_out[pixel] = jnp.concatenate([last[:, 0:256], last[:, 256:512]], axis=0).astype(BF)
        return carry

    pixels(weighted_pack, 0)
    halo_start(halo_out.at[pl.ds(0, PIX)], halo_in.at[pl.ds(PIX, PIX)], 4, 1)
    gate_back_tile(0)
    depth_grad_tile(0)
    depth_grad_tile(1)
    for k in range(19):
        depth_grad[k : k + 1] = rows_sum(depth_part[k, 0] + depth_part[k, 1])
    halo_finish(halo_out.at[pl.ds(0, PIX)], halo_in.at[pl.ds(PIX, PIX)], 4, 1)

    def act_grad_body(pixel, row, across, carry):
        ahead = halo_in[PIX + pixel].astype(F32)
        before = jnp.concatenate([ahead[0:8], ahead[8:16]], axis=1)
        zero, one = weighted[pixel, 0], weighted[pixel, 1]
        value = temp[pixel] + jnp.concatenate([before - zero, zero - one], axis=0)
        temp[pixel] = value.astype(BF).astype(F32)
        return carry

    pixels(act_grad_body, 0)

    def reduced_rows(pixel):
        return reduced[pixel]

    slope_sums(reduced_rows, 1, 4)

    wide_weight_wait(expand_grad, 2)

    def conv_grad_copy(tap):
        slot = cot.at[0:32, :, pl.ds(tap % 4 * COLUMNS, COLUMNS)]
        return pltpu.make_async_copy(slot, conv_grad.at[tap], store_sem.at[3 + tap % 4])

    for tap in range(9):
        value = dot_rows(window(gated, tap // 3, tap % 3), window(back_pad, 1, 1)).astype(BF)
        if tap >= 4:
            conv_grad_copy(tap - 4).wait()
        cot[0:32, :, pl.ds(tap % 4 * COLUMNS, COLUMNS)] = value.reshape(32, 16, COLUMNS)
        conv_grad_copy(tap).start()

    def store_back(pixel, row, across, value):
        back[pixel] = value

    slope_finish(reduced_rows, 1, 4, store_back)

    spill_in.wait()

    def input_grad(tile, carry):
        at = pl.ds(pl.multiple_of(tile * WIDE_TILE, WIDE_TILE), WIDE_TILE)
        value = dot_back(flat(back[...]), reduce_w[at, :]) + flat(skip[:, :, at])
        skip[:, :, at] = value.reshape(PIX, 16, WIDE_TILE)
        unit = (flat(outer[:, :, at]) - wide_norm[0, 0:1, at]) * wide_norm[0, 1:2, at]
        wide_src[3, 0:1, at] = rows_sum(value)
        wide_src[3, 1:2, at] = rows_sum(value * unit)
        return carry

    lax.fori_loop(0, 2048 // WIDE_TILE, input_grad, 0)
    wide_start(3)
    for tap in range(5, 9):
        conv_grad_copy(tap).wait()

    def tall_weight_grad(left, target, at):
        def slot(tile):
            columns = pl.ds(tile // 2 * COLUMNS, COLUMNS)
            return cot.at[tile % 2 * 16 : tile % 2 * 16 + 16, :, columns]

        copies = []
        for tile in range(8):
            columns = pl.ds(tile * WIDE_TILE, WIDE_TILE)
            value = dot_rows(flat(left[:, :, columns]), flat(back[...])).astype(BF)
            slot(tile)[...] = value.reshape(16, 16, COLUMNS)
            copies.append(
                pltpu.make_async_copy(
                    slot(tile), target.at[tile * 16 : tile * 16 + 16], store_sem.at[at + tile]
                )
            )
            copies[-1].start()
        return copies

    copies = tall_weight_grad(block_input, reduce_grad, 3)
    total = wide_finish(3)
    biases_wide_grad[0:1] = total[0:1]
    gains_wide_grad[0:1] = total[1:2]
    wide_pixels(functools.partial(wide_back, 0))
    narrow(up)

    def inner_rows(pixel):
        return inner[pixel]

    slope_sums(inner_rows, 0, 5)
    for copy in copies:
        copy.wait()
    wide_weight_grad(active, up_grad, 2)
    slope_finish(inner_rows, 0, 5, store_back)

    def last_pack(pixel, row, across, carry):
        last = back[pixel].astype(F32)[8:16]
        halo_out[PIX + pixel] = jnp.concatenate([last[:, 0:256], last[:, 256:512]], axis=0).astype(BF)
        return carry

    pixels(last_pack, 0)
    halo_start(halo_out.at[pl.ds(PIX, PIX)], halo_in.at[pl.ds(2 * PIX, PIX)], 5, 1)
    wide_weight_wait(up_grad, 2)
    copies = tall_weight_grad(frame, down_grad, 3)
    halo_finish(halo_out.at[pl.ds(PIX, PIX)], halo_in.at[pl.ds(2 * PIX, PIX)], 5, 1)

    def change_grad(pixel, row, across, carry):
        ahead = halo_in[2 * PIX + pixel].astype(F32)
        before = jnp.concatenate([ahead[0:8], ahead[8:16]], axis=1) * past_weight[...]
        zero, one = halves(back[pixel].astype(F32) * step_weight[...])
        active[pixel] = jnp.concatenate([before - zero, zero - one], axis=0).astype(BF)
        return carry

    pixels(change_grad, 0)

    def tokens_part(tile):
        at = pl.ds(tile * WIDE_TILE, WIDE_TILE)
        return pltpu.make_async_copy(
            skip.at[:, :, at], tokens_grad_hbm.at[:, :, at], store_sem.at[11 + tile]
        )

    for tile in range(8):
        at = pl.ds(tile * WIDE_TILE, WIDE_TILE)
        value = dot_back(flat(active[...]), down[at, :]) + flat(skip[:, :, at])
        skip[:, :, at] = value.reshape(PIX, 16, WIDE_TILE)
        tokens_part(tile).start()
    for tile in range(8):
        tokens_part(tile).wait()
    for copy in copies:
        copy.wait()


def fused_body(
    tokens, segment_index, crop_video, stem_down, stem_up, reduce_weight, conv_weight, expand_weight,
    depth_near, depth_far, gate_bias, gains_mid, biases_mid, gains_wide, biases_wide, cotangent,
):
    segs, clips = lax.axis_size("seg"), lax.axis_size("clip")
    seg_here = lax.axis_index("seg")
    amount = tokens.shape[0] * tokens.shape[1] * PIX * segs * clips
    spacing = (segment_index[:, 1:] - segment_index[:, :-1]).astype(F32)
    full_weight = jnp.concatenate([1.0 / spacing, jnp.zeros((spacing.shape[0], 1), F32)], axis=1)
    padded_weight = jnp.concatenate([jnp.zeros((spacing.shape[0], 1), F32), full_weight], axis=1)
    three = lax.dynamic_slice_in_dim(padded_weight, seg_here * 2, 3, 1).T.reshape(24, 1)
    three = jnp.broadcast_to(three, (24, COLUMNS))
    past_weight, step_weight = three[0:8], three[8:24]

    def rows_first(field):
        return field.transpose(2, 1, 0, 3).reshape(PIX, 16, 2048)

    depth = jnp.broadcast_to(
        jnp.concatenate([depth_near, depth_far], axis=0)[:, None, :], (18, 8, COLUMNS)
    )
    whole = pl.BlockSpec(memory_space=pl.ANY)
    near = pl.BlockSpec(memory_space=pltpu.VMEM)
    field = (PIX, 16, 2048)
    slim = (PIX, 16, COLUMNS)
    split = (PIX, 2, 8, COLUMNS)
    out_shapes = (
        (field, BF, whole), (field, F32, whole),
        ((128, 16, 512), BF, whole), ((32, 16, 2048), BF, whole), ((128, 16, 512), BF, whole),
        ((9, 32, 16, 512), BF, whole), ((32, 16, 2048), BF, whole), (field, F32, whole),
        ((8, 2048), F32, near), ((19, 512), F32, near),
        ((3, 512), F32, near), ((3, 512), F32, near), ((2, 2048), F32, near), ((2, 2048), F32, near),
    )
    scratch = [
        pltpu.VMEM(field, BF), pltpu.VMEM(field, BF), pltpu.VMEM(field, F32), pltpu.VMEM(field, F32),
        pltpu.VMEM(field, BF), pltpu.VMEM(field, BF),
        pltpu.VMEM(slim, F32), pltpu.VMEM(slim, BF), pltpu.VMEM(slim, F32), pltpu.VMEM(slim, BF),
        pltpu.VMEM(split, F32), pltpu.VMEM(split, F32), pltpu.VMEM(split, F32), pltpu.VMEM(slim, BF),
        pltpu.VMEM((9, 9, 16, 512), BF), pltpu.VMEM((9, 9, 16, 512), BF),
        pltpu.VMEM(slim, F32), pltpu.VMEM(slim, BF),
        pltpu.VMEM((2 * PIX, 16, 256), BF), pltpu.VMEM((3 * PIX, 16, 256), BF),
        pltpu.VMEM((2048, 512), BF), pltpu.VMEM((512, 2048), BF), pltpu.VMEM((2048, 512), BF),
        pltpu.VMEM((9, 512, 512), BF), pltpu.VMEM((512, 2048), BF),
        pltpu.VMEM((6, 2, 512), F32), pltpu.VMEM((6, segs * clips, 2, 512), F32),
        pltpu.VMEM((4, 2, 2048), F32), pltpu.VMEM((4, 2, 2048), F32),
        pltpu.VMEM((4, segs, 2, 2048), F32), pltpu.VMEM((4, clips, 2, 2048), F32),
        pltpu.VMEM((3, 2, 512), F32), pltpu.VMEM((2, 2, 2048), F32),
        pltpu.VMEM((19, 2, 8, 512), F32),
        pltpu.SemaphoreType.DMA((7,)), pltpu.SemaphoreType.DMA((19,)), pltpu.SemaphoreType.DMA((2, 6)),
        pltpu.SemaphoreType.DMA((2, 6)), pltpu.SemaphoreType.DMA((4, 4)),
    ]
    outs = pl.pallas_call(
        functools.partial(block_kernel, segs, clips, amount),
        out_shape=tuple(jax.ShapeDtypeStruct(s, d) for s, d, unused in out_shapes),
        in_specs=[whole] * 7 + [near] * 8,
        out_specs=tuple(m for unused, unused_too, m in out_shapes),
        scratch_shapes=scratch,
        compiler_params=pltpu.CompilerParams(
            collective_id=0, has_side_effects=True, vmem_limit_bytes=VMEM_BYTES
        ),
    )(
        rows_first(tokens), rows_first(cotangent), stem_down, stem_up, reduce_weight, conv_weight,
        expand_weight, depth, gate_bias[None], gains_mid, biases_mid, gains_wide, biases_wide,
        step_weight, past_weight,
    )
    (
        act, tokens_grad, down_grad, up_grad, reduce_grad, conv_grad, expand_grad, unused,
        pooled, depth_grad, gains_mid_grad, biases_mid_grad, gains_wide_grad, biases_wide_grad,
    ) = outs

    def clips_first(value):
        return value.reshape(PIX, 2, 8, 2048).transpose(2, 1, 0, 3)

    video_total = tokens.shape[0] * clips // 2
    membership = (crop_video[:, None] == jnp.arange(video_total, dtype=jnp.int32)[None, :]).astype(F32)
    video_part = jnp.dot(membership.T, pooled / (SEGS * PIX), precision=lax.Precision.HIGHEST)
    count_part = jnp.sum(membership, axis=0) * (seg_here == 0).astype(F32)
    video_sums, video_counts, depth_sum = lax.psum(
        (video_part, count_part, depth_grad), ("seg", "clip")
    )

    def shares(value, axis):
        part = lax.psum_scatter(value, "clip", scatter_dimension=axis, tiled=True)
        return lax.psum(part.astype(BF), "seg").astype(F32)

    return (
        clips_first(act),
        video_sums / video_counts[:, None],
        clips_first(tokens_grad),
        shares(down_grad.reshape(2048, 512), 0),
        shares(up_grad.reshape(512, 2048), 0),
        shares(reduce_grad.reshape(2048, 512), 0),
        shares(conv_grad.reshape(9, 512, 512), 1),
        shares(expand_grad.reshape(512, 2048), 0),
        depth_sum[0:9],
        depth_sum[9:18],
        depth_sum[18],
        gains_mid_grad,
        biases_mid_grad,
        gains_wide_grad,
        biases_wide_grad,
    )


VMEM_BYTES = 62 << 20


def solution(mesh):
    def either(tokens, *others):
        fits = tokens.shape == (8, 2, PIX, 2048)
        return (fused_body if fits else body)(tokens, *others)

    return jax.shard_map(
        either,
        mesh=mesh,
        in_specs=(
            P("clip", "seg", None, None),
            P("clip", None),
            P("clip"),
            P(),
            P(),
            P(),
            P(),
            P(),
            P(),
            P(),
            P(),
            P(),
            P(),
            P(),
            P(),
            P("clip", "seg", None, None),
        ),
        out_specs=(
            P("clip", "seg", None, None),
            P(),
            P("clip", "seg", None, None),
            P("clip", None),
            P("clip", None),
            P("clip", None),
            P(None, "clip", None),
            P("clip", None),
            P(),
            P(),
            P(),
            P(),
            P(),
            P(),
            P(),
        ),
        check_vma=False,
    )
```

```python
import functools

import jax
import jax.numpy as jnp
from jax import lax
from jax.experimental import pallas as pl
from jax.experimental.pallas import tpu as pltpu
from jax.sharding import PartitionSpec as P

HEIGHT = 7
WIDTH = 7
SEGS = 8
PIX = 49


NORM_EPSILON = 1e-05


MESH = pl.DeviceIdType.MESH


def exchange(source, landing, send_sem, recv_sem, axis, count):
    here = lax.axis_index(axis)
    for step in range(1, count):
        pltpu.make_async_remote_copy(
            source,
            landing.at[here],
            send_sem,
            recv_sem,
            device_id={axis: lax.rem(here + step, count)},
            device_id_type=MESH,
        ).start()
    landing[pl.ds(here, 1)] = source[...][None]
    arrived = landing.at[pl.ds(0, count - 1)]
    pltpu.make_async_copy(arrived, arrived, recv_sem).wait()
    total = landing[0]
    for rank in range(1, count):
        total = total + landing[rank]
    pltpu.make_async_copy(arrived, arrived, send_sem).wait()
    return total


def sum_kernel(segs, clips, values, result, middle, seg_land, clip_land, sems):
    barrier = pltpu.get_barrier_semaphore()
    for axis, count in (("seg", segs), ("clip", clips)):
        here = lax.axis_index(axis)
        for step in range(1, count):
            pl.semaphore_signal(
                barrier,
                inc=1,
                device_id={axis: lax.rem(here + step, count)},
                device_id_type=MESH,
            )
    pl.semaphore_wait(barrier, segs + clips - 2)
    middle[...] = exchange(values, seg_land, sems.at[0], sems.at[1], "seg", segs)
    result[...] = exchange(middle, clip_land, sems.at[2], sems.at[3], "clip", clips)


def sum_everywhere(first, second):
    segs, clips = lax.axis_size("seg"), lax.axis_size("clip")
    width = first.shape[0]
    summed = pl.pallas_call(
        functools.partial(sum_kernel, segs, clips),
        out_shape=jax.ShapeDtypeStruct((2, width), jnp.float32),
        in_specs=[pl.BlockSpec(memory_space=pltpu.VMEM)],
        out_specs=pl.BlockSpec(memory_space=pltpu.VMEM),
        scratch_shapes=[
            pltpu.VMEM((2, width), jnp.float32),
            pltpu.VMEM((segs, 2, width), jnp.float32),
            pltpu.VMEM((clips, 2, width), jnp.float32),
            pltpu.SemaphoreType.DMA((4,)),
        ],
        compiler_params=pltpu.CompilerParams(
            collective_id=0 if width < 1024 else 1, has_side_effects=True
        ),
    )(jnp.stack([first, second]))
    return summed[0], summed[1]


def shifted(block, axis, distance):
    devices = range(lax.axis_size(axis))
    route = [(i - distance, i) for i in devices if i - distance in devices]
    return lax.ppermute(block, axis, route)


def row_product(left_side, weight):
    return lax.dot_general(
        left_side,
        weight,
        (((left_side.ndim - 1,), (0,)), ((), ())),
        preferred_element_type=jnp.float32,
    )


def back_product(gradient, weight):
    return lax.dot_general(
        gradient,
        weight,
        (((gradient.ndim - 1,), (1,)), ((), ())),
        preferred_element_type=jnp.float32,
    )


def weight_gradient(left_side, gradient):
    return jnp.einsum("cspk,cspo->ko", left_side, gradient, preferred_element_type=jnp.float32)


def smooth(values):
    return jax.nn.gelu(values, approximate=True)


def depth_conv(field, kernel, reach):
    leading = field.shape[:2]
    planes = field.reshape(leading + (HEIGHT, WIDTH, field.shape[3]))
    padded = jnp.pad(planes, ((0, 0), (0, 0), (reach, reach), (reach, reach), (0, 0)))
    result = jnp.zeros_like(planes)
    for position in range(9):
        down = position // 3 * reach
        across = position % 3 * reach
        result = (
            result
            + padded[:, :, down : down + HEIGHT, across : across + WIDTH, :] * kernel[position]
        )
    return result.reshape(field.shape)


def gate_apply(active, change, near_kernel, far_kernel, offsets):
    mixed = depth_conv(change, near_kernel, 1) + depth_conv(change, far_kernel, 2) + offsets
    return active * (1.0 + jax.nn.sigmoid(mixed))


def frame_planes(field):
    planes = field.reshape(field.shape[:2] + (HEIGHT, WIDTH, field.shape[3]))
    return jnp.pad(planes, ((0, 0), (0, 0), (1, 1), (1, 1), (0, 0)))


def frame_conv(field, weight):
    padded = frame_planes(field)
    result = jnp.zeros(field.shape[:2] + (HEIGHT, WIDTH, weight.shape[2]), jnp.float32)
    for position in range(9):
        down = position // 3
        across = position % 3
        result = result + row_product(
            padded[:, :, down : down + HEIGHT, across : across + WIDTH, :], weight[position]
        )
    return result.reshape(field.shape[:3] + (weight.shape[2],))


def frame_conv_back(field, weight, gradient):
    padded = frame_planes(field)
    planes = gradient.reshape(gradient.shape[:2] + (HEIGHT, WIDTH, gradient.shape[3]))
    field_grad = jnp.zeros(padded.shape, jnp.float32)
    kernel_grads = []
    for position in range(9):
        down = position // 3
        across = position % 3
        window = padded[:, :, down : down + HEIGHT, across : across + WIDTH, :]
        kernel_grads.append(
            jnp.einsum("csijk,csijo->ko", window, planes, preferred_element_type=jnp.float32)
        )
        field_grad = field_grad.at[:, :, down : down + HEIGHT, across : across + WIDTH, :].add(
            back_product(planes, weight[position])
        )
    inner = field_grad[:, :, 1 : 1 + HEIGHT, 1 : 1 + WIDTH, :]
    return (inner.reshape(field.shape), jnp.stack(kernel_grads))


def body(
    tokens,
    segment_index,
    crop_video,
    stem_down,
    stem_up,
    reduce_weight,
    conv_weight,
    expand_weight,
    depth_near,
    depth_far,
    gate_bias,
    gains_mid,
    biases_mid,
    gains_wide,
    biases_wide,
    cotangent,
):
    seg_count = lax.axis_size("seg")
    clip_count = lax.axis_size("clip")
    seg_here = lax.axis_index("seg")
    local_segs = tokens.shape[1]
    amount = tokens.shape[0] * local_segs * tokens.shape[2] * seg_count * clip_count
    spacing = (segment_index[:, 1:] - segment_index[:, :-1]).astype(jnp.float32)
    full_weight = jnp.concatenate(
        [1.0 / spacing, jnp.zeros((spacing.shape[0], 1), jnp.float32)], axis=1
    )
    local_weight = lax.dynamic_slice_in_dim(full_weight, seg_here * local_segs, local_segs, 1)

    def gather_stats(values):
        return sum_everywhere(
            jnp.sum(values, axis=(0, 1, 2)), jnp.sum(values * values, axis=(0, 1, 2))
        )

    def normalize(values, first_sum, second_sum, scales, shifts):
        center = first_sum / amount
        spread = second_sum / amount - center * center
        return (values - center) * lax.rsqrt(spread + NORM_EPSILON) * scales + shifts

    def norm_smooth(values, first_sum, second_sum, scales, shifts):
        return smooth(normalize(values, first_sum, second_sum, scales, shifts))

    def block_finish(values, first_sum, second_sum, scales, shifts, skipped):
        return smooth(skipped + normalize(values, first_sum, second_sum, scales, shifts))

    def norm_back(piece, primals, gradient):
        unused, pull = jax.vjp(piece, *primals)
        pulled = pull(gradient)
        first_grad, second_grad = sum_everywhere(pulled[1], pulled[2])
        values = primals[0]
        return (pulled[0] + first_grad + 2.0 * values * second_grad,) + tuple(pulled[3:])

    frames = tokens.astype(jnp.float32)
    following = shifted(tokens[:, :1], "seg", -1).astype(jnp.float32)
    later = jnp.concatenate([frames[:, 1:], following], axis=1)
    frame_change = ((later - frames) * local_weight[:, :, None, None]).astype(jnp.bfloat16)
    stem_inner = row_product(frame_change, stem_down)
    inner_sums = gather_stats(stem_inner)
    stem_active = norm_smooth(
        stem_inner, inner_sums[0], inner_sums[1], gains_mid[0], biases_mid[0]
    ).astype(jnp.bfloat16)
    stem_outer = row_product(stem_active, stem_up)
    outer_sums = gather_stats(stem_outer)
    block_input = (
        frames + normalize(stem_outer, outer_sums[0], outer_sums[1], gains_wide[0], biases_wide[0])
    ).astype(jnp.bfloat16)
    reduced = row_product(block_input, reduce_weight)
    reduced_sums = gather_stats(reduced)
    reduced_act = norm_smooth(
        reduced, reduced_sums[0], reduced_sums[1], gains_mid[1], biases_mid[1]
    ).astype(jnp.bfloat16)
    channel_act = lax.all_to_all(
        reduced_act, "seg", split_axis=3, concat_axis=1, tiled=True
    ).astype(jnp.float32)
    narrow = channel_act.shape[3]
    near_local = lax.dynamic_slice_in_dim(depth_near, seg_here * narrow, narrow, 1)
    far_local = lax.dynamic_slice_in_dim(depth_far, seg_here * narrow, narrow, 1)
    offset_local = lax.dynamic_slice_in_dim(gate_bias, seg_here * narrow, narrow, 0)
    shifted_act = jnp.concatenate([channel_act[:, 1:], jnp.zeros_like(channel_act[:, :1])], axis=1)
    act_change = (shifted_act - channel_act) * full_weight[:, :, None, None]
    gated_channels = gate_apply(
        channel_act, act_change, near_local, far_local, offset_local
    ).astype(jnp.bfloat16)
    gated = lax.all_to_all(gated_channels, "seg", split_axis=1, concat_axis=3, tiled=True)
    convolved = frame_conv(gated, conv_weight)
    conv_sums = gather_stats(convolved)
    conv_act = norm_smooth(
        convolved, conv_sums[0], conv_sums[1], gains_mid[2], biases_mid[2]
    ).astype(jnp.bfloat16)
    expanded = row_product(conv_act, expand_weight)
    expanded_sums = gather_stats(expanded)
    residual = block_input.astype(jnp.float32)
    block_output = block_finish(
        expanded, expanded_sums[0], expanded_sums[1], gains_wide[1], biases_wide[1], residual
    )
    activations = block_output.astype(jnp.bfloat16)
    video_total = tokens.shape[0] * clip_count // 2
    pooled = jnp.sum(block_output, axis=(1, 2)) / (SEGS * PIX)
    membership = (crop_video[:, None] == jnp.arange(video_total, dtype=jnp.int32)[None, :]).astype(
        jnp.float32
    )
    video_part = jnp.dot(membership.T, pooled, precision=lax.Precision.HIGHEST)
    count_part = jnp.sum(membership, axis=0) * (seg_here == 0).astype(jnp.float32)
    video_sums, video_counts = lax.psum((video_part, count_part), ("seg", "clip"))
    video_means = video_sums / video_counts[:, None]
    grad_output = cotangent.astype(jnp.float32)
    grad_expanded, wide_gain_one, wide_bias_one, grad_skip = norm_back(
        block_finish,
        (expanded, expanded_sums[0], expanded_sums[1], gains_wide[1], biases_wide[1], residual),
        grad_output,
    )
    grad_expanded = grad_expanded.astype(jnp.bfloat16)
    expand_grad = weight_gradient(conv_act, grad_expanded)
    grad_conv_act = back_product(grad_expanded, expand_weight)
    grad_convolved, mid_gain_two, mid_bias_two = norm_back(
        norm_smooth,
        (convolved, conv_sums[0], conv_sums[1], gains_mid[2], biases_mid[2]),
        grad_conv_act,
    )
    grad_convolved = grad_convolved.astype(jnp.bfloat16)
    grad_gated, conv_grad = frame_conv_back(gated, conv_weight, grad_convolved)
    grad_gated = grad_gated.astype(jnp.bfloat16)
    grad_gated_channels = lax.all_to_all(
        grad_gated, "seg", split_axis=3, concat_axis=1, tiled=True
    ).astype(jnp.float32)
    unused_gate, gate_pull = jax.vjp(
        gate_apply, channel_act, act_change, near_local, far_local, offset_local
    )
    grad_direct, grad_change, near_part, far_part, offset_part = gate_pull(grad_gated_channels)
    weighted = grad_change * full_weight[:, :, None, None]
    grad_act_channels = (
        grad_direct
        + jnp.concatenate([jnp.zeros_like(weighted[:, :1]), weighted[:, :-1]], axis=1)
        - weighted
    ).astype(jnp.bfloat16)
    grad_reduced_act = lax.all_to_all(
        grad_act_channels, "seg", split_axis=1, concat_axis=3, tiled=True
    ).astype(jnp.float32)
    near_grad = lax.dynamic_update_slice_in_dim(
        jnp.zeros_like(depth_near), near_part, seg_here * narrow, 1
    )
    far_grad = lax.dynamic_update_slice_in_dim(
        jnp.zeros_like(depth_far), far_part, seg_here * narrow, 1
    )
    gate_bias_grad = lax.dynamic_update_slice_in_dim(
        jnp.zeros_like(gate_bias), offset_part, seg_here * narrow, 0
    )
    grad_reduced, mid_gain_one, mid_bias_one = norm_back(
        norm_smooth,
        (reduced, reduced_sums[0], reduced_sums[1], gains_mid[1], biases_mid[1]),
        grad_reduced_act,
    )
    grad_reduced = grad_reduced.astype(jnp.bfloat16)
    reduce_grad = weight_gradient(block_input, grad_reduced)
    grad_block_input = back_product(grad_reduced, reduce_weight) + grad_skip
    grad_stem_outer, wide_gain_zero, wide_bias_zero = norm_back(
        normalize,
        (stem_outer, outer_sums[0], outer_sums[1], gains_wide[0], biases_wide[0]),
        grad_block_input,
    )
    grad_stem_outer = grad_stem_outer.astype(jnp.bfloat16)
    stem_up_grad = weight_gradient(stem_active, grad_stem_outer)
    grad_stem_active = back_product(grad_stem_outer, stem_up)
    grad_stem_inner, mid_gain_zero, mid_bias_zero = norm_back(
        norm_smooth,
        (stem_inner, inner_sums[0], inner_sums[1], gains_mid[0], biases_mid[0]),
        grad_stem_active,
    )
    grad_stem_inner = grad_stem_inner.astype(jnp.bfloat16)
    stem_down_grad = weight_gradient(frame_change, grad_stem_inner)
    grad_change_in = back_product(grad_stem_inner, stem_down)
    weighted_in = grad_change_in * local_weight[:, :, None, None]
    earlier = shifted(weighted_in[:, -1:].astype(jnp.bfloat16), "seg", 1).astype(jnp.float32)
    tokens_grad = (
        grad_block_input + jnp.concatenate([earlier, weighted_in[:, :-1]], axis=1) - weighted_in
    )
    members = (
        near_grad,
        far_grad,
        gate_bias_grad,
        jnp.stack([mid_gain_zero, mid_gain_one, mid_gain_two]),
        jnp.stack([mid_bias_zero, mid_bias_one, mid_bias_two]),
        jnp.stack([wide_gain_zero, wide_gain_one]),
        jnp.stack([wide_bias_zero, wide_bias_one]),
    )
    flat_grads = jnp.concatenate([member.reshape(-1) for member in members])
    summed_small = lax.psum(flat_grads, ("seg", "clip"))
    unpacked = []
    cursor = 0
    for member in members:
        unpacked.append(summed_small[cursor : cursor + member.size].reshape(member.shape))
        cursor = cursor + member.size
    shares = (
        lax.psum_scatter(
            stem_down_grad.astype(jnp.bfloat16), "clip", scatter_dimension=0, tiled=True
        ).astype(jnp.float32),
        lax.psum_scatter(
            stem_up_grad.astype(jnp.bfloat16), "clip", scatter_dimension=0, tiled=True
        ).astype(jnp.float32),
        lax.psum_scatter(
            reduce_grad.astype(jnp.bfloat16), "clip", scatter_dimension=0, tiled=True
        ).astype(jnp.float32),
        lax.psum_scatter(
            conv_grad.astype(jnp.bfloat16), "clip", scatter_dimension=1, tiled=True
        ).astype(jnp.float32),
        lax.psum_scatter(
            expand_grad.astype(jnp.bfloat16), "clip", scatter_dimension=0, tiled=True
        ).astype(jnp.float32),
    )
    big = (
        lax.psum(shares[0].astype(jnp.bfloat16), "seg").astype(jnp.float32),
        lax.psum(shares[1].astype(jnp.bfloat16), "seg").astype(jnp.float32),
        lax.psum(shares[2].astype(jnp.bfloat16), "seg").astype(jnp.float32),
        lax.psum(shares[3].astype(jnp.bfloat16), "seg").astype(jnp.float32),
        lax.psum(shares[4].astype(jnp.bfloat16), "seg").astype(jnp.float32),
    )
    return (
        activations,
        video_means,
        tokens_grad,
        big[0],
        big[1],
        big[2],
        big[3],
        big[4],
        unpacked[0],
        unpacked[1],
        unpacked[2],
        unpacked[3],
        unpacked[4],
        unpacked[5],
        unpacked[6],
    )


ROOT_TWO_OVER_PI = 0.7978845608
CUBIC = 0.044715


def smooth_pair(values):
    square = values * values
    bent = jnp.tanh(values * (ROOT_TWO_OVER_PI + ROOT_TWO_OVER_PI * CUBIC * square))
    half = 0.5 + 0.5 * bent
    slope = half * (
        1.0
        + values * (1.0 - bent) * (ROOT_TWO_OVER_PI + 3.0 * ROOT_TWO_OVER_PI * CUBIC * square)
    )
    return values * half, slope


def smooth_value(values):
    square = values * values
    bent = jnp.tanh(values * (ROOT_TWO_OVER_PI + ROOT_TWO_OVER_PI * CUBIC * square))
    return values * (0.5 + 0.5 * bent)


def rows_sum(values):
    return jnp.sum(values, axis=0, keepdims=True)


def flat(values):
    return values.reshape(-1, values.shape[-1])


def dot(left, right):
    return jnp.dot(left, right, preferred_element_type=jnp.float32)


def dot_back(left, right):
    return lax.dot_general(left, right, (((1,), (1,)), ((), ())), preferred_element_type=jnp.float32)


def dot_rows(left, right):
    return lax.dot_general(left, right, (((0,), (0,)), ((), ())), preferred_element_type=jnp.float32)


BF = jnp.bfloat16
F32 = jnp.float32
WIDE_TILE = 256
COLUMNS = 512


def near_taps():
    return [(a - 1, b - 1) for a in range(3) for b in range(3)]


def far_taps():
    return [(2 * (a - 1), 2 * (b - 1)) for a in range(3) for b in range(3)]


def block_kernel(segs, clips, amount, *refs):
    (
        tokens_hbm, cot_hbm, down_hbm, up_hbm, reduce_hbm, conv_hbm, expand_hbm,
        depth, gate_bias, gains_mid, biases_mid, gains_wide, biases_wide, step_weight, past_weight, crop_id,
        act_hbm, tokens_grad_hbm, down_grad, up_grad, reduce_grad, conv_grad, expand_grad, spill, frame_spill,
        video_means, depth_grad, gains_mid_grad, biases_mid_grad, gains_wide_grad, biases_wide_grad,
        tok, frame, outer, skip, cot, wide,
        inner, active, reduced, acts, change, gates, conv, conv_act, gated, back_pad, temp, back,
        halo_out, halo_in,
        down, up, reduce_w, conv_w, expand_w,
        slim_src, slim_land, wide_src, wide_mid, wide_seg, wide_clip,
        slim_norm, wide_norm, pool, video_src,
        load_sem, store_sem, halo_sem, slim_sem, wide_sem, ring_sem, video_sem,
    ) = refs
    seg = lax.axis_index("seg")
    clip = lax.axis_index("clip")
    devices = segs * clips
    me = seg * clips + clip
    scale = 1.0 / amount

    def peer_of(step):
        peer = lax.rem(me + step, devices)
        return (peer // clips, lax.rem(peer, clips))

    barrier = pltpu.get_barrier_semaphore()

    def greet(step, carry):
        pl.semaphore_signal(barrier, inc=1, device_id=peer_of(step), device_id_type=MESH)
        return carry

    lax.fori_loop(1, devices, greet, 0)

    def column_group(group):
        return pl.ds(group * COLUMNS, COLUMNS)

    class Loads:
        def __init__(self, at, pairs):
            self.copies = [
                pltpu.make_async_copy(source, target, load_sem.at[at + k])
                for k, (source, target) in enumerate(pairs)
            ]
            for copy in self.copies:
                copy.start()

        def wait(self):
            for copy in self.copies:
                copy.wait()

    def by_group(source, target):
        return [(source.at[:, :, :, column_group(g)], target.at[g]) for g in range(4)]

    loads = {
        "tok": Loads(0, [(tokens_hbm, tok)]),
        "down": Loads(1, [(down_hbm, down)]),
        "up": Loads(2, by_group(up_hbm, up)),
        "reduce": Loads(6, [(reduce_hbm, reduce_w)]),
        "conv": Loads(7, [(conv_hbm, conv_w)]),
        "expand": Loads(8, by_group(expand_hbm, expand_w)),
        "cot": Loads(
            12,
            [(cot_hbm.at[:, :, column_group(g)], cot.at[pl.ds(g * PIX, PIX)]) for g in range(4)],
        ),
    }

    def slim_start(at):
        def one(step, carry):
            pltpu.make_async_remote_copy(
                slim_src.at[at], slim_land.at[at, me], slim_sem.at[0, at], slim_sem.at[1, at],
                device_id=peer_of(step), device_id_type=MESH,
            ).start()
            return carry

        lax.fori_loop(1, devices, one, 0)
        slim_land[at, pl.ds(me, 1)] = slim_src[at][None]

    def gather_wait(landing, count, sem):
        arrived = landing.at[pl.ds(0, count - 1)]
        pltpu.make_async_copy(arrived, arrived, sem).wait()

    def slot_total(landing, count):
        total = landing[0]
        for rank in range(1, count):
            total = total + landing[rank]
        return total

    def slim_finish(at):
        land = slim_land.at[at]
        gather_wait(land, devices, slim_sem.at[1, at])
        total = slot_total(land, devices)
        gather_wait(land, devices, slim_sem.at[0, at])
        return total

    def axis_start(source, landing, axis, count, send, recv):
        here = lax.axis_index(axis)
        for step in range(1, count):
            pltpu.make_async_remote_copy(
                source, landing.at[here], send, recv,
                device_id={axis: lax.rem(here + step, count)}, device_id_type=MESH,
            ).start()
        landing[pl.ds(here, 1)] = source[...][None]

    def wide_start(at):
        axis_start(wide_src.at[at], wide_seg.at[at], "seg", segs, wide_sem.at[0, at], wide_sem.at[1, at])
        gather_wait(wide_seg.at[at], segs, wide_sem.at[1, at])
        wide_mid[at] = slot_total(wide_seg.at[at], segs)
        gather_wait(wide_seg.at[at], segs, wide_sem.at[0, at])
        axis_start(wide_mid.at[at], wide_clip.at[at], "clip", clips, wide_sem.at[2, at], wide_sem.at[3, at])

    def wide_finish(at):
        gather_wait(wide_clip.at[at], clips, wide_sem.at[3, at])
        total = slot_total(wide_clip.at[at], clips)
        gather_wait(wide_clip.at[at], clips, wide_sem.at[2, at])
        return total

    def keep_norm(total, kept):
        center = total[0:1] * scale
        spread = total[1:2] * scale - center * center
        kept[0:1] = center
        kept[1:2] = lax.rsqrt(spread + NORM_EPSILON)

    def pixels(body, start):
        def line(row, carry):
            for across in range(WIDTH):
                carry = body(row * WIDTH + across, row, across, carry)
            return carry

        return lax.fori_loop(0, HEIGHT, line, start)

    def halves(values):
        return values[0:8], values[8:16]

    def fold(values):
        return values[0:8] + values[8:16]

    slim_zero = jnp.zeros((8, COLUMNS), F32)

    def spread_row(row):
        return jnp.broadcast_to(row, (8, row.shape[-1]))

    def both(values):
        return jnp.concatenate([values, values], axis=0)

    def row16(row):
        return jnp.broadcast_to(row, (16, row.shape[-1]))

    def halo_start(source, target, at, ahead):
        copy = pltpu.make_async_remote_copy(
            source, target, halo_sem.at[0, at], halo_sem.at[1, at],
            device_id={"seg": jnp.clip(seg + ahead, 0, segs - 1)}, device_id_type=MESH,
        )
        can = seg < segs - 1 if ahead > 0 else seg > 0

        @pl.when(can)
        def _():
            copy.start()

    def halo_finish(source, target, at, ahead):
        copy = pltpu.make_async_remote_copy(
            source, target, halo_sem.at[0, at], halo_sem.at[1, at],
            device_id={"seg": jnp.clip(seg + ahead, 0, segs - 1)}, device_id_type=MESH,
        )
        sends = seg < segs - 1 if ahead > 0 else seg > 0
        takes = seg > 0 if ahead > 0 else seg < segs - 1

        @pl.when(takes)
        def _():
            copy.wait_recv()

        @pl.when(jnp.logical_not(takes))
        def _():
            target[...] = jnp.zeros_like(target)

        @pl.when(sends)
        def _():
            copy.wait_send()

    product, product_next = change, conv
    loads["tok"].wait()
    loads["down"].wait()
    for tile in range(2):
        at = pl.ds(tile * WIDE_TILE, WIDE_TILE)
        value = dot(flat(tok[...]), flat(down[:, :, :, :, at]))
        product[:, :, :, at] = value.reshape(PIX, 2, 8, WIDE_TILE)
        if tile == 0:
            pl.semaphore_wait(barrier, devices - 1)
        halo_start(product.at[:, 0, :, at], product_next.at[:, 0, :, at], tile, -1)
    for tile in range(2):
        at = pl.ds(tile * WIDE_TILE, WIDE_TILE)
        halo_finish(product.at[:, 0, :, at], product_next.at[:, 0, :, at], tile, -1)

    def inner_body(pixel, row, across, carry):
        first, second = carry
        zero, one, after = product[pixel, 0], product[pixel, 1], product_next[pixel, 0]
        early = (one - zero) * step_weight[0:8]
        late = (after - one) * step_weight[8:16]
        inner[pixel] = jnp.concatenate([early, late], axis=0)
        return first + early + late, second + early * early + late * late

    first, second = pixels(inner_body, (slim_zero, slim_zero))
    slim_src[0, 0:1] = rows_sum(first)
    slim_src[0, 1:2] = rows_sum(second)
    slim_start(0)

    token_out, token_in = wide.at[:, :, pl.ds(0, 1024)], wide.at[:, :, pl.ds(1024, 1024)]

    def token_pack(pixel, row, across, carry):
        value = tok[pixel].astype(F32)[0:8]
        wide[pixel, :, pl.ds(0, 1024)] = jnp.concatenate(
            [value[:, 0:1024], value[:, 1024:2048]], axis=0
        ).astype(BF)
        return carry

    pixels(token_pack, 0)
    halo_start(token_out, token_in, 2, -1)

    keep_norm(slim_finish(0), slim_norm.at[0])

    def activate(source, target, at):
        center, rate = row16(slim_norm[at, 0:1]), row16(slim_norm[at, 1:2] * gains_mid[at : at + 1])
        bias = row16(biases_mid[at : at + 1])

        def body(pixel, row, across, carry):
            target[pixel] = smooth_value((source[pixel] - center) * rate + bias).astype(BF)
            return carry

        pixels(body, 0)

    activate(inner, active, 0)

    loads["up"].wait()

    def widen(source, weight, sums):
        def body(tile, carry):
            at = pl.ds(pl.multiple_of(tile * WIDE_TILE, WIDE_TILE), WIDE_TILE)
            lanes = pl.ds(pl.multiple_of(lax.rem(tile, 2) * WIDE_TILE, WIDE_TILE), WIDE_TILE)
            value = dot(flat(source[...]), flat(weight[tile // 2, :, :, :, lanes]))
            outer[:, :, at] = value.reshape(PIX, 16, WIDE_TILE)
            wide_src[sums, 0:1, at] = rows_sum(value)
            wide_src[sums, 1:2, at] = rows_sum(value * value)
            return carry

        lax.fori_loop(0, 2048 // WIDE_TILE, body, 0)

    widen(active, up, 0)
    wide_start(0)

    def frame_start(pixel, row, across, carry):
        for part in range(4):
            at = pl.ds(part * COLUMNS, COLUMNS)
            zero, one = halves(tok[pixel, :, at].astype(F32))
            frame[part * PIX + pixel] = jnp.concatenate(
                [(one - zero) * step_weight[0:8], one], axis=0
            ).astype(BF)
        return carry

    pixels(frame_start, 0)
    keep_norm(wide_finish(0), wide_norm.at[0])

    def wide_pixels(body, parts=4):
        def part(at, carry):
            columns = pl.ds(pl.multiple_of(at * COLUMNS, COLUMNS), COLUMNS)
            body(at, columns)
            return carry

        lax.fori_loop(0, parts, part, 0)

    def input_part(group, columns):
        center = row16(wide_norm[0, 0:1, columns])
        rate = row16(wide_norm[0, 1:2, columns] * gains_wide[0:1, columns])
        bias = row16(biases_wide[0:1, columns])

        def body(pixel, row, across, carry):
            value = (outer[pixel, :, columns] - center) * rate + bias
            tok[pixel, :, columns] = (tok[pixel, :, columns].astype(F32) + value).astype(BF)
            return carry

        pixels(body, 0)

    wide_pixels(input_part)
    block_input = tok
    spill_out = pltpu.make_async_copy(outer, spill, store_sem.at[0])
    spill_out.start()

    loads["reduce"].wait()
    for tile in range(2):
        at = pl.ds(tile * WIDE_TILE, WIDE_TILE)
        value = dot(flat(block_input[...]), flat(reduce_w[:, :, :, :, at]))
        reduced[:, :, at] = value.reshape(PIX, 16, WIDE_TILE)
        slim_src[1, 0:1, at] = rows_sum(value)
        slim_src[1, 1:2, at] = rows_sum(value * value)
    slim_start(1)
    halo_finish(token_out, token_in, 2, -1)

    def frame_finish(pixel, row, across, carry):
        ahead = wide[pixel, :, pl.ds(1024, 1024)].astype(F32)
        for part in range(4):
            zero, one = halves(frame[part * PIX + pixel].astype(F32))
            half, low = (0, part) if part < 2 else (8, part - 2)
            after = ahead[half : half + 8, low * COLUMNS : (low + 1) * COLUMNS]
            frame[part * PIX + pixel] = jnp.concatenate(
                [zero, (after - one) * step_weight[8:16]], axis=0
            ).astype(BF)
        return carry

    pixels(frame_finish, 0)
    frame_out = [
        pltpu.make_async_copy(
            frame.at[pl.ds(g * PIX, PIX)], frame_spill.at[:, :, column_group(g)], store_sem.at[2 + g]
        )
        for g in range(4)
    ]
    for copy in frame_out:
        copy.start()
    keep_norm(slim_finish(1), slim_norm.at[1])

    def act_parts():
        center, rate = row16(slim_norm[1, 0:1]), row16(slim_norm[1, 1:2] * gains_mid[1:2])
        bias = row16(biases_mid[1:2])

        def body(pixel, row, across, carry):
            value = smooth_value((reduced[pixel] - center) * rate + bias).astype(BF)
            acts[pixel] = value
            lead = value.astype(F32)[0:8]
            halo_out[pixel] = jnp.concatenate([lead[:, 0:256], lead[:, 256:512]], axis=0).astype(BF)
            return carry

        pixels(body, 0)

    act_parts()
    halo_start(halo_out, halo_in, 3, -1)

    def change_early(pixel, row, across, carry):
        zero, one = halves(acts[pixel].astype(F32))
        change[pixel, 0] = (one - zero) * step_weight[0:8]
        change[pixel, 1] = one
        return carry

    pixels(change_early, 0)

    def lanes_of(tile):
        return pl.ds(pl.multiple_of(tile * 128, 128), 128)

    def inside(row, column):
        return 0 <= row < HEIGHT and 0 <= column < WIDTH

    def gate_tile(which):
        def body(tile, carry):
            lanes = lanes_of(tile)
            kernels = [depth[k, :, lanes] for k in range(18)]
            middle = kernels[4] + kernels[13]
            offsets = jnp.broadcast_to(gate_bias[0:1, lanes], (8, 128))
            field = [change[p, which, :, lanes] for p in range(PIX)]
            for i in range(HEIGHT):
                for j in range(WIDTH):
                    mixed = offsets + middle * field[i * WIDTH + j]
                    for base, taps in ((0, near_taps()), (9, far_taps())):
                        for k, (di, dj) in enumerate(taps):
                            if (di or dj) and inside(i + di, j + dj):
                                mixed = mixed + kernels[base + k] * field[(i + di) * WIDTH + j + dj]
                    gates[i * WIDTH + j, which, :, lanes] = 0.5 + 0.5 * jnp.tanh(0.5 * mixed)
            return carry

        lax.fori_loop(0, 4, body, 0)

    gate_tile(0)
    halo_finish(halo_out, halo_in, 3, -1)

    def change_late(pixel, row, across, carry):
        ahead = halo_in[pixel].astype(F32)
        after = jnp.concatenate([ahead[0:8], ahead[8:16]], axis=1)
        change[pixel, 1] = (after - change[pixel, 1]) * step_weight[8:16]
        return carry

    pixels(change_late, 0)
    gate_tile(1)

    for side in range(9):
        edge = jnp.zeros((16, COLUMNS), BF)
        for pad in (gated, back_pad):
            pad[0, side] = edge
            pad[8, side] = edge
            pad[side, 0] = edge
            pad[side, 8] = edge

    def gated_body(pixel, row, across, carry):
        both_gates = jnp.concatenate([gates[pixel, 0], gates[pixel, 1]], axis=0)
        gated[row + 1, across + 1] = (acts[pixel].astype(F32) * (1.0 + both_gates)).astype(BF)
        return carry

    pixels(gated_body, 0)

    loads["conv"].wait()

    def window(pad, a, b):
        return flat(pad[a : a + HEIGHT, b : b + WIDTH])

    for tile in range(2):
        at = pl.ds(tile * WIDE_TILE, WIDE_TILE)
        value = dot(window(gated, 0, 0), flat(conv_w[0, :, :, :, at]))
        for tap in range(1, 9):
            value = value + dot(window(gated, tap // 3, tap % 3), flat(conv_w[tap, :, :, :, at]))
        conv[:, :, :, at] = value.reshape(PIX, 2, 8, WIDE_TILE)
        slim_src[2, 0:1, at] = rows_sum(value)
        slim_src[2, 1:2, at] = rows_sum(value * value)
    slim_start(2)
    spill_out.wait()
    loads["expand"].wait()
    loads["cot"].wait()
    keep_norm(slim_finish(2), slim_norm.at[2])

    def conv_rows(pixel):
        return conv[pixel].reshape(16, COLUMNS)

    def conv_act_part():
        center, rate = row16(slim_norm[2, 0:1]), row16(slim_norm[2, 1:2] * gains_mid[2:3])
        bias = row16(biases_mid[2:3])

        def body(pixel, row, across, carry):
            conv_act[pixel] = smooth_value((conv_rows(pixel) - center) * rate + bias).astype(BF)
            return carry

        pixels(body, 0)

    conv_act_part()
    widen(conv_act, expand_w, 1)
    wide_start(1)
    keep_norm(wide_finish(1), wide_norm.at[1])

    def output_part(group, columns):
        center = row16(wide_norm[1, 0:1, columns])
        rate = row16(wide_norm[1, 1:2, columns])
        gain = row16(gains_wide[1:2, columns])
        bias = row16(biases_wide[1:2, columns])

        def body(pixel, row, across, carry):
            pool, shift, stretch = carry
            unit = (outer[pixel, :, columns] - center) * rate
            value, slope = smooth_pair(block_input[pixel, :, columns].astype(F32) + unit * gain + bias)
            incoming = cot[group * PIX + pixel].astype(F32) * slope
            cot[group * PIX + pixel] = value.astype(BF)
            skip[pixel, :, columns] = incoming
            return pool + fold(value), shift + fold(incoming), stretch + fold(incoming * unit)

        pool, shift, stretch = pixels(body, (slim_zero, slim_zero, slim_zero))
        video_src[group] = pool
        wide_src[2, 0:1, columns] = rows_sum(shift)
        wide_src[2, 1:2, columns] = rows_sum(stretch)

    wide_pixels(output_part)
    wide_start(2)
    act_out = [
        pltpu.make_async_copy(
            cot.at[pl.ds(g * PIX, PIX)], act_hbm.at[:, :, column_group(g)], store_sem.at[6 + g]
        )
        for g in range(4)
    ]
    for copy in act_out:
        copy.start()
    total = wide_finish(2)
    biases_wide_grad[1:2] = total[0:1]
    gains_wide_grad[1:2] = total[1:2]

    def wide_back(at, group, columns):
        center = row16(wide_norm[at, 0:1, columns])
        rate = row16(wide_norm[at, 1:2, columns])
        factor = rate * row16(gains_wide[at : at + 1, columns])
        shift = row16(biases_wide_grad[at : at + 1, columns] * scale)
        stretch = row16(gains_wide_grad[at : at + 1, columns] * scale) * rate

        def body(pixel, row, across, carry):
            value = skip[pixel, :, columns] - shift - (outer[pixel, :, columns] - center) * stretch
            wide[pixel, :, columns] = (value * factor).astype(BF)
            return carry

        pixels(body, 0)

    wide_pixels(functools.partial(wide_back, 1))
    spill_in = pltpu.make_async_copy(spill, outer, store_sem.at[0])
    spill_in.start()

    def narrow(weight):
        for tile in range(2):
            at = pl.ds(tile * WIDE_TILE, WIDE_TILE)
            value = dot_back(flat(wide[:, :, column_group(0)]), flat(weight[0, tile]))
            for g in range(1, 4):
                value = value + dot_back(flat(wide[:, :, column_group(g)]), flat(weight[g, tile]))
            temp[:, :, at] = value.reshape(PIX, 16, WIDE_TILE)

    narrow(expand_w)

    def slope_sums(source, norm, sums):
        center, rate = row16(slim_norm[norm, 0:1]), row16(slim_norm[norm, 1:2])
        gain, bias = row16(gains_mid[norm : norm + 1]), row16(biases_mid[norm : norm + 1])

        def body(pixel, row, across, carry):
            shift, stretch = carry
            unit = (source(pixel) - center) * rate
            unused, slope = smooth_pair(unit * gain + bias)
            value = temp[pixel] * slope
            temp[pixel] = value
            return shift + fold(value), stretch + fold(value * unit)

        shift, stretch = pixels(body, (slim_zero, slim_zero))
        slim_src[sums, 0:1] = rows_sum(shift)
        slim_src[sums, 1:2] = rows_sum(stretch)
        slim_start(sums)

    def slope_finish(source, norm, sums, store):
        total = slim_finish(sums)
        biases_mid_grad[norm : norm + 1] = total[0:1]
        gains_mid_grad[norm : norm + 1] = total[1:2]
        center, rate = row16(slim_norm[norm, 0:1]), row16(slim_norm[norm, 1:2])
        factor = rate * row16(gains_mid[norm : norm + 1])
        shift = row16(total[0:1] * scale)
        stretch = row16(total[1:2] * scale) * rate

        def body(pixel, row, across, carry):
            value = temp[pixel] - shift - (source(pixel) - center) * stretch
            store(pixel, row, across, (value * factor).astype(BF))
            return carry

        pixels(body, 0)

    for copy in act_out:
        copy.wait()
    for copy in frame_out:
        copy.wait()
    slope_sums(conv_rows, 2, 3)

    column, core = seg // 2, lax.rem(seg, 2)
    layer, line = clip // 2, lax.rem(clip, 2)
    to_core = {"seg": seg + 1 - 2 * core}
    to_column = {"seg": seg + 2 - 4 * column}
    to_corner = {"seg": 3 - seg}
    to_line = {"clip": clip + 1 - 2 * line}
    own = layer * 4 + line * 2

    class Ring:
        def __init__(self, at, slots, shared, single, places):
            self.at, self.slots, self.shared, self.single = at, slots, shared, single
            self.count = shared + 2 * single
            self.mine = shared + column * single
            self.other = shared + (1 - column) * single
            sizes = {
                "core": 16 * self.count, "line_a": 8 * shared, "layer_a": 8 * shared, "column_a": 2 * shared,
                "column_b": 16 * single, "line_b": 8 * single, "layer_b": 8 * single, "final": 4 * self.count,
            }
            self.land, self.kinds = {}, {}
            for number, (kind, size) in enumerate(sizes.items()):
                ref, base = places[kind]
                self.land[kind] = (ref, base)
                self.kinds[kind] = number

        def tiles(self, kind, start, size):
            ref, base = self.land[kind]
            return ref.at[pl.ds(base + start, size)]

        def send(self, kind, source, start, size, device):
            sems = [ring_sem.at[way, self.at, self.kinds[kind]] for way in range(2)]
            pltpu.make_async_remote_copy(
                source, self.tiles(kind, start, size), sems[0], sems[1],
                device_id=device, device_id_type=MESH,
            ).start()

        def wait(self, kind, size, sent=None):
            for way, amount in ((1, size), (0, size if sent is None else sent)):
                span = pool.at[pl.ds(0, amount)]
                pltpu.make_async_copy(span, span, ring_sem.at[way, self.at, self.kinds[kind]]).wait()

        def add(self, kind, amount, place, of_land=None):
            ref, base = self.land[kind]

            def body(tile, carry):
                slot, inside_slot = place(tile)
                value = self.slots[slot, core, inside_slot].astype(F32) + ref[base + tile].astype(F32)
                self.slots[slot, core, inside_slot] = value.astype(BF)
                return carry

            lax.fori_loop(0, amount, body, 0, unroll=2)

        def gather(self, kind, amount, slot_of, store):
            ref, base = self.land[kind]
            for item in range(amount):
                for half in range(2):
                    ref[pl.ds(base + (item * 4 + layer) * 2 + half, 1)] = self.slots[
                        slot_of(item), core, pl.ds(own + half, 1)
                    ]
                    value = ref[base + item * 8 + half].astype(F32)
                    for k in range(1, 4):
                        value = value + ref[base + (item * 4 + k) * 2 + half].astype(F32)
                    store(item, half, value.astype(BF))

        def stage0(self):
            for slot in range(self.count):
                self.send("core", self.slots.at[slot, 1 - core], slot * 16, 16, to_core)

        def send_line(self, kind, amount, slot_of):
            for item in range(amount):
                for k in range(4):
                    source = self.slots.at[slot_of(item), core, pl.ds(k * 4 + (1 - line) * 2, 2)]
                    self.send(kind, source, (item * 4 + k) * 2, 2, to_line)

        def send_layer(self, kind, amount, slot_of):
            for item in range(amount):
                for step in range(1, 4):
                    there = lax.rem(layer + step, 4)
                    source = self.slots.at[slot_of(item), core, pl.ds(there * 4 + line * 2, 2)]
                    self.send(kind, source, (item * 4 + layer) * 2, 2, {"clip": there * 2 + line})

        def stage1(self):
            self.wait("core", 16 * self.count)
            self.add("core", 16 * self.count, lambda tile: (tile // 16, lax.rem(tile, 16)))
            self.send_line("line_a", self.shared, lambda item: item)
            for item in range(self.single):
                self.send("column_b", self.slots.at[self.other + item, core], item * 16, 16, to_column)

        def line_place(self, first):
            return lambda tile: (
                first + tile // 8, lax.rem(tile, 8) // 2 * 4 + line * 2 + lax.rem(tile, 2)
            )

        def stage2(self):
            self.wait("line_a", 8 * self.shared)
            self.add("line_a", 8 * self.shared, self.line_place(0))
            self.send_layer("layer_a", self.shared, lambda item: item)
            self.wait("column_b", 16 * self.single)
            self.add("column_b", 16 * self.single, lambda tile: (self.mine + tile // 16, lax.rem(tile, 16)))
            self.send_line("line_b", self.single, lambda item: self.mine + item)

        def stage3(self):
            self.wait("line_b", 8 * self.single)
            self.add("line_b", 8 * self.single, self.line_place(self.mine))
            self.send_layer("layer_b", self.single, lambda item: self.mine + item)
            self.wait("layer_a", 6 * self.shared)

            def store(item, half, value):
                self.slots[item, core, pl.ds(own + half, 1)] = value[None]

            self.gather("layer_a", self.shared, lambda item: item, store)
            for item in range(self.shared):
                self.send("column_a", self.slots.at[item, core, pl.ds(own, 2)], item * 2, 2, to_column)

        def stage4(self):
            final, start = self.land["final"]
            here = start + core * self.count * 2
            self.wait("column_a", 2 * self.shared)
            ref, base = self.land["column_a"]
            for item in range(self.shared):
                for half in range(2):
                    value = (
                        self.slots[item, core, pl.ds(own + half, 1)].astype(F32)
                        + ref[base + item * 2 + half].astype(F32)[None]
                    )
                    final[pl.ds(here + item * 2 + half, 1)] = value.astype(BF)
                at = core * self.count * 2 + item * 2
                self.send("final", self.tiles("final", at, 2), at, 2, to_core)
            self.wait("layer_b", 6 * self.single)

            def store(item, half, value):
                final[pl.ds(here + (self.mine + item) * 2 + half, 1)] = value[None]

            self.gather("layer_b", self.single, lambda item: self.mine + item, store)
            for item in range(self.single):
                at = (core * self.count + self.mine + item) * 2
                for device in (to_core, to_column, to_corner):
                    self.send("final", self.tiles("final", at, 2), at, 2, device)

        def stage5(self):
            arrive = 2 * (self.shared + 3 * self.single)
            self.wait("final", arrive)

        def result(self, half, slot, part):
            final, start = self.land["final"]
            return final[start + (half * self.count + slot) * 2 + part].astype(F32)

    KINDS = ("core", "line_a", "layer_a", "column_a", "column_b", "line_b", "layer_b", "final")

    def places(spans):
        return {kind: span for kind, span in zip(KINDS, spans)}

    def packed(ref, start, shared, single):
        count = shared + 2 * single
        sizes = (16 * count, 8 * shared, 8 * shared, 2 * shared, 16 * single, 8 * single, 8 * single, 4 * count)
        spans = []
        for size in sizes:
            spans.append((ref, start))
            start = start + size
        return places(spans)

    ring_expand = Ring(0, expand_w, 2, 1, packed(cot, 0, 2, 1))
    ring_conv = Ring(1, conv_w, 5, 2, packed(pool, 0, 5, 2))
    ring_reduce = Ring(2, reduce_w, 2, 1, packed(frame, 0, 2, 1))
    ring_up = Ring(3, up, 2, 1, packed(cot, 0, 2, 1))
    ring_down = Ring(
        4, expand_w, 2, 1,
        places(
            (
                (pool, 334), (frame, 148), (cot, 148), (cot, 164),
                (frame, 164), (cot, 168), (cot, 176), (frame, 180),
            )
        ),
    )

    def put_rows(slots, slot, value):
        parts = value.astype(BF).reshape(8, 2, 2, 16, COLUMNS)
        for half in range(2):
            slots[slot, half] = parts[:, half].reshape(16, 16, COLUMNS)

    def wide_weight_grad(left, slots):
        def body(slot, carry):
            columns = pl.ds(pl.multiple_of(slot * COLUMNS, COLUMNS), COLUMNS)
            put_rows(slots, slot, dot_rows(flat(left[...]), flat(wide[:, :, columns])))
            return carry

        lax.fori_loop(0, 4, body, 0)

    def tall_weight_grad(left, slots):
        def body(block, carry):
            columns = pl.ds(pl.multiple_of(block * WIDE_TILE, WIDE_TILE), WIDE_TILE)
            value = dot_rows(flat(left[:, :, columns]), flat(back[...])).astype(BF)
            parts = value.reshape(2, 4, 2, 16, COLUMNS)
            for half in range(2):
                for slot in range(4):
                    slots[slot, half, pl.ds(block * 2, 2)] = parts[half, slot]
            return carry

        lax.fori_loop(0, 8, body, 0)

    def conv_weight_grad():
        for tap in range(9):
            put_rows(conv_w, tap, dot_rows(window(gated, tap // 3, tap % 3), window(back_pad, 1, 1)))

    wide_weight_grad(conv_act, expand_w)

    def store_conv(pixel, row, across, value):
        back_pad[row + 1, across + 1] = value

    slope_finish(conv_rows, 2, 3, store_conv)
    ring_expand.stage0()

    grad_gated = conv_act
    for tile in range(2):
        at = pl.ds(tile * WIDE_TILE, WIDE_TILE)
        value = dot_back(window(back_pad, 2, 2), flat(conv_w[0, tile]))
        for tap in range(1, 9):
            value = value + dot_back(window(back_pad, 2 - tap // 3, 2 - tap % 3), flat(conv_w[tap, tile]))
        grad_gated[:, :, at] = value.astype(BF).reshape(PIX, 16, WIDE_TILE)
    ring_expand.stage1()

    grad_mixed = conv

    def mixed_body(pixel, row, across, carry):
        incoming = grad_gated[pixel].astype(F32)
        both_gates = jnp.concatenate([gates[pixel, 0], gates[pixel, 1]], axis=0)
        value = incoming * acts[pixel].astype(F32) * both_gates * (1.0 - both_gates)
        grad_mixed[pixel] = value.reshape(2, 8, COLUMNS)
        temp[pixel] = incoming * (1.0 + both_gates)
        return carry

    pixels(mixed_body, 0)
    weighted = gates

    def gate_back_tile(which):
        def body(tile, carry):
            lanes = lanes_of(tile)
            kernels = [depth[k, :, lanes] for k in range(18)]
            middle = kernels[4] + kernels[13]
            weight = step_weight[which * 8 : which * 8 + 8, 0:128]
            field = [grad_mixed[p, which, :, lanes] for p in range(PIX)]
            for i in range(HEIGHT):
                for j in range(WIDTH):
                    value = middle * field[i * WIDTH + j]
                    for base, taps in ((0, near_taps()), (9, far_taps())):
                        for k, (di, dj) in enumerate(taps):
                            if (di or dj) and inside(i - di, j - dj):
                                value = value + kernels[base + k] * field[(i - di) * WIDTH + j - dj]
                    weighted[i * WIDTH + j, which, :, lanes] = value * weight
            return carry

        lax.fori_loop(0, 4, body, 0)

    def depth_grad_tile():
        def body(tile, carry):
            lanes = lanes_of(tile)
            totals = [None] * 19
            for which in range(2):
                field = [grad_mixed[p, which, :, lanes] for p in range(PIX)]

                def grow(k, term):
                    totals[k] = term if totals[k] is None else totals[k] + term

                for p in range(PIX):
                    grow(18, field[p])
                for base, taps in ((0, near_taps()), (9, far_taps())):
                    for k, (di, dj) in enumerate(taps):
                        for i in range(HEIGHT):
                            for j in range(WIDTH):
                                if inside(i + di, j + dj):
                                    there = (i + di) * WIDTH + j + dj
                                    grow(base + k, field[i * WIDTH + j] * change[there, which, :, lanes])
            for k in range(19):
                video_src[4 + k // 8, k % 8 : k % 8 + 1, lanes] = rows_sum(totals[k])
            return carry

        lax.fori_loop(0, 4, body, 0)
        video_src[6, 3:8] = jnp.zeros((5, COLUMNS), F32)

    gate_back_tile(1)

    def weighted_pack(pixel, row, across, carry):
        last = weighted[pixel, 1]
        halo_out[pixel] = jnp.concatenate([last[:, 0:256], last[:, 256:512]], axis=0).astype(BF)
        return carry

    pixels(weighted_pack, 0)
    halo_start(halo_out, halo_in, 4, 1)
    gate_back_tile(0)
    ring_expand.stage2()
    depth_grad_tile()
    halo_finish(halo_out, halo_in, 4, 1)

    def act_grad_body(pixel, row, across, carry):
        ahead = halo_in[pixel].astype(F32)
        before = jnp.concatenate([ahead[0:8], ahead[8:16]], axis=1)
        zero, one = weighted[pixel, 0], weighted[pixel, 1]
        value = temp[pixel] + jnp.concatenate([before - zero, zero - one], axis=0)
        temp[pixel] = value.astype(BF).astype(F32)
        return carry

    pixels(act_grad_body, 0)

    def reduced_rows(pixel):
        return reduced[pixel]

    slope_sums(reduced_rows, 1, 4)
    ring_expand.stage3()
    conv_weight_grad()
    ring_conv.stage0()

    def store_back(pixel, row, across, value):
        back[pixel] = value

    slope_finish(reduced_rows, 1, 4, store_back)
    ring_expand.stage4()

    def video_span(way, at, ref):
        pltpu.make_async_copy(ref, ref, video_sem.at[way, at]).wait()

    def seg_spread(source, target, at):
        for step in range(1, segs):
            pltpu.make_async_remote_copy(
                source, target, video_sem.at[0, at], video_sem.at[1, at],
                device_id={"seg": lax.rem(seg + step, segs)}, device_id_type=MESH,
            ).start()

    def video_first():
        seg_spread(video_src, change.at[pl.ds(seg * 7, 7), 0], 0)
        change[pl.ds(seg * 7, 7), 0] = video_src[...]

    def video_second():
        for way in range(2):
            video_span(way, 0, change.at[pl.ds(0, 21), 0])

        def total(read):
            value = read(0)
            for rank in range(1, segs):
                value = value + read(rank * 7)
            return value

        quarter = pl.ds(pl.multiple_of(seg * 128, 128), 128)
        conv[clip, 0] = total(lambda base: change[base + seg, 0])
        for k in range(3):
            conv[clip, 1, :, pl.ds(k * 128, 128)] = total(lambda base: change[base + 4 + k, 0, :, quarter])
        conv[clip, 1, :, pl.ds(384, 128)] = crop_id[...]
        for step in range(1, clips):
            pltpu.make_async_remote_copy(
                conv.at[clip], conv.at[clip], video_sem.at[0, 1], video_sem.at[1, 1],
                device_id={"clip": lax.rem(clip + step, clips)}, device_id_type=MESH,
            ).start()

    def video_third():
        for way in range(2):
            video_span(way, 1, conv.at[pl.ds(0, clips - 1)])
        sums = jnp.concatenate([conv[k, 0] for k in range(clips)], axis=0)
        names = jnp.concatenate([conv[k, 1, :, pl.ds(384, 128)] for k in range(clips)], axis=0)
        lane = lax.broadcasted_iota(jnp.int32, names.shape, 1).astype(F32)
        member = (names == lane).astype(F32)

        def gather(values):
            return lax.dot_general(
                member, values, (((0,), (0,)), ((), ())),
                precision=lax.Precision.HIGHEST, preferred_element_type=F32,
            )[0:32]

        counts = gather(jnp.ones_like(names))
        means = gather(sums) / jnp.concatenate([counts * (SEGS * PIX)] * 4, axis=1)
        grads = conv[0, 1]
        for k in range(1, clips):
            grads = grads + conv[k, 1]
        gates[pl.ds(seg * 5, 4), 0] = means.reshape(4, 8, COLUMNS)
        gates[pl.ds(seg * 5 + 4, 1), 0] = grads[None]
        mine = gates.at[pl.ds(seg * 5, 5), 0]
        seg_spread(mine, mine, 2)

    def video_last():
        for way in range(2):
            video_span(way, 2, gates.at[pl.ds(0, 15), 0])
        for rank in range(segs):
            for k in range(4):
                video_means[k * 8 : k * 8 + 8, column_group(rank)] = gates[rank * 5 + k, 0]
            for k in range(3):
                depth_grad[k * 8 : k * 8 + 8, pl.ds(rank * 128, 128)] = gates[
                    rank * 5 + 4, 0, :, pl.ds(k * 128, 128)
                ]

    video_first()

    spill_in.wait()

    def input_grad(tile, carry):
        at = pl.ds(pl.multiple_of(tile * WIDE_TILE, WIDE_TILE), WIDE_TILE)
        weight = flat(reduce_w[tile // 2, lax.rem(tile, 2)])
        value = dot_back(flat(back[...]), weight) + flat(skip[:, :, at])
        skip[:, :, at] = value.reshape(PIX, 16, WIDE_TILE)
        unit = (flat(outer[:, :, at]) - wide_norm[0, 0:1, at]) * wide_norm[0, 1:2, at]
        wide_src[3, 0:1, at] = rows_sum(value)
        wide_src[3, 1:2, at] = rows_sum(value * unit)
        return carry

    lax.fori_loop(0, 2048 // WIDE_TILE, input_grad, 0)
    ring_conv.stage1()
    ring_expand.stage5()
    expand_kept = [
        [ring_expand.result(half, slot, part) for part in range(2)] for half in range(2) for slot in range(4)
    ]
    for index, pair in enumerate(expand_kept):
        for part in range(2):
            reduced[index * 2 + part] = pair[part]
    wide_start(3)
    video_second()
    tall_weight_grad(block_input, reduce_w)
    ring_reduce.stage0()
    frame_in = pltpu.make_async_copy(frame_spill, tok, store_sem.at[1])
    frame_in.start()
    total = wide_finish(3)
    biases_wide_grad[0:1] = total[0:1]
    gains_wide_grad[0:1] = total[1:2]
    wide_pixels(functools.partial(wide_back, 0))
    ring_reduce.stage1()
    narrow(up)
    ring_conv.stage2()

    def inner_rows(pixel):
        return inner[pixel]

    slope_sums(inner_rows, 0, 5)
    wide_weight_grad(active, up)
    ring_up.stage0()
    video_third()
    ring_reduce.stage2()
    slope_finish(inner_rows, 0, 5, store_back)

    def last_pack(pixel, row, across, carry):
        last = back[pixel].astype(F32)[8:16]
        halo_out[pixel] = jnp.concatenate([last[:, 0:256], last[:, 256:512]], axis=0).astype(BF)
        return carry

    pixels(last_pack, 0)
    halo_start(halo_out, halo_in, 5, 1)
    ring_up.stage1()
    frame_in.wait()
    tall_weight_grad(tok, expand_w)
    ring_down.stage0()
    ring_conv.stage3()
    halo_finish(halo_out, halo_in, 5, 1)

    def change_grad(pixel, row, across, carry):
        ahead = halo_in[pixel].astype(F32)
        before = jnp.concatenate([ahead[0:8], ahead[8:16]], axis=1) * past_weight[...]
        zero, one = halves(back[pixel].astype(F32) * step_weight[...])
        active[pixel] = jnp.concatenate([before - zero, zero - one], axis=0).astype(BF)
        return carry

    pixels(change_grad, 0)
    ring_down.stage1()
    ring_reduce.stage3()
    ring_up.stage2()

    def tokens_part(tile):
        at = pl.ds(tile * WIDE_TILE, WIDE_TILE)
        return pltpu.make_async_copy(
            skip.at[:, :, at], tokens_grad_hbm.at[:, :, at], store_sem.at[11 + tile]
        )

    for tile in range(8):
        at = pl.ds(tile * WIDE_TILE, WIDE_TILE)
        value = dot_back(flat(active[...]), flat(down[tile // 2, tile % 2])) + flat(skip[:, :, at])
        skip[:, :, at] = value.reshape(PIX, 16, WIDE_TILE)
        tokens_part(tile).start()

    ring_conv.stage4()
    ring_down.stage2()
    ring_reduce.stage4()
    ring_up.stage3()
    ring_down.stage3()
    ring_conv.stage5()
    ring_up.stage4()
    ring_reduce.stage5()
    video_last()

    def flush(index, source, target):
        copy = pltpu.make_async_copy(source, target, store_sem.at[20 + index])
        copy.start()
        return copy

    def tall_out(index, ring, target, first):
        for half in range(2):
            for slot in range(4):
                for part in range(2):
                    outer[first + half * 8 + slot * 2 + part, :, column_group(1)] = ring.result(half, slot, part)
        return flush(index, outer.at[pl.ds(first, 16), :, column_group(1)], target)

    def wide_out(index, read, target, first):
        for half in range(2):
            for slot in range(4):
                for part in range(2):
                    outer[first + half * 2 + part, :, column_group(slot)] = read(half, slot, part)
        return flush(index, outer.at[pl.ds(first, 4)], target)

    copies = [wide_out(0, lambda half, slot, part: reduced[(half * 4 + slot) * 2 + part], expand_grad, 40)]
    for tap in range(9):
        for half in range(2):
            for part in range(2):
                outer[tap * 4 + half * 2 + part, :, column_group(0)] = ring_conv.result(half, tap, part)
    copies.append(flush(1, outer.at[pl.ds(0, 36), :, column_group(0)], conv_grad))
    copies.append(tall_out(2, ring_reduce, reduce_grad, 16))
    ring_down.stage4()
    ring_up.stage5()
    copies.append(wide_out(3, ring_up.result, up_grad, 36))
    ring_down.stage5()
    copies.append(tall_out(4, ring_down, down_grad, 0))
    for tile in range(8):
        tokens_part(tile).wait()
    for copy in copies:
        copy.wait()


def fused_body(
    tokens, segment_index, crop_video, stem_down, stem_up, reduce_weight, conv_weight, expand_weight,
    depth_near, depth_far, gate_bias, gains_mid, biases_mid, gains_wide, biases_wide, cotangent,
):
    segs, clips = lax.axis_size("seg"), lax.axis_size("clip")
    seg_here = lax.axis_index("seg")
    amount = tokens.shape[0] * tokens.shape[1] * PIX * segs * clips
    spacing = (segment_index[:, 1:] - segment_index[:, :-1]).astype(F32)
    full_weight = jnp.concatenate([1.0 / spacing, jnp.zeros((spacing.shape[0], 1), F32)], axis=1)
    padded_weight = jnp.concatenate([jnp.zeros((spacing.shape[0], 1), F32), full_weight], axis=1)
    three = lax.dynamic_slice_in_dim(padded_weight, seg_here * 2, 3, 1).T.reshape(24, 1)
    three = jnp.broadcast_to(three, (24, COLUMNS))
    past_weight, step_weight = three[0:8], three[8:24]
    crop_id = jnp.broadcast_to(crop_video.astype(F32)[:, None], (8, 128))

    def rows_first(field):
        return field.transpose(2, 1, 0, 3).reshape(PIX, 16, 2048)

    depth = jnp.broadcast_to(
        jnp.concatenate([depth_near, depth_far], axis=0)[:, None, :], (18, 8, COLUMNS)
    )
    whole = pl.BlockSpec(memory_space=pl.ANY)
    near = pl.BlockSpec(memory_space=pltpu.VMEM)
    field = (PIX, 16, 2048)
    slim = (PIX, 16, COLUMNS)
    split = (PIX, 2, 8, COLUMNS)
    out_shapes = (
        (field, BF, whole), (field, F32, whole),
        ((16, 16, 512), F32, whole), ((4, 16, 2048), F32, whole), ((16, 16, 512), F32, whole),
        ((36, 16, 512), F32, whole), ((4, 16, 2048), F32, whole), (field, F32, whole), (field, BF, whole),
        ((32, 2048), F32, near), ((24, 512), F32, near),
        ((3, 512), F32, near), ((3, 512), F32, near), ((2, 2048), F32, near), ((2, 2048), F32, near),
    )
    tiles = (4 * PIX, 16, COLUMNS)
    weight = (4, 2, 16, 16, COLUMNS)
    scratch = [
        pltpu.VMEM(field, BF), pltpu.VMEM(tiles, BF), pltpu.VMEM(field, F32), pltpu.VMEM(field, F32),
        pltpu.VMEM(tiles, BF), pltpu.VMEM(field, BF),
        pltpu.VMEM(slim, F32), pltpu.VMEM(slim, BF), pltpu.VMEM(slim, F32), pltpu.VMEM(slim, BF),
        pltpu.VMEM(split, F32), pltpu.VMEM(split, F32), pltpu.VMEM(split, F32), pltpu.VMEM(slim, BF),
        pltpu.VMEM((9, 9, 16, 512), BF), pltpu.VMEM((9, 9, 16, 512), BF),
        pltpu.VMEM(slim, F32), pltpu.VMEM(slim, BF),
        pltpu.VMEM((PIX, 16, 256), BF), pltpu.VMEM((PIX, 16, 256), BF),
        pltpu.VMEM(weight, BF), pltpu.VMEM(weight, BF), pltpu.VMEM(weight, BF),
        pltpu.VMEM((9,) + weight[1:], BF), pltpu.VMEM(weight, BF),
        pltpu.VMEM((6, 2, 512), F32), pltpu.VMEM((6, segs * clips, 2, 512), F32),
        pltpu.VMEM((4, 2, 2048), F32), pltpu.VMEM((4, 2, 2048), F32),
        pltpu.VMEM((4, segs, 2, 2048), F32), pltpu.VMEM((4, clips, 2, 2048), F32),
        pltpu.VMEM((3, 2, 512), F32), pltpu.VMEM((2, 2, 2048), F32),
        pltpu.VMEM((POOL_TILES, 16, COLUMNS), BF), pltpu.VMEM((7, 8, COLUMNS), F32),
        pltpu.SemaphoreType.DMA((16,)), pltpu.SemaphoreType.DMA((32,)), pltpu.SemaphoreType.DMA((2, 6)),
        pltpu.SemaphoreType.DMA((2, 6)), pltpu.SemaphoreType.DMA((4, 4)),
        pltpu.SemaphoreType.DMA((2, 5, 8)), pltpu.SemaphoreType.DMA((2, 3)),
    ]
    outs = pl.pallas_call(
        functools.partial(block_kernel, segs, clips, amount),
        out_shape=tuple(jax.ShapeDtypeStruct(s, d) for s, d, unused in out_shapes),
        in_specs=[whole] * 7 + [near] * 9,
        out_specs=tuple(m for unused, unused_too, m in out_shapes),
        scratch_shapes=scratch,
        compiler_params=pltpu.CompilerParams(
            collective_id=0, has_side_effects=True, vmem_limit_bytes=VMEM_BYTES
        ),
    )(
        rows_first(tokens), rows_first(cotangent), stem_down.reshape(weight),
        stem_up.reshape(2, 16, 16, 2048), reduce_weight.reshape(weight),
        conv_weight.reshape((9,) + weight[1:]), expand_weight.reshape(2, 16, 16, 2048),
        depth, gate_bias[None], gains_mid, biases_mid, gains_wide, biases_wide,
        step_weight, past_weight, crop_id,
    )
    (
        act, tokens_grad, down_grad, up_grad, reduce_grad, conv_grad, expand_grad, unused, unused_too,
        video_means, depth_sum, gains_mid_grad, biases_mid_grad, gains_wide_grad, biases_wide_grad,
    ) = outs

    def clips_first(value):
        return value.reshape(PIX, 2, 8, 2048).transpose(2, 1, 0, 3)

    return (
        clips_first(act),
        video_means,
        clips_first(tokens_grad),
        down_grad.reshape(256, 512),
        up_grad.reshape(64, 2048),
        reduce_grad.reshape(256, 512),
        conv_grad.reshape(9, 64, 512),
        expand_grad.reshape(64, 2048),
        depth_sum[0:9],
        depth_sum[9:18],
        depth_sum[18],
        gains_mid_grad,
        biases_mid_grad,
        gains_wide_grad,
        biases_wide_grad,
    )


POOL_TILES = 334 + 64
VMEM_BYTES = 63 << 20


def solution(mesh):
    def either(tokens, *others):
        fits = tokens.shape == (8, 2, PIX, 2048) and (lax.axis_size("seg"), lax.axis_size("clip")) == (4, 8)
        return (fused_body if fits else body)(tokens, *others)

    return jax.shard_map(
        either,
        mesh=mesh,
        in_specs=(
            P("clip", "seg", None, None),
            P("clip", None),
            P("clip"),
            P(),
            P(),
            P(),
            P(),
            P(),
            P(),
            P(),
            P(),
            P(),
            P(),
            P(),
            P(),
            P("clip", "seg", None, None),
        ),
        out_specs=(
            P("clip", "seg", None, None),
            P(),
            P("clip", "seg", None, None),
            P("clip", None),
            P("clip", None),
            P("clip", None),
            P(None, "clip", None),
            P("clip", None),
            P(),
            P(),
            P(),
            P(),
            P(),
            P(),
            P(),
        ),
        check_vma=False,
    )
```

```python
import functools

import jax
import jax.numpy as jnp
from jax import lax
from jax.experimental import pallas as pl
from jax.experimental.pallas import tpu as pltpu
from jax.sharding import PartitionSpec as P

HEIGHT = 7
WIDTH = 7
SEGS = 8
PIX = 49


NORM_EPSILON = 1e-05


MESH = pl.DeviceIdType.MESH


def exchange(source, landing, send_sem, recv_sem, axis, count):
    here = lax.axis_index(axis)
    for step in range(1, count):
        pltpu.make_async_remote_copy(
            source,
            landing.at[here],
            send_sem,
            recv_sem,
            device_id={axis: lax.rem(here + step, count)},
            device_id_type=MESH,
        ).start()
    landing[pl.ds(here, 1)] = source[...][None]
    arrived = landing.at[pl.ds(0, count - 1)]
    pltpu.make_async_copy(arrived, arrived, recv_sem).wait()
    total = landing[0]
    for rank in range(1, count):
        total = total + landing[rank]
    pltpu.make_async_copy(arrived, arrived, send_sem).wait()
    return total


def sum_kernel(segs, clips, values, result, middle, seg_land, clip_land, sems):
    barrier = pltpu.get_barrier_semaphore()
    for axis, count in (("seg", segs), ("clip", clips)):
        here = lax.axis_index(axis)
        for step in range(1, count):
            pl.semaphore_signal(
                barrier,
                inc=1,
                device_id={axis: lax.rem(here + step, count)},
                device_id_type=MESH,
            )
    pl.semaphore_wait(barrier, segs + clips - 2)
    middle[...] = exchange(values, seg_land, sems.at[0], sems.at[1], "seg", segs)
    result[...] = exchange(middle, clip_land, sems.at[2], sems.at[3], "clip", clips)


def sum_everywhere(first, second):
    segs, clips = lax.axis_size("seg"), lax.axis_size("clip")
    width = first.shape[0]
    summed = pl.pallas_call(
        functools.partial(sum_kernel, segs, clips),
        out_shape=jax.ShapeDtypeStruct((2, width), jnp.float32),
        in_specs=[pl.BlockSpec(memory_space=pltpu.VMEM)],
        out_specs=pl.BlockSpec(memory_space=pltpu.VMEM),
        scratch_shapes=[
            pltpu.VMEM((2, width), jnp.float32),
            pltpu.VMEM((segs, 2, width), jnp.float32),
            pltpu.VMEM((clips, 2, width), jnp.float32),
            pltpu.SemaphoreType.DMA((4,)),
        ],
        compiler_params=pltpu.CompilerParams(
            collective_id=0 if width < 1024 else 1, has_side_effects=True
        ),
    )(jnp.stack([first, second]))
    return summed[0], summed[1]


def shifted(block, axis, distance):
    devices = range(lax.axis_size(axis))
    route = [(i - distance, i) for i in devices if i - distance in devices]
    return lax.ppermute(block, axis, route)


def row_product(left_side, weight):
    return lax.dot_general(
        left_side,
        weight,
        (((left_side.ndim - 1,), (0,)), ((), ())),
        preferred_element_type=jnp.float32,
    )


def back_product(gradient, weight):
    return lax.dot_general(
        gradient,
        weight,
        (((gradient.ndim - 1,), (1,)), ((), ())),
        preferred_element_type=jnp.float32,
    )


def weight_gradient(left_side, gradient):
    return jnp.einsum("cspk,cspo->ko", left_side, gradient, preferred_element_type=jnp.float32)


def smooth(values):
    return jax.nn.gelu(values, approximate=True)


def depth_conv(field, kernel, reach):
    leading = field.shape[:2]
    planes = field.reshape(leading + (HEIGHT, WIDTH, field.shape[3]))
    padded = jnp.pad(planes, ((0, 0), (0, 0), (reach, reach), (reach, reach), (0, 0)))
    result = jnp.zeros_like(planes)
    for position in range(9):
        down = position // 3 * reach
        across = position % 3 * reach
        result = (
            result
            + padded[:, :, down : down + HEIGHT, across : across + WIDTH, :] * kernel[position]
        )
    return result.reshape(field.shape)


def gate_apply(active, change, near_kernel, far_kernel, offsets):
    mixed = depth_conv(change, near_kernel, 1) + depth_conv(change, far_kernel, 2) + offsets
    return active * (1.0 + jax.nn.sigmoid(mixed))


def frame_planes(field):
    planes = field.reshape(field.shape[:2] + (HEIGHT, WIDTH, field.shape[3]))
    return jnp.pad(planes, ((0, 0), (0, 0), (1, 1), (1, 1), (0, 0)))


def frame_conv(field, weight):
    padded = frame_planes(field)
    result = jnp.zeros(field.shape[:2] + (HEIGHT, WIDTH, weight.shape[2]), jnp.float32)
    for position in range(9):
        down = position // 3
        across = position % 3
        result = result + row_product(
            padded[:, :, down : down + HEIGHT, across : across + WIDTH, :], weight[position]
        )
    return result.reshape(field.shape[:3] + (weight.shape[2],))


def frame_conv_back(field, weight, gradient):
    padded = frame_planes(field)
    planes = gradient.reshape(gradient.shape[:2] + (HEIGHT, WIDTH, gradient.shape[3]))
    field_grad = jnp.zeros(padded.shape, jnp.float32)
    kernel_grads = []
    for position in range(9):
        down = position // 3
        across = position % 3
        window = padded[:, :, down : down + HEIGHT, across : across + WIDTH, :]
        kernel_grads.append(
            jnp.einsum("csijk,csijo->ko", window, planes, preferred_element_type=jnp.float32)
        )
        field_grad = field_grad.at[:, :, down : down + HEIGHT, across : across + WIDTH, :].add(
            back_product(planes, weight[position])
        )
    inner = field_grad[:, :, 1 : 1 + HEIGHT, 1 : 1 + WIDTH, :]
    return (inner.reshape(field.shape), jnp.stack(kernel_grads))


def body(
    tokens,
    segment_index,
    crop_video,
    stem_down,
    stem_up,
    reduce_weight,
    conv_weight,
    expand_weight,
    depth_near,
    depth_far,
    gate_bias,
    gains_mid,
    biases_mid,
    gains_wide,
    biases_wide,
    cotangent,
):
    seg_count = lax.axis_size("seg")
    clip_count = lax.axis_size("clip")
    seg_here = lax.axis_index("seg")
    local_segs = tokens.shape[1]
    amount = tokens.shape[0] * local_segs * tokens.shape[2] * seg_count * clip_count
    spacing = (segment_index[:, 1:] - segment_index[:, :-1]).astype(jnp.float32)
    full_weight = jnp.concatenate(
        [1.0 / spacing, jnp.zeros((spacing.shape[0], 1), jnp.float32)], axis=1
    )
    local_weight = lax.dynamic_slice_in_dim(full_weight, seg_here * local_segs, local_segs, 1)

    def gather_stats(values):
        return sum_everywhere(
            jnp.sum(values, axis=(0, 1, 2)), jnp.sum(values * values, axis=(0, 1, 2))
        )

    def normalize(values, first_sum, second_sum, scales, shifts):
        center = first_sum / amount
        spread = second_sum / amount - center * center
        return (values - center) * lax.rsqrt(spread + NORM_EPSILON) * scales + shifts

    def norm_smooth(values, first_sum, second_sum, scales, shifts):
        return smooth(normalize(values, first_sum, second_sum, scales, shifts))

    def block_finish(values, first_sum, second_sum, scales, shifts, skipped):
        return smooth(skipped + normalize(values, first_sum, second_sum, scales, shifts))

    def norm_back(piece, primals, gradient):
        unused, pull = jax.vjp(piece, *primals)
        pulled = pull(gradient)
        first_grad, second_grad = sum_everywhere(pulled[1], pulled[2])
        values = primals[0]
        return (pulled[0] + first_grad + 2.0 * values * second_grad,) + tuple(pulled[3:])

    frames = tokens.astype(jnp.float32)
    following = shifted(tokens[:, :1], "seg", -1).astype(jnp.float32)
    later = jnp.concatenate([frames[:, 1:], following], axis=1)
    frame_change = ((later - frames) * local_weight[:, :, None, None]).astype(jnp.bfloat16)
    stem_inner = row_product(frame_change, stem_down)
    inner_sums = gather_stats(stem_inner)
    stem_active = norm_smooth(
        stem_inner, inner_sums[0], inner_sums[1], gains_mid[0], biases_mid[0]
    ).astype(jnp.bfloat16)
    stem_outer = row_product(stem_active, stem_up)
    outer_sums = gather_stats(stem_outer)
    block_input = (
        frames + normalize(stem_outer, outer_sums[0], outer_sums[1], gains_wide[0], biases_wide[0])
    ).astype(jnp.bfloat16)
    reduced = row_product(block_input, reduce_weight)
    reduced_sums = gather_stats(reduced)
    reduced_act = norm_smooth(
        reduced, reduced_sums[0], reduced_sums[1], gains_mid[1], biases_mid[1]
    ).astype(jnp.bfloat16)
    channel_act = lax.all_to_all(
        reduced_act, "seg", split_axis=3, concat_axis=1, tiled=True
    ).astype(jnp.float32)
    narrow = channel_act.shape[3]
    near_local = lax.dynamic_slice_in_dim(depth_near, seg_here * narrow, narrow, 1)
    far_local = lax.dynamic_slice_in_dim(depth_far, seg_here * narrow, narrow, 1)
    offset_local = lax.dynamic_slice_in_dim(gate_bias, seg_here * narrow, narrow, 0)
    shifted_act = jnp.concatenate([channel_act[:, 1:], jnp.zeros_like(channel_act[:, :1])], axis=1)
    act_change = (shifted_act - channel_act) * full_weight[:, :, None, None]
    gated_channels = gate_apply(
        channel_act, act_change, near_local, far_local, offset_local
    ).astype(jnp.bfloat16)
    gated = lax.all_to_all(gated_channels, "seg", split_axis=1, concat_axis=3, tiled=True)
    convolved = frame_conv(gated, conv_weight)
    conv_sums = gather_stats(convolved)
    conv_act = norm_smooth(
        convolved, conv_sums[0], conv_sums[1], gains_mid[2], biases_mid[2]
    ).astype(jnp.bfloat16)
    expanded = row_product(conv_act, expand_weight)
    expanded_sums = gather_stats(expanded)
    residual = block_input.astype(jnp.float32)
    block_output = block_finish(
        expanded, expanded_sums[0], expanded_sums[1], gains_wide[1], biases_wide[1], residual
    )
    activations = block_output.astype(jnp.bfloat16)
    video_total = tokens.shape[0] * clip_count // 2
    pooled = jnp.sum(block_output, axis=(1, 2)) / (SEGS * PIX)
    membership = (crop_video[:, None] == jnp.arange(video_total, dtype=jnp.int32)[None, :]).astype(
        jnp.float32
    )
    video_part = jnp.dot(membership.T, pooled, precision=lax.Precision.HIGHEST)
    count_part = jnp.sum(membership, axis=0) * (seg_here == 0).astype(jnp.float32)
    video_sums, video_counts = lax.psum((video_part, count_part), ("seg", "clip"))
    video_means = video_sums / video_counts[:, None]
    grad_output = cotangent.astype(jnp.float32)
    grad_expanded, wide_gain_one, wide_bias_one, grad_skip = norm_back(
        block_finish,
        (expanded, expanded_sums[0], expanded_sums[1], gains_wide[1], biases_wide[1], residual),
        grad_output,
    )
    grad_expanded = grad_expanded.astype(jnp.bfloat16)
    expand_grad = weight_gradient(conv_act, grad_expanded)
    grad_conv_act = back_product(grad_expanded, expand_weight)
    grad_convolved, mid_gain_two, mid_bias_two = norm_back(
        norm_smooth,
        (convolved, conv_sums[0], conv_sums[1], gains_mid[2], biases_mid[2]),
        grad_conv_act,
    )
    grad_convolved = grad_convolved.astype(jnp.bfloat16)
    grad_gated, conv_grad = frame_conv_back(gated, conv_weight, grad_convolved)
    grad_gated = grad_gated.astype(jnp.bfloat16)
    grad_gated_channels = lax.all_to_all(
        grad_gated, "seg", split_axis=3, concat_axis=1, tiled=True
    ).astype(jnp.float32)
    unused_gate, gate_pull = jax.vjp(
        gate_apply, channel_act, act_change, near_local, far_local, offset_local
    )
    grad_direct, grad_change, near_part, far_part, offset_part = gate_pull(grad_gated_channels)
    weighted = grad_change * full_weight[:, :, None, None]
    grad_act_channels = (
        grad_direct
        + jnp.concatenate([jnp.zeros_like(weighted[:, :1]), weighted[:, :-1]], axis=1)
        - weighted
    ).astype(jnp.bfloat16)
    grad_reduced_act = lax.all_to_all(
        grad_act_channels, "seg", split_axis=1, concat_axis=3, tiled=True
    ).astype(jnp.float32)
    near_grad = lax.dynamic_update_slice_in_dim(
        jnp.zeros_like(depth_near), near_part, seg_here * narrow, 1
    )
    far_grad = lax.dynamic_update_slice_in_dim(
        jnp.zeros_like(depth_far), far_part, seg_here * narrow, 1
    )
    gate_bias_grad = lax.dynamic_update_slice_in_dim(
        jnp.zeros_like(gate_bias), offset_part, seg_here * narrow, 0
    )
    grad_reduced, mid_gain_one, mid_bias_one = norm_back(
        norm_smooth,
        (reduced, reduced_sums[0], reduced_sums[1], gains_mid[1], biases_mid[1]),
        grad_reduced_act,
    )
    grad_reduced = grad_reduced.astype(jnp.bfloat16)
    reduce_grad = weight_gradient(block_input, grad_reduced)
    grad_block_input = back_product(grad_reduced, reduce_weight) + grad_skip
    grad_stem_outer, wide_gain_zero, wide_bias_zero = norm_back(
        normalize,
        (stem_outer, outer_sums[0], outer_sums[1], gains_wide[0], biases_wide[0]),
        grad_block_input,
    )
    grad_stem_outer = grad_stem_outer.astype(jnp.bfloat16)
    stem_up_grad = weight_gradient(stem_active, grad_stem_outer)
    grad_stem_active = back_product(grad_stem_outer, stem_up)
    grad_stem_inner, mid_gain_zero, mid_bias_zero = norm_back(
        norm_smooth,
        (stem_inner, inner_sums[0], inner_sums[1], gains_mid[0], biases_mid[0]),
        grad_stem_active,
    )
    grad_stem_inner = grad_stem_inner.astype(jnp.bfloat16)
    stem_down_grad = weight_gradient(frame_change, grad_stem_inner)
    grad_change_in = back_product(grad_stem_inner, stem_down)
    weighted_in = grad_change_in * local_weight[:, :, None, None]
    earlier = shifted(weighted_in[:, -1:].astype(jnp.bfloat16), "seg", 1).astype(jnp.float32)
    tokens_grad = (
        grad_block_input + jnp.concatenate([earlier, weighted_in[:, :-1]], axis=1) - weighted_in
    )
    members = (
        near_grad,
        far_grad,
        gate_bias_grad,
        jnp.stack([mid_gain_zero, mid_gain_one, mid_gain_two]),
        jnp.stack([mid_bias_zero, mid_bias_one, mid_bias_two]),
        jnp.stack([wide_gain_zero, wide_gain_one]),
        jnp.stack([wide_bias_zero, wide_bias_one]),
    )
    flat_grads = jnp.concatenate([member.reshape(-1) for member in members])
    summed_small = lax.psum(flat_grads, ("seg", "clip"))
    unpacked = []
    cursor = 0
    for member in members:
        unpacked.append(summed_small[cursor : cursor + member.size].reshape(member.shape))
        cursor = cursor + member.size
    shares = (
        lax.psum_scatter(
            stem_down_grad.astype(jnp.bfloat16), "clip", scatter_dimension=0, tiled=True
        ).astype(jnp.float32),
        lax.psum_scatter(
            stem_up_grad.astype(jnp.bfloat16), "clip", scatter_dimension=0, tiled=True
        ).astype(jnp.float32),
        lax.psum_scatter(
            reduce_grad.astype(jnp.bfloat16), "clip", scatter_dimension=0, tiled=True
        ).astype(jnp.float32),
        lax.psum_scatter(
            conv_grad.astype(jnp.bfloat16), "clip", scatter_dimension=1, tiled=True
        ).astype(jnp.float32),
        lax.psum_scatter(
            expand_grad.astype(jnp.bfloat16), "clip", scatter_dimension=0, tiled=True
        ).astype(jnp.float32),
    )
    big = (
        lax.psum(shares[0].astype(jnp.bfloat16), "seg").astype(jnp.float32),
        lax.psum(shares[1].astype(jnp.bfloat16), "seg").astype(jnp.float32),
        lax.psum(shares[2].astype(jnp.bfloat16), "seg").astype(jnp.float32),
        lax.psum(shares[3].astype(jnp.bfloat16), "seg").astype(jnp.float32),
        lax.psum(shares[4].astype(jnp.bfloat16), "seg").astype(jnp.float32),
    )
    return (
        activations,
        video_means,
        tokens_grad,
        big[0],
        big[1],
        big[2],
        big[3],
        big[4],
        unpacked[0],
        unpacked[1],
        unpacked[2],
        unpacked[3],
        unpacked[4],
        unpacked[5],
        unpacked[6],
    )


ROOT_TWO_OVER_PI = 0.7978845608
CUBIC = 0.044715


def smooth_pair(values):
    square = values * values
    bent = jnp.tanh(values * (ROOT_TWO_OVER_PI + ROOT_TWO_OVER_PI * CUBIC * square))
    half = 0.5 + 0.5 * bent
    slope = half * (
        1.0
        + values * (1.0 - bent) * (ROOT_TWO_OVER_PI + 3.0 * ROOT_TWO_OVER_PI * CUBIC * square)
    )
    return values * half, slope


def smooth_value(values):
    square = values * values
    bent = jnp.tanh(values * (ROOT_TWO_OVER_PI + ROOT_TWO_OVER_PI * CUBIC * square))
    return values * (0.5 + 0.5 * bent)


def rows_sum(values):
    return jnp.sum(values, axis=0, keepdims=True)


def flat(values):
    return values.reshape(-1, values.shape[-1])


def dot(left, right):
    return jnp.dot(left, right, preferred_element_type=jnp.float32)


def dot_back(left, right):
    return lax.dot_general(left, right, (((1,), (1,)), ((), ())), preferred_element_type=jnp.float32)


def dot_rows(left, right):
    return lax.dot_general(left, right, (((0,), (0,)), ((), ())), preferred_element_type=jnp.float32)


BF = jnp.bfloat16
F32 = jnp.float32
WIDE_TILE = 256
COLUMNS = 512


def near_taps():
    return [(a - 1, b - 1) for a in range(3) for b in range(3)]


def far_taps():
    return [(2 * (a - 1), 2 * (b - 1)) for a in range(3) for b in range(3)]


def block_kernel(segs, clips, amount, *refs):
    (
        tokens_hbm, cot_hbm, down_hbm, up_hbm, reduce_hbm, conv_hbm, expand_hbm,
        near, far, gate_bias, gains_mid, biases_mid, gains_wide, biases_wide, frames_at, crops_at,
        act_hbm, tokens_grad_hbm, down_grad, up_grad, reduce_grad, conv_grad, expand_grad, spill, frame_spill,
        video_means, depth_grad, gains_mid_grad, biases_mid_grad, gains_wide_grad, biases_wide_grad,
        tok, frame, outer, skip, cot, wide,
        inner, active, reduced, acts, change, gates, conv, conv_act, gated, back_pad, temp, back,
        halo_out, halo_in,
        down, up, reduce_w, conv_w, expand_w,
        slim_src, slim_land, wide_src, wide_mid, wide_seg, wide_clip,
        slim_norm, wide_norm, pool, video_src, depth, step_weight, past_weight, crop_id,
        load_sem, store_sem, halo_sem, slim_sem, wide_sem, ring_sem, video_sem,
    ) = refs
    seg = lax.axis_index("seg")
    clip = lax.axis_index("clip")
    devices = segs * clips
    me = seg * clips + clip
    scale = 1.0 / amount

    def peer_of(step):
        peer = lax.rem(me + step, devices)
        return (peer // clips, lax.rem(peer, clips))

    barrier = pltpu.get_barrier_semaphore()

    def greet(step, carry):
        pl.semaphore_signal(barrier, inc=1, device_id=peer_of(step), device_id_type=MESH)
        return carry

    lax.fori_loop(1, devices, greet, 0)

    def column_group(group):
        return pl.ds(group * COLUMNS, COLUMNS)

    class Loads:
        def __init__(self, at, pairs):
            self.copies = [
                pltpu.make_async_copy(source, target, load_sem.at[at + k])
                for k, (source, target) in enumerate(pairs)
            ]
            for copy in self.copies:
                copy.start()

        def wait(self):
            for copy in self.copies:
                copy.wait()

    def by_group(source, target):
        return [(source.at[:, :, :, column_group(g)], target.at[g]) for g in range(4)]

    loads = {
        "tok": Loads(0, [(tokens_hbm, tok)]),
        "down": Loads(1, [(down_hbm, down)]),
        "up": Loads(2, by_group(up_hbm, up)),
        "reduce": Loads(6, [(reduce_hbm, reduce_w)]),
        "conv": Loads(7, [(conv_hbm, conv_w)]),
        "expand": Loads(8, by_group(expand_hbm, expand_w)),
        "cot": Loads(
            12,
            [(cot_hbm.at[:, :, column_group(g)], cot.at[pl.ds(g * PIX, PIX)]) for g in range(4)],
        ),
    }

    segment = lax.broadcasted_iota(jnp.int32, (8, SEGS), 1)

    def frame_at(which):
        return jnp.sum(jnp.where(segment == which, frames_at[...].astype(F32), 0.0), axis=1, keepdims=True)

    def weight_at(which):
        inside_clip = jnp.logical_and(which >= 0, which < SEGS - 1)
        spacing = jnp.where(inside_clip, frame_at(which + 1) - frame_at(which), 1.0)
        return jnp.broadcast_to(jnp.where(inside_clip, 1.0 / spacing, 0.0), (8, COLUMNS))

    past_weight[...] = weight_at(seg * 2 - 1)
    step_weight[0:8] = weight_at(seg * 2)
    step_weight[8:16] = weight_at(seg * 2 + 1)
    names = jnp.broadcast_to(crops_at[...].astype(F32), (8, 8))
    diagonal = segment == lax.broadcasted_iota(jnp.int32, (8, SEGS), 0)
    crop_id[...] = jnp.broadcast_to(
        jnp.sum(jnp.where(diagonal, names, 0.0), axis=1, keepdims=True), (8, 128)
    )
    for k in range(9):
        depth[k] = jnp.broadcast_to(near[k : k + 1], (8, COLUMNS))
        depth[9 + k] = jnp.broadcast_to(far[k : k + 1], (8, COLUMNS))

    def slim_start(at):
        def one(step, carry):
            pltpu.make_async_remote_copy(
                slim_src.at[at], slim_land.at[at, me], slim_sem.at[0, at], slim_sem.at[1, at],
                device_id=peer_of(step), device_id_type=MESH,
            ).start()
            return carry

        lax.fori_loop(1, devices, one, 0)
        slim_land[at, pl.ds(me, 1)] = slim_src[at][None]

    def gather_wait(landing, count, sem):
        arrived = landing.at[pl.ds(0, count - 1)]
        pltpu.make_async_copy(arrived, arrived, sem).wait()

    def slot_total(landing, count):
        total = landing[0]
        for rank in range(1, count):
            total = total + landing[rank]
        return total

    def slim_finish(at):
        land = slim_land.at[at]
        gather_wait(land, devices, slim_sem.at[1, at])
        total = slot_total(land, devices)
        gather_wait(land, devices, slim_sem.at[0, at])
        return total

    def axis_start(source, landing, axis, count, send, recv):
        here = lax.axis_index(axis)
        for step in range(1, count):
            pltpu.make_async_remote_copy(
                source, landing.at[here], send, recv,
                device_id={axis: lax.rem(here + step, count)}, device_id_type=MESH,
            ).start()
        landing[pl.ds(here, 1)] = source[...][None]

    def wide_start(at):
        axis_start(wide_src.at[at], wide_seg.at[at], "seg", segs, wide_sem.at[0, at], wide_sem.at[1, at])
        gather_wait(wide_seg.at[at], segs, wide_sem.at[1, at])
        wide_mid[at] = slot_total(wide_seg.at[at], segs)
        gather_wait(wide_seg.at[at], segs, wide_sem.at[0, at])
        axis_start(wide_mid.at[at], wide_clip.at[at], "clip", clips, wide_sem.at[2, at], wide_sem.at[3, at])

    def wide_finish(at):
        gather_wait(wide_clip.at[at], clips, wide_sem.at[3, at])
        total = slot_total(wide_clip.at[at], clips)
        gather_wait(wide_clip.at[at], clips, wide_sem.at[2, at])
        return total

    def keep_norm(total, kept):
        center = total[0:1] * scale
        spread = total[1:2] * scale - center * center
        kept[0:1] = center
        kept[1:2] = lax.rsqrt(spread + NORM_EPSILON)

    def pixels(body, start):
        def line(row, carry):
            for across in range(WIDTH):
                carry = body(row * WIDTH + across, row, across, carry)
            return carry

        return lax.fori_loop(0, HEIGHT, line, start)

    def halves(values):
        return values[0:8], values[8:16]

    def fold(values):
        return values[0:8] + values[8:16]

    slim_zero = jnp.zeros((8, COLUMNS), F32)

    def spread_row(row):
        return jnp.broadcast_to(row, (8, row.shape[-1]))

    def both(values):
        return jnp.concatenate([values, values], axis=0)

    def row16(row):
        return jnp.broadcast_to(row, (16, row.shape[-1]))

    def halo_start(source, target, at, ahead):
        copy = pltpu.make_async_remote_copy(
            source, target, halo_sem.at[0, at], halo_sem.at[1, at],
            device_id={"seg": jnp.clip(seg + ahead, 0, segs - 1)}, device_id_type=MESH,
        )
        can = seg < segs - 1 if ahead > 0 else seg > 0

        @pl.when(can)
        def _():
            copy.start()

    def halo_finish(source, target, at, ahead):
        copy = pltpu.make_async_remote_copy(
            source, target, halo_sem.at[0, at], halo_sem.at[1, at],
            device_id={"seg": jnp.clip(seg + ahead, 0, segs - 1)}, device_id_type=MESH,
        )
        sends = seg < segs - 1 if ahead > 0 else seg > 0
        takes = seg > 0 if ahead > 0 else seg < segs - 1

        @pl.when(takes)
        def _():
            copy.wait_recv()

        @pl.when(jnp.logical_not(takes))
        def _():
            target[...] = jnp.zeros_like(target)

        @pl.when(sends)
        def _():
            copy.wait_send()

    product, product_next = change, conv
    loads["tok"].wait()
    loads["down"].wait()
    for tile in range(2):
        at = pl.ds(tile * WIDE_TILE, WIDE_TILE)
        value = dot(flat(tok[...]), flat(down[:, :, :, :, at]))
        product[:, :, :, at] = value.reshape(PIX, 2, 8, WIDE_TILE)
        if tile == 0:
            pl.semaphore_wait(barrier, devices - 1)
        halo_start(product.at[:, 0, :, at], product_next.at[:, 0, :, at], tile, -1)
    for tile in range(2):
        at = pl.ds(tile * WIDE_TILE, WIDE_TILE)
        halo_finish(product.at[:, 0, :, at], product_next.at[:, 0, :, at], tile, -1)

    def inner_body(pixel, row, across, carry):
        first, second = carry
        zero, one, after = product[pixel, 0], product[pixel, 1], product_next[pixel, 0]
        early = (one - zero) * step_weight[0:8]
        late = (after - one) * step_weight[8:16]
        inner[pixel] = jnp.concatenate([early, late], axis=0)
        return first + early + late, second + early * early + late * late

    first, second = pixels(inner_body, (slim_zero, slim_zero))
    slim_src[0, 0:1] = rows_sum(first)
    slim_src[0, 1:2] = rows_sum(second)
    slim_start(0)

    token_out, token_in = wide.at[:, :, pl.ds(0, 1024)], wide.at[:, :, pl.ds(1024, 1024)]

    def token_pack(pixel, row, across, carry):
        value = tok[pixel].astype(F32)[0:8]
        wide[pixel, :, pl.ds(0, 1024)] = jnp.concatenate(
            [value[:, 0:1024], value[:, 1024:2048]], axis=0
        ).astype(BF)
        return carry

    pixels(token_pack, 0)
    halo_start(token_out, token_in, 2, -1)

    keep_norm(slim_finish(0), slim_norm.at[0])

    def activate(source, target, at):
        center, rate = row16(slim_norm[at, 0:1]), row16(slim_norm[at, 1:2] * gains_mid[at : at + 1])
        bias = row16(biases_mid[at : at + 1])

        def body(pixel, row, across, carry):
            target[pixel] = smooth_value((source[pixel] - center) * rate + bias).astype(BF)
            return carry

        pixels(body, 0)

    activate(inner, active, 0)

    loads["up"].wait()

    def widen(source, weight, sums):
        def body(tile, carry):
            at = pl.ds(pl.multiple_of(tile * WIDE_TILE, WIDE_TILE), WIDE_TILE)
            lanes = pl.ds(pl.multiple_of(lax.rem(tile, 2) * WIDE_TILE, WIDE_TILE), WIDE_TILE)
            value = dot(flat(source[...]), flat(weight[tile // 2, :, :, :, lanes]))
            outer[:, :, at] = value.reshape(PIX, 16, WIDE_TILE)
            wide_src[sums, 0:1, at] = rows_sum(value)
            wide_src[sums, 1:2, at] = rows_sum(value * value)
            return carry

        lax.fori_loop(0, 2048 // WIDE_TILE, body, 0)

    widen(active, up, 0)
    wide_start(0)

    def frame_start(pixel, row, across, carry):
        for part in range(4):
            at = pl.ds(part * COLUMNS, COLUMNS)
            zero, one = halves(tok[pixel, :, at].astype(F32))
            frame[part * PIX + pixel] = jnp.concatenate(
                [(one - zero) * step_weight[0:8], one], axis=0
            ).astype(BF)
        return carry

    pixels(frame_start, 0)
    keep_norm(wide_finish(0), wide_norm.at[0])

    def wide_pixels(body, parts=4):
        def part(at, carry):
            columns = pl.ds(pl.multiple_of(at * COLUMNS, COLUMNS), COLUMNS)
            body(at, columns)
            return carry

        lax.fori_loop(0, parts, part, 0)

    def input_part(group, columns):
        center = row16(wide_norm[0, 0:1, columns])
        rate = row16(wide_norm[0, 1:2, columns] * gains_wide[0:1, columns])
        bias = row16(biases_wide[0:1, columns])

        def body(pixel, row, across, carry):
            value = (outer[pixel, :, columns] - center) * rate + bias
            tok[pixel, :, columns] = (tok[pixel, :, columns].astype(F32) + value).astype(BF)
            return carry

        pixels(body, 0)

    wide_pixels(input_part)
    block_input = tok
    spill_out = pltpu.make_async_copy(outer, spill, store_sem.at[0])
    spill_out.start()

    loads["reduce"].wait()
    for tile in range(2):
        at = pl.ds(tile * WIDE_TILE, WIDE_TILE)
        value = dot(flat(block_input[...]), flat(reduce_w[:, :, :, :, at]))
        reduced[:, :, at] = value.reshape(PIX, 16, WIDE_TILE)
        slim_src[1, 0:1, at] = rows_sum(value)
        slim_src[1, 1:2, at] = rows_sum(value * value)
    slim_start(1)
    halo_finish(token_out, token_in, 2, -1)

    def frame_finish(pixel, row, across, carry):
        ahead = wide[pixel, :, pl.ds(1024, 1024)].astype(F32)
        for part in range(4):
            zero, one = halves(frame[part * PIX + pixel].astype(F32))
            half, low = (0, part) if part < 2 else (8, part - 2)
            after = ahead[half : half + 8, low * COLUMNS : (low + 1) * COLUMNS]
            frame[part * PIX + pixel] = jnp.concatenate(
                [zero, (after - one) * step_weight[8:16]], axis=0
            ).astype(BF)
        return carry

    pixels(frame_finish, 0)
    frame_out = [
        pltpu.make_async_copy(
            frame.at[pl.ds(g * PIX, PIX)], frame_spill.at[:, :, column_group(g)], store_sem.at[2 + g]
        )
        for g in range(4)
    ]
    for copy in frame_out:
        copy.start()
    keep_norm(slim_finish(1), slim_norm.at[1])

    def act_parts():
        center, rate = row16(slim_norm[1, 0:1]), row16(slim_norm[1, 1:2] * gains_mid[1:2])
        bias = row16(biases_mid[1:2])

        def body(pixel, row, across, carry):
            value = smooth_value((reduced[pixel] - center) * rate + bias).astype(BF)
            acts[pixel] = value
            lead = value.astype(F32)[0:8]
            halo_out[pixel] = jnp.concatenate([lead[:, 0:256], lead[:, 256:512]], axis=0).astype(BF)
            return carry

        pixels(body, 0)

    act_parts()
    halo_start(halo_out, halo_in, 3, -1)

    def change_early(pixel, row, across, carry):
        zero, one = halves(acts[pixel].astype(F32))
        change[pixel, 0] = (one - zero) * step_weight[0:8]
        change[pixel, 1] = one
        return carry

    pixels(change_early, 0)

    def lanes_of(tile):
        return pl.ds(pl.multiple_of(tile * 128, 128), 128)

    def inside(row, column):
        return 0 <= row < HEIGHT and 0 <= column < WIDTH

    def gate_tile(which):
        def body(tile, carry):
            lanes = lanes_of(tile)
            kernels = [depth[k, :, lanes] for k in range(18)]
            middle = kernels[4] + kernels[13]
            offsets = jnp.broadcast_to(gate_bias[0:1, lanes], (8, 128))
            field = [change[p, which, :, lanes] for p in range(PIX)]
            for i in range(HEIGHT):
                for j in range(WIDTH):
                    mixed = offsets + middle * field[i * WIDTH + j]
                    for base, taps in ((0, near_taps()), (9, far_taps())):
                        for k, (di, dj) in enumerate(taps):
                            if (di or dj) and inside(i + di, j + dj):
                                mixed = mixed + kernels[base + k] * field[(i + di) * WIDTH + j + dj]
                    gates[i * WIDTH + j, which, :, lanes] = 0.5 + 0.5 * jnp.tanh(0.5 * mixed)
            return carry

        lax.fori_loop(0, 4, body, 0)

    gate_tile(0)
    halo_finish(halo_out, halo_in, 3, -1)

    def change_late(pixel, row, across, carry):
        ahead = halo_in[pixel].astype(F32)
        after = jnp.concatenate([ahead[0:8], ahead[8:16]], axis=1)
        change[pixel, 1] = (after - change[pixel, 1]) * step_weight[8:16]
        return carry

    pixels(change_late, 0)
    gate_tile(1)

    for side in range(9):
        edge = jnp.zeros((16, COLUMNS), BF)
        for pad in (gated, back_pad):
            pad[0, side] = edge
            pad[8, side] = edge
            pad[side, 0] = edge
            pad[side, 8] = edge

    def gated_body(pixel, row, across, carry):
        both_gates = jnp.concatenate([gates[pixel, 0], gates[pixel, 1]], axis=0)
        gated[row + 1, across + 1] = (acts[pixel].astype(F32) * (1.0 + both_gates)).astype(BF)
        return carry

    pixels(gated_body, 0)

    loads["conv"].wait()

    def window(pad, a, b):
        return flat(pad[a : a + HEIGHT, b : b + WIDTH])

    for tile in range(2):
        at = pl.ds(tile * WIDE_TILE, WIDE_TILE)
        value = dot(window(gated, 0, 0), flat(conv_w[0, :, :, :, at]))
        for tap in range(1, 9):
            value = value + dot(window(gated, tap // 3, tap % 3), flat(conv_w[tap, :, :, :, at]))
        conv[:, :, :, at] = value.reshape(PIX, 2, 8, WIDE_TILE)
        slim_src[2, 0:1, at] = rows_sum(value)
        slim_src[2, 1:2, at] = rows_sum(value * value)
    slim_start(2)
    spill_out.wait()
    loads["expand"].wait()
    loads["cot"].wait()
    keep_norm(slim_finish(2), slim_norm.at[2])

    def conv_rows(pixel):
        return conv[pixel].reshape(16, COLUMNS)

    def conv_act_part():
        center, rate = row16(slim_norm[2, 0:1]), row16(slim_norm[2, 1:2] * gains_mid[2:3])
        bias = row16(biases_mid[2:3])

        def body(pixel, row, across, carry):
            conv_act[pixel] = smooth_value((conv_rows(pixel) - center) * rate + bias).astype(BF)
            return carry

        pixels(body, 0)

    conv_act_part()
    widen(conv_act, expand_w, 1)
    wide_start(1)
    keep_norm(wide_finish(1), wide_norm.at[1])

    def output_part(group, columns):
        center = row16(wide_norm[1, 0:1, columns])
        rate = row16(wide_norm[1, 1:2, columns])
        gain = row16(gains_wide[1:2, columns])
        bias = row16(biases_wide[1:2, columns])

        def body(pixel, row, across, carry):
            pool, shift, stretch = carry
            unit = (outer[pixel, :, columns] - center) * rate
            value, slope = smooth_pair(block_input[pixel, :, columns].astype(F32) + unit * gain + bias)
            incoming = cot[group * PIX + pixel].astype(F32) * slope
            cot[group * PIX + pixel] = value.astype(BF)
            skip[pixel, :, columns] = incoming
            return pool + fold(value), shift + fold(incoming), stretch + fold(incoming * unit)

        pool, shift, stretch = pixels(body, (slim_zero, slim_zero, slim_zero))
        video_src[group] = pool
        wide_src[2, 0:1, columns] = rows_sum(shift)
        wide_src[2, 1:2, columns] = rows_sum(stretch)

    wide_pixels(output_part)
    wide_start(2)
    act_out = [
        pltpu.make_async_copy(
            cot.at[pl.ds(g * PIX, PIX)], act_hbm.at[:, :, column_group(g)], store_sem.at[6 + g]
        )
        for g in range(4)
    ]
    for copy in act_out:
        copy.start()
    total = wide_finish(2)
    biases_wide_grad[1:2] = total[0:1]
    gains_wide_grad[1:2] = total[1:2]

    def wide_back(at, group, columns):
        center = row16(wide_norm[at, 0:1, columns])
        rate = row16(wide_norm[at, 1:2, columns])
        factor = rate * row16(gains_wide[at : at + 1, columns])
        shift = row16(biases_wide_grad[at : at + 1, columns] * scale)
        stretch = row16(gains_wide_grad[at : at + 1, columns] * scale) * rate

        def body(pixel, row, across, carry):
            value = skip[pixel, :, columns] - shift - (outer[pixel, :, columns] - center) * stretch
            wide[pixel, :, columns] = (value * factor).astype(BF)
            return carry

        pixels(body, 0)

    wide_pixels(functools.partial(wide_back, 1))
    spill_in = pltpu.make_async_copy(spill, outer, store_sem.at[0])
    spill_in.start()

    def narrow(weight):
        for tile in range(2):
            at = pl.ds(tile * WIDE_TILE, WIDE_TILE)
            value = dot_back(flat(wide[:, :, column_group(0)]), flat(weight[0, tile]))
            for g in range(1, 4):
                value = value + dot_back(flat(wide[:, :, column_group(g)]), flat(weight[g, tile]))
            temp[:, :, at] = value.reshape(PIX, 16, WIDE_TILE)

    narrow(expand_w)

    def slope_sums(source, norm, sums):
        center, rate = row16(slim_norm[norm, 0:1]), row16(slim_norm[norm, 1:2])
        gain, bias = row16(gains_mid[norm : norm + 1]), row16(biases_mid[norm : norm + 1])

        def body(pixel, row, across, carry):
            shift, stretch = carry
            unit = (source(pixel) - center) * rate
            unused, slope = smooth_pair(unit * gain + bias)
            value = temp[pixel] * slope
            temp[pixel] = value
            return shift + fold(value), stretch + fold(value * unit)

        shift, stretch = pixels(body, (slim_zero, slim_zero))
        slim_src[sums, 0:1] = rows_sum(shift)
        slim_src[sums, 1:2] = rows_sum(stretch)
        slim_start(sums)

    def slope_finish(source, norm, sums, store):
        total = slim_finish(sums)
        biases_mid_grad[norm : norm + 1] = total[0:1]
        gains_mid_grad[norm : norm + 1] = total[1:2]
        center, rate = row16(slim_norm[norm, 0:1]), row16(slim_norm[norm, 1:2])
        factor = rate * row16(gains_mid[norm : norm + 1])
        shift = row16(total[0:1] * scale)
        stretch = row16(total[1:2] * scale) * rate

        def body(pixel, row, across, carry):
            value = temp[pixel] - shift - (source(pixel) - center) * stretch
            store(pixel, row, across, (value * factor).astype(BF))
            return carry

        pixels(body, 0)

    for copy in act_out:
        copy.wait()
    for copy in frame_out:
        copy.wait()
    slope_sums(conv_rows, 2, 3)

    column, core = seg // 2, lax.rem(seg, 2)
    layer, line = clip // 2, lax.rem(clip, 2)
    to_core = {"seg": seg + 1 - 2 * core}
    to_column = {"seg": seg + 2 - 4 * column}
    to_corner = {"seg": 3 - seg}
    to_line = {"clip": clip + 1 - 2 * line}
    own = layer * 4 + line * 2

    class Ring:
        def __init__(self, at, slots, shared, single, places):
            self.at, self.slots, self.shared, self.single = at, slots, shared, single
            self.count = shared + 2 * single
            self.mine = shared + column * single
            self.other = shared + (1 - column) * single
            sizes = {
                "core": 16 * self.count, "line_a": 8 * shared, "layer_a": 8 * shared, "column_a": 2 * shared,
                "column_b": 16 * single, "line_b": 8 * single, "layer_b": 8 * single, "final": 4 * self.count,
            }
            self.land, self.kinds = {}, {}
            for number, (kind, size) in enumerate(sizes.items()):
                ref, base = places[kind]
                self.land[kind] = (ref, base)
                self.kinds[kind] = number

        def tiles(self, kind, start, size):
            ref, base = self.land[kind]
            return ref.at[pl.ds(base + start, size)]

        def send(self, kind, source, start, size, device):
            sems = [ring_sem.at[way, self.at, self.kinds[kind]] for way in range(2)]
            pltpu.make_async_remote_copy(
                source, self.tiles(kind, start, size), sems[0], sems[1],
                device_id=device, device_id_type=MESH,
            ).start()

        def wait(self, kind, size, sent=None):
            for way, amount in ((1, size), (0, size if sent is None else sent)):
                span = pool.at[pl.ds(0, amount)]
                pltpu.make_async_copy(span, span, ring_sem.at[way, self.at, self.kinds[kind]]).wait()

        def add_slots(self, kind, amount, slot_of):
            ref, base = self.land[kind]
            for item in range(amount):
                slot = slot_of(item)
                self.slots[slot, core] = self.slots[slot, core] + ref[pl.ds(base + item * 16, 16)]

        def add_lines(self, kind, amount, slot_of):
            ref, base = self.land[kind]
            for item in range(amount):
                for k in range(4):
                    here = pl.ds(k * 4 + line * 2, 2)
                    self.slots[slot_of(item), core, here] = (
                        self.slots[slot_of(item), core, here] + ref[pl.ds(base + (item * 4 + k) * 2, 2)]
                    )

        def gather(self, kind, amount, slot_of, store):
            ref, base = self.land[kind]
            for item in range(amount):
                ref[pl.ds(base + (item * 4 + layer) * 2, 2)] = self.slots[slot_of(item), core, pl.ds(own, 2)]
                value = ref[pl.ds(base + item * 8, 2)].astype(F32)
                for k in range(1, 4):
                    value = value + ref[pl.ds(base + (item * 4 + k) * 2, 2)].astype(F32)
                store(item, value.astype(BF))

        def stage0(self):
            for slot in range(self.count):
                self.send("core", self.slots.at[slot, 1 - core], slot * 16, 16, to_core)

        def send_line(self, kind, amount, slot_of):
            for item in range(amount):
                for k in range(4):
                    source = self.slots.at[slot_of(item), core, pl.ds(k * 4 + (1 - line) * 2, 2)]
                    self.send(kind, source, (item * 4 + k) * 2, 2, to_line)

        def send_layer(self, kind, amount, slot_of):
            for item in range(amount):
                for step in range(1, 4):
                    there = lax.rem(layer + step, 4)
                    source = self.slots.at[slot_of(item), core, pl.ds(there * 4 + line * 2, 2)]
                    self.send(kind, source, (item * 4 + layer) * 2, 2, {"clip": there * 2 + line})

        def stage1(self):
            self.wait("core", 16 * self.count)
            self.add_slots("core", self.count, lambda item: item)
            self.send_line("line_a", self.shared, lambda item: item)
            for item in range(self.single):
                self.send("column_b", self.slots.at[self.other + item, core], item * 16, 16, to_column)

        def stage2(self):
            self.wait("line_a", 8 * self.shared)
            self.add_lines("line_a", self.shared, lambda item: item)
            self.send_layer("layer_a", self.shared, lambda item: item)
            self.wait("column_b", 16 * self.single)
            self.add_slots("column_b", self.single, lambda item: self.mine + item)
            self.send_line("line_b", self.single, lambda item: self.mine + item)

        def stage3(self):
            self.wait("line_b", 8 * self.single)
            self.add_lines("line_b", self.single, lambda item: self.mine + item)
            self.send_layer("layer_b", self.single, lambda item: self.mine + item)
            self.wait("layer_a", 6 * self.shared)

            def store(item, value):
                self.slots[item, core, pl.ds(own, 2)] = value

            self.gather("layer_a", self.shared, lambda item: item, store)
            for item in range(self.shared):
                self.send("column_a", self.slots.at[item, core, pl.ds(own, 2)], item * 2, 2, to_column)

        def stage4(self):
            final, start = self.land["final"]
            here = start + core * self.count * 2
            self.wait("column_a", 2 * self.shared)
            ref, base = self.land["column_a"]
            for item in range(self.shared):
                final[pl.ds(here + item * 2, 2)] = (
                    self.slots[item, core, pl.ds(own, 2)] + ref[pl.ds(base + item * 2, 2)]
                )
                at = core * self.count * 2 + item * 2
                self.send("final", self.tiles("final", at, 2), at, 2, to_core)
            self.wait("layer_b", 6 * self.single)

            def store(item, value):
                final[pl.ds(here + (self.mine + item) * 2, 2)] = value

            self.gather("layer_b", self.single, lambda item: self.mine + item, store)
            for item in range(self.single):
                at = (core * self.count + self.mine + item) * 2
                for device in (to_core, to_column, to_corner):
                    self.send("final", self.tiles("final", at, 2), at, 2, device)

        def stage5(self):
            arrive = 2 * (self.shared + 3 * self.single)
            self.wait("final", arrive)

        def result(self, half, slot, part):
            final, start = self.land["final"]
            return final[start + (half * self.count + slot) * 2 + part].astype(F32)

    KINDS = ("core", "line_a", "layer_a", "column_a", "column_b", "line_b", "layer_b", "final")

    def places(spans):
        return {kind: span for kind, span in zip(KINDS, spans)}

    def packed(ref, start, shared, single):
        count = shared + 2 * single
        sizes = (16 * count, 8 * shared, 8 * shared, 2 * shared, 16 * single, 8 * single, 8 * single, 4 * count)
        spans = []
        for size in sizes:
            spans.append((ref, start))
            start = start + size
        return places(spans)

    ring_expand = Ring(0, expand_w, 2, 1, packed(cot, 0, 2, 1))
    ring_conv = Ring(1, conv_w.at[pl.ds(0, 4)], 2, 1, packed(pool, 0, 2, 1))
    ring_more = Ring(5, conv_w.at[pl.ds(4, 5)], 3, 1, packed(pool, 148, 3, 1))
    ring_reduce = Ring(2, reduce_w, 2, 1, packed(frame, 0, 2, 1))
    ring_down = Ring(4, expand_w, 2, 1, packed(cot, 0, 2, 1))
    ring_up = Ring(
        3, up, 2, 1,
        places(
            (
                (pool, 334), (frame, 148), (cot, 148), (cot, 164),
                (frame, 164), (cot, 168), (cot, 176), (frame, 180),
            )
        ),
    )

    def put_rows(slots, slot, value):
        parts = value.astype(BF).reshape(8, 2, 2, 16, COLUMNS)
        for half in range(2):
            slots[slot, half] = parts[:, half].reshape(16, 16, COLUMNS)

    def wide_weight_grad(left, slots):
        def body(slot, carry):
            columns = pl.ds(pl.multiple_of(slot * COLUMNS, COLUMNS), COLUMNS)
            put_rows(slots, slot, dot_rows(flat(left[...]), flat(wide[:, :, columns])))
            return carry

        lax.fori_loop(0, 4, body, 0)

    def tall_weight_grad(left, slots):
        def body(block, carry):
            columns = pl.ds(pl.multiple_of(block * WIDE_TILE, WIDE_TILE), WIDE_TILE)
            value = dot_rows(flat(left[:, :, columns]), flat(back[...])).astype(BF)
            parts = value.reshape(2, 4, 2, 16, COLUMNS)
            for half in range(2):
                for slot in range(4):
                    slots[slot, half, pl.ds(block * 2, 2)] = parts[half, slot]
            return carry

        lax.fori_loop(0, 8, body, 0)

    def conv_weight_grad(taps):
        for tap in taps:
            put_rows(conv_w, tap, dot_rows(window(gated, tap // 3, tap % 3), window(back_pad, 1, 1)))

    wide_weight_grad(conv_act, expand_w)

    def store_conv(pixel, row, across, value):
        back_pad[row + 1, across + 1] = value

    slope_finish(conv_rows, 2, 3, store_conv)
    ring_expand.stage0()

    grad_gated = conv_act
    for tile in range(2):
        at = pl.ds(tile * WIDE_TILE, WIDE_TILE)
        value = dot_back(window(back_pad, 2, 2), flat(conv_w[0, tile]))
        for tap in range(1, 9):
            value = value + dot_back(window(back_pad, 2 - tap // 3, 2 - tap % 3), flat(conv_w[tap, tile]))
        grad_gated[:, :, at] = value.astype(BF).reshape(PIX, 16, WIDE_TILE)
    ring_expand.stage1()
    conv_weight_grad(range(0, 4))
    ring_conv.stage0()
    conv_weight_grad(range(4, 9))
    ring_more.stage0()

    grad_mixed = conv

    def mixed_body(pixel, row, across, carry):
        incoming = grad_gated[pixel].astype(F32)
        both_gates = jnp.concatenate([gates[pixel, 0], gates[pixel, 1]], axis=0)
        value = incoming * acts[pixel].astype(F32) * both_gates * (1.0 - both_gates)
        grad_mixed[pixel] = value.reshape(2, 8, COLUMNS)
        temp[pixel] = incoming * (1.0 + both_gates)
        return carry

    pixels(mixed_body, 0)
    weighted = gates

    def gate_back_tile(which):
        def body(tile, carry):
            lanes = lanes_of(tile)
            kernels = [depth[k, :, lanes] for k in range(18)]
            middle = kernels[4] + kernels[13]
            weight = step_weight[which * 8 : which * 8 + 8, 0:128]
            field = [grad_mixed[p, which, :, lanes] for p in range(PIX)]
            for i in range(HEIGHT):
                for j in range(WIDTH):
                    value = middle * field[i * WIDTH + j]
                    for base, taps in ((0, near_taps()), (9, far_taps())):
                        for k, (di, dj) in enumerate(taps):
                            if (di or dj) and inside(i - di, j - dj):
                                value = value + kernels[base + k] * field[(i - di) * WIDTH + j - dj]
                    weighted[i * WIDTH + j, which, :, lanes] = value * weight
            return carry

        lax.fori_loop(0, 4, body, 0)

    def depth_grad_tile():
        def body(tile, carry):
            lanes = lanes_of(tile)
            totals = [None] * 19
            for which in range(2):
                field = [grad_mixed[p, which, :, lanes] for p in range(PIX)]

                def grow(k, term):
                    totals[k] = term if totals[k] is None else totals[k] + term

                for p in range(PIX):
                    grow(18, field[p])
                for base, taps in ((0, near_taps()), (9, far_taps())):
                    for k, (di, dj) in enumerate(taps):
                        for i in range(HEIGHT):
                            for j in range(WIDTH):
                                if inside(i + di, j + dj):
                                    there = (i + di) * WIDTH + j + dj
                                    grow(base + k, field[i * WIDTH + j] * change[there, which, :, lanes])
            for k in range(19):
                video_src[4 + k // 8, k % 8 : k % 8 + 1, lanes] = rows_sum(totals[k])
            return carry

        lax.fori_loop(0, 4, body, 0)
        video_src[6, 3:8] = jnp.zeros((5, COLUMNS), F32)

    gate_back_tile(1)

    def weighted_pack(pixel, row, across, carry):
        last = weighted[pixel, 1]
        halo_out[pixel] = jnp.concatenate([last[:, 0:256], last[:, 256:512]], axis=0).astype(BF)
        return carry

    pixels(weighted_pack, 0)
    halo_start(halo_out, halo_in, 4, 1)
    gate_back_tile(0)
    ring_expand.stage2()
    ring_conv.stage1()
    halo_finish(halo_out, halo_in, 4, 1)

    def act_grad_body(pixel, row, across, carry):
        ahead = halo_in[pixel].astype(F32)
        before = jnp.concatenate([ahead[0:8], ahead[8:16]], axis=1)
        zero, one = weighted[pixel, 0], weighted[pixel, 1]
        value = temp[pixel] + jnp.concatenate([before - zero, zero - one], axis=0)
        temp[pixel] = value.astype(BF).astype(F32)
        return carry

    pixels(act_grad_body, 0)

    def reduced_rows(pixel):
        return reduced[pixel]

    slope_sums(reduced_rows, 1, 4)
    depth_grad_tile()

    def store_back(pixel, row, across, value):
        back[pixel] = value

    slope_finish(reduced_rows, 1, 4, store_back)
    ring_expand.stage3()
    ring_conv.stage2()

    def video_span(way, at, ref):
        pltpu.make_async_copy(ref, ref, video_sem.at[way, at]).wait()

    def seg_spread(source, target, at):
        for step in range(1, segs):
            pltpu.make_async_remote_copy(
                source, target, video_sem.at[0, at], video_sem.at[1, at],
                device_id={"seg": lax.rem(seg + step, segs)}, device_id_type=MESH,
            ).start()

    def video_first():
        seg_spread(video_src, change.at[pl.ds(seg * 7, 7), 0], 0)
        change[pl.ds(seg * 7, 7), 0] = video_src[...]

    def video_second():
        for way in range(2):
            video_span(way, 0, change.at[pl.ds(0, 21), 0])

        def total(read):
            value = read(0)
            for rank in range(1, segs):
                value = value + read(rank * 7)
            return value

        quarter = pl.ds(pl.multiple_of(seg * 128, 128), 128)
        conv[clip, 0] = total(lambda base: change[base + seg, 0])
        for k in range(3):
            conv[clip, 1, :, pl.ds(k * 128, 128)] = total(lambda base: change[base + 4 + k, 0, :, quarter])
        conv[clip, 1, :, pl.ds(384, 128)] = crop_id[...]
        for step in range(1, clips):
            pltpu.make_async_remote_copy(
                conv.at[clip], conv.at[clip], video_sem.at[0, 1], video_sem.at[1, 1],
                device_id={"clip": lax.rem(clip + step, clips)}, device_id_type=MESH,
            ).start()

    def video_third():
        for way in range(2):
            video_span(way, 1, conv.at[pl.ds(0, clips - 1)])
        sums = jnp.concatenate([conv[k, 0] for k in range(clips)], axis=0)
        names = jnp.concatenate([conv[k, 1, :, pl.ds(384, 128)] for k in range(clips)], axis=0)
        lane = lax.broadcasted_iota(jnp.int32, names.shape, 1).astype(F32)
        member = (names == lane).astype(F32)

        def gather(values):
            return lax.dot_general(
                member, values, (((0,), (0,)), ((), ())),
                precision=lax.Precision.HIGHEST, preferred_element_type=F32,
            )[0:32]

        counts = gather(jnp.ones_like(names))
        means = gather(sums) / jnp.concatenate([counts * (SEGS * PIX)] * 4, axis=1)
        grads = conv[0, 1]
        for k in range(1, clips):
            grads = grads + conv[k, 1]
        gates[pl.ds(seg * 5, 4), 0] = means.reshape(4, 8, COLUMNS)
        gates[pl.ds(seg * 5 + 4, 1), 0] = grads[None]
        mine = gates.at[pl.ds(seg * 5, 5), 0]
        seg_spread(mine, mine, 2)

    def video_last():
        for way in range(2):
            video_span(way, 2, gates.at[pl.ds(0, 15), 0])
        for rank in range(segs):
            for k in range(4):
                video_means[k * 8 : k * 8 + 8, column_group(rank)] = gates[rank * 5 + k, 0]
            for k in range(3):
                depth_grad[k * 8 : k * 8 + 8, pl.ds(rank * 128, 128)] = gates[
                    rank * 5 + 4, 0, :, pl.ds(k * 128, 128)
                ]


    spill_in.wait()

    def input_grad(tile, carry):
        at = pl.ds(pl.multiple_of(tile * WIDE_TILE, WIDE_TILE), WIDE_TILE)
        weight = flat(reduce_w[tile // 2, lax.rem(tile, 2)])
        value = dot_back(flat(back[...]), weight) + flat(skip[:, :, at])
        skip[:, :, at] = value.reshape(PIX, 16, WIDE_TILE)
        unit = (flat(outer[:, :, at]) - wide_norm[0, 0:1, at]) * wide_norm[0, 1:2, at]
        wide_src[3, 0:1, at] = rows_sum(value)
        wide_src[3, 1:2, at] = rows_sum(value * unit)
        return carry

    lax.fori_loop(0, 2048 // WIDE_TILE, input_grad, 0)
    wide_start(3)
    tall_weight_grad(block_input, reduce_w)
    ring_reduce.stage0()
    frame_in = pltpu.make_async_copy(frame_spill, tok, store_sem.at[1])
    frame_in.start()
    total = wide_finish(3)
    ring_more.stage1()
    ring_expand.stage4()
    biases_wide_grad[0:1] = total[0:1]
    gains_wide_grad[0:1] = total[1:2]
    wide_pixels(functools.partial(wide_back, 0))
    ring_conv.stage3()
    narrow(up)

    def inner_rows(pixel):
        return inner[pixel]

    ring_expand.stage5()
    expand_kept = [
        [ring_expand.result(half, slot, part) for part in range(2)] for half in range(2) for slot in range(4)
    ]
    for index, pair in enumerate(expand_kept):
        for part in range(2):
            reduced[index * 2 + part] = pair[part]
    slope_sums(inner_rows, 0, 5)
    wide_weight_grad(active, up)
    ring_up.stage0()
    slope_finish(inner_rows, 0, 5, store_back)
    video_first()

    def last_pack(pixel, row, across, carry):
        last = back[pixel].astype(F32)[8:16]
        halo_out[pixel] = jnp.concatenate([last[:, 0:256], last[:, 256:512]], axis=0).astype(BF)
        return carry

    pixels(last_pack, 0)
    halo_start(halo_out, halo_in, 5, 1)
    ring_reduce.stage1()
    ring_more.stage2()
    ring_conv.stage4()
    ring_up.stage1()
    frame_in.wait()
    tall_weight_grad(tok, expand_w)
    ring_down.stage0()
    ring_down.stage1()
    ring_reduce.stage2()
    ring_more.stage3()
    halo_finish(halo_out, halo_in, 5, 1)

    def change_grad(pixel, row, across, carry):
        ahead = halo_in[pixel].astype(F32)
        before = jnp.concatenate([ahead[0:8], ahead[8:16]], axis=1) * past_weight[...]
        zero, one = halves(back[pixel].astype(F32) * step_weight[...])
        active[pixel] = jnp.concatenate([before - zero, zero - one], axis=0).astype(BF)
        return carry

    pixels(change_grad, 0)
    ring_up.stage2()

    def tokens_part(group):
        columns = column_group(group)
        return pltpu.make_async_copy(
            skip.at[:, :, columns], tokens_grad_hbm.at[:, :, columns], store_sem.at[11 + group]
        )

    for tile in range(8):
        at = pl.ds(tile * WIDE_TILE, WIDE_TILE)
        value = dot_back(flat(active[...]), flat(down[tile // 2, tile % 2])) + flat(skip[:, :, at])
        skip[:, :, at] = value.reshape(PIX, 16, WIDE_TILE)
        if tile % 2 == 1:
            tokens_part(tile // 2).start()
    video_second()

    ring_reduce.stage3()
    ring_more.stage4()
    ring_down.stage2()
    ring_up.stage3()
    ring_reduce.stage4()
    video_third()
    ring_conv.stage5()
    ring_more.stage5()

    def flush(index, source, target):
        copy = pltpu.make_async_copy(source, target, store_sem.at[20 + index])
        copy.start()
        return copy

    def tall_out(index, ring, target, first):
        for half in range(2):
            for slot in range(4):
                for part in range(2):
                    outer[first + half * 8 + slot * 2 + part, :, column_group(1)] = ring.result(half, slot, part)
        return flush(index, outer.at[pl.ds(first, 16), :, column_group(1)], target)

    def wide_out(index, read, target, first):
        for half in range(2):
            for slot in range(4):
                for part in range(2):
                    outer[first + half * 2 + part, :, column_group(slot)] = read(half, slot, part)
        return flush(index, outer.at[pl.ds(first, 4)], target)

    copies = [wide_out(0, lambda half, slot, part: reduced[(half * 4 + slot) * 2 + part], expand_grad, 40)]
    for tap in range(9):
        ring, slot = (ring_conv, tap) if tap < 4 else (ring_more, tap - 4)
        for half in range(2):
            for part in range(2):
                outer[tap * 4 + half * 2 + part, :, column_group(0)] = ring.result(half, slot, part)
    copies.append(flush(1, outer.at[pl.ds(0, 36), :, column_group(0)], conv_grad))
    ring_down.stage3()
    ring_up.stage4()
    ring_reduce.stage5()
    copies.append(tall_out(2, ring_reduce, reduce_grad, 16))
    ring_down.stage4()
    ring_up.stage5()
    copies.append(wide_out(3, ring_up.result, up_grad, 36))
    video_last()
    ring_down.stage5()
    copies.append(tall_out(4, ring_down, down_grad, 0))
    for group in range(4):
        tokens_part(group).wait()
    for copy in copies:
        copy.wait()


def hand_over(*refs):
    tokens_grad, *grads = refs[0:6]
    small, (tokens_out, *outs), buffers, sems = refs[6:12], refs[12:26], refs[26:32], refs[32]
    held, *kept = buffers

    def load(group):
        columns = pl.ds(group * COLUMNS, COLUMNS)
        return pltpu.make_async_copy(
            tokens_grad.at[:, :, columns], held.at[:, :, columns], sems.at[group]
        )

    def store(group, part, clip_at):
        columns = pl.ds(group * COLUMNS, COLUMNS)
        return pltpu.make_async_copy(
            held.at[:, part * 8 + clip_at, columns], tokens_out.at[clip_at, :, part, columns], sems.at[4 + group]
        )

    for group in range(4):
        load(group).start()
    copies = [pltpu.make_async_copy(a, b, sems.at[8 + at]) for at, (a, b) in enumerate(zip(grads, kept))]
    for copy in copies:
        copy.start()
    outs[5][...] = small[0][...]
    outs[6][...] = small[1][0:9]
    outs[7][...] = small[1][9:18]
    outs[8][...] = small[1][18:19]
    for source, target in zip(small[2:], outs[9:]):
        target[...] = source[...]
    for group in range(4):
        load(group).wait()
        for part in range(2):
            for clip_at in range(8):
                store(group, part, clip_at).start()
    for copy in copies:
        copy.wait()
    copies = [pltpu.make_async_copy(a, b, sems.at[8 + at]) for at, (a, b) in enumerate(zip(kept, outs))]
    for copy in copies:
        copy.start()
    for copy in copies:
        copy.wait()
    for group in range(4):
        span = held.at[:, :, pl.ds(group * COLUMNS, COLUMNS)]
        pltpu.make_async_copy(span, span, sems.at[4 + group]).wait()


def fused_body(
    tokens, segment_index, crop_video, stem_down, stem_up, reduce_weight, conv_weight, expand_weight,
    depth_near, depth_far, gate_bias, gains_mid, biases_mid, gains_wide, biases_wide, cotangent,
):
    segs, clips = lax.axis_size("seg"), lax.axis_size("clip")
    amount = tokens.shape[0] * tokens.shape[1] * PIX * segs * clips
    def rows_first(field):
        return field.transpose(2, 1, 0, 3).reshape(PIX, 16, 2048)

    whole = pl.BlockSpec(memory_space=pl.ANY)
    near = pl.BlockSpec(memory_space=pltpu.VMEM)
    field = (PIX, 16, 2048)
    slim = (PIX, 16, COLUMNS)
    split = (PIX, 2, 8, COLUMNS)
    out_shapes = (
        (field, BF, whole), (field, F32, whole),
        ((16, 16, 512), F32, whole), ((4, 16, 2048), F32, whole), ((16, 16, 512), F32, whole),
        ((36, 16, 512), F32, whole), ((4, 16, 2048), F32, whole), (field, F32, whole), (field, BF, whole),
        ((32, 2048), F32, near), ((24, 512), F32, near),
        ((3, 512), F32, near), ((3, 512), F32, near), ((2, 2048), F32, near), ((2, 2048), F32, near),
    )
    tiles = (4 * PIX, 16, COLUMNS)
    weight = (4, 2, 16, 16, COLUMNS)
    scratch = [
        pltpu.VMEM(field, BF), pltpu.VMEM(tiles, BF), pltpu.VMEM(field, F32), pltpu.VMEM(field, F32),
        pltpu.VMEM(tiles, BF), pltpu.VMEM(field, BF),
        pltpu.VMEM(slim, F32), pltpu.VMEM(slim, BF), pltpu.VMEM(slim, F32), pltpu.VMEM(slim, BF),
        pltpu.VMEM(split, F32), pltpu.VMEM(split, F32), pltpu.VMEM(split, F32), pltpu.VMEM(slim, BF),
        pltpu.VMEM((9, 9, 16, 512), BF), pltpu.VMEM((9, 9, 16, 512), BF),
        pltpu.VMEM(slim, F32), pltpu.VMEM(slim, BF),
        pltpu.VMEM((PIX, 16, 256), BF), pltpu.VMEM((PIX, 16, 256), BF),
        pltpu.VMEM(weight, BF), pltpu.VMEM(weight, BF), pltpu.VMEM(weight, BF),
        pltpu.VMEM((9,) + weight[1:], BF), pltpu.VMEM(weight, BF),
        pltpu.VMEM((6, 2, 512), F32), pltpu.VMEM((6, segs * clips, 2, 512), F32),
        pltpu.VMEM((4, 2, 2048), F32), pltpu.VMEM((4, 2, 2048), F32),
        pltpu.VMEM((4, segs, 2, 2048), F32), pltpu.VMEM((4, clips, 2, 2048), F32),
        pltpu.VMEM((3, 2, 512), F32), pltpu.VMEM((2, 2, 2048), F32),
        pltpu.VMEM((POOL_TILES, 16, COLUMNS), BF), pltpu.VMEM((7, 8, COLUMNS), F32),
        pltpu.VMEM((18, 8, COLUMNS), F32), pltpu.VMEM((16, COLUMNS), F32), pltpu.VMEM((8, COLUMNS), F32),
        pltpu.VMEM((8, 128), F32),
        pltpu.SemaphoreType.DMA((16,)), pltpu.SemaphoreType.DMA((32,)), pltpu.SemaphoreType.DMA((2, 6)),
        pltpu.SemaphoreType.DMA((2, 6)), pltpu.SemaphoreType.DMA((4, 4)),
        pltpu.SemaphoreType.DMA((2, 6, 8)), pltpu.SemaphoreType.DMA((2, 3)),
    ]
    outs = pl.pallas_call(
        functools.partial(block_kernel, segs, clips, amount),
        out_shape=tuple(jax.ShapeDtypeStruct(s, d) for s, d, unused in out_shapes),
        in_specs=[whole] * 7 + [near] * 9,
        out_specs=tuple(m for unused, unused_too, m in out_shapes),
        scratch_shapes=scratch,
        compiler_params=pltpu.CompilerParams(
            collective_id=0, has_side_effects=True, vmem_limit_bytes=VMEM_BYTES
        ),
    )(
        rows_first(tokens), rows_first(cotangent), stem_down.reshape(weight),
        stem_up.reshape(2, 16, 16, 2048), reduce_weight.reshape(weight),
        conv_weight.reshape((9,) + weight[1:]), expand_weight.reshape(2, 16, 16, 2048),
        depth_near, depth_far, gate_bias[None], gains_mid, biases_mid, gains_wide, biases_wide,
        segment_index, crop_video[None],
    )
    (
        act, tokens_grad, down_grad, up_grad, reduce_grad, conv_grad, expand_grad, unused, unused_too,
        video_means, depth_sum, gains_mid_grad, biases_mid_grad, gains_wide_grad, biases_wide_grad,
    ) = outs

    big = (tokens_grad, down_grad, up_grad, reduce_grad, conv_grad, expand_grad)
    small = (video_means, depth_sum, gains_mid_grad, biases_mid_grad, gains_wide_grad, biases_wide_grad)
    depth_shapes = ((9, 512), (9, 512), (1, 512))
    small_shapes = (video_means.shape,) + depth_shapes + tuple(x.shape for x in small[2:])
    handed = pl.pallas_call(
        hand_over,
        out_shape=(jax.ShapeDtypeStruct((8, PIX, 2, 2048), F32),)
        + tuple(jax.ShapeDtypeStruct(x.shape, F32) for x in big[1:])
        + tuple(jax.ShapeDtypeStruct(x, F32) for x in small_shapes),
        in_specs=[whole] * 6 + [near] * 6,
        out_specs=(whole,) * 6 + (near,) * 8,
        scratch_shapes=[pltpu.VMEM(x.shape, F32) for x in big] + [pltpu.SemaphoreType.DMA((13,))],
        compiler_params=pltpu.CompilerParams(vmem_limit_bytes=VMEM_BYTES),
    )(*big, *small)
    (
        tokens_grad, down_grad, up_grad, reduce_grad, conv_grad, expand_grad,
        video_means, near_grad, far_grad, gate_grad,
        gains_mid_grad, biases_mid_grad, gains_wide_grad, biases_wide_grad,
    ) = handed

    def clips_first(value):
        return value.reshape(PIX, 2, 8, 2048).transpose(2, 1, 0, 3)

    return (
        clips_first(act),
        video_means,
        tokens_grad.transpose(0, 2, 1, 3),
        down_grad.reshape(256, 512),
        up_grad.reshape(64, 2048),
        reduce_grad.reshape(256, 512),
        conv_grad.reshape(9, 64, 512),
        expand_grad.reshape(64, 2048),
        near_grad,
        far_grad,
        gate_grad[0],
        gains_mid_grad,
        biases_mid_grad,
        gains_wide_grad,
        biases_wide_grad,
    )


POOL_TILES = 334 + 64
VMEM_BYTES = 63 << 20


def solution(mesh):
    def either(tokens, *others):
        devices = (lax.axis_size("seg"), lax.axis_size("clip"))
        fits = tokens.shape == (8, 2, PIX, 2048) and devices == (4, 8)
        return (fused_body if fits else body)(tokens, *others)

    return jax.shard_map(
        either,
        mesh=mesh,
        in_specs=(
            P("clip", "seg", None, None),
            P("clip", None),
            P("clip"),
            P(),
            P(),
            P(),
            P(),
            P(),
            P(),
            P(),
            P(),
            P(),
            P(),
            P(),
            P(),
            P("clip", "seg", None, None),
        ),
        out_specs=(
            P("clip", "seg", None, None),
            P(),
            P("clip", "seg", None, None),
            P("clip", None),
            P("clip", None),
            P("clip", None),
            P(None, "clip", None),
            P("clip", None),
            P(),
            P(),
            P(),
            P(),
            P(),
            P(),
            P(),
        ),
        check_vma=False,
    )
```

```python
import functools

import jax
import jax.numpy as jnp
from jax import lax
from jax.experimental import pallas as pl
from jax.experimental.pallas import tpu as pltpu
from jax.sharding import PartitionSpec as P

HEIGHT = 7
WIDTH = 7
SEGS = 8
PIX = 49


NORM_EPSILON = 1e-05


MESH = pl.DeviceIdType.MESH


def exchange(source, landing, send_sem, recv_sem, axis, count):
    here = lax.axis_index(axis)
    for step in range(1, count):
        pltpu.make_async_remote_copy(
            source,
            landing.at[here],
            send_sem,
            recv_sem,
            device_id={axis: lax.rem(here + step, count)},
            device_id_type=MESH,
        ).start()
    landing[pl.ds(here, 1)] = source[...][None]
    arrived = landing.at[pl.ds(0, count - 1)]
    pltpu.make_async_copy(arrived, arrived, recv_sem).wait()
    total = landing[0]
    for rank in range(1, count):
        total = total + landing[rank]
    pltpu.make_async_copy(arrived, arrived, send_sem).wait()
    return total


def sum_kernel(segs, clips, values, result, middle, seg_land, clip_land, sems):
    barrier = pltpu.get_barrier_semaphore()
    for axis, count in (("seg", segs), ("clip", clips)):
        here = lax.axis_index(axis)
        for step in range(1, count):
            pl.semaphore_signal(
                barrier,
                inc=1,
                device_id={axis: lax.rem(here + step, count)},
                device_id_type=MESH,
            )
    pl.semaphore_wait(barrier, segs + clips - 2)
    middle[...] = exchange(values, seg_land, sems.at[0], sems.at[1], "seg", segs)
    result[...] = exchange(middle, clip_land, sems.at[2], sems.at[3], "clip", clips)


def sum_everywhere(first, second):
    segs, clips = lax.axis_size("seg"), lax.axis_size("clip")
    width = first.shape[0]
    summed = pl.pallas_call(
        functools.partial(sum_kernel, segs, clips),
        out_shape=jax.ShapeDtypeStruct((2, width), jnp.float32),
        in_specs=[pl.BlockSpec(memory_space=pltpu.VMEM)],
        out_specs=pl.BlockSpec(memory_space=pltpu.VMEM),
        scratch_shapes=[
            pltpu.VMEM((2, width), jnp.float32),
            pltpu.VMEM((segs, 2, width), jnp.float32),
            pltpu.VMEM((clips, 2, width), jnp.float32),
            pltpu.SemaphoreType.DMA((4,)),
        ],
        compiler_params=pltpu.CompilerParams(
            collective_id=0 if width < 1024 else 1, has_side_effects=True
        ),
    )(jnp.stack([first, second]))
    return summed[0], summed[1]


def shifted(block, axis, distance):
    devices = range(lax.axis_size(axis))
    route = [(i - distance, i) for i in devices if i - distance in devices]
    return lax.ppermute(block, axis, route)


def row_product(left_side, weight):
    return lax.dot_general(
        left_side,
        weight,
        (((left_side.ndim - 1,), (0,)), ((), ())),
        preferred_element_type=jnp.float32,
    )


def back_product(gradient, weight):
    return lax.dot_general(
        gradient,
        weight,
        (((gradient.ndim - 1,), (1,)), ((), ())),
        preferred_element_type=jnp.float32,
    )


def weight_gradient(left_side, gradient):
    return jnp.einsum("cspk,cspo->ko", left_side, gradient, preferred_element_type=jnp.float32)


def smooth(values):
    return jax.nn.gelu(values, approximate=True)


def depth_conv(field, kernel, reach):
    leading = field.shape[:2]
    planes = field.reshape(leading + (HEIGHT, WIDTH, field.shape[3]))
    padded = jnp.pad(planes, ((0, 0), (0, 0), (reach, reach), (reach, reach), (0, 0)))
    result = jnp.zeros_like(planes)
    for position in range(9):
        down = position // 3 * reach
        across = position % 3 * reach
        result = (
            result
            + padded[:, :, down : down + HEIGHT, across : across + WIDTH, :] * kernel[position]
        )
    return result.reshape(field.shape)


def gate_apply(active, change, near_kernel, far_kernel, offsets):
    mixed = depth_conv(change, near_kernel, 1) + depth_conv(change, far_kernel, 2) + offsets
    return active * (1.0 + jax.nn.sigmoid(mixed))


def frame_planes(field):
    planes = field.reshape(field.shape[:2] + (HEIGHT, WIDTH, field.shape[3]))
    return jnp.pad(planes, ((0, 0), (0, 0), (1, 1), (1, 1), (0, 0)))


def frame_conv(field, weight):
    padded = frame_planes(field)
    result = jnp.zeros(field.shape[:2] + (HEIGHT, WIDTH, weight.shape[2]), jnp.float32)
    for position in range(9):
        down = position // 3
        across = position % 3
        result = result + row_product(
            padded[:, :, down : down + HEIGHT, across : across + WIDTH, :], weight[position]
        )
    return result.reshape(field.shape[:3] + (weight.shape[2],))


def frame_conv_back(field, weight, gradient):
    padded = frame_planes(field)
    planes = gradient.reshape(gradient.shape[:2] + (HEIGHT, WIDTH, gradient.shape[3]))
    field_grad = jnp.zeros(padded.shape, jnp.float32)
    kernel_grads = []
    for position in range(9):
        down = position // 3
        across = position % 3
        window = padded[:, :, down : down + HEIGHT, across : across + WIDTH, :]
        kernel_grads.append(
            jnp.einsum("csijk,csijo->ko", window, planes, preferred_element_type=jnp.float32)
        )
        field_grad = field_grad.at[:, :, down : down + HEIGHT, across : across + WIDTH, :].add(
            back_product(planes, weight[position])
        )
    inner = field_grad[:, :, 1 : 1 + HEIGHT, 1 : 1 + WIDTH, :]
    return (inner.reshape(field.shape), jnp.stack(kernel_grads))


def body(
    tokens,
    segment_index,
    crop_video,
    stem_down,
    stem_up,
    reduce_weight,
    conv_weight,
    expand_weight,
    depth_near,
    depth_far,
    gate_bias,
    gains_mid,
    biases_mid,
    gains_wide,
    biases_wide,
    cotangent,
):
    seg_count = lax.axis_size("seg")
    clip_count = lax.axis_size("clip")
    seg_here = lax.axis_index("seg")
    local_segs = tokens.shape[1]
    amount = tokens.shape[0] * local_segs * tokens.shape[2] * seg_count * clip_count
    spacing = (segment_index[:, 1:] - segment_index[:, :-1]).astype(jnp.float32)
    full_weight = jnp.concatenate(
        [1.0 / spacing, jnp.zeros((spacing.shape[0], 1), jnp.float32)], axis=1
    )
    local_weight = lax.dynamic_slice_in_dim(full_weight, seg_here * local_segs, local_segs, 1)

    def gather_stats(values):
        return sum_everywhere(
            jnp.sum(values, axis=(0, 1, 2)), jnp.sum(values * values, axis=(0, 1, 2))
        )

    def normalize(values, first_sum, second_sum, scales, shifts):
        center = first_sum / amount
        spread = second_sum / amount - center * center
        return (values - center) * lax.rsqrt(spread + NORM_EPSILON) * scales + shifts

    def norm_smooth(values, first_sum, second_sum, scales, shifts):
        return smooth(normalize(values, first_sum, second_sum, scales, shifts))

    def block_finish(values, first_sum, second_sum, scales, shifts, skipped):
        return smooth(skipped + normalize(values, first_sum, second_sum, scales, shifts))

    def norm_back(piece, primals, gradient):
        unused, pull = jax.vjp(piece, *primals)
        pulled = pull(gradient)
        first_grad, second_grad = sum_everywhere(pulled[1], pulled[2])
        values = primals[0]
        return (pulled[0] + first_grad + 2.0 * values * second_grad,) + tuple(pulled[3:])

    frames = tokens.astype(jnp.float32)
    following = shifted(tokens[:, :1], "seg", -1).astype(jnp.float32)
    later = jnp.concatenate([frames[:, 1:], following], axis=1)
    frame_change = ((later - frames) * local_weight[:, :, None, None]).astype(jnp.bfloat16)
    stem_inner = row_product(frame_change, stem_down)
    inner_sums = gather_stats(stem_inner)
    stem_active = norm_smooth(
        stem_inner, inner_sums[0], inner_sums[1], gains_mid[0], biases_mid[0]
    ).astype(jnp.bfloat16)
    stem_outer = row_product(stem_active, stem_up)
    outer_sums = gather_stats(stem_outer)
    block_input = (
        frames + normalize(stem_outer, outer_sums[0], outer_sums[1], gains_wide[0], biases_wide[0])
    ).astype(jnp.bfloat16)
    reduced = row_product(block_input, reduce_weight)
    reduced_sums = gather_stats(reduced)
    reduced_act = norm_smooth(
        reduced, reduced_sums[0], reduced_sums[1], gains_mid[1], biases_mid[1]
    ).astype(jnp.bfloat16)
    channel_act = lax.all_to_all(
        reduced_act, "seg", split_axis=3, concat_axis=1, tiled=True
    ).astype(jnp.float32)
    narrow = channel_act.shape[3]
    near_local = lax.dynamic_slice_in_dim(depth_near, seg_here * narrow, narrow, 1)
    far_local = lax.dynamic_slice_in_dim(depth_far, seg_here * narrow, narrow, 1)
    offset_local = lax.dynamic_slice_in_dim(gate_bias, seg_here * narrow, narrow, 0)
    shifted_act = jnp.concatenate([channel_act[:, 1:], jnp.zeros_like(channel_act[:, :1])], axis=1)
    act_change = (shifted_act - channel_act) * full_weight[:, :, None, None]
    gated_channels = gate_apply(
        channel_act, act_change, near_local, far_local, offset_local
    ).astype(jnp.bfloat16)
    gated = lax.all_to_all(gated_channels, "seg", split_axis=1, concat_axis=3, tiled=True)
    convolved = frame_conv(gated, conv_weight)
    conv_sums = gather_stats(convolved)
    conv_act = norm_smooth(
        convolved, conv_sums[0], conv_sums[1], gains_mid[2], biases_mid[2]
    ).astype(jnp.bfloat16)
    expanded = row_product(conv_act, expand_weight)
    expanded_sums = gather_stats(expanded)
    residual = block_input.astype(jnp.float32)
    block_output = block_finish(
        expanded, expanded_sums[0], expanded_sums[1], gains_wide[1], biases_wide[1], residual
    )
    activations = block_output.astype(jnp.bfloat16)
    video_total = tokens.shape[0] * clip_count // 2
    pooled = jnp.sum(block_output, axis=(1, 2)) / (SEGS * PIX)
    membership = (crop_video[:, None] == jnp.arange(video_total, dtype=jnp.int32)[None, :]).astype(
        jnp.float32
    )
    video_part = jnp.dot(membership.T, pooled, precision=lax.Precision.HIGHEST)
    count_part = jnp.sum(membership, axis=0) * (seg_here == 0).astype(jnp.float32)
    video_sums, video_counts = lax.psum((video_part, count_part), ("seg", "clip"))
    video_means = video_sums / video_counts[:, None]
    grad_output = cotangent.astype(jnp.float32)
    grad_expanded, wide_gain_one, wide_bias_one, grad_skip = norm_back(
        block_finish,
        (expanded, expanded_sums[0], expanded_sums[1], gains_wide[1], biases_wide[1], residual),
        grad_output,
    )
    grad_expanded = grad_expanded.astype(jnp.bfloat16)
    expand_grad = weight_gradient(conv_act, grad_expanded)
    grad_conv_act = back_product(grad_expanded, expand_weight)
    grad_convolved, mid_gain_two, mid_bias_two = norm_back(
        norm_smooth,
        (convolved, conv_sums[0], conv_sums[1], gains_mid[2], biases_mid[2]),
        grad_conv_act,
    )
    grad_convolved = grad_convolved.astype(jnp.bfloat16)
    grad_gated, conv_grad = frame_conv_back(gated, conv_weight, grad_convolved)
    grad_gated = grad_gated.astype(jnp.bfloat16)
    grad_gated_channels = lax.all_to_all(
        grad_gated, "seg", split_axis=3, concat_axis=1, tiled=True
    ).astype(jnp.float32)
    unused_gate, gate_pull = jax.vjp(
        gate_apply, channel_act, act_change, near_local, far_local, offset_local
    )
    grad_direct, grad_change, near_part, far_part, offset_part = gate_pull(grad_gated_channels)
    weighted = grad_change * full_weight[:, :, None, None]
    grad_act_channels = (
        grad_direct
        + jnp.concatenate([jnp.zeros_like(weighted[:, :1]), weighted[:, :-1]], axis=1)
        - weighted
    ).astype(jnp.bfloat16)
    grad_reduced_act = lax.all_to_all(
        grad_act_channels, "seg", split_axis=1, concat_axis=3, tiled=True
    ).astype(jnp.float32)
    near_grad = lax.dynamic_update_slice_in_dim(
        jnp.zeros_like(depth_near), near_part, seg_here * narrow, 1
    )
    far_grad = lax.dynamic_update_slice_in_dim(
        jnp.zeros_like(depth_far), far_part, seg_here * narrow, 1
    )
    gate_bias_grad = lax.dynamic_update_slice_in_dim(
        jnp.zeros_like(gate_bias), offset_part, seg_here * narrow, 0
    )
    grad_reduced, mid_gain_one, mid_bias_one = norm_back(
        norm_smooth,
        (reduced, reduced_sums[0], reduced_sums[1], gains_mid[1], biases_mid[1]),
        grad_reduced_act,
    )
    grad_reduced = grad_reduced.astype(jnp.bfloat16)
    reduce_grad = weight_gradient(block_input, grad_reduced)
    grad_block_input = back_product(grad_reduced, reduce_weight) + grad_skip
    grad_stem_outer, wide_gain_zero, wide_bias_zero = norm_back(
        normalize,
        (stem_outer, outer_sums[0], outer_sums[1], gains_wide[0], biases_wide[0]),
        grad_block_input,
    )
    grad_stem_outer = grad_stem_outer.astype(jnp.bfloat16)
    stem_up_grad = weight_gradient(stem_active, grad_stem_outer)
    grad_stem_active = back_product(grad_stem_outer, stem_up)
    grad_stem_inner, mid_gain_zero, mid_bias_zero = norm_back(
        norm_smooth,
        (stem_inner, inner_sums[0], inner_sums[1], gains_mid[0], biases_mid[0]),
        grad_stem_active,
    )
    grad_stem_inner = grad_stem_inner.astype(jnp.bfloat16)
    stem_down_grad = weight_gradient(frame_change, grad_stem_inner)
    grad_change_in = back_product(grad_stem_inner, stem_down)
    weighted_in = grad_change_in * local_weight[:, :, None, None]
    earlier = shifted(weighted_in[:, -1:].astype(jnp.bfloat16), "seg", 1).astype(jnp.float32)
    tokens_grad = (
        grad_block_input + jnp.concatenate([earlier, weighted_in[:, :-1]], axis=1) - weighted_in
    )
    members = (
        near_grad,
        far_grad,
        gate_bias_grad,
        jnp.stack([mid_gain_zero, mid_gain_one, mid_gain_two]),
        jnp.stack([mid_bias_zero, mid_bias_one, mid_bias_two]),
        jnp.stack([wide_gain_zero, wide_gain_one]),
        jnp.stack([wide_bias_zero, wide_bias_one]),
    )
    flat_grads = jnp.concatenate([member.reshape(-1) for member in members])
    summed_small = lax.psum(flat_grads, ("seg", "clip"))
    unpacked = []
    cursor = 0
    for member in members:
        unpacked.append(summed_small[cursor : cursor + member.size].reshape(member.shape))
        cursor = cursor + member.size
    shares = (
        lax.psum_scatter(
            stem_down_grad.astype(jnp.bfloat16), "clip", scatter_dimension=0, tiled=True
        ).astype(jnp.float32),
        lax.psum_scatter(
            stem_up_grad.astype(jnp.bfloat16), "clip", scatter_dimension=0, tiled=True
        ).astype(jnp.float32),
        lax.psum_scatter(
            reduce_grad.astype(jnp.bfloat16), "clip", scatter_dimension=0, tiled=True
        ).astype(jnp.float32),
        lax.psum_scatter(
            conv_grad.astype(jnp.bfloat16), "clip", scatter_dimension=1, tiled=True
        ).astype(jnp.float32),
        lax.psum_scatter(
            expand_grad.astype(jnp.bfloat16), "clip", scatter_dimension=0, tiled=True
        ).astype(jnp.float32),
    )
    big = (
        lax.psum(shares[0].astype(jnp.bfloat16), "seg").astype(jnp.float32),
        lax.psum(shares[1].astype(jnp.bfloat16), "seg").astype(jnp.float32),
        lax.psum(shares[2].astype(jnp.bfloat16), "seg").astype(jnp.float32),
        lax.psum(shares[3].astype(jnp.bfloat16), "seg").astype(jnp.float32),
        lax.psum(shares[4].astype(jnp.bfloat16), "seg").astype(jnp.float32),
    )
    return (
        activations,
        video_means,
        tokens_grad,
        big[0],
        big[1],
        big[2],
        big[3],
        big[4],
        unpacked[0],
        unpacked[1],
        unpacked[2],
        unpacked[3],
        unpacked[4],
        unpacked[5],
        unpacked[6],
    )


ROOT_TWO_OVER_PI = 0.7978845608
CUBIC = 0.044715


def smooth_pair(values):
    square = values * values
    bent = jnp.tanh(values * (ROOT_TWO_OVER_PI + ROOT_TWO_OVER_PI * CUBIC * square))
    half = 0.5 + 0.5 * bent
    slope = half * (
        1.0
        + values * (1.0 - bent) * (ROOT_TWO_OVER_PI + 3.0 * ROOT_TWO_OVER_PI * CUBIC * square)
    )
    return values * half, slope


def smooth_value(values):
    square = values * values
    bent = jnp.tanh(values * (ROOT_TWO_OVER_PI + ROOT_TWO_OVER_PI * CUBIC * square))
    return values * (0.5 + 0.5 * bent)


def rows_sum(values):
    return jnp.sum(values, axis=0, keepdims=True)


def flat(values):
    return values.reshape(-1, values.shape[-1])


def dot(left, right):
    return jnp.dot(left, right, preferred_element_type=jnp.float32)


def dot_back(left, right):
    return lax.dot_general(left, right, (((1,), (1,)), ((), ())), preferred_element_type=jnp.float32)


def dot_rows(left, right):
    return lax.dot_general(left, right, (((0,), (0,)), ((), ())), preferred_element_type=jnp.float32)


BF = jnp.bfloat16
F32 = jnp.float32
WIDE_TILE = 256
COLUMNS = 512


def near_taps():
    return [(a - 1, b - 1) for a in range(3) for b in range(3)]


def far_taps():
    return [(2 * (a - 1), 2 * (b - 1)) for a in range(3) for b in range(3)]


def block_kernel(segs, clips, amount, *refs):
    (
        tokens_hbm, cot_hbm, down_hbm, up_hbm, reduce_hbm, conv_hbm, expand_hbm,
        near, far, gate_bias, gains_mid, biases_mid, gains_wide, biases_wide, frames_at, crops_at,
        act_hbm, tokens_grad_hbm, down_grad, up_grad, reduce_grad, conv_grad, expand_grad, spill, frame_spill,
        video_means, near_grad, far_grad, gate_grad,
        gains_mid_grad, biases_mid_grad, gains_wide_grad, biases_wide_grad,
        tok, frame, outer, skip, cot, wide,
        inner, active, reduced, acts, change, gates, conv, conv_act, gated, back_pad, temp, back,
        halo_out, halo_in,
        down, up, reduce_w, conv_w, expand_w,
        slim_src, slim_land, wide_src, wide_mid, wide_seg, wide_clip,
        slim_norm, wide_norm, pool, video_src, depth, step_weight, past_weight, crop_id,
        load_sem, store_sem, halo_sem, slim_sem, wide_sem, ring_sem, video_sem,
    ) = refs
    seg = lax.axis_index("seg")
    clip = lax.axis_index("clip")
    devices = segs * clips
    me = seg * clips + clip
    scale = 1.0 / amount

    def peer_of(step):
        peer = lax.rem(me + step, devices)
        return (peer // clips, lax.rem(peer, clips))

    barrier = pltpu.get_barrier_semaphore()

    def greet(step, carry):
        pl.semaphore_signal(barrier, inc=1, device_id=peer_of(step), device_id_type=MESH)
        return carry

    lax.fori_loop(1, devices, greet, 0)

    def column_group(group):
        return pl.ds(group * COLUMNS, COLUMNS)

    class Loads:
        def __init__(self, at, pairs):
            self.copies = [
                pltpu.make_async_copy(source, target, load_sem.at[at + k])
                for k, (source, target) in enumerate(pairs)
            ]
            for copy in self.copies:
                copy.start()

        def wait(self):
            for copy in self.copies:
                copy.wait()

    def by_group(source, target):
        return [(source.at[:, :, :, column_group(g)], target.at[g]) for g in range(4)]

    loads = {
        "tok": Loads(0, [(tokens_hbm, tok)]),
        "down": Loads(1, [(down_hbm, down)]),
        "up": Loads(2, by_group(up_hbm, up)),
        "reduce": Loads(6, [(reduce_hbm, reduce_w)]),
        "conv": Loads(7, [(conv_hbm, conv_w)]),
        "expand": Loads(8, by_group(expand_hbm, expand_w)),
        "cot": Loads(
            12,
            [(cot_hbm.at[:, :, column_group(g)], cot.at[pl.ds(g * PIX, PIX)]) for g in range(4)],
        ),
    }

    segment = lax.broadcasted_iota(jnp.int32, (8, SEGS), 1)

    def frame_at(which):
        return jnp.sum(jnp.where(segment == which, frames_at[...].astype(F32), 0.0), axis=1, keepdims=True)

    def weight_at(which):
        inside_clip = jnp.logical_and(which >= 0, which < SEGS - 1)
        spacing = jnp.where(inside_clip, frame_at(which + 1) - frame_at(which), 1.0)
        return jnp.broadcast_to(jnp.where(inside_clip, 1.0 / spacing, 0.0), (8, COLUMNS))

    past_weight[...] = weight_at(seg * 2 - 1)
    step_weight[0:8] = weight_at(seg * 2)
    step_weight[8:16] = weight_at(seg * 2 + 1)
    names = jnp.broadcast_to(crops_at[...].astype(F32), (8, 8))
    diagonal = segment == lax.broadcasted_iota(jnp.int32, (8, SEGS), 0)
    crop_id[...] = jnp.broadcast_to(
        jnp.sum(jnp.where(diagonal, names, 0.0), axis=1, keepdims=True), (8, 128)
    )
    for k in range(9):
        depth[k] = jnp.broadcast_to(near[k : k + 1], (8, COLUMNS))
        depth[9 + k] = jnp.broadcast_to(far[k : k + 1], (8, COLUMNS))

    def slim_start(at):
        def one(step, carry):
            pltpu.make_async_remote_copy(
                slim_src.at[at], slim_land.at[at, me], slim_sem.at[0, at], slim_sem.at[1, at],
                device_id=peer_of(step), device_id_type=MESH,
            ).start()
            return carry

        lax.fori_loop(1, devices, one, 0)
        slim_land[at, pl.ds(me, 1)] = slim_src[at][None]

    def gather_wait(landing, count, sem):
        arrived = landing.at[pl.ds(0, count - 1)]
        pltpu.make_async_copy(arrived, arrived, sem).wait()

    def slot_total(landing, count):
        total = landing[0]
        for rank in range(1, count):
            total = total + landing[rank]
        return total

    def slim_finish(at):
        land = slim_land.at[at]
        gather_wait(land, devices, slim_sem.at[1, at])
        total = slot_total(land, devices)
        gather_wait(land, devices, slim_sem.at[0, at])
        return total

    def axis_start(source, landing, axis, count, send, recv):
        here = lax.axis_index(axis)
        for step in range(1, count):
            pltpu.make_async_remote_copy(
                source, landing.at[here], send, recv,
                device_id={axis: lax.rem(here + step, count)}, device_id_type=MESH,
            ).start()
        landing[pl.ds(here, 1)] = source[...][None]

    def wide_first(at):
        axis_start(wide_src.at[at], wide_seg.at[at], "seg", segs, wide_sem.at[0, at], wide_sem.at[1, at])

    def wide_second(at):
        gather_wait(wide_seg.at[at], segs, wide_sem.at[1, at])
        wide_mid[at] = slot_total(wide_seg.at[at], segs)
        gather_wait(wide_seg.at[at], segs, wide_sem.at[0, at])
        axis_start(wide_mid.at[at], wide_clip.at[at], "clip", clips, wide_sem.at[2, at], wide_sem.at[3, at])

    def wide_half(half):
        return pl.ds(half * 1024, 1024)

    def wide_finish(at):
        gather_wait(wide_clip.at[at], clips, wide_sem.at[3, at])
        total = slot_total(wide_clip.at[at], clips)
        gather_wait(wide_clip.at[at], clips, wide_sem.at[2, at])
        return total

    def keep_norm(total, kept):
        center = total[0:1] * scale
        spread = total[1:2] * scale - center * center
        kept[0:1] = center
        kept[1:2] = lax.rsqrt(spread + NORM_EPSILON)

    def pixels(body, start):
        def line(row, carry):
            for across in range(WIDTH):
                carry = body(row * WIDTH + across, row, across, carry)
            return carry

        return lax.fori_loop(0, HEIGHT, line, start)

    def halves(values):
        return values[0:8], values[8:16]

    def fold(values):
        return values[0:8] + values[8:16]

    slim_zero = jnp.zeros((8, COLUMNS), F32)

    def spread_row(row):
        return jnp.broadcast_to(row, (8, row.shape[-1]))

    def both(values):
        return jnp.concatenate([values, values], axis=0)

    def row16(row):
        return jnp.broadcast_to(row, (16, row.shape[-1]))

    def halo_start(source, target, at, ahead):
        copy = pltpu.make_async_remote_copy(
            source, target, halo_sem.at[0, at], halo_sem.at[1, at],
            device_id={"seg": jnp.clip(seg + ahead, 0, segs - 1)}, device_id_type=MESH,
        )
        can = seg < segs - 1 if ahead > 0 else seg > 0

        @pl.when(can)
        def _():
            copy.start()

    def halo_finish(source, target, at, ahead):
        copy = pltpu.make_async_remote_copy(
            source, target, halo_sem.at[0, at], halo_sem.at[1, at],
            device_id={"seg": jnp.clip(seg + ahead, 0, segs - 1)}, device_id_type=MESH,
        )
        sends = seg < segs - 1 if ahead > 0 else seg > 0
        takes = seg > 0 if ahead > 0 else seg < segs - 1

        @pl.when(takes)
        def _():
            copy.wait_recv()

        @pl.when(jnp.logical_not(takes))
        def _():
            target[...] = jnp.zeros_like(target)

        @pl.when(sends)
        def _():
            copy.wait_send()

    product, product_next = change, conv
    loads["tok"].wait()
    loads["down"].wait()
    for tile in range(2):
        at = pl.ds(tile * WIDE_TILE, WIDE_TILE)
        value = dot(flat(tok[...]), flat(down[:, :, :, :, at]))
        product[:, :, :, at] = value.reshape(PIX, 2, 8, WIDE_TILE)
        if tile == 0:
            pl.semaphore_wait(barrier, devices - 1)
        halo_start(product.at[:, 0, :, at], product_next.at[:, 0, :, at], tile, -1)
    for tile in range(2):
        at = pl.ds(tile * WIDE_TILE, WIDE_TILE)
        halo_finish(product.at[:, 0, :, at], product_next.at[:, 0, :, at], tile, -1)

    def inner_body(pixel, row, across, carry):
        first, second = carry
        zero, one, after = product[pixel, 0], product[pixel, 1], product_next[pixel, 0]
        early = (one - zero) * step_weight[0:8]
        late = (after - one) * step_weight[8:16]
        inner[pixel] = jnp.concatenate([early, late], axis=0)
        return first + early + late, second + early * early + late * late

    first, second = pixels(inner_body, (slim_zero, slim_zero))
    slim_src[0, 0:1] = rows_sum(first)
    slim_src[0, 1:2] = rows_sum(second)
    slim_start(0)

    token_out, token_in = wide.at[:, :, pl.ds(0, 1024)], wide.at[:, :, pl.ds(1024, 1024)]

    def token_pack(pixel, row, across, carry):
        value = tok[pixel].astype(F32)[0:8]
        wide[pixel, :, pl.ds(0, 1024)] = jnp.concatenate(
            [value[:, 0:1024], value[:, 1024:2048]], axis=0
        ).astype(BF)
        return carry

    pixels(token_pack, 0)
    halo_start(token_out, token_in, 2, -1)

    keep_norm(slim_finish(0), slim_norm.at[0])

    def activate(source, target, at):
        center, rate = row16(slim_norm[at, 0:1]), row16(slim_norm[at, 1:2] * gains_mid[at : at + 1])
        bias = row16(biases_mid[at : at + 1])

        def body(pixel, row, across, carry):
            target[pixel] = smooth_value((source[pixel] - center) * rate + bias).astype(BF)
            return carry

        pixels(body, 0)

    activate(inner, active, 0)

    loads["up"].wait()

    def widen(source, weight, sums):
        for half in range(2):

            def body(part, carry):
                tile = half * 4 + part
                at = pl.ds(pl.multiple_of(tile * WIDE_TILE, WIDE_TILE), WIDE_TILE)
                lanes = pl.ds(pl.multiple_of(lax.rem(part, 2) * WIDE_TILE, WIDE_TILE), WIDE_TILE)
                value = dot(flat(source[...]), flat(weight[half * 2 + part // 2, :, :, :, lanes]))
                outer[:, :, at] = value.reshape(PIX, 16, WIDE_TILE)
                here = pl.ds(pl.multiple_of(part * WIDE_TILE, WIDE_TILE), WIDE_TILE)
                wide_src[sums * 2 + half, 0:1, here] = rows_sum(value)
                wide_src[sums * 2 + half, 1:2, here] = rows_sum(value * value)
                return carry

            lax.fori_loop(0, 4, body, 0)
            wide_first(sums * 2 + half)

    widen(active, up, 0)
    wide_second(0)
    wide_second(1)

    def frame_start(pixel, row, across, carry):
        for part in range(4):
            at = pl.ds(part * COLUMNS, COLUMNS)
            zero, one = halves(tok[pixel, :, at].astype(F32))
            frame[part * PIX + pixel] = jnp.concatenate(
                [(one - zero) * step_weight[0:8], one], axis=0
            ).astype(BF)
        return carry

    pixels(frame_start, 0)

    def wide_pixels(body, half):
        def part(at, carry):
            columns = pl.ds(pl.multiple_of(at * COLUMNS, COLUMNS), COLUMNS)
            body(at, columns)
            return carry

        lax.fori_loop(half * 2, half * 2 + 2, part, 0)

    def input_part(group, columns):
        center = row16(wide_norm[0, 0:1, columns])
        rate = row16(wide_norm[0, 1:2, columns] * gains_wide[0:1, columns])
        bias = row16(biases_wide[0:1, columns])

        def body(pixel, row, across, carry):
            value = (outer[pixel, :, columns] - center) * rate + bias
            tok[pixel, :, columns] = (tok[pixel, :, columns].astype(F32) + value).astype(BF)
            return carry

        pixels(body, 0)

    for half in range(2):
        keep_norm(wide_finish(half), wide_norm.at[0, :, wide_half(half)])
        wide_pixels(input_part, half)
    block_input = tok
    spill_out = pltpu.make_async_copy(outer, spill, store_sem.at[0])
    spill_out.start()

    loads["reduce"].wait()
    for tile in range(2):
        at = pl.ds(tile * WIDE_TILE, WIDE_TILE)
        value = dot(flat(block_input[...]), flat(reduce_w[:, :, :, :, at]))
        reduced[:, :, at] = value.reshape(PIX, 16, WIDE_TILE)
        slim_src[1, 0:1, at] = rows_sum(value)
        slim_src[1, 1:2, at] = rows_sum(value * value)
    slim_start(1)
    halo_finish(token_out, token_in, 2, -1)

    def frame_finish(pixel, row, across, carry):
        ahead = wide[pixel, :, pl.ds(1024, 1024)].astype(F32)
        for part in range(4):
            zero, one = halves(frame[part * PIX + pixel].astype(F32))
            half, low = (0, part) if part < 2 else (8, part - 2)
            after = ahead[half : half + 8, low * COLUMNS : (low + 1) * COLUMNS]
            frame[part * PIX + pixel] = jnp.concatenate(
                [zero, (after - one) * step_weight[8:16]], axis=0
            ).astype(BF)
        return carry

    pixels(frame_finish, 0)
    frame_out = [
        pltpu.make_async_copy(
            frame.at[pl.ds(g * PIX, PIX)], frame_spill.at[:, :, column_group(g)], store_sem.at[2 + g]
        )
        for g in range(4)
    ]
    for copy in frame_out:
        copy.start()
    keep_norm(slim_finish(1), slim_norm.at[1])

    def act_parts():
        center, rate = row16(slim_norm[1, 0:1]), row16(slim_norm[1, 1:2] * gains_mid[1:2])
        bias = row16(biases_mid[1:2])

        def body(pixel, row, across, carry):
            value = smooth_value((reduced[pixel] - center) * rate + bias).astype(BF)
            acts[pixel] = value
            lead = value.astype(F32)[0:8]
            halo_out[pixel] = jnp.concatenate([lead[:, 0:256], lead[:, 256:512]], axis=0).astype(BF)
            return carry

        pixels(body, 0)

    act_parts()
    halo_start(halo_out, halo_in, 3, -1)

    def change_early(pixel, row, across, carry):
        zero, one = halves(acts[pixel].astype(F32))
        change[pixel, 0] = (one - zero) * step_weight[0:8]
        change[pixel, 1] = one
        return carry

    pixels(change_early, 0)

    def lanes_of(tile):
        return pl.ds(pl.multiple_of(tile * 128, 128), 128)

    def inside(row, column):
        return 0 <= row < HEIGHT and 0 <= column < WIDTH

    def gate_tile(which):
        def body(tile, carry):
            lanes = lanes_of(tile)
            kernels = [depth[k, :, lanes] for k in range(18)]
            middle = kernels[4] + kernels[13]
            offsets = jnp.broadcast_to(gate_bias[0:1, lanes], (8, 128))
            field = [change[p, which, :, lanes] for p in range(PIX)]
            for i in range(HEIGHT):
                for j in range(WIDTH):
                    mixed = offsets + middle * field[i * WIDTH + j]
                    for base, taps in ((0, near_taps()), (9, far_taps())):
                        for k, (di, dj) in enumerate(taps):
                            if (di or dj) and inside(i + di, j + dj):
                                mixed = mixed + kernels[base + k] * field[(i + di) * WIDTH + j + dj]
                    gates[i * WIDTH + j, which, :, lanes] = 0.5 + 0.5 * jnp.tanh(0.5 * mixed)
            return carry

        lax.fori_loop(0, 4, body, 0)

    gate_tile(0)
    halo_finish(halo_out, halo_in, 3, -1)

    def change_late(pixel, row, across, carry):
        ahead = halo_in[pixel].astype(F32)
        after = jnp.concatenate([ahead[0:8], ahead[8:16]], axis=1)
        change[pixel, 1] = (after - change[pixel, 1]) * step_weight[8:16]
        return carry

    pixels(change_late, 0)
    gate_tile(1)

    for side in range(9):
        edge = jnp.zeros((16, COLUMNS), BF)
        for pad in (gated, back_pad):
            pad[0, side] = edge
            pad[8, side] = edge
            pad[side, 0] = edge
            pad[side, 8] = edge

    def gated_body(pixel, row, across, carry):
        both_gates = jnp.concatenate([gates[pixel, 0], gates[pixel, 1]], axis=0)
        gated[row + 1, across + 1] = (acts[pixel].astype(F32) * (1.0 + both_gates)).astype(BF)
        return carry

    pixels(gated_body, 0)

    loads["conv"].wait()

    def window(pad, a, b):
        return flat(pad[a : a + HEIGHT, b : b + WIDTH])

    for tile in range(2):
        at = pl.ds(tile * WIDE_TILE, WIDE_TILE)
        value = dot(window(gated, 0, 0), flat(conv_w[0, :, :, :, at]))
        for tap in range(1, 9):
            value = value + dot(window(gated, tap // 3, tap % 3), flat(conv_w[tap, :, :, :, at]))
        conv[:, :, :, at] = value.reshape(PIX, 2, 8, WIDE_TILE)
        slim_src[2, 0:1, at] = rows_sum(value)
        slim_src[2, 1:2, at] = rows_sum(value * value)
    slim_start(2)
    spill_out.wait()
    loads["expand"].wait()
    loads["cot"].wait()
    keep_norm(slim_finish(2), slim_norm.at[2])

    def conv_rows(pixel):
        return conv[pixel].reshape(16, COLUMNS)

    def conv_act_part():
        center, rate = row16(slim_norm[2, 0:1]), row16(slim_norm[2, 1:2] * gains_mid[2:3])
        bias = row16(biases_mid[2:3])

        def body(pixel, row, across, carry):
            conv_act[pixel] = smooth_value((conv_rows(pixel) - center) * rate + bias).astype(BF)
            return carry

        pixels(body, 0)

    conv_act_part()
    widen(conv_act, expand_w, 1)
    wide_second(2)
    wide_second(3)

    def output_part(group, columns):
        center = row16(wide_norm[1, 0:1, columns])
        rate = row16(wide_norm[1, 1:2, columns])
        gain = row16(gains_wide[1:2, columns])
        bias = row16(biases_wide[1:2, columns])

        def body(pixel, row, across, carry):
            pool, shift, stretch = carry
            unit = (outer[pixel, :, columns] - center) * rate
            value, slope = smooth_pair(block_input[pixel, :, columns].astype(F32) + unit * gain + bias)
            incoming = cot[group * PIX + pixel].astype(F32) * slope
            cot[group * PIX + pixel] = value.astype(BF)
            skip[pixel, :, columns] = incoming
            return pool + fold(value), shift + fold(incoming), stretch + fold(incoming * unit)

        pool, shift, stretch = pixels(body, (slim_zero, slim_zero, slim_zero))
        video_src[group] = pool
        here = pl.ds(pl.multiple_of(lax.rem(group, 2) * COLUMNS, COLUMNS), COLUMNS)
        wide_src[4 + group // 2, 0:1, here] = rows_sum(shift)
        wide_src[4 + group // 2, 1:2, here] = rows_sum(stretch)

    for half in range(2):
        keep_norm(wide_finish(2 + half), wide_norm.at[1, :, wide_half(half)])
        wide_pixels(output_part, half)
        wide_first(4 + half)
    wide_second(4)
    wide_second(5)
    act_out = [
        pltpu.make_async_copy(
            cot.at[pl.ds(g * PIX, PIX)], act_hbm.at[:, :, column_group(g)], store_sem.at[6 + g]
        )
        for g in range(4)
    ]
    for copy in act_out:
        copy.start()

    def wide_grads(sums, at, half):
        total = wide_finish(sums * 2 + half)
        biases_wide_grad[at : at + 1, wide_half(half)] = total[0:1]
        gains_wide_grad[at : at + 1, wide_half(half)] = total[1:2]

    def wide_back(at, group, columns):
        center = row16(wide_norm[at, 0:1, columns])
        rate = row16(wide_norm[at, 1:2, columns])
        factor = rate * row16(gains_wide[at : at + 1, columns])
        shift = row16(biases_wide_grad[at : at + 1, columns] * scale)
        stretch = row16(gains_wide_grad[at : at + 1, columns] * scale) * rate

        def body(pixel, row, across, carry):
            value = skip[pixel, :, columns] - shift - (outer[pixel, :, columns] - center) * stretch
            wide[pixel, :, columns] = (value * factor).astype(BF)
            return carry

        pixels(body, 0)

    for half in range(2):
        wide_grads(2, 1, half)
        wide_pixels(functools.partial(wide_back, 1), half)
    spill_in = pltpu.make_async_copy(spill, outer, store_sem.at[0])
    spill_in.start()

    def narrow(weight):
        for tile in range(2):
            at = pl.ds(tile * WIDE_TILE, WIDE_TILE)
            value = dot_back(flat(wide[:, :, column_group(0)]), flat(weight[0, tile]))
            for g in range(1, 4):
                value = value + dot_back(flat(wide[:, :, column_group(g)]), flat(weight[g, tile]))
            temp[:, :, at] = value.reshape(PIX, 16, WIDE_TILE)

    narrow(expand_w)

    def slope_sums(source, norm, sums):
        center, rate = row16(slim_norm[norm, 0:1]), row16(slim_norm[norm, 1:2])
        gain, bias = row16(gains_mid[norm : norm + 1]), row16(biases_mid[norm : norm + 1])

        def body(pixel, row, across, carry):
            shift, stretch = carry
            unit = (source(pixel) - center) * rate
            unused, slope = smooth_pair(unit * gain + bias)
            value = temp[pixel] * slope
            temp[pixel] = value
            return shift + fold(value), stretch + fold(value * unit)

        shift, stretch = pixels(body, (slim_zero, slim_zero))
        slim_src[sums, 0:1] = rows_sum(shift)
        slim_src[sums, 1:2] = rows_sum(stretch)
        slim_start(sums)

    def slope_finish(source, norm, sums, store):
        total = slim_finish(sums)
        biases_mid_grad[norm : norm + 1] = total[0:1]
        gains_mid_grad[norm : norm + 1] = total[1:2]
        center, rate = row16(slim_norm[norm, 0:1]), row16(slim_norm[norm, 1:2])
        factor = rate * row16(gains_mid[norm : norm + 1])
        shift = row16(total[0:1] * scale)
        stretch = row16(total[1:2] * scale) * rate

        def body(pixel, row, across, carry):
            value = temp[pixel] - shift - (source(pixel) - center) * stretch
            store(pixel, row, across, (value * factor).astype(BF))
            return carry

        pixels(body, 0)

    for copy in act_out:
        copy.wait()
    for copy in frame_out:
        copy.wait()
    slope_sums(conv_rows, 2, 3)

    column, core = seg // 2, lax.rem(seg, 2)
    layer, line = clip // 2, lax.rem(clip, 2)
    to_core = {"seg": seg + 1 - 2 * core}
    to_column = {"seg": seg + 2 - 4 * column}
    to_corner = {"seg": 3 - seg}
    to_line = {"clip": clip + 1 - 2 * line}
    own = layer * 4 + line * 2

    class Ring:
        def __init__(self, at, slots, shared, single, places):
            self.at, self.slots, self.shared, self.single = at, slots, shared, single
            self.count = shared + 2 * single
            self.mine = shared + column * single
            self.other = shared + (1 - column) * single
            sizes = {
                "core": 16 * self.count, "line_a": 8 * shared, "layer_a": 8 * shared, "column_a": 2 * shared,
                "column_b": 16 * single, "line_b": 8 * single, "layer_b": 8 * single, "final": 4 * self.count,
            }
            self.land, self.kinds = {}, {}
            for number, (kind, size) in enumerate(sizes.items()):
                ref, base = places[kind]
                self.land[kind] = (ref, base)
                self.kinds[kind] = number

        def tiles(self, kind, start, size):
            ref, base = self.land[kind]
            return ref.at[pl.ds(base + start, size)]

        def send(self, kind, source, start, size, device):
            sems = [ring_sem.at[way, self.at, self.kinds[kind]] for way in range(2)]
            pltpu.make_async_remote_copy(
                source, self.tiles(kind, start, size), sems[0], sems[1],
                device_id=device, device_id_type=MESH,
            ).start()

        def wait(self, kind, size, sent=None):
            for way, amount in ((1, size), (0, size if sent is None else sent)):
                span = pool.at[pl.ds(0, amount)]
                pltpu.make_async_copy(span, span, ring_sem.at[way, self.at, self.kinds[kind]]).wait()

        def add_slots(self, kind, amount, slot_of):
            ref, base = self.land[kind]
            for item in range(amount):
                slot = slot_of(item)
                self.slots[slot, core] = self.slots[slot, core] + ref[pl.ds(base + item * 16, 16)]

        def add_lines(self, kind, amount, slot_of):
            ref, base = self.land[kind]
            for item in range(amount):
                for k in range(4):
                    here = pl.ds(k * 4 + line * 2, 2)
                    self.slots[slot_of(item), core, here] = (
                        self.slots[slot_of(item), core, here] + ref[pl.ds(base + (item * 4 + k) * 2, 2)]
                    )

        def gather(self, kind, amount, slot_of, store):
            ref, base = self.land[kind]
            for item in range(amount):
                ref[pl.ds(base + (item * 4 + layer) * 2, 2)] = self.slots[slot_of(item), core, pl.ds(own, 2)]
                value = ref[pl.ds(base + item * 8, 2)].astype(F32)
                for k in range(1, 4):
                    value = value + ref[pl.ds(base + (item * 4 + k) * 2, 2)].astype(F32)
                store(item, value.astype(BF))

        def stage0(self):
            for slot in range(self.count):
                self.send("core", self.slots.at[slot, 1 - core], slot * 16, 16, to_core)

        def send_line(self, kind, amount, slot_of):
            for item in range(amount):
                for k in range(4):
                    source = self.slots.at[slot_of(item), core, pl.ds(k * 4 + (1 - line) * 2, 2)]
                    self.send(kind, source, (item * 4 + k) * 2, 2, to_line)

        def send_layer(self, kind, amount, slot_of):
            for item in range(amount):
                for step in range(1, 4):
                    there = lax.rem(layer + step, 4)
                    source = self.slots.at[slot_of(item), core, pl.ds(there * 4 + line * 2, 2)]
                    self.send(kind, source, (item * 4 + layer) * 2, 2, {"clip": there * 2 + line})

        def stage1(self):
            self.wait("core", 16 * self.count)
            self.add_slots("core", self.count, lambda item: item)
            self.send_line("line_a", self.shared, lambda item: item)
            for item in range(self.single):
                self.send("column_b", self.slots.at[self.other + item, core], item * 16, 16, to_column)

        def stage2(self):
            self.wait("line_a", 8 * self.shared)
            self.add_lines("line_a", self.shared, lambda item: item)
            self.send_layer("layer_a", self.shared, lambda item: item)
            self.wait("column_b", 16 * self.single)
            self.add_slots("column_b", self.single, lambda item: self.mine + item)
            self.send_line("line_b", self.single, lambda item: self.mine + item)

        def stage3(self):
            self.wait("line_b", 8 * self.single)
            self.add_lines("line_b", self.single, lambda item: self.mine + item)
            self.send_layer("layer_b", self.single, lambda item: self.mine + item)
            self.wait("layer_a", 6 * self.shared)

            def store(item, value):
                self.slots[item, core, pl.ds(own, 2)] = value

            self.gather("layer_a", self.shared, lambda item: item, store)
            for item in range(self.shared):
                self.send("column_a", self.slots.at[item, core, pl.ds(own, 2)], item * 2, 2, to_column)

        def stage4(self):
            final, start = self.land["final"]
            here = start + core * self.count * 2
            self.wait("column_a", 2 * self.shared)
            ref, base = self.land["column_a"]
            for item in range(self.shared):
                final[pl.ds(here + item * 2, 2)] = (
                    self.slots[item, core, pl.ds(own, 2)] + ref[pl.ds(base + item * 2, 2)]
                )
                at = core * self.count * 2 + item * 2
                self.send("final", self.tiles("final", at, 2), at, 2, to_core)
            self.wait("layer_b", 6 * self.single)

            def store(item, value):
                final[pl.ds(here + (self.mine + item) * 2, 2)] = value

            self.gather("layer_b", self.single, lambda item: self.mine + item, store)
            for item in range(self.single):
                at = (core * self.count + self.mine + item) * 2
                for device in (to_core, to_column, to_corner):
                    self.send("final", self.tiles("final", at, 2), at, 2, device)

        def stage5(self):
            arrive = 2 * (self.shared + 3 * self.single)
            self.wait("final", arrive)

        def result(self, half, slot, part):
            final, start = self.land["final"]
            return final[start + (half * self.count + slot) * 2 + part].astype(F32)

    KINDS = ("core", "line_a", "layer_a", "column_a", "column_b", "line_b", "layer_b", "final")

    def places(spans):
        return {kind: span for kind, span in zip(KINDS, spans)}

    def packed(ref, start, shared, single):
        count = shared + 2 * single
        sizes = (16 * count, 8 * shared, 8 * shared, 2 * shared, 16 * single, 8 * single, 8 * single, 4 * count)
        spans = []
        for size in sizes:
            spans.append((ref, start))
            start = start + size
        return places(spans)

    ring_expand = Ring(0, expand_w, 2, 1, packed(cot, 0, 2, 1))
    ring_conv = Ring(1, conv_w.at[pl.ds(0, 4)], 2, 1, packed(pool, 0, 2, 1))
    ring_more = Ring(5, conv_w.at[pl.ds(4, 5)], 3, 1, packed(pool, 148, 3, 1))
    ring_reduce = Ring(2, reduce_w, 2, 1, packed(frame, 0, 2, 1))
    ring_down = Ring(4, expand_w, 2, 1, packed(cot, 0, 2, 1))
    ring_up = Ring(
        3, up, 2, 1,
        places(
            (
                (pool, 334), (frame, 148), (cot, 148), (cot, 164),
                (frame, 164), (cot, 168), (cot, 176), (frame, 180),
            )
        ),
    )

    def put_rows(slots, slot, value):
        parts = value.astype(BF).reshape(8, 2, 2, 16, COLUMNS)
        for half in range(2):
            slots[slot, half] = parts[:, half].reshape(16, 16, COLUMNS)

    def wide_weight_grad(left, slots):
        def body(slot, carry):
            columns = pl.ds(pl.multiple_of(slot * COLUMNS, COLUMNS), COLUMNS)
            put_rows(slots, slot, dot_rows(flat(left[...]), flat(wide[:, :, columns])))
            return carry

        lax.fori_loop(0, 4, body, 0)

    def tall_weight_grad(left, slots):
        def body(block, carry):
            columns = pl.ds(pl.multiple_of(block * WIDE_TILE, WIDE_TILE), WIDE_TILE)
            value = dot_rows(flat(left[:, :, columns]), flat(back[...])).astype(BF)
            parts = value.reshape(2, 4, 2, 16, COLUMNS)
            for half in range(2):
                for slot in range(4):
                    slots[slot, half, pl.ds(block * 2, 2)] = parts[half, slot]
            return carry

        lax.fori_loop(0, 8, body, 0)

    def conv_weight_grad(taps):
        for tap in taps:
            put_rows(conv_w, tap, dot_rows(window(gated, tap // 3, tap % 3), window(back_pad, 1, 1)))

    wide_weight_grad(conv_act, expand_w)

    def store_conv(pixel, row, across, value):
        back_pad[row + 1, across + 1] = value

    slope_finish(conv_rows, 2, 3, store_conv)
    ring_expand.stage0()

    grad_gated = conv_act
    for tile in range(2):
        at = pl.ds(tile * WIDE_TILE, WIDE_TILE)
        value = dot_back(window(back_pad, 2, 2), flat(conv_w[0, tile]))
        for tap in range(1, 9):
            value = value + dot_back(window(back_pad, 2 - tap // 3, 2 - tap % 3), flat(conv_w[tap, tile]))
        grad_gated[:, :, at] = value.astype(BF).reshape(PIX, 16, WIDE_TILE)
    ring_expand.stage1()
    conv_weight_grad(range(0, 4))
    ring_conv.stage0()

    grad_mixed = conv

    def mixed_body(pixel, row, across, carry):
        incoming = grad_gated[pixel].astype(F32)
        both_gates = jnp.concatenate([gates[pixel, 0], gates[pixel, 1]], axis=0)
        value = incoming * acts[pixel].astype(F32) * both_gates * (1.0 - both_gates)
        grad_mixed[pixel] = value.reshape(2, 8, COLUMNS)
        temp[pixel] = incoming * (1.0 + both_gates)
        return carry

    pixels(mixed_body, 0)
    weighted = gates

    def gate_back_tile(which):
        def body(tile, carry):
            lanes = lanes_of(tile)
            kernels = [depth[k, :, lanes] for k in range(18)]
            middle = kernels[4] + kernels[13]
            weight = step_weight[which * 8 : which * 8 + 8, 0:128]
            field = [grad_mixed[p, which, :, lanes] for p in range(PIX)]
            for i in range(HEIGHT):
                for j in range(WIDTH):
                    value = middle * field[i * WIDTH + j]
                    for base, taps in ((0, near_taps()), (9, far_taps())):
                        for k, (di, dj) in enumerate(taps):
                            if (di or dj) and inside(i - di, j - dj):
                                value = value + kernels[base + k] * field[(i - di) * WIDTH + j - dj]
                    weighted[i * WIDTH + j, which, :, lanes] = value * weight
            return carry

        lax.fori_loop(0, 4, body, 0)

    def depth_grad_tile():
        def body(tile, carry):
            lanes = lanes_of(tile)
            totals = [None] * 19
            for which in range(2):
                field = [grad_mixed[p, which, :, lanes] for p in range(PIX)]

                def grow(k, term):
                    totals[k] = term if totals[k] is None else totals[k] + term

                for p in range(PIX):
                    grow(18, field[p])
                for base, taps in ((0, near_taps()), (9, far_taps())):
                    for k, (di, dj) in enumerate(taps):
                        for i in range(HEIGHT):
                            for j in range(WIDTH):
                                if inside(i + di, j + dj):
                                    there = (i + di) * WIDTH + j + dj
                                    grow(base + k, field[i * WIDTH + j] * change[there, which, :, lanes])
            for k in range(19):
                video_src[4 + k // 8, k % 8 : k % 8 + 1, lanes] = rows_sum(totals[k])
            return carry

        lax.fori_loop(0, 4, body, 0)
        video_src[6, 3:8] = jnp.zeros((5, COLUMNS), F32)

    gate_back_tile(1)

    def weighted_pack(pixel, row, across, carry):
        last = weighted[pixel, 1]
        halo_out[pixel] = jnp.concatenate([last[:, 0:256], last[:, 256:512]], axis=0).astype(BF)
        return carry

    pixels(weighted_pack, 0)
    halo_start(halo_out, halo_in, 4, 1)
    gate_back_tile(0)
    ring_expand.stage2()
    ring_conv.stage1()
    halo_finish(halo_out, halo_in, 4, 1)

    def act_grad_body(pixel, row, across, carry):
        ahead = halo_in[pixel].astype(F32)
        before = jnp.concatenate([ahead[0:8], ahead[8:16]], axis=1)
        zero, one = weighted[pixel, 0], weighted[pixel, 1]
        value = temp[pixel] + jnp.concatenate([before - zero, zero - one], axis=0)
        temp[pixel] = value.astype(BF).astype(F32)
        return carry

    pixels(act_grad_body, 0)

    def reduced_rows(pixel):
        return reduced[pixel]

    slope_sums(reduced_rows, 1, 4)
    depth_grad_tile()
    conv_weight_grad(range(4, 9))
    ring_more.stage0()

    def store_back(pixel, row, across, value):
        back[pixel] = value

    slope_finish(reduced_rows, 1, 4, store_back)
    ring_expand.stage3()
    ring_conv.stage2()

    def video_span(way, at, ref):
        pltpu.make_async_copy(ref, ref, video_sem.at[way, at]).wait()

    def seg_spread(source, target, at):
        for step in range(1, segs):
            pltpu.make_async_remote_copy(
                source, target, video_sem.at[0, at], video_sem.at[1, at],
                device_id={"seg": lax.rem(seg + step, segs)}, device_id_type=MESH,
            ).start()

    def video_first():
        seg_spread(video_src, change.at[pl.ds(seg * 7, 7), 0], 0)
        change[pl.ds(seg * 7, 7), 0] = video_src[...]

    def video_second():
        for way in range(2):
            video_span(way, 0, change.at[pl.ds(0, 21), 0])

        def total(read):
            value = read(0)
            for rank in range(1, segs):
                value = value + read(rank * 7)
            return value

        quarter = pl.ds(pl.multiple_of(seg * 128, 128), 128)
        conv[clip, 0] = total(lambda base: change[base + seg, 0])
        for k in range(3):
            conv[clip, 1, :, pl.ds(k * 128, 128)] = total(lambda base: change[base + 4 + k, 0, :, quarter])
        conv[clip, 1, :, pl.ds(384, 128)] = crop_id[...]
        for step in range(1, clips):
            pltpu.make_async_remote_copy(
                conv.at[clip], conv.at[clip], video_sem.at[0, 1], video_sem.at[1, 1],
                device_id={"clip": lax.rem(clip + step, clips)}, device_id_type=MESH,
            ).start()

    def video_third():
        for way in range(2):
            video_span(way, 1, conv.at[pl.ds(0, clips - 1)])
        sums = jnp.concatenate([conv[k, 0] for k in range(clips)], axis=0)
        names = jnp.concatenate([conv[k, 1, :, pl.ds(384, 128)] for k in range(clips)], axis=0)
        lane = lax.broadcasted_iota(jnp.int32, names.shape, 1).astype(F32)
        member = (names == lane).astype(F32)

        def gather(values):
            return lax.dot_general(
                member, values, (((0,), (0,)), ((), ())),
                precision=lax.Precision.HIGHEST, preferred_element_type=F32,
            )[0:32]

        counts = gather(jnp.ones_like(names))
        means = gather(sums) / jnp.concatenate([counts * (SEGS * PIX)] * 4, axis=1)
        grads = conv[0, 1]
        for k in range(1, clips):
            grads = grads + conv[k, 1]
        gates[pl.ds(seg * 5, 4), 0] = means.reshape(4, 8, COLUMNS)
        gates[pl.ds(seg * 5 + 4, 1), 0] = grads[None]
        mine = gates.at[pl.ds(seg * 5, 5), 0]
        seg_spread(mine, mine, 2)

    def video_last():
        for way in range(2):
            video_span(way, 2, gates.at[pl.ds(0, 15), 0])
        for rank in range(segs):
            for k in range(4):
                video_means[k * 8 : k * 8 + 8, column_group(rank)] = gates[rank * 5 + k, 0]
            lanes = pl.ds(rank * 128, 128)
            parts = [gates[rank * 5 + 4, 0, :, pl.ds(k * 128, 128)] for k in range(3)]
            near_grad[0:8, lanes] = parts[0]
            near_grad[8:9, lanes] = parts[1][0:1]
            far_grad[0:7, lanes] = parts[1][1:8]
            far_grad[7:9, lanes] = parts[2][0:2]
            gate_grad[0:1, lanes] = parts[2][2:3]


    spill_in.wait()

    for half in range(2):

        def input_grad(part, carry):
            tile = half * 4 + part
            at = pl.ds(pl.multiple_of(tile * WIDE_TILE, WIDE_TILE), WIDE_TILE)
            weight = flat(reduce_w[half * 2 + part // 2, lax.rem(part, 2)])
            value = dot_back(flat(back[...]), weight) + flat(skip[:, :, at])
            skip[:, :, at] = value.reshape(PIX, 16, WIDE_TILE)
            unit = (flat(outer[:, :, at]) - wide_norm[0, 0:1, at]) * wide_norm[0, 1:2, at]
            here = pl.ds(pl.multiple_of(part * WIDE_TILE, WIDE_TILE), WIDE_TILE)
            wide_src[6 + half, 0:1, here] = rows_sum(value)
            wide_src[6 + half, 1:2, here] = rows_sum(value * unit)
            return carry

        lax.fori_loop(0, 4, input_grad, 0)
        wide_first(6 + half)
    wide_second(6)
    wide_second(7)
    ring_more.stage1()
    tall_weight_grad(block_input, reduce_w)
    ring_reduce.stage0()
    frame_in = pltpu.make_async_copy(frame_spill, tok, store_sem.at[1])
    frame_in.start()
    ring_expand.stage4()
    for half in range(2):
        wide_grads(3, 0, half)
        wide_pixels(functools.partial(wide_back, 0), half)
    ring_conv.stage3()
    narrow(up)

    def inner_rows(pixel):
        return inner[pixel]

    ring_expand.stage5()
    expand_kept = [
        [ring_expand.result(half, slot, part) for part in range(2)] for half in range(2) for slot in range(4)
    ]
    for index, pair in enumerate(expand_kept):
        for part in range(2):
            reduced[index * 2 + part] = pair[part]
    slope_sums(inner_rows, 0, 5)
    ring_reduce.stage1()
    ring_more.stage2()
    wide_weight_grad(active, up)
    ring_up.stage0()
    slope_finish(inner_rows, 0, 5, store_back)
    video_first()

    def last_pack(pixel, row, across, carry):
        last = back[pixel].astype(F32)[8:16]
        halo_out[pixel] = jnp.concatenate([last[:, 0:256], last[:, 256:512]], axis=0).astype(BF)
        return carry

    pixels(last_pack, 0)
    halo_start(halo_out, halo_in, 5, 1)
    ring_conv.stage4()
    ring_up.stage1()
    frame_in.wait()
    tall_weight_grad(tok, expand_w)
    ring_down.stage0()
    ring_down.stage1()
    ring_reduce.stage2()
    ring_more.stage3()
    halo_finish(halo_out, halo_in, 5, 1)

    def change_grad(pixel, row, across, carry):
        ahead = halo_in[pixel].astype(F32)
        before = jnp.concatenate([ahead[0:8], ahead[8:16]], axis=1) * past_weight[...]
        zero, one = halves(back[pixel].astype(F32) * step_weight[...])
        active[pixel] = jnp.concatenate([before - zero, zero - one], axis=0).astype(BF)
        return carry

    pixels(change_grad, 0)
    ring_up.stage2()

    def tokens_part(group):
        columns = column_group(group)
        return pltpu.make_async_copy(
            skip.at[:, :, columns], tokens_grad_hbm.at[:, :, columns], store_sem.at[11 + group]
        )

    for tile in range(8):
        at = pl.ds(tile * WIDE_TILE, WIDE_TILE)
        value = dot_back(flat(active[...]), flat(down[tile // 2, tile % 2])) + flat(skip[:, :, at])
        skip[:, :, at] = value.reshape(PIX, 16, WIDE_TILE)
        if tile % 2 == 1:
            tokens_part(tile // 2).start()
    video_second()

    ring_reduce.stage3()
    ring_more.stage4()
    ring_down.stage2()
    ring_up.stage3()
    ring_reduce.stage4()
    video_third()
    ring_conv.stage5()
    ring_more.stage5()

    def flush(index, source, target):
        copy = pltpu.make_async_copy(source, target, store_sem.at[20 + index])
        copy.start()
        return copy

    def tall_out(index, ring, target, first):
        for half in range(2):
            for slot in range(4):
                for part in range(2):
                    outer[first + half * 8 + slot * 2 + part, :, column_group(1)] = ring.result(half, slot, part)
        return flush(index, outer.at[pl.ds(first, 16), :, column_group(1)], target)

    def wide_out(index, read, target, first):
        for half in range(2):
            for slot in range(4):
                for part in range(2):
                    outer[first + half * 2 + part, :, column_group(slot)] = read(half, slot, part)
        return flush(index, outer.at[pl.ds(first, 4)], target)

    copies = [wide_out(0, lambda half, slot, part: reduced[(half * 4 + slot) * 2 + part], expand_grad, 40)]
    for tap in range(9):
        ring, slot = (ring_conv, tap) if tap < 4 else (ring_more, tap - 4)
        for half in range(2):
            for part in range(2):
                outer[tap * 4 + half * 2 + part, :, column_group(0)] = ring.result(half, slot, part)
    copies.append(flush(1, outer.at[pl.ds(0, 36), :, column_group(0)], conv_grad))
    ring_down.stage3()
    ring_up.stage4()
    ring_reduce.stage5()
    copies.append(tall_out(2, ring_reduce, reduce_grad, 16))
    ring_down.stage4()
    ring_up.stage5()
    copies.append(wide_out(3, ring_up.result, up_grad, 36))
    video_last()
    ring_down.stage5()
    copies.append(tall_out(4, ring_down, down_grad, 0))
    for group in range(4):
        tokens_part(group).wait()
    for copy in copies:
        copy.wait()


def hand_over(count, *refs):
    tokens_grad, *grads = refs[0:count]
    tokens_out, *outs = refs[count : 2 * count]
    held, *kept = refs[2 * count : 3 * count]
    sems = refs[3 * count]

    def load(group):
        columns = pl.ds(group * COLUMNS, COLUMNS)
        return pltpu.make_async_copy(
            tokens_grad.at[:, :, columns], held.at[:, :, columns], sems.at[0, group]
        )

    def store(group, part, clip_at):
        columns = pl.ds(group * COLUMNS, COLUMNS)
        return pltpu.make_async_copy(
            held.at[:, part * 8 + clip_at, columns], tokens_out.at[clip_at, :, part, columns], sems.at[1, group]
        )

    def move(way, at):
        source, target = (grads[at], kept[at]) if way == 0 else (kept[at], outs[at])
        return pltpu.make_async_copy(source, target, sems.at[way, 4 + at])

    for group in range(4):
        load(group).start()
    for at in range(count - 1):
        move(0, at).start()
    for group in range(4):
        load(group).wait()
        for part in range(2):
            for clip_at in range(8):
                store(group, part, clip_at).start()
    for at in range(count - 1):
        move(0, at).wait()
        move(1, at).start()
    for at in range(count - 1):
        move(1, at).wait()
    for group in range(4):
        span = held.at[:, :, pl.ds(group * COLUMNS, COLUMNS)]
        pltpu.make_async_copy(span, span, sems.at[1, group]).wait()


def fused_body(
    tokens, segment_index, crop_video, stem_down, stem_up, reduce_weight, conv_weight, expand_weight,
    depth_near, depth_far, gate_bias, gains_mid, biases_mid, gains_wide, biases_wide, cotangent,
):
    segs, clips = lax.axis_size("seg"), lax.axis_size("clip")
    amount = tokens.shape[0] * tokens.shape[1] * PIX * segs * clips
    def rows_first(field):
        return field.transpose(2, 1, 0, 3).reshape(PIX, 16, 2048)

    whole = pl.BlockSpec(memory_space=pl.ANY)
    near = pl.BlockSpec(memory_space=pltpu.VMEM)
    field = (PIX, 16, 2048)
    slim = (PIX, 16, COLUMNS)
    split = (PIX, 2, 8, COLUMNS)
    out_shapes = (
        (field, BF, whole), (field, F32, whole),
        ((16, 16, 512), F32, whole), ((4, 16, 2048), F32, whole), ((16, 16, 512), F32, whole),
        ((36, 16, 512), F32, whole), ((4, 16, 2048), F32, whole), (field, F32, whole), (field, BF, whole),
        ((32, 2048), F32, near), ((9, 512), F32, near), ((9, 512), F32, near), ((1, 512), F32, near),
        ((3, 512), F32, near), ((3, 512), F32, near), ((2, 2048), F32, near), ((2, 2048), F32, near),
    )
    tiles = (4 * PIX, 16, COLUMNS)
    weight = (4, 2, 16, 16, COLUMNS)
    scratch = [
        pltpu.VMEM(field, BF), pltpu.VMEM(tiles, BF), pltpu.VMEM(field, F32), pltpu.VMEM(field, F32),
        pltpu.VMEM(tiles, BF), pltpu.VMEM(field, BF),
        pltpu.VMEM(slim, F32), pltpu.VMEM(slim, BF), pltpu.VMEM(slim, F32), pltpu.VMEM(slim, BF),
        pltpu.VMEM(split, F32), pltpu.VMEM(split, F32), pltpu.VMEM(split, F32), pltpu.VMEM(slim, BF),
        pltpu.VMEM((9, 9, 16, 512), BF), pltpu.VMEM((9, 9, 16, 512), BF),
        pltpu.VMEM(slim, F32), pltpu.VMEM(slim, BF),
        pltpu.VMEM((PIX, 16, 256), BF), pltpu.VMEM((PIX, 16, 256), BF),
        pltpu.VMEM(weight, BF), pltpu.VMEM(weight, BF), pltpu.VMEM(weight, BF),
        pltpu.VMEM((9,) + weight[1:], BF), pltpu.VMEM(weight, BF),
        pltpu.VMEM((6, 2, 512), F32), pltpu.VMEM((6, segs * clips, 2, 512), F32),
        pltpu.VMEM((8, 2, 1024), F32), pltpu.VMEM((8, 2, 1024), F32),
        pltpu.VMEM((8, segs, 2, 1024), F32), pltpu.VMEM((8, clips, 2, 1024), F32),
        pltpu.VMEM((3, 2, 512), F32), pltpu.VMEM((2, 2, 2048), F32),
        pltpu.VMEM((POOL_TILES, 16, COLUMNS), BF), pltpu.VMEM((7, 8, COLUMNS), F32),
        pltpu.VMEM((18, 8, COLUMNS), F32), pltpu.VMEM((16, COLUMNS), F32), pltpu.VMEM((8, COLUMNS), F32),
        pltpu.VMEM((8, 128), F32),
        pltpu.SemaphoreType.DMA((16,)), pltpu.SemaphoreType.DMA((32,)), pltpu.SemaphoreType.DMA((2, 6)),
        pltpu.SemaphoreType.DMA((2, 6)), pltpu.SemaphoreType.DMA((4, 8)),
        pltpu.SemaphoreType.DMA((2, 6, 8)), pltpu.SemaphoreType.DMA((2, 3)),
    ]
    outs = pl.pallas_call(
        functools.partial(block_kernel, segs, clips, amount),
        out_shape=tuple(jax.ShapeDtypeStruct(s, d) for s, d, unused in out_shapes),
        in_specs=[whole] * 7 + [near] * 9,
        out_specs=tuple(m for unused, unused_too, m in out_shapes),
        scratch_shapes=scratch,
        compiler_params=pltpu.CompilerParams(
            collective_id=0, has_side_effects=True, vmem_limit_bytes=VMEM_BYTES
        ),
    )(
        rows_first(tokens), rows_first(cotangent), stem_down.reshape(weight),
        stem_up.reshape(2, 16, 16, 2048), reduce_weight.reshape(weight),
        conv_weight.reshape((9,) + weight[1:]), expand_weight.reshape(2, 16, 16, 2048),
        depth_near, depth_far, gate_bias[None], gains_mid, biases_mid, gains_wide, biases_wide,
        segment_index, crop_video[None],
    )
    act, *results = outs[0:7]
    results = results + list(outs[9:])
    handed = pl.pallas_call(
        functools.partial(hand_over, len(results)),
        out_shape=(jax.ShapeDtypeStruct((8, PIX, 2, 2048), F32),)
        + tuple(jax.ShapeDtypeStruct(x.shape, F32) for x in results[1:]),
        in_specs=[whole] * len(results),
        out_specs=(whole,) * len(results),
        scratch_shapes=[pltpu.VMEM(x.shape, F32) for x in results]
        + [pltpu.SemaphoreType.DMA((2, len(results) + 3))],
        compiler_params=pltpu.CompilerParams(vmem_limit_bytes=VMEM_BYTES),
    )(*results)
    (
        tokens_grad, down_grad, up_grad, reduce_grad, conv_grad, expand_grad,
        video_means, near_grad, far_grad, gate_grad,
        gains_mid_grad, biases_mid_grad, gains_wide_grad, biases_wide_grad,
    ) = handed

    def clips_first(value):
        return value.reshape(PIX, 2, 8, 2048).transpose(2, 1, 0, 3)

    return (
        clips_first(act),
        video_means,
        tokens_grad.transpose(0, 2, 1, 3),
        down_grad.reshape(256, 512),
        up_grad.reshape(64, 2048),
        reduce_grad.reshape(256, 512),
        conv_grad.reshape(9, 64, 512),
        expand_grad.reshape(64, 2048),
        near_grad,
        far_grad,
        gate_grad[0],
        gains_mid_grad,
        biases_mid_grad,
        gains_wide_grad,
        biases_wide_grad,
    )


POOL_TILES = 334 + 64
VMEM_BYTES = 63 << 20


def solution(mesh):
    def either(tokens, *others):
        devices = (lax.axis_size("seg"), lax.axis_size("clip"))
        fits = tokens.shape == (8, 2, PIX, 2048) and devices == (4, 8)
        return (fused_body if fits else body)(tokens, *others)

    return jax.shard_map(
        either,
        mesh=mesh,
        in_specs=(
            P("clip", "seg", None, None),
            P("clip", None),
            P("clip"),
            P(),
            P(),
            P(),
            P(),
            P(),
            P(),
            P(),
            P(),
            P(),
            P(),
            P(),
            P(),
            P("clip", "seg", None, None),
        ),
        out_specs=(
            P("clip", "seg", None, None),
            P(),
            P("clip", "seg", None, None),
            P("clip", None),
            P("clip", None),
            P("clip", None),
            P(None, "clip", None),
            P("clip", None),
            P(),
            P(),
            P(),
            P(),
            P(),
            P(),
            P(),
        ),
        check_vma=False,
    )
```

```python
import functools

import jax
import jax.numpy as jnp
from jax import lax
from jax.experimental import pallas as pl
from jax.experimental.pallas import tpu as pltpu
from jax.sharding import PartitionSpec as P

HEIGHT = 7
WIDTH = 7
SEGS = 8
PIX = 49


NORM_EPSILON = 1e-05


MESH = pl.DeviceIdType.MESH


def exchange(source, landing, send_sem, recv_sem, axis, count):
    here = lax.axis_index(axis)
    for step in range(1, count):
        pltpu.make_async_remote_copy(
            source,
            landing.at[here],
            send_sem,
            recv_sem,
            device_id={axis: lax.rem(here + step, count)},
            device_id_type=MESH,
        ).start()
    landing[pl.ds(here, 1)] = source[...][None]
    arrived = landing.at[pl.ds(0, count - 1)]
    pltpu.make_async_copy(arrived, arrived, recv_sem).wait()
    total = landing[0]
    for rank in range(1, count):
        total = total + landing[rank]
    pltpu.make_async_copy(arrived, arrived, send_sem).wait()
    return total


def sum_kernel(segs, clips, values, result, middle, seg_land, clip_land, sems):
    barrier = pltpu.get_barrier_semaphore()
    for axis, count in (("seg", segs), ("clip", clips)):
        here = lax.axis_index(axis)
        for step in range(1, count):
            pl.semaphore_signal(
                barrier,
                inc=1,
                device_id={axis: lax.rem(here + step, count)},
                device_id_type=MESH,
            )
    pl.semaphore_wait(barrier, segs + clips - 2)
    middle[...] = exchange(values, seg_land, sems.at[0], sems.at[1], "seg", segs)
    result[...] = exchange(middle, clip_land, sems.at[2], sems.at[3], "clip", clips)


def sum_everywhere(first, second):
    segs, clips = lax.axis_size("seg"), lax.axis_size("clip")
    width = first.shape[0]
    summed = pl.pallas_call(
        functools.partial(sum_kernel, segs, clips),
        out_shape=jax.ShapeDtypeStruct((2, width), jnp.float32),
        in_specs=[pl.BlockSpec(memory_space=pltpu.VMEM)],
        out_specs=pl.BlockSpec(memory_space=pltpu.VMEM),
        scratch_shapes=[
            pltpu.VMEM((2, width), jnp.float32),
            pltpu.VMEM((segs, 2, width), jnp.float32),
            pltpu.VMEM((clips, 2, width), jnp.float32),
            pltpu.SemaphoreType.DMA((4,)),
        ],
        compiler_params=pltpu.CompilerParams(
            collective_id=0 if width < 1024 else 1, has_side_effects=True
        ),
    )(jnp.stack([first, second]))
    return summed[0], summed[1]


def shifted(block, axis, distance):
    devices = range(lax.axis_size(axis))
    route = [(i - distance, i) for i in devices if i - distance in devices]
    return lax.ppermute(block, axis, route)


def row_product(left_side, weight):
    return lax.dot_general(
        left_side,
        weight,
        (((left_side.ndim - 1,), (0,)), ((), ())),
        preferred_element_type=jnp.float32,
    )


def back_product(gradient, weight):
    return lax.dot_general(
        gradient,
        weight,
        (((gradient.ndim - 1,), (1,)), ((), ())),
        preferred_element_type=jnp.float32,
    )


def weight_gradient(left_side, gradient):
    return jnp.einsum("cspk,cspo->ko", left_side, gradient, preferred_element_type=jnp.float32)


def smooth(values):
    return jax.nn.gelu(values, approximate=True)


def depth_conv(field, kernel, reach):
    leading = field.shape[:2]
    planes = field.reshape(leading + (HEIGHT, WIDTH, field.shape[3]))
    padded = jnp.pad(planes, ((0, 0), (0, 0), (reach, reach), (reach, reach), (0, 0)))
    result = jnp.zeros_like(planes)
    for position in range(9):
        down = position // 3 * reach
        across = position % 3 * reach
        result = (
            result
            + padded[:, :, down : down + HEIGHT, across : across + WIDTH, :] * kernel[position]
        )
    return result.reshape(field.shape)


def gate_apply(active, change, near_kernel, far_kernel, offsets):
    mixed = depth_conv(change, near_kernel, 1) + depth_conv(change, far_kernel, 2) + offsets
    return active * (1.0 + jax.nn.sigmoid(mixed))


def frame_planes(field):
    planes = field.reshape(field.shape[:2] + (HEIGHT, WIDTH, field.shape[3]))
    return jnp.pad(planes, ((0, 0), (0, 0), (1, 1), (1, 1), (0, 0)))


def frame_conv(field, weight):
    padded = frame_planes(field)
    result = jnp.zeros(field.shape[:2] + (HEIGHT, WIDTH, weight.shape[2]), jnp.float32)
    for position in range(9):
        down = position // 3
        across = position % 3
        result = result + row_product(
            padded[:, :, down : down + HEIGHT, across : across + WIDTH, :], weight[position]
        )
    return result.reshape(field.shape[:3] + (weight.shape[2],))


def frame_conv_back(field, weight, gradient):
    padded = frame_planes(field)
    planes = gradient.reshape(gradient.shape[:2] + (HEIGHT, WIDTH, gradient.shape[3]))
    field_grad = jnp.zeros(padded.shape, jnp.float32)
    kernel_grads = []
    for position in range(9):
        down = position // 3
        across = position % 3
        window = padded[:, :, down : down + HEIGHT, across : across + WIDTH, :]
        kernel_grads.append(
            jnp.einsum("csijk,csijo->ko", window, planes, preferred_element_type=jnp.float32)
        )
        field_grad = field_grad.at[:, :, down : down + HEIGHT, across : across + WIDTH, :].add(
            back_product(planes, weight[position])
        )
    inner = field_grad[:, :, 1 : 1 + HEIGHT, 1 : 1 + WIDTH, :]
    return (inner.reshape(field.shape), jnp.stack(kernel_grads))


def body(
    tokens,
    segment_index,
    crop_video,
    stem_down,
    stem_up,
    reduce_weight,
    conv_weight,
    expand_weight,
    depth_near,
    depth_far,
    gate_bias,
    gains_mid,
    biases_mid,
    gains_wide,
    biases_wide,
    cotangent,
):
    seg_count = lax.axis_size("seg")
    clip_count = lax.axis_size("clip")
    seg_here = lax.axis_index("seg")
    local_segs = tokens.shape[1]
    amount = tokens.shape[0] * local_segs * tokens.shape[2] * seg_count * clip_count
    spacing = (segment_index[:, 1:] - segment_index[:, :-1]).astype(jnp.float32)
    full_weight = jnp.concatenate(
        [1.0 / spacing, jnp.zeros((spacing.shape[0], 1), jnp.float32)], axis=1
    )
    local_weight = lax.dynamic_slice_in_dim(full_weight, seg_here * local_segs, local_segs, 1)

    def gather_stats(values):
        return sum_everywhere(
            jnp.sum(values, axis=(0, 1, 2)), jnp.sum(values * values, axis=(0, 1, 2))
        )

    def normalize(values, first_sum, second_sum, scales, shifts):
        center = first_sum / amount
        spread = second_sum / amount - center * center
        return (values - center) * lax.rsqrt(spread + NORM_EPSILON) * scales + shifts

    def norm_smooth(values, first_sum, second_sum, scales, shifts):
        return smooth(normalize(values, first_sum, second_sum, scales, shifts))

    def block_finish(values, first_sum, second_sum, scales, shifts, skipped):
        return smooth(skipped + normalize(values, first_sum, second_sum, scales, shifts))

    def norm_back(piece, primals, gradient):
        unused, pull = jax.vjp(piece, *primals)
        pulled = pull(gradient)
        first_grad, second_grad = sum_everywhere(pulled[1], pulled[2])
        values = primals[0]
        return (pulled[0] + first_grad + 2.0 * values * second_grad,) + tuple(pulled[3:])

    frames = tokens.astype(jnp.float32)
    following = shifted(tokens[:, :1], "seg", -1).astype(jnp.float32)
    later = jnp.concatenate([frames[:, 1:], following], axis=1)
    frame_change = ((later - frames) * local_weight[:, :, None, None]).astype(jnp.bfloat16)
    stem_inner = row_product(frame_change, stem_down)
    inner_sums = gather_stats(stem_inner)
    stem_active = norm_smooth(
        stem_inner, inner_sums[0], inner_sums[1], gains_mid[0], biases_mid[0]
    ).astype(jnp.bfloat16)
    stem_outer = row_product(stem_active, stem_up)
    outer_sums = gather_stats(stem_outer)
    block_input = (
        frames + normalize(stem_outer, outer_sums[0], outer_sums[1], gains_wide[0], biases_wide[0])
    ).astype(jnp.bfloat16)
    reduced = row_product(block_input, reduce_weight)
    reduced_sums = gather_stats(reduced)
    reduced_act = norm_smooth(
        reduced, reduced_sums[0], reduced_sums[1], gains_mid[1], biases_mid[1]
    ).astype(jnp.bfloat16)
    channel_act = lax.all_to_all(
        reduced_act, "seg", split_axis=3, concat_axis=1, tiled=True
    ).astype(jnp.float32)
    narrow = channel_act.shape[3]
    near_local = lax.dynamic_slice_in_dim(depth_near, seg_here * narrow, narrow, 1)
    far_local = lax.dynamic_slice_in_dim(depth_far, seg_here * narrow, narrow, 1)
    offset_local = lax.dynamic_slice_in_dim(gate_bias, seg_here * narrow, narrow, 0)
    shifted_act = jnp.concatenate([channel_act[:, 1:], jnp.zeros_like(channel_act[:, :1])], axis=1)
    act_change = (shifted_act - channel_act) * full_weight[:, :, None, None]
    gated_channels = gate_apply(
        channel_act, act_change, near_local, far_local, offset_local
    ).astype(jnp.bfloat16)
    gated = lax.all_to_all(gated_channels, "seg", split_axis=1, concat_axis=3, tiled=True)
    convolved = frame_conv(gated, conv_weight)
    conv_sums = gather_stats(convolved)
    conv_act = norm_smooth(
        convolved, conv_sums[0], conv_sums[1], gains_mid[2], biases_mid[2]
    ).astype(jnp.bfloat16)
    expanded = row_product(conv_act, expand_weight)
    expanded_sums = gather_stats(expanded)
    residual = block_input.astype(jnp.float32)
    block_output = block_finish(
        expanded, expanded_sums[0], expanded_sums[1], gains_wide[1], biases_wide[1], residual
    )
    activations = block_output.astype(jnp.bfloat16)
    video_total = tokens.shape[0] * clip_count // 2
    pooled = jnp.sum(block_output, axis=(1, 2)) / (SEGS * PIX)
    membership = (crop_video[:, None] == jnp.arange(video_total, dtype=jnp.int32)[None, :]).astype(
        jnp.float32
    )
    video_part = jnp.dot(membership.T, pooled, precision=lax.Precision.HIGHEST)
    count_part = jnp.sum(membership, axis=0) * (seg_here == 0).astype(jnp.float32)
    video_sums, video_counts = lax.psum((video_part, count_part), ("seg", "clip"))
    video_means = video_sums / video_counts[:, None]
    grad_output = cotangent.astype(jnp.float32)
    grad_expanded, wide_gain_one, wide_bias_one, grad_skip = norm_back(
        block_finish,
        (expanded, expanded_sums[0], expanded_sums[1], gains_wide[1], biases_wide[1], residual),
        grad_output,
    )
    grad_expanded = grad_expanded.astype(jnp.bfloat16)
    expand_grad = weight_gradient(conv_act, grad_expanded)
    grad_conv_act = back_product(grad_expanded, expand_weight)
    grad_convolved, mid_gain_two, mid_bias_two = norm_back(
        norm_smooth,
        (convolved, conv_sums[0], conv_sums[1], gains_mid[2], biases_mid[2]),
        grad_conv_act,
    )
    grad_convolved = grad_convolved.astype(jnp.bfloat16)
    grad_gated, conv_grad = frame_conv_back(gated, conv_weight, grad_convolved)
    grad_gated = grad_gated.astype(jnp.bfloat16)
    grad_gated_channels = lax.all_to_all(
        grad_gated, "seg", split_axis=3, concat_axis=1, tiled=True
    ).astype(jnp.float32)
    unused_gate, gate_pull = jax.vjp(
        gate_apply, channel_act, act_change, near_local, far_local, offset_local
    )
    grad_direct, grad_change, near_part, far_part, offset_part = gate_pull(grad_gated_channels)
    weighted = grad_change * full_weight[:, :, None, None]
    grad_act_channels = (
        grad_direct
        + jnp.concatenate([jnp.zeros_like(weighted[:, :1]), weighted[:, :-1]], axis=1)
        - weighted
    ).astype(jnp.bfloat16)
    grad_reduced_act = lax.all_to_all(
        grad_act_channels, "seg", split_axis=1, concat_axis=3, tiled=True
    ).astype(jnp.float32)
    near_grad = lax.dynamic_update_slice_in_dim(
        jnp.zeros_like(depth_near), near_part, seg_here * narrow, 1
    )
    far_grad = lax.dynamic_update_slice_in_dim(
        jnp.zeros_like(depth_far), far_part, seg_here * narrow, 1
    )
    gate_bias_grad = lax.dynamic_update_slice_in_dim(
        jnp.zeros_like(gate_bias), offset_part, seg_here * narrow, 0
    )
    grad_reduced, mid_gain_one, mid_bias_one = norm_back(
        norm_smooth,
        (reduced, reduced_sums[0], reduced_sums[1], gains_mid[1], biases_mid[1]),
        grad_reduced_act,
    )
    grad_reduced = grad_reduced.astype(jnp.bfloat16)
    reduce_grad = weight_gradient(block_input, grad_reduced)
    grad_block_input = back_product(grad_reduced, reduce_weight) + grad_skip
    grad_stem_outer, wide_gain_zero, wide_bias_zero = norm_back(
        normalize,
        (stem_outer, outer_sums[0], outer_sums[1], gains_wide[0], biases_wide[0]),
        grad_block_input,
    )
    grad_stem_outer = grad_stem_outer.astype(jnp.bfloat16)
    stem_up_grad = weight_gradient(stem_active, grad_stem_outer)
    grad_stem_active = back_product(grad_stem_outer, stem_up)
    grad_stem_inner, mid_gain_zero, mid_bias_zero = norm_back(
        norm_smooth,
        (stem_inner, inner_sums[0], inner_sums[1], gains_mid[0], biases_mid[0]),
        grad_stem_active,
    )
    grad_stem_inner = grad_stem_inner.astype(jnp.bfloat16)
    stem_down_grad = weight_gradient(frame_change, grad_stem_inner)
    grad_change_in = back_product(grad_stem_inner, stem_down)
    weighted_in = grad_change_in * local_weight[:, :, None, None]
    earlier = shifted(weighted_in[:, -1:].astype(jnp.bfloat16), "seg", 1).astype(jnp.float32)
    tokens_grad = (
        grad_block_input + jnp.concatenate([earlier, weighted_in[:, :-1]], axis=1) - weighted_in
    )
    members = (
        near_grad,
        far_grad,
        gate_bias_grad,
        jnp.stack([mid_gain_zero, mid_gain_one, mid_gain_two]),
        jnp.stack([mid_bias_zero, mid_bias_one, mid_bias_two]),
        jnp.stack([wide_gain_zero, wide_gain_one]),
        jnp.stack([wide_bias_zero, wide_bias_one]),
    )
    flat_grads = jnp.concatenate([member.reshape(-1) for member in members])
    summed_small = lax.psum(flat_grads, ("seg", "clip"))
    unpacked = []
    cursor = 0
    for member in members:
        unpacked.append(summed_small[cursor : cursor + member.size].reshape(member.shape))
        cursor = cursor + member.size
    shares = (
        lax.psum_scatter(
            stem_down_grad.astype(jnp.bfloat16), "clip", scatter_dimension=0, tiled=True
        ).astype(jnp.float32),
        lax.psum_scatter(
            stem_up_grad.astype(jnp.bfloat16), "clip", scatter_dimension=0, tiled=True
        ).astype(jnp.float32),
        lax.psum_scatter(
            reduce_grad.astype(jnp.bfloat16), "clip", scatter_dimension=0, tiled=True
        ).astype(jnp.float32),
        lax.psum_scatter(
            conv_grad.astype(jnp.bfloat16), "clip", scatter_dimension=1, tiled=True
        ).astype(jnp.float32),
        lax.psum_scatter(
            expand_grad.astype(jnp.bfloat16), "clip", scatter_dimension=0, tiled=True
        ).astype(jnp.float32),
    )
    big = (
        lax.psum(shares[0].astype(jnp.bfloat16), "seg").astype(jnp.float32),
        lax.psum(shares[1].astype(jnp.bfloat16), "seg").astype(jnp.float32),
        lax.psum(shares[2].astype(jnp.bfloat16), "seg").astype(jnp.float32),
        lax.psum(shares[3].astype(jnp.bfloat16), "seg").astype(jnp.float32),
        lax.psum(shares[4].astype(jnp.bfloat16), "seg").astype(jnp.float32),
    )
    return (
        activations,
        video_means,
        tokens_grad,
        big[0],
        big[1],
        big[2],
        big[3],
        big[4],
        unpacked[0],
        unpacked[1],
        unpacked[2],
        unpacked[3],
        unpacked[4],
        unpacked[5],
        unpacked[6],
    )


ROOT_TWO_OVER_PI = 0.7978845608
CUBIC = 0.044715


def smooth_pair(values):
    square = values * values
    bent = jnp.tanh(values * (ROOT_TWO_OVER_PI + ROOT_TWO_OVER_PI * CUBIC * square))
    half = 0.5 + 0.5 * bent
    slope = half * (
        1.0
        + values * (1.0 - bent) * (ROOT_TWO_OVER_PI + 3.0 * ROOT_TWO_OVER_PI * CUBIC * square)
    )
    return values * half, slope


def smooth_value(values):
    square = values * values
    bent = jnp.tanh(values * (ROOT_TWO_OVER_PI + ROOT_TWO_OVER_PI * CUBIC * square))
    return values * (0.5 + 0.5 * bent)


def rows_sum(values):
    return jnp.sum(values, axis=0, keepdims=True)


def flat(values):
    return values.reshape(-1, values.shape[-1])


def dot(left, right):
    return jnp.dot(left, right, preferred_element_type=jnp.float32)


def dot_back(left, right):
    return lax.dot_general(left, right, (((1,), (1,)), ((), ())), preferred_element_type=jnp.float32)


def dot_rows(left, right):
    return lax.dot_general(left, right, (((0,), (0,)), ((), ())), preferred_element_type=jnp.float32)


BF = jnp.bfloat16
F32 = jnp.float32
WIDE_TILE = 256
COLUMNS = 512


def near_taps():
    return [(a - 1, b - 1) for a in range(3) for b in range(3)]


def far_taps():
    return [(2 * (a - 1), 2 * (b - 1)) for a in range(3) for b in range(3)]


def block_kernel(segs, clips, amount, *refs):
    (
        tokens_hbm, cot_hbm, down_hbm, up_hbm, reduce_hbm, conv_hbm, expand_hbm,
        near, far, gate_bias, gains_mid, biases_mid, gains_wide, biases_wide, frames_at, crops_at,
        act_hbm, tokens_grad_hbm, down_grad, up_grad, reduce_grad, conv_grad, expand_grad, spill, frame_spill,
        video_means, near_grad, far_grad, gate_grad,
        gains_mid_grad, biases_mid_grad, gains_wide_grad, biases_wide_grad,
        tok, frame, outer, skip, cot, wide,
        inner, active, reduced, acts, change, gates, conv, conv_act, gated, back_pad, temp, back,
        halo_out, halo_in,
        down, up, reduce_w, conv_w, expand_w,
        slim_src, slim_land, wide_src, wide_mid, wide_seg, wide_clip,
        slim_norm, wide_norm, pool, video_src, depth, step_weight, past_weight, crop_id,
        load_sem, store_sem, halo_sem, slim_sem, wide_sem, ring_sem, video_sem,
    ) = refs
    seg = lax.axis_index("seg")
    clip = lax.axis_index("clip")
    devices = segs * clips
    me = seg * clips + clip
    scale = 1.0 / amount

    def peer_of(step):
        peer = lax.rem(me + step, devices)
        return (peer // clips, lax.rem(peer, clips))

    barrier = pltpu.get_barrier_semaphore()

    def greet(step, carry):
        pl.semaphore_signal(barrier, inc=1, device_id=peer_of(step), device_id_type=MESH)
        return carry

    lax.fori_loop(1, devices, greet, 0)

    def column_group(group):
        return pl.ds(group * COLUMNS, COLUMNS)

    class Loads:
        def __init__(self, at, pairs):
            self.copies = [
                pltpu.make_async_copy(source, target, load_sem.at[at + k])
                for k, (source, target) in enumerate(pairs)
            ]
            for copy in self.copies:
                copy.start()

        def wait(self):
            for copy in self.copies:
                copy.wait()

    def by_group(source, target):
        return [(source.at[:, :, :, column_group(g)], target.at[g]) for g in range(4)]

    loads = {
        "tok": Loads(0, [(tokens_hbm, tok)]),
        "down": Loads(1, [(down_hbm, down)]),
        "up": Loads(2, by_group(up_hbm, up)),
        "reduce": Loads(6, [(reduce_hbm, reduce_w)]),
        "conv": Loads(7, [(conv_hbm, conv_w)]),
        "expand": Loads(8, by_group(expand_hbm, expand_w)),
        "cot": Loads(
            12,
            [(cot_hbm.at[:, :, column_group(g)], cot.at[pl.ds(g * PIX, PIX)]) for g in range(4)],
        ),
    }

    segment = lax.broadcasted_iota(jnp.int32, (8, SEGS), 1)

    def frame_at(which):
        return jnp.sum(jnp.where(segment == which, frames_at[...].astype(F32), 0.0), axis=1, keepdims=True)

    def weight_at(which):
        inside_clip = jnp.logical_and(which >= 0, which < SEGS - 1)
        spacing = jnp.where(inside_clip, frame_at(which + 1) - frame_at(which), 1.0)
        return jnp.broadcast_to(jnp.where(inside_clip, 1.0 / spacing, 0.0), (8, COLUMNS))

    past_weight[...] = weight_at(seg * 2 - 1)
    step_weight[0:8] = weight_at(seg * 2)
    step_weight[8:16] = weight_at(seg * 2 + 1)
    names = jnp.broadcast_to(crops_at[...].astype(F32), (8, 8))
    diagonal = segment == lax.broadcasted_iota(jnp.int32, (8, SEGS), 0)
    crop_id[...] = jnp.broadcast_to(
        jnp.sum(jnp.where(diagonal, names, 0.0), axis=1, keepdims=True), (8, 128)
    )
    for k in range(9):
        depth[k] = jnp.broadcast_to(near[k : k + 1], (8, COLUMNS))
        depth[9 + k] = jnp.broadcast_to(far[k : k + 1], (8, COLUMNS))

    def slim_start(at):
        def one(step, carry):
            pltpu.make_async_remote_copy(
                slim_src.at[at], slim_land.at[at, me], slim_sem.at[0, at], slim_sem.at[1, at],
                device_id=peer_of(step), device_id_type=MESH,
            ).start()
            return carry

        lax.fori_loop(1, devices, one, 0)
        slim_land[at, pl.ds(me, 1)] = slim_src[at][None]

    def gather_wait(landing, count, sem):
        arrived = landing.at[pl.ds(0, count - 1)]
        pltpu.make_async_copy(arrived, arrived, sem).wait()

    def slot_total(landing, count):
        total = landing[0]
        for rank in range(1, count):
            total = total + landing[rank]
        return total

    def slim_finish(at):
        land = slim_land.at[at]
        gather_wait(land, devices, slim_sem.at[1, at])
        total = slot_total(land, devices)
        gather_wait(land, devices, slim_sem.at[0, at])
        return total

    def axis_start(source, landing, axis, count, send, recv):
        here = lax.axis_index(axis)
        for step in range(1, count):
            pltpu.make_async_remote_copy(
                source, landing.at[here], send, recv,
                device_id={axis: lax.rem(here + step, count)}, device_id_type=MESH,
            ).start()
        landing[pl.ds(here, 1)] = source[...][None]

    def wide_first(at):
        axis_start(wide_src.at[at], wide_seg.at[at], "seg", segs, wide_sem.at[0, at], wide_sem.at[1, at])

    def wide_second(at):
        gather_wait(wide_seg.at[at], segs, wide_sem.at[1, at])
        wide_mid[at] = slot_total(wide_seg.at[at], segs)
        gather_wait(wide_seg.at[at], segs, wide_sem.at[0, at])
        axis_start(wide_mid.at[at], wide_clip.at[at], "clip", clips, wide_sem.at[2, at], wide_sem.at[3, at])

    def wide_half(half):
        return pl.ds(half * 1024, 1024)

    def wide_finish(at):
        gather_wait(wide_clip.at[at], clips, wide_sem.at[3, at])
        total = slot_total(wide_clip.at[at], clips)
        gather_wait(wide_clip.at[at], clips, wide_sem.at[2, at])
        return total

    def keep_norm(total, kept):
        center = total[0:1] * scale
        spread = total[1:2] * scale - center * center
        kept[0:1] = center
        kept[1:2] = lax.rsqrt(spread + NORM_EPSILON)

    def pixels(body, start):
        def line(row, carry):
            for across in range(WIDTH):
                carry = body(row * WIDTH + across, row, across, carry)
            return carry

        return lax.fori_loop(0, HEIGHT, line, start)

    def halves(values):
        return values[0:8], values[8:16]

    def fold(values):
        return values[0:8] + values[8:16]

    slim_zero = jnp.zeros((8, COLUMNS), F32)

    def spread_row(row):
        return jnp.broadcast_to(row, (8, row.shape[-1]))

    def both(values):
        return jnp.concatenate([values, values], axis=0)

    def row16(row):
        return jnp.broadcast_to(row, (16, row.shape[-1]))

    def halo_start(source, target, at, ahead):
        copy = pltpu.make_async_remote_copy(
            source, target, halo_sem.at[0, at], halo_sem.at[1, at],
            device_id={"seg": jnp.clip(seg + ahead, 0, segs - 1)}, device_id_type=MESH,
        )
        can = seg < segs - 1 if ahead > 0 else seg > 0

        @pl.when(can)
        def _():
            copy.start()

    def halo_finish(source, target, at, ahead):
        copy = pltpu.make_async_remote_copy(
            source, target, halo_sem.at[0, at], halo_sem.at[1, at],
            device_id={"seg": jnp.clip(seg + ahead, 0, segs - 1)}, device_id_type=MESH,
        )
        sends = seg < segs - 1 if ahead > 0 else seg > 0
        takes = seg > 0 if ahead > 0 else seg < segs - 1

        @pl.when(takes)
        def _():
            copy.wait_recv()

        @pl.when(jnp.logical_not(takes))
        def _():
            target[...] = jnp.zeros_like(target)

        @pl.when(sends)
        def _():
            copy.wait_send()

    product, product_next = change, conv
    loads["tok"].wait()
    loads["down"].wait()
    for tile in range(2):
        at = pl.ds(tile * WIDE_TILE, WIDE_TILE)
        value = dot(flat(tok[...]), flat(down[:, :, :, :, at]))
        product[:, :, :, at] = value.reshape(PIX, 2, 8, WIDE_TILE)
        if tile == 0:
            pl.semaphore_wait(barrier, devices - 1)
        halo_start(product.at[:, 0, :, at], product_next.at[:, 0, :, at], tile, -1)
    for tile in range(2):
        at = pl.ds(tile * WIDE_TILE, WIDE_TILE)
        halo_finish(product.at[:, 0, :, at], product_next.at[:, 0, :, at], tile, -1)

    def inner_body(pixel, row, across, carry):
        first, second = carry
        zero, one, after = product[pixel, 0], product[pixel, 1], product_next[pixel, 0]
        early = (one - zero) * step_weight[0:8]
        late = (after - one) * step_weight[8:16]
        inner[pixel] = jnp.concatenate([early, late], axis=0)
        return first + early + late, second + early * early + late * late

    first, second = pixels(inner_body, (slim_zero, slim_zero))
    slim_src[0, 0:1] = rows_sum(first)
    slim_src[0, 1:2] = rows_sum(second)
    slim_start(0)

    token_out, token_in = wide.at[:, :, pl.ds(0, 1024)], wide.at[:, :, pl.ds(1024, 1024)]

    def token_pack(pixel, row, across, carry):
        value = tok[pixel].astype(F32)[0:8]
        wide[pixel, :, pl.ds(0, 1024)] = jnp.concatenate(
            [value[:, 0:1024], value[:, 1024:2048]], axis=0
        ).astype(BF)
        return carry

    pixels(token_pack, 0)
    halo_start(token_out, token_in, 2, -1)

    keep_norm(slim_finish(0), slim_norm.at[0])

    def activate(source, target, at):
        center, rate = row16(slim_norm[at, 0:1]), row16(slim_norm[at, 1:2] * gains_mid[at : at + 1])
        bias = row16(biases_mid[at : at + 1])

        def body(pixel, row, across, carry):
            target[pixel] = smooth_value((source[pixel] - center) * rate + bias).astype(BF)
            return carry

        pixels(body, 0)

    activate(inner, active, 0)

    loads["up"].wait()

    def widen(source, weight, sums):
        for half in range(2):

            def body(part, carry):
                tile = half * 4 + part
                at = pl.ds(pl.multiple_of(tile * WIDE_TILE, WIDE_TILE), WIDE_TILE)
                lanes = pl.ds(pl.multiple_of(lax.rem(part, 2) * WIDE_TILE, WIDE_TILE), WIDE_TILE)
                value = dot(flat(source[...]), flat(weight[half * 2 + part // 2, :, :, :, lanes]))
                outer[:, :, at] = value.reshape(PIX, 16, WIDE_TILE)
                here = pl.ds(pl.multiple_of(part * WIDE_TILE, WIDE_TILE), WIDE_TILE)
                wide_src[sums * 2 + half, 0:1, here] = rows_sum(value)
                wide_src[sums * 2 + half, 1:2, here] = rows_sum(value * value)
                return carry

            lax.fori_loop(0, 4, body, 0)
            wide_first(sums * 2 + half)

    widen(active, up, 0)
    wide_second(0)
    wide_second(1)

    def frame_start(pixel, row, across, carry):
        for part in range(4):
            at = pl.ds(part * COLUMNS, COLUMNS)
            zero, one = halves(tok[pixel, :, at].astype(F32))
            frame[part * PIX + pixel] = jnp.concatenate(
                [(one - zero) * step_weight[0:8], one], axis=0
            ).astype(BF)
        return carry

    pixels(frame_start, 0)

    def wide_pixels(body, half):
        def part(at, carry):
            columns = pl.ds(pl.multiple_of(at * COLUMNS, COLUMNS), COLUMNS)
            body(at, columns)
            return carry

        lax.fori_loop(half * 2, half * 2 + 2, part, 0)

    def input_part(group, columns):
        center = row16(wide_norm[0, 0:1, columns])
        rate = row16(wide_norm[0, 1:2, columns] * gains_wide[0:1, columns])
        bias = row16(biases_wide[0:1, columns])

        def body(pixel, row, across, carry):
            value = (outer[pixel, :, columns] - center) * rate + bias
            tok[pixel, :, columns] = (tok[pixel, :, columns].astype(F32) + value).astype(BF)
            return carry

        pixels(body, 0)

    for half in range(2):
        keep_norm(wide_finish(half), wide_norm.at[0, :, wide_half(half)])
        wide_pixels(input_part, half)
    block_input = tok
    spill_out = pltpu.make_async_copy(outer, spill, store_sem.at[0])
    spill_out.start()

    loads["reduce"].wait()
    for tile in range(2):
        at = pl.ds(tile * WIDE_TILE, WIDE_TILE)
        value = dot(flat(block_input[...]), flat(reduce_w[:, :, :, :, at]))
        reduced[:, :, at] = value.reshape(PIX, 16, WIDE_TILE)
        slim_src[1, 0:1, at] = rows_sum(value)
        slim_src[1, 1:2, at] = rows_sum(value * value)
    slim_start(1)
    halo_finish(token_out, token_in, 2, -1)

    def frame_finish(pixel, row, across, carry):
        ahead = wide[pixel, :, pl.ds(1024, 1024)].astype(F32)
        for part in range(4):
            zero, one = halves(frame[part * PIX + pixel].astype(F32))
            half, low = (0, part) if part < 2 else (8, part - 2)
            after = ahead[half : half + 8, low * COLUMNS : (low + 1) * COLUMNS]
            frame[part * PIX + pixel] = jnp.concatenate(
                [zero, (after - one) * step_weight[8:16]], axis=0
            ).astype(BF)
        return carry

    pixels(frame_finish, 0)
    frame_out = [
        pltpu.make_async_copy(
            frame.at[pl.ds(g * PIX, PIX)], frame_spill.at[:, :, column_group(g)], store_sem.at[2 + g]
        )
        for g in range(4)
    ]
    for copy in frame_out:
        copy.start()
    keep_norm(slim_finish(1), slim_norm.at[1])

    def act_parts():
        center, rate = row16(slim_norm[1, 0:1]), row16(slim_norm[1, 1:2] * gains_mid[1:2])
        bias = row16(biases_mid[1:2])

        def body(pixel, row, across, carry):
            value = smooth_value((reduced[pixel] - center) * rate + bias).astype(BF)
            acts[pixel] = value
            lead = value.astype(F32)[0:8]
            halo_out[pixel] = jnp.concatenate([lead[:, 0:256], lead[:, 256:512]], axis=0).astype(BF)
            return carry

        pixels(body, 0)

    act_parts()
    halo_start(halo_out, halo_in, 3, -1)

    def change_early(pixel, row, across, carry):
        zero, one = halves(acts[pixel].astype(F32))
        change[pixel, 0] = (one - zero) * step_weight[0:8]
        change[pixel, 1] = one
        return carry

    pixels(change_early, 0)

    def lanes_of(tile):
        return pl.ds(pl.multiple_of(tile * 128, 128), 128)

    def inside(row, column):
        return 0 <= row < HEIGHT and 0 <= column < WIDTH

    def gate_tile(which):
        def body(tile, carry):
            lanes = lanes_of(tile)
            kernels = [depth[k, :, lanes] for k in range(18)]
            middle = kernels[4] + kernels[13]
            offsets = jnp.broadcast_to(gate_bias[0:1, lanes], (8, 128))
            field = [change[p, which, :, lanes] for p in range(PIX)]
            for i in range(HEIGHT):
                for j in range(WIDTH):
                    mixed = offsets + middle * field[i * WIDTH + j]
                    for base, taps in ((0, near_taps()), (9, far_taps())):
                        for k, (di, dj) in enumerate(taps):
                            if (di or dj) and inside(i + di, j + dj):
                                mixed = mixed + kernels[base + k] * field[(i + di) * WIDTH + j + dj]
                    gates[i * WIDTH + j, which, :, lanes] = 0.5 + 0.5 * jnp.tanh(0.5 * mixed)
            return carry

        lax.fori_loop(0, 4, body, 0)

    gate_tile(0)
    halo_finish(halo_out, halo_in, 3, -1)

    def change_late(pixel, row, across, carry):
        ahead = halo_in[pixel].astype(F32)
        after = jnp.concatenate([ahead[0:8], ahead[8:16]], axis=1)
        change[pixel, 1] = (after - change[pixel, 1]) * step_weight[8:16]
        return carry

    pixels(change_late, 0)
    gate_tile(1)

    for side in range(9):
        edge = jnp.zeros((16, COLUMNS), BF)
        for pad in (gated, back_pad):
            pad[0, side] = edge
            pad[8, side] = edge
            pad[side, 0] = edge
            pad[side, 8] = edge

    def gated_body(pixel, row, across, carry):
        both_gates = jnp.concatenate([gates[pixel, 0], gates[pixel, 1]], axis=0)
        gated[row + 1, across + 1] = (acts[pixel].astype(F32) * (1.0 + both_gates)).astype(BF)
        return carry

    pixels(gated_body, 0)

    loads["conv"].wait()

    def window(pad, a, b):
        return flat(pad[a : a + HEIGHT, b : b + WIDTH])

    for tile in range(2):
        at = pl.ds(tile * WIDE_TILE, WIDE_TILE)
        value = dot(window(gated, 0, 0), flat(conv_w[0, :, :, :, at]))
        for tap in range(1, 9):
            value = value + dot(window(gated, tap // 3, tap % 3), flat(conv_w[tap, :, :, :, at]))
        conv[:, :, :, at] = value.reshape(PIX, 2, 8, WIDE_TILE)
        slim_src[2, 0:1, at] = rows_sum(value)
        slim_src[2, 1:2, at] = rows_sum(value * value)
    slim_start(2)
    spill_out.wait()
    loads["expand"].wait()
    loads["cot"].wait()
    keep_norm(slim_finish(2), slim_norm.at[2])

    def conv_rows(pixel):
        return conv[pixel].reshape(16, COLUMNS)

    def conv_act_part():
        center, rate = row16(slim_norm[2, 0:1]), row16(slim_norm[2, 1:2] * gains_mid[2:3])
        bias = row16(biases_mid[2:3])

        def body(pixel, row, across, carry):
            conv_act[pixel] = smooth_value((conv_rows(pixel) - center) * rate + bias).astype(BF)
            return carry

        pixels(body, 0)

    conv_act_part()
    widen(conv_act, expand_w, 1)
    wide_second(2)
    wide_second(3)

    def output_part(group, columns):
        center = row16(wide_norm[1, 0:1, columns])
        rate = row16(wide_norm[1, 1:2, columns])
        gain = row16(gains_wide[1:2, columns])
        bias = row16(biases_wide[1:2, columns])

        def body(pixel, row, across, carry):
            pool, shift, stretch = carry
            unit = (outer[pixel, :, columns] - center) * rate
            value, slope = smooth_pair(block_input[pixel, :, columns].astype(F32) + unit * gain + bias)
            incoming = cot[group * PIX + pixel].astype(F32) * slope
            cot[group * PIX + pixel] = value.astype(BF)
            skip[pixel, :, columns] = incoming
            return pool + fold(value), shift + fold(incoming), stretch + fold(incoming * unit)

        pool, shift, stretch = pixels(body, (slim_zero, slim_zero, slim_zero))
        video_src[group] = pool
        here = pl.ds(pl.multiple_of(lax.rem(group, 2) * COLUMNS, COLUMNS), COLUMNS)
        wide_src[4 + group // 2, 0:1, here] = rows_sum(shift)
        wide_src[4 + group // 2, 1:2, here] = rows_sum(stretch)

    for half in range(2):
        keep_norm(wide_finish(2 + half), wide_norm.at[1, :, wide_half(half)])
        wide_pixels(output_part, half)
        wide_first(4 + half)
    wide_second(4)
    wide_second(5)
    act_out = [
        pltpu.make_async_copy(
            cot.at[pl.ds(g * PIX, PIX)], act_hbm.at[:, :, column_group(g)], store_sem.at[6 + g]
        )
        for g in range(4)
    ]
    for copy in act_out:
        copy.start()

    def wide_grads(sums, at, half):
        total = wide_finish(sums * 2 + half)
        biases_wide_grad[at : at + 1, wide_half(half)] = total[0:1]
        gains_wide_grad[at : at + 1, wide_half(half)] = total[1:2]

    def wide_back(at, group, columns):
        center = row16(wide_norm[at, 0:1, columns])
        rate = row16(wide_norm[at, 1:2, columns])
        factor = rate * row16(gains_wide[at : at + 1, columns])
        shift = row16(biases_wide_grad[at : at + 1, columns] * scale)
        stretch = row16(gains_wide_grad[at : at + 1, columns] * scale) * rate

        def body(pixel, row, across, carry):
            value = skip[pixel, :, columns] - shift - (outer[pixel, :, columns] - center) * stretch
            wide[pixel, :, columns] = (value * factor).astype(BF)
            return carry

        pixels(body, 0)

    for half in range(2):
        wide_grads(2, 1, half)
        wide_pixels(functools.partial(wide_back, 1), half)
    spill_in = pltpu.make_async_copy(spill, outer, store_sem.at[0])
    spill_in.start()

    def narrow(weight):
        for tile in range(2):
            at = pl.ds(tile * WIDE_TILE, WIDE_TILE)
            value = dot_back(flat(wide[:, :, column_group(0)]), flat(weight[0, tile]))
            for g in range(1, 4):
                value = value + dot_back(flat(wide[:, :, column_group(g)]), flat(weight[g, tile]))
            temp[:, :, at] = value.reshape(PIX, 16, WIDE_TILE)

    narrow(expand_w)

    def slope_sums(source, norm, sums):
        center, rate = row16(slim_norm[norm, 0:1]), row16(slim_norm[norm, 1:2])
        gain, bias = row16(gains_mid[norm : norm + 1]), row16(biases_mid[norm : norm + 1])

        def body(pixel, row, across, carry):
            shift, stretch = carry
            unit = (source(pixel) - center) * rate
            unused, slope = smooth_pair(unit * gain + bias)
            value = temp[pixel] * slope
            temp[pixel] = value
            return shift + fold(value), stretch + fold(value * unit)

        shift, stretch = pixels(body, (slim_zero, slim_zero))
        slim_src[sums, 0:1] = rows_sum(shift)
        slim_src[sums, 1:2] = rows_sum(stretch)
        slim_start(sums)

    def slope_finish(source, norm, sums, store):
        total = slim_finish(sums)
        biases_mid_grad[norm : norm + 1] = total[0:1]
        gains_mid_grad[norm : norm + 1] = total[1:2]
        center, rate = row16(slim_norm[norm, 0:1]), row16(slim_norm[norm, 1:2])
        factor = rate * row16(gains_mid[norm : norm + 1])
        shift = row16(total[0:1] * scale)
        stretch = row16(total[1:2] * scale) * rate

        def body(pixel, row, across, carry):
            value = temp[pixel] - shift - (source(pixel) - center) * stretch
            store(pixel, row, across, (value * factor).astype(BF))
            return carry

        pixels(body, 0)

    for copy in act_out:
        copy.wait()
    for copy in frame_out:
        copy.wait()
    slope_sums(conv_rows, 2, 3)

    column, core = seg // 2, lax.rem(seg, 2)
    layer, line = clip // 2, lax.rem(clip, 2)
    to_core = {"seg": seg + 1 - 2 * core}
    to_column = {"seg": seg + 2 - 4 * column}
    to_corner = {"seg": 3 - seg}
    to_line = {"clip": clip + 1 - 2 * line}
    own = layer * 4 + line * 2

    class Ring:
        def __init__(self, at, slots, shared, single, places):
            self.at, self.slots, self.shared, self.single = at, slots, shared, single
            self.count = shared + 2 * single
            self.mine = shared + column * single
            self.other = shared + (1 - column) * single
            sizes = {
                "core": 16 * self.count, "line_a": 8 * shared, "layer_a": 8 * shared, "column_a": 2 * shared,
                "column_b": 16 * single, "line_b": 8 * single, "layer_b": 8 * single, "final": 4 * self.count,
            }
            self.land, self.kinds = {}, {}
            for number, (kind, size) in enumerate(sizes.items()):
                ref, base = places[kind]
                self.land[kind] = (ref, base)
                self.kinds[kind] = number

        def tiles(self, kind, start, size):
            ref, base = self.land[kind]
            return ref.at[pl.ds(base + start, size)]

        def send(self, kind, source, start, size, device):
            sems = [ring_sem.at[way, self.at, self.kinds[kind]] for way in range(2)]
            pltpu.make_async_remote_copy(
                source, self.tiles(kind, start, size), sems[0], sems[1],
                device_id=device, device_id_type=MESH,
            ).start()

        def wait(self, kind, size, sent=None):
            for way, amount in ((1, size), (0, size if sent is None else sent)):
                span = pool.at[pl.ds(0, amount)]
                pltpu.make_async_copy(span, span, ring_sem.at[way, self.at, self.kinds[kind]]).wait()

        def add_slots(self, kind, amount, slot_of):
            ref, base = self.land[kind]
            for item in range(amount):
                slot = slot_of(item)
                self.slots[slot, core] = self.slots[slot, core] + ref[pl.ds(base + item * 16, 16)]

        def add_lines(self, kind, amount, slot_of):
            ref, base = self.land[kind]
            for item in range(amount):
                for k in range(4):
                    here = pl.ds(k * 4 + line * 2, 2)
                    self.slots[slot_of(item), core, here] = (
                        self.slots[slot_of(item), core, here] + ref[pl.ds(base + (item * 4 + k) * 2, 2)]
                    )

        def gather(self, kind, amount, slot_of, store):
            ref, base = self.land[kind]
            for item in range(amount):
                ref[pl.ds(base + (item * 4 + layer) * 2, 2)] = self.slots[slot_of(item), core, pl.ds(own, 2)]
                value = ref[pl.ds(base + item * 8, 2)].astype(F32)
                for k in range(1, 4):
                    value = value + ref[pl.ds(base + (item * 4 + k) * 2, 2)].astype(F32)
                store(item, value.astype(BF))

        def stage0(self):
            for slot in range(self.count):
                self.send("core", self.slots.at[slot, 1 - core], slot * 16, 16, to_core)

        def send_line(self, kind, amount, slot_of):
            for item in range(amount):
                for k in range(4):
                    source = self.slots.at[slot_of(item), core, pl.ds(k * 4 + (1 - line) * 2, 2)]
                    self.send(kind, source, (item * 4 + k) * 2, 2, to_line)

        def send_layer(self, kind, amount, slot_of):
            for item in range(amount):
                for step in range(1, 4):
                    there = lax.rem(layer + step, 4)
                    source = self.slots.at[slot_of(item), core, pl.ds(there * 4 + line * 2, 2)]
                    self.send(kind, source, (item * 4 + layer) * 2, 2, {"clip": there * 2 + line})

        def stage1(self):
            self.wait("core", 16 * self.count)
            self.add_slots("core", self.count, lambda item: item)
            self.send_line("line_a", self.shared, lambda item: item)
            for item in range(self.single):
                self.send("column_b", self.slots.at[self.other + item, core], item * 16, 16, to_column)

        def stage2(self):
            self.wait("line_a", 8 * self.shared)
            self.add_lines("line_a", self.shared, lambda item: item)
            self.send_layer("layer_a", self.shared, lambda item: item)
            self.wait("column_b", 16 * self.single)
            self.add_slots("column_b", self.single, lambda item: self.mine + item)
            self.send_line("line_b", self.single, lambda item: self.mine + item)

        def stage3(self):
            self.wait("line_b", 8 * self.single)
            self.add_lines("line_b", self.single, lambda item: self.mine + item)
            self.send_layer("layer_b", self.single, lambda item: self.mine + item)
            self.wait("layer_a", 6 * self.shared)

            def store(item, value):
                self.slots[item, core, pl.ds(own, 2)] = value

            self.gather("layer_a", self.shared, lambda item: item, store)
            for item in range(self.shared):
                self.send("column_a", self.slots.at[item, core, pl.ds(own, 2)], item * 2, 2, to_column)

        def stage4(self):
            final, start = self.land["final"]
            here = start + core * self.count * 2
            self.wait("column_a", 2 * self.shared)
            ref, base = self.land["column_a"]
            for item in range(self.shared):
                final[pl.ds(here + item * 2, 2)] = (
                    self.slots[item, core, pl.ds(own, 2)] + ref[pl.ds(base + item * 2, 2)]
                )
                at = core * self.count * 2 + item * 2
                self.send("final", self.tiles("final", at, 2), at, 2, to_core)
            self.wait("layer_b", 6 * self.single)

            def store(item, value):
                final[pl.ds(here + (self.mine + item) * 2, 2)] = value

            self.gather("layer_b", self.single, lambda item: self.mine + item, store)
            for item in range(self.single):
                at = (core * self.count + self.mine + item) * 2
                for device in (to_core, to_column, to_corner):
                    self.send("final", self.tiles("final", at, 2), at, 2, device)

        def stage5(self):
            arrive = 2 * (self.shared + 3 * self.single)
            self.wait("final", arrive)

        def result(self, half, slot, part):
            final, start = self.land["final"]
            return final[start + (half * self.count + slot) * 2 + part].astype(F32)

    KINDS = ("core", "line_a", "layer_a", "column_a", "column_b", "line_b", "layer_b", "final")

    def places(spans):
        return {kind: span for kind, span in zip(KINDS, spans)}

    def packed(ref, start, shared, single):
        count = shared + 2 * single
        sizes = (16 * count, 8 * shared, 8 * shared, 2 * shared, 16 * single, 8 * single, 8 * single, 4 * count)
        spans = []
        for size in sizes:
            spans.append((ref, start))
            start = start + size
        return places(spans)

    ring_expand = Ring(0, expand_w, 2, 1, packed(cot, 0, 2, 1))
    ring_conv = Ring(1, conv_w.at[pl.ds(0, 4)], 2, 1, packed(pool, 0, 2, 1))
    ring_more = Ring(5, conv_w.at[pl.ds(4, 5)], 3, 1, packed(pool, 148, 3, 1))
    ring_reduce = Ring(2, reduce_w, 2, 1, packed(frame, 0, 2, 1))
    ring_down = Ring(4, expand_w, 2, 1, packed(cot, 0, 2, 1))
    ring_up = Ring(
        3, up, 2, 1,
        places(
            (
                (pool, 334), (frame, 148), (cot, 148), (cot, 164),
                (frame, 164), (cot, 168), (cot, 176), (frame, 180),
            )
        ),
    )

    def put_rows(slots, slot, value):
        parts = value.astype(BF).reshape(8, 2, 2, 16, COLUMNS)
        for half in range(2):
            slots[slot, half] = parts[:, half].reshape(16, 16, COLUMNS)

    def wide_weight_grad(left, slots):
        def body(slot, carry):
            columns = pl.ds(pl.multiple_of(slot * COLUMNS, COLUMNS), COLUMNS)
            put_rows(slots, slot, dot_rows(flat(left[...]), flat(wide[:, :, columns])))
            return carry

        lax.fori_loop(0, 4, body, 0)

    def tall_weight_grad(left, slots):
        def body(block, carry):
            columns = pl.ds(pl.multiple_of(block * WIDE_TILE, WIDE_TILE), WIDE_TILE)
            value = dot_rows(flat(left[:, :, columns]), flat(back[...])).astype(BF)
            parts = value.reshape(2, 4, 2, 16, COLUMNS)
            for half in range(2):
                for slot in range(4):
                    slots[slot, half, pl.ds(block * 2, 2)] = parts[half, slot]
            return carry

        lax.fori_loop(0, 8, body, 0)

    def conv_weight_grad(taps):
        for tap in taps:
            put_rows(conv_w, tap, dot_rows(window(gated, tap // 3, tap % 3), window(back_pad, 1, 1)))

    wide_weight_grad(conv_act, expand_w)

    def store_conv(pixel, row, across, value):
        back_pad[row + 1, across + 1] = value

    slope_finish(conv_rows, 2, 3, store_conv)
    ring_expand.stage0()

    grad_gated = conv_act
    for tile in range(2):
        at = pl.ds(tile * WIDE_TILE, WIDE_TILE)
        value = dot_back(window(back_pad, 2, 2), flat(conv_w[0, tile]))
        for tap in range(1, 9):
            value = value + dot_back(window(back_pad, 2 - tap // 3, 2 - tap % 3), flat(conv_w[tap, tile]))
        grad_gated[:, :, at] = value.astype(BF).reshape(PIX, 16, WIDE_TILE)
    ring_expand.stage1()
    conv_weight_grad(range(0, 4))
    ring_conv.stage0()

    grad_mixed = conv

    def mixed_body(pixel, row, across, carry):
        incoming = grad_gated[pixel].astype(F32)
        both_gates = jnp.concatenate([gates[pixel, 0], gates[pixel, 1]], axis=0)
        value = incoming * acts[pixel].astype(F32) * both_gates * (1.0 - both_gates)
        grad_mixed[pixel] = value.reshape(2, 8, COLUMNS)
        temp[pixel] = incoming * (1.0 + both_gates)
        return carry

    pixels(mixed_body, 0)
    weighted = gates

    def gate_back_tile(which):
        def body(tile, carry):
            lanes = lanes_of(tile)
            kernels = [depth[k, :, lanes] for k in range(18)]
            middle = kernels[4] + kernels[13]
            weight = step_weight[which * 8 : which * 8 + 8, 0:128]
            field = [grad_mixed[p, which, :, lanes] for p in range(PIX)]
            for i in range(HEIGHT):
                for j in range(WIDTH):
                    value = middle * field[i * WIDTH + j]
                    for base, taps in ((0, near_taps()), (9, far_taps())):
                        for k, (di, dj) in enumerate(taps):
                            if (di or dj) and inside(i - di, j - dj):
                                value = value + kernels[base + k] * field[(i - di) * WIDTH + j - dj]
                    weighted[i * WIDTH + j, which, :, lanes] = value * weight
            return carry

        lax.fori_loop(0, 4, body, 0)

    def depth_grad_tile():
        def body(tile, carry):
            lanes = lanes_of(tile)
            totals = [None] * 19
            for which in range(2):
                field = [grad_mixed[p, which, :, lanes] for p in range(PIX)]

                def grow(k, term):
                    totals[k] = term if totals[k] is None else totals[k] + term

                for p in range(PIX):
                    grow(18, field[p])
                for base, taps in ((0, near_taps()), (9, far_taps())):
                    for k, (di, dj) in enumerate(taps):
                        for i in range(HEIGHT):
                            for j in range(WIDTH):
                                if inside(i + di, j + dj):
                                    there = (i + di) * WIDTH + j + dj
                                    grow(base + k, field[i * WIDTH + j] * change[there, which, :, lanes])
            for k in range(19):
                video_src[4 + k // 8, k % 8 : k % 8 + 1, lanes] = rows_sum(totals[k])
            return carry

        lax.fori_loop(0, 4, body, 0)
        video_src[6, 3:8] = jnp.zeros((5, COLUMNS), F32)

    gate_back_tile(1)

    def weighted_pack(pixel, row, across, carry):
        last = weighted[pixel, 1]
        halo_out[pixel] = jnp.concatenate([last[:, 0:256], last[:, 256:512]], axis=0).astype(BF)
        return carry

    pixels(weighted_pack, 0)
    halo_start(halo_out, halo_in, 4, 1)
    gate_back_tile(0)
    ring_expand.stage2()
    ring_conv.stage1()
    halo_finish(halo_out, halo_in, 4, 1)

    def act_grad_body(pixel, row, across, carry):
        ahead = halo_in[pixel].astype(F32)
        before = jnp.concatenate([ahead[0:8], ahead[8:16]], axis=1)
        zero, one = weighted[pixel, 0], weighted[pixel, 1]
        value = temp[pixel] + jnp.concatenate([before - zero, zero - one], axis=0)
        temp[pixel] = value.astype(BF).astype(F32)
        return carry

    pixels(act_grad_body, 0)

    def reduced_rows(pixel):
        return reduced[pixel]

    slope_sums(reduced_rows, 1, 4)
    depth_grad_tile()
    conv_weight_grad(range(4, 9))
    ring_more.stage0()

    def store_back(pixel, row, across, value):
        back[pixel] = value

    slope_finish(reduced_rows, 1, 4, store_back)
    ring_expand.stage3()
    ring_conv.stage2()

    def video_span(way, at, ref):
        pltpu.make_async_copy(ref, ref, video_sem.at[way, at]).wait()

    def seg_spread(source, target, at):
        for step in range(1, segs):
            pltpu.make_async_remote_copy(
                source, target, video_sem.at[0, at], video_sem.at[1, at],
                device_id={"seg": lax.rem(seg + step, segs)}, device_id_type=MESH,
            ).start()

    def video_first():
        seg_spread(video_src, change.at[pl.ds(seg * 7, 7), 0], 0)
        change[pl.ds(seg * 7, 7), 0] = video_src[...]

    def video_second():
        for way in range(2):
            video_span(way, 0, change.at[pl.ds(0, 21), 0])

        def total(read):
            value = read(0)
            for rank in range(1, segs):
                value = value + read(rank * 7)
            return value

        quarter = pl.ds(pl.multiple_of(seg * 128, 128), 128)
        conv[clip, 0] = total(lambda base: change[base + seg, 0])
        for k in range(3):
            conv[clip, 1, :, pl.ds(k * 128, 128)] = total(lambda base: change[base + 4 + k, 0, :, quarter])
        conv[clip, 1, :, pl.ds(384, 128)] = crop_id[...]
        for step in range(1, clips):
            pltpu.make_async_remote_copy(
                conv.at[clip], conv.at[clip], video_sem.at[0, 1], video_sem.at[1, 1],
                device_id={"clip": lax.rem(clip + step, clips)}, device_id_type=MESH,
            ).start()

    def video_third():
        for way in range(2):
            video_span(way, 1, conv.at[pl.ds(0, clips - 1)])
        sums = jnp.concatenate([conv[k, 0] for k in range(clips)], axis=0)
        names = jnp.concatenate([conv[k, 1, :, pl.ds(384, 128)] for k in range(clips)], axis=0)
        lane = lax.broadcasted_iota(jnp.int32, names.shape, 1).astype(F32)
        member = (names == lane).astype(F32)

        def gather(values):
            return lax.dot_general(
                member, values, (((0,), (0,)), ((), ())),
                precision=lax.Precision.HIGHEST, preferred_element_type=F32,
            )[0:32]

        counts = gather(jnp.ones_like(names))
        means = gather(sums) / jnp.concatenate([counts * (SEGS * PIX)] * 4, axis=1)
        grads = conv[0, 1]
        for k in range(1, clips):
            grads = grads + conv[k, 1]
        gates[pl.ds(seg * 5, 4), 0] = means.reshape(4, 8, COLUMNS)
        gates[pl.ds(seg * 5 + 4, 1), 0] = grads[None]
        mine = gates.at[pl.ds(seg * 5, 5), 0]
        seg_spread(mine, mine, 2)

    def video_last():
        for way in range(2):
            video_span(way, 2, gates.at[pl.ds(0, 15), 0])
        for rank in range(segs):
            for k in range(4):
                video_means[k * 8 : k * 8 + 8, column_group(rank)] = gates[rank * 5 + k, 0]
            lanes = pl.ds(rank * 128, 128)
            parts = [gates[rank * 5 + 4, 0, :, pl.ds(k * 128, 128)] for k in range(3)]
            near_grad[0:8, lanes] = parts[0]
            near_grad[8:9, lanes] = parts[1][0:1]
            far_grad[0:7, lanes] = parts[1][1:8]
            far_grad[7:9, lanes] = parts[2][0:2]
            gate_grad[0:1, lanes] = parts[2][2:3]


    spill_in.wait()

    for half in range(2):

        def input_grad(part, carry):
            tile = half * 4 + part
            at = pl.ds(pl.multiple_of(tile * WIDE_TILE, WIDE_TILE), WIDE_TILE)
            weight = flat(reduce_w[half * 2 + part // 2, lax.rem(part, 2)])
            value = dot_back(flat(back[...]), weight) + flat(skip[:, :, at])
            skip[:, :, at] = value.reshape(PIX, 16, WIDE_TILE)
            unit = (flat(outer[:, :, at]) - wide_norm[0, 0:1, at]) * wide_norm[0, 1:2, at]
            here = pl.ds(pl.multiple_of(part * WIDE_TILE, WIDE_TILE), WIDE_TILE)
            wide_src[6 + half, 0:1, here] = rows_sum(value)
            wide_src[6 + half, 1:2, here] = rows_sum(value * unit)
            return carry

        lax.fori_loop(0, 4, input_grad, 0)
        wide_first(6 + half)
    wide_second(6)
    wide_second(7)
    ring_more.stage1()
    tall_weight_grad(block_input, reduce_w)
    ring_reduce.stage0()
    frame_in = pltpu.make_async_copy(frame_spill, tok, store_sem.at[1])
    frame_in.start()
    ring_expand.stage4()
    for half in range(2):
        wide_grads(3, 0, half)
        wide_pixels(functools.partial(wide_back, 0), half)
    ring_conv.stage3()
    narrow(up)

    def inner_rows(pixel):
        return inner[pixel]

    ring_expand.stage5()
    expand_kept = [
        [ring_expand.result(half, slot, part) for part in range(2)] for half in range(2) for slot in range(4)
    ]
    for index, pair in enumerate(expand_kept):
        for part in range(2):
            reduced[index * 2 + part] = pair[part]
    slope_sums(inner_rows, 0, 5)
    ring_reduce.stage1()
    ring_more.stage2()
    wide_weight_grad(active, up)
    ring_up.stage0()
    slope_finish(inner_rows, 0, 5, store_back)
    video_first()

    def last_pack(pixel, row, across, carry):
        last = back[pixel].astype(F32)[8:16]
        halo_out[pixel] = jnp.concatenate([last[:, 0:256], last[:, 256:512]], axis=0).astype(BF)
        return carry

    pixels(last_pack, 0)
    halo_start(halo_out, halo_in, 5, 1)
    ring_conv.stage4()
    ring_up.stage1()
    frame_in.wait()
    tall_weight_grad(tok, expand_w)
    ring_down.stage0()
    ring_reduce.stage2()
    ring_down.stage1()
    ring_more.stage3()
    halo_finish(halo_out, halo_in, 5, 1)

    def change_grad(pixel, row, across, carry):
        ahead = halo_in[pixel].astype(F32)
        before = jnp.concatenate([ahead[0:8], ahead[8:16]], axis=1) * past_weight[...]
        zero, one = halves(back[pixel].astype(F32) * step_weight[...])
        active[pixel] = jnp.concatenate([before - zero, zero - one], axis=0).astype(BF)
        return carry

    pixels(change_grad, 0)
    ring_up.stage2()

    def tokens_part(group):
        columns = column_group(group)
        return pltpu.make_async_copy(
            skip.at[:, :, columns], tokens_grad_hbm.at[:, :, columns], store_sem.at[11 + group]
        )

    for tile in range(8):
        at = pl.ds(tile * WIDE_TILE, WIDE_TILE)
        value = dot_back(flat(active[...]), flat(down[tile // 2, tile % 2])) + flat(skip[:, :, at])
        skip[:, :, at] = value.reshape(PIX, 16, WIDE_TILE)
        if tile % 2 == 1:
            tokens_part(tile // 2).start()
    video_second()

    ring_reduce.stage3()
    ring_more.stage4()
    ring_down.stage2()
    ring_up.stage3()
    ring_reduce.stage4()
    video_third()
    ring_conv.stage5()
    ring_more.stage5()

    def flush(index, source, target):
        copy = pltpu.make_async_copy(source, target, store_sem.at[20 + index])
        copy.start()
        return copy

    def tall_out(index, ring, target, first):
        for half in range(2):
            for slot in range(4):
                for part in range(2):
                    outer[first + half * 8 + slot * 2 + part, :, column_group(1)] = ring.result(half, slot, part)
        return flush(index, outer.at[pl.ds(first, 16), :, column_group(1)], target)

    def wide_out(index, read, target, first):
        for half in range(2):
            for slot in range(4):
                for part in range(2):
                    outer[first + half * 2 + part, :, column_group(slot)] = read(half, slot, part)
        return flush(index, outer.at[pl.ds(first, 4)], target)

    copies = [wide_out(0, lambda half, slot, part: reduced[(half * 4 + slot) * 2 + part], expand_grad, 40)]
    for tap in range(9):
        ring, slot = (ring_conv, tap) if tap < 4 else (ring_more, tap - 4)
        for half in range(2):
            for part in range(2):
                outer[tap * 4 + half * 2 + part, :, column_group(0)] = ring.result(half, slot, part)
    copies.append(flush(1, outer.at[pl.ds(0, 36), :, column_group(0)], conv_grad))
    ring_down.stage3()
    ring_up.stage4()
    ring_reduce.stage5()
    copies.append(tall_out(2, ring_reduce, reduce_grad, 16))
    ring_down.stage4()
    ring_up.stage5()
    copies.append(wide_out(3, ring_up.result, up_grad, 36))
    video_last()
    ring_down.stage5()
    copies.append(tall_out(4, ring_down, down_grad, 0))
    for group in range(4):
        tokens_part(group).wait()
    for copy in copies:
        copy.wait()


def hand_over(count, *refs):
    tokens_grad, *grads = refs[0:count]
    tokens_out, *outs = refs[count : 2 * count]
    held, *kept = refs[2 * count : 3 * count]
    sems = refs[3 * count]

    def load(group):
        columns = pl.ds(group * COLUMNS, COLUMNS)
        return pltpu.make_async_copy(
            tokens_grad.at[:, :, columns], held.at[:, :, columns], sems.at[0, group]
        )

    def store(group, part, clip_at):
        columns = pl.ds(group * COLUMNS, COLUMNS)
        return pltpu.make_async_copy(
            held.at[:, part * 8 + clip_at, columns], tokens_out.at[clip_at, :, part, columns], sems.at[1, group]
        )

    def move(way, at):
        source, target = (grads[at], kept[at]) if way == 0 else (kept[at], outs[at])
        return pltpu.make_async_copy(source, target, sems.at[way, 4 + at])

    for group in range(4):
        load(group).start()
    for at in range(count - 1):
        move(0, at).start()
    for group in range(4):
        load(group).wait()
        for part in range(2):
            for clip_at in range(8):
                store(group, part, clip_at).start()
    for at in range(count - 1):
        move(0, at).wait()
        move(1, at).start()
    for at in range(count - 1):
        move(1, at).wait()
    for group in range(4):
        span = held.at[:, :, pl.ds(group * COLUMNS, COLUMNS)]
        pltpu.make_async_copy(span, span, sems.at[1, group]).wait()


def fused_body(
    tokens, segment_index, crop_video, stem_down, stem_up, reduce_weight, conv_weight, expand_weight,
    depth_near, depth_far, gate_bias, gains_mid, biases_mid, gains_wide, biases_wide, cotangent,
):
    segs, clips = lax.axis_size("seg"), lax.axis_size("clip")
    amount = tokens.shape[0] * tokens.shape[1] * PIX * segs * clips
    def rows_first(field):
        return field.transpose(2, 1, 0, 3).reshape(PIX, 16, 2048)

    whole = pl.BlockSpec(memory_space=pl.ANY)
    near = pl.BlockSpec(memory_space=pltpu.VMEM)
    field = (PIX, 16, 2048)
    slim = (PIX, 16, COLUMNS)
    split = (PIX, 2, 8, COLUMNS)
    out_shapes = (
        (field, BF, whole), (field, F32, whole),
        ((16, 16, 512), F32, whole), ((4, 16, 2048), F32, whole), ((16, 16, 512), F32, whole),
        ((36, 16, 512), F32, whole), ((4, 16, 2048), F32, whole), (field, F32, whole), (field, BF, whole),
        ((32, 2048), F32, near), ((9, 512), F32, near), ((9, 512), F32, near), ((1, 512), F32, near),
        ((3, 512), F32, near), ((3, 512), F32, near), ((2, 2048), F32, near), ((2, 2048), F32, near),
    )
    tiles = (4 * PIX, 16, COLUMNS)
    weight = (4, 2, 16, 16, COLUMNS)
    scratch = [
        pltpu.VMEM(field, BF), pltpu.VMEM(tiles, BF), pltpu.VMEM(field, F32), pltpu.VMEM(field, F32),
        pltpu.VMEM(tiles, BF), pltpu.VMEM(field, BF),
        pltpu.VMEM(slim, F32), pltpu.VMEM(slim, BF), pltpu.VMEM(slim, F32), pltpu.VMEM(slim, BF),
        pltpu.VMEM(split, F32), pltpu.VMEM(split, F32), pltpu.VMEM(split, F32), pltpu.VMEM(slim, BF),
        pltpu.VMEM((9, 9, 16, 512), BF), pltpu.VMEM((9, 9, 16, 512), BF),
        pltpu.VMEM(slim, F32), pltpu.VMEM(slim, BF),
        pltpu.VMEM((PIX, 16, 256), BF), pltpu.VMEM((PIX, 16, 256), BF),
        pltpu.VMEM(weight, BF), pltpu.VMEM(weight, BF), pltpu.VMEM(weight, BF),
        pltpu.VMEM((9,) + weight[1:], BF), pltpu.VMEM(weight, BF),
        pltpu.VMEM((6, 2, 512), F32), pltpu.VMEM((6, segs * clips, 2, 512), F32),
        pltpu.VMEM((8, 2, 1024), F32), pltpu.VMEM((8, 2, 1024), F32),
        pltpu.VMEM((8, segs, 2, 1024), F32), pltpu.VMEM((8, clips, 2, 1024), F32),
        pltpu.VMEM((3, 2, 512), F32), pltpu.VMEM((2, 2, 2048), F32),
        pltpu.VMEM((POOL_TILES, 16, COLUMNS), BF), pltpu.VMEM((7, 8, COLUMNS), F32),
        pltpu.VMEM((18, 8, COLUMNS), F32), pltpu.VMEM((16, COLUMNS), F32), pltpu.VMEM((8, COLUMNS), F32),
        pltpu.VMEM((8, 128), F32),
        pltpu.SemaphoreType.DMA((16,)), pltpu.SemaphoreType.DMA((32,)), pltpu.SemaphoreType.DMA((2, 6)),
        pltpu.SemaphoreType.DMA((2, 6)), pltpu.SemaphoreType.DMA((4, 8)),
        pltpu.SemaphoreType.DMA((2, 6, 8)), pltpu.SemaphoreType.DMA((2, 3)),
    ]
    outs = pl.pallas_call(
        functools.partial(block_kernel, segs, clips, amount),
        out_shape=tuple(jax.ShapeDtypeStruct(s, d) for s, d, unused in out_shapes),
        in_specs=[whole] * 7 + [near] * 9,
        out_specs=tuple(m for unused, unused_too, m in out_shapes),
        scratch_shapes=scratch,
        compiler_params=pltpu.CompilerParams(
            collective_id=0, has_side_effects=True, vmem_limit_bytes=VMEM_BYTES
        ),
    )(
        rows_first(tokens), rows_first(cotangent), stem_down.reshape(weight),
        stem_up.reshape(2, 16, 16, 2048), reduce_weight.reshape(weight),
        conv_weight.reshape((9,) + weight[1:]), expand_weight.reshape(2, 16, 16, 2048),
        depth_near, depth_far, gate_bias[None], gains_mid, biases_mid, gains_wide, biases_wide,
        segment_index, crop_video[None],
    )
    act, *results = outs[0:7]
    results = results + list(outs[9:])
    handed = pl.pallas_call(
        functools.partial(hand_over, len(results)),
        out_shape=(jax.ShapeDtypeStruct((8, PIX, 2, 2048), F32),)
        + tuple(jax.ShapeDtypeStruct(x.shape, F32) for x in results[1:]),
        in_specs=[whole] * len(results),
        out_specs=(whole,) * len(results),
        scratch_shapes=[pltpu.VMEM(x.shape, F32) for x in results]
        + [pltpu.SemaphoreType.DMA((2, len(results) + 3))],
        compiler_params=pltpu.CompilerParams(vmem_limit_bytes=VMEM_BYTES),
    )(*results)
    (
        tokens_grad, down_grad, up_grad, reduce_grad, conv_grad, expand_grad,
        video_means, near_grad, far_grad, gate_grad,
        gains_mid_grad, biases_mid_grad, gains_wide_grad, biases_wide_grad,
    ) = handed

    def clips_first(value):
        return value.reshape(PIX, 2, 8, 2048).transpose(2, 1, 0, 3)

    return (
        clips_first(act),
        video_means,
        tokens_grad.transpose(0, 2, 1, 3),
        down_grad.reshape(256, 512),
        up_grad.reshape(64, 2048),
        reduce_grad.reshape(256, 512),
        conv_grad.reshape(9, 64, 512),
        expand_grad.reshape(64, 2048),
        near_grad,
        far_grad,
        gate_grad[0],
        gains_mid_grad,
        biases_mid_grad,
        gains_wide_grad,
        biases_wide_grad,
    )


POOL_TILES = 334 + 64
VMEM_BYTES = 63 << 20


def solution(mesh):
    def either(tokens, *others):
        devices = (lax.axis_size("seg"), lax.axis_size("clip"))
        fits = tokens.shape == (8, 2, PIX, 2048) and devices == (4, 8)
        return (fused_body if fits else body)(tokens, *others)

    return jax.shard_map(
        either,
        mesh=mesh,
        in_specs=(
            P("clip", "seg", None, None),
            P("clip", None),
            P("clip"),
            P(),
            P(),
            P(),
            P(),
            P(),
            P(),
            P(),
            P(),
            P(),
            P(),
            P(),
            P(),
            P("clip", "seg", None, None),
        ),
        out_specs=(
            P("clip", "seg", None, None),
            P(),
            P("clip", "seg", None, None),
            P("clip", None),
            P("clip", None),
            P("clip", None),
            P(None, "clip", None),
            P("clip", None),
            P(),
            P(),
            P(),
            P(),
            P(),
            P(),
            P(),
        ),
        check_vma=False,
    )
```

```python
import functools

import jax
import jax.numpy as jnp
from jax import lax
from jax.experimental import pallas as pl
from jax.experimental.pallas import tpu as pltpu
from jax.sharding import PartitionSpec as P

HEIGHT = 7
WIDTH = 7
SEGS = 8
PIX = 49


NORM_EPSILON = 1e-05


MESH = pl.DeviceIdType.MESH


def exchange(source, landing, send_sem, recv_sem, axis, count):
    here = lax.axis_index(axis)
    for step in range(1, count):
        pltpu.make_async_remote_copy(
            source,
            landing.at[here],
            send_sem,
            recv_sem,
            device_id={axis: lax.rem(here + step, count)},
            device_id_type=MESH,
        ).start()
    landing[pl.ds(here, 1)] = source[...][None]
    arrived = landing.at[pl.ds(0, count - 1)]
    pltpu.make_async_copy(arrived, arrived, recv_sem).wait()
    total = landing[0]
    for rank in range(1, count):
        total = total + landing[rank]
    pltpu.make_async_copy(arrived, arrived, send_sem).wait()
    return total


def sum_kernel(segs, clips, values, result, middle, seg_land, clip_land, sems):
    barrier = pltpu.get_barrier_semaphore()
    for axis, count in (("seg", segs), ("clip", clips)):
        here = lax.axis_index(axis)
        for step in range(1, count):
            pl.semaphore_signal(
                barrier,
                inc=1,
                device_id={axis: lax.rem(here + step, count)},
                device_id_type=MESH,
            )
    pl.semaphore_wait(barrier, segs + clips - 2)
    middle[...] = exchange(values, seg_land, sems.at[0], sems.at[1], "seg", segs)
    result[...] = exchange(middle, clip_land, sems.at[2], sems.at[3], "clip", clips)


def sum_everywhere(first, second):
    segs, clips = lax.axis_size("seg"), lax.axis_size("clip")
    width = first.shape[0]
    summed = pl.pallas_call(
        functools.partial(sum_kernel, segs, clips),
        out_shape=jax.ShapeDtypeStruct((2, width), jnp.float32),
        in_specs=[pl.BlockSpec(memory_space=pltpu.VMEM)],
        out_specs=pl.BlockSpec(memory_space=pltpu.VMEM),
        scratch_shapes=[
            pltpu.VMEM((2, width), jnp.float32),
            pltpu.VMEM((segs, 2, width), jnp.float32),
            pltpu.VMEM((clips, 2, width), jnp.float32),
            pltpu.SemaphoreType.DMA((4,)),
        ],
        compiler_params=pltpu.CompilerParams(
            collective_id=0 if width < 1024 else 1, has_side_effects=True
        ),
    )(jnp.stack([first, second]))
    return summed[0], summed[1]


def shifted(block, axis, distance):
    devices = range(lax.axis_size(axis))
    route = [(i - distance, i) for i in devices if i - distance in devices]
    return lax.ppermute(block, axis, route)


def row_product(left_side, weight):
    return lax.dot_general(
        left_side,
        weight,
        (((left_side.ndim - 1,), (0,)), ((), ())),
        preferred_element_type=jnp.float32,
    )


def back_product(gradient, weight):
    return lax.dot_general(
        gradient,
        weight,
        (((gradient.ndim - 1,), (1,)), ((), ())),
        preferred_element_type=jnp.float32,
    )


def weight_gradient(left_side, gradient):
    return jnp.einsum("cspk,cspo->ko", left_side, gradient, preferred_element_type=jnp.float32)


def smooth(values):
    return jax.nn.gelu(values, approximate=True)


def depth_conv(field, kernel, reach):
    leading = field.shape[:2]
    planes = field.reshape(leading + (HEIGHT, WIDTH, field.shape[3]))
    padded = jnp.pad(planes, ((0, 0), (0, 0), (reach, reach), (reach, reach), (0, 0)))
    result = jnp.zeros_like(planes)
    for position in range(9):
        down = position // 3 * reach
        across = position % 3 * reach
        result = (
            result
            + padded[:, :, down : down + HEIGHT, across : across + WIDTH, :] * kernel[position]
        )
    return result.reshape(field.shape)


def gate_apply(active, change, near_kernel, far_kernel, offsets):
    mixed = depth_conv(change, near_kernel, 1) + depth_conv(change, far_kernel, 2) + offsets
    return active * (1.0 + jax.nn.sigmoid(mixed))


def frame_planes(field):
    planes = field.reshape(field.shape[:2] + (HEIGHT, WIDTH, field.shape[3]))
    return jnp.pad(planes, ((0, 0), (0, 0), (1, 1), (1, 1), (0, 0)))


def frame_conv(field, weight):
    padded = frame_planes(field)
    result = jnp.zeros(field.shape[:2] + (HEIGHT, WIDTH, weight.shape[2]), jnp.float32)
    for position in range(9):
        down = position // 3
        across = position % 3
        result = result + row_product(
            padded[:, :, down : down + HEIGHT, across : across + WIDTH, :], weight[position]
        )
    return result.reshape(field.shape[:3] + (weight.shape[2],))


def frame_conv_back(field, weight, gradient):
    padded = frame_planes(field)
    planes = gradient.reshape(gradient.shape[:2] + (HEIGHT, WIDTH, gradient.shape[3]))
    field_grad = jnp.zeros(padded.shape, jnp.float32)
    kernel_grads = []
    for position in range(9):
        down = position // 3
        across = position % 3
        window = padded[:, :, down : down + HEIGHT, across : across + WIDTH, :]
        kernel_grads.append(
            jnp.einsum("csijk,csijo->ko", window, planes, preferred_element_type=jnp.float32)
        )
        field_grad = field_grad.at[:, :, down : down + HEIGHT, across : across + WIDTH, :].add(
            back_product(planes, weight[position])
        )
    inner = field_grad[:, :, 1 : 1 + HEIGHT, 1 : 1 + WIDTH, :]
    return (inner.reshape(field.shape), jnp.stack(kernel_grads))


def body(
    tokens,
    segment_index,
    crop_video,
    stem_down,
    stem_up,
    reduce_weight,
    conv_weight,
    expand_weight,
    depth_near,
    depth_far,
    gate_bias,
    gains_mid,
    biases_mid,
    gains_wide,
    biases_wide,
    cotangent,
):
    seg_count = lax.axis_size("seg")
    clip_count = lax.axis_size("clip")
    seg_here = lax.axis_index("seg")
    local_segs = tokens.shape[1]
    amount = tokens.shape[0] * local_segs * tokens.shape[2] * seg_count * clip_count
    spacing = (segment_index[:, 1:] - segment_index[:, :-1]).astype(jnp.float32)
    full_weight = jnp.concatenate(
        [1.0 / spacing, jnp.zeros((spacing.shape[0], 1), jnp.float32)], axis=1
    )
    local_weight = lax.dynamic_slice_in_dim(full_weight, seg_here * local_segs, local_segs, 1)

    def gather_stats(values):
        return sum_everywhere(
            jnp.sum(values, axis=(0, 1, 2)), jnp.sum(values * values, axis=(0, 1, 2))
        )

    def normalize(values, first_sum, second_sum, scales, shifts):
        center = first_sum / amount
        spread = second_sum / amount - center * center
        return (values - center) * lax.rsqrt(spread + NORM_EPSILON) * scales + shifts

    def norm_smooth(values, first_sum, second_sum, scales, shifts):
        return smooth(normalize(values, first_sum, second_sum, scales, shifts))

    def block_finish(values, first_sum, second_sum, scales, shifts, skipped):
        return smooth(skipped + normalize(values, first_sum, second_sum, scales, shifts))

    def norm_back(piece, primals, gradient):
        unused, pull = jax.vjp(piece, *primals)
        pulled = pull(gradient)
        first_grad, second_grad = sum_everywhere(pulled[1], pulled[2])
        values = primals[0]
        return (pulled[0] + first_grad + 2.0 * values * second_grad,) + tuple(pulled[3:])

    frames = tokens.astype(jnp.float32)
    following = shifted(tokens[:, :1], "seg", -1).astype(jnp.float32)
    later = jnp.concatenate([frames[:, 1:], following], axis=1)
    frame_change = ((later - frames) * local_weight[:, :, None, None]).astype(jnp.bfloat16)
    stem_inner = row_product(frame_change, stem_down)
    inner_sums = gather_stats(stem_inner)
    stem_active = norm_smooth(
        stem_inner, inner_sums[0], inner_sums[1], gains_mid[0], biases_mid[0]
    ).astype(jnp.bfloat16)
    stem_outer = row_product(stem_active, stem_up)
    outer_sums = gather_stats(stem_outer)
    block_input = (
        frames + normalize(stem_outer, outer_sums[0], outer_sums[1], gains_wide[0], biases_wide[0])
    ).astype(jnp.bfloat16)
    reduced = row_product(block_input, reduce_weight)
    reduced_sums = gather_stats(reduced)
    reduced_act = norm_smooth(
        reduced, reduced_sums[0], reduced_sums[1], gains_mid[1], biases_mid[1]
    ).astype(jnp.bfloat16)
    channel_act = lax.all_to_all(
        reduced_act, "seg", split_axis=3, concat_axis=1, tiled=True
    ).astype(jnp.float32)
    narrow = channel_act.shape[3]
    near_local = lax.dynamic_slice_in_dim(depth_near, seg_here * narrow, narrow, 1)
    far_local = lax.dynamic_slice_in_dim(depth_far, seg_here * narrow, narrow, 1)
    offset_local = lax.dynamic_slice_in_dim(gate_bias, seg_here * narrow, narrow, 0)
    shifted_act = jnp.concatenate([channel_act[:, 1:], jnp.zeros_like(channel_act[:, :1])], axis=1)
    act_change = (shifted_act - channel_act) * full_weight[:, :, None, None]
    gated_channels = gate_apply(
        channel_act, act_change, near_local, far_local, offset_local
    ).astype(jnp.bfloat16)
    gated = lax.all_to_all(gated_channels, "seg", split_axis=1, concat_axis=3, tiled=True)
    convolved = frame_conv(gated, conv_weight)
    conv_sums = gather_stats(convolved)
    conv_act = norm_smooth(
        convolved, conv_sums[0], conv_sums[1], gains_mid[2], biases_mid[2]
    ).astype(jnp.bfloat16)
    expanded = row_product(conv_act, expand_weight)
    expanded_sums = gather_stats(expanded)
    residual = block_input.astype(jnp.float32)
    block_output = block_finish(
        expanded, expanded_sums[0], expanded_sums[1], gains_wide[1], biases_wide[1], residual
    )
    activations = block_output.astype(jnp.bfloat16)
    video_total = tokens.shape[0] * clip_count // 2
    pooled = jnp.sum(block_output, axis=(1, 2)) / (SEGS * PIX)
    membership = (crop_video[:, None] == jnp.arange(video_total, dtype=jnp.int32)[None, :]).astype(
        jnp.float32
    )
    video_part = jnp.dot(membership.T, pooled, precision=lax.Precision.HIGHEST)
    count_part = jnp.sum(membership, axis=0) * (seg_here == 0).astype(jnp.float32)
    video_sums, video_counts = lax.psum((video_part, count_part), ("seg", "clip"))
    video_means = video_sums / video_counts[:, None]
    grad_output = cotangent.astype(jnp.float32)
    grad_expanded, wide_gain_one, wide_bias_one, grad_skip = norm_back(
        block_finish,
        (expanded, expanded_sums[0], expanded_sums[1], gains_wide[1], biases_wide[1], residual),
        grad_output,
    )
    grad_expanded = grad_expanded.astype(jnp.bfloat16)
    expand_grad = weight_gradient(conv_act, grad_expanded)
    grad_conv_act = back_product(grad_expanded, expand_weight)
    grad_convolved, mid_gain_two, mid_bias_two = norm_back(
        norm_smooth,
        (convolved, conv_sums[0], conv_sums[1], gains_mid[2], biases_mid[2]),
        grad_conv_act,
    )
    grad_convolved = grad_convolved.astype(jnp.bfloat16)
    grad_gated, conv_grad = frame_conv_back(gated, conv_weight, grad_convolved)
    grad_gated = grad_gated.astype(jnp.bfloat16)
    grad_gated_channels = lax.all_to_all(
        grad_gated, "seg", split_axis=3, concat_axis=1, tiled=True
    ).astype(jnp.float32)
    unused_gate, gate_pull = jax.vjp(
        gate_apply, channel_act, act_change, near_local, far_local, offset_local
    )
    grad_direct, grad_change, near_part, far_part, offset_part = gate_pull(grad_gated_channels)
    weighted = grad_change * full_weight[:, :, None, None]
    grad_act_channels = (
        grad_direct
        + jnp.concatenate([jnp.zeros_like(weighted[:, :1]), weighted[:, :-1]], axis=1)
        - weighted
    ).astype(jnp.bfloat16)
    grad_reduced_act = lax.all_to_all(
        grad_act_channels, "seg", split_axis=1, concat_axis=3, tiled=True
    ).astype(jnp.float32)
    near_grad = lax.dynamic_update_slice_in_dim(
        jnp.zeros_like(depth_near), near_part, seg_here * narrow, 1
    )
    far_grad = lax.dynamic_update_slice_in_dim(
        jnp.zeros_like(depth_far), far_part, seg_here * narrow, 1
    )
    gate_bias_grad = lax.dynamic_update_slice_in_dim(
        jnp.zeros_like(gate_bias), offset_part, seg_here * narrow, 0
    )
    grad_reduced, mid_gain_one, mid_bias_one = norm_back(
        norm_smooth,
        (reduced, reduced_sums[0], reduced_sums[1], gains_mid[1], biases_mid[1]),
        grad_reduced_act,
    )
    grad_reduced = grad_reduced.astype(jnp.bfloat16)
    reduce_grad = weight_gradient(block_input, grad_reduced)
    grad_block_input = back_product(grad_reduced, reduce_weight) + grad_skip
    grad_stem_outer, wide_gain_zero, wide_bias_zero = norm_back(
        normalize,
        (stem_outer, outer_sums[0], outer_sums[1], gains_wide[0], biases_wide[0]),
        grad_block_input,
    )
    grad_stem_outer = grad_stem_outer.astype(jnp.bfloat16)
    stem_up_grad = weight_gradient(stem_active, grad_stem_outer)
    grad_stem_active = back_product(grad_stem_outer, stem_up)
    grad_stem_inner, mid_gain_zero, mid_bias_zero = norm_back(
        norm_smooth,
        (stem_inner, inner_sums[0], inner_sums[1], gains_mid[0], biases_mid[0]),
        grad_stem_active,
    )
    grad_stem_inner = grad_stem_inner.astype(jnp.bfloat16)
    stem_down_grad = weight_gradient(frame_change, grad_stem_inner)
    grad_change_in = back_product(grad_stem_inner, stem_down)
    weighted_in = grad_change_in * local_weight[:, :, None, None]
    earlier = shifted(weighted_in[:, -1:].astype(jnp.bfloat16), "seg", 1).astype(jnp.float32)
    tokens_grad = (
        grad_block_input + jnp.concatenate([earlier, weighted_in[:, :-1]], axis=1) - weighted_in
    )
    members = (
        near_grad,
        far_grad,
        gate_bias_grad,
        jnp.stack([mid_gain_zero, mid_gain_one, mid_gain_two]),
        jnp.stack([mid_bias_zero, mid_bias_one, mid_bias_two]),
        jnp.stack([wide_gain_zero, wide_gain_one]),
        jnp.stack([wide_bias_zero, wide_bias_one]),
    )
    flat_grads = jnp.concatenate([member.reshape(-1) for member in members])
    summed_small = lax.psum(flat_grads, ("seg", "clip"))
    unpacked = []
    cursor = 0
    for member in members:
        unpacked.append(summed_small[cursor : cursor + member.size].reshape(member.shape))
        cursor = cursor + member.size
    shares = (
        lax.psum_scatter(
            stem_down_grad.astype(jnp.bfloat16), "clip", scatter_dimension=0, tiled=True
        ).astype(jnp.float32),
        lax.psum_scatter(
            stem_up_grad.astype(jnp.bfloat16), "clip", scatter_dimension=0, tiled=True
        ).astype(jnp.float32),
        lax.psum_scatter(
            reduce_grad.astype(jnp.bfloat16), "clip", scatter_dimension=0, tiled=True
        ).astype(jnp.float32),
        lax.psum_scatter(
            conv_grad.astype(jnp.bfloat16), "clip", scatter_dimension=1, tiled=True
        ).astype(jnp.float32),
        lax.psum_scatter(
            expand_grad.astype(jnp.bfloat16), "clip", scatter_dimension=0, tiled=True
        ).astype(jnp.float32),
    )
    big = (
        lax.psum(shares[0].astype(jnp.bfloat16), "seg").astype(jnp.float32),
        lax.psum(shares[1].astype(jnp.bfloat16), "seg").astype(jnp.float32),
        lax.psum(shares[2].astype(jnp.bfloat16), "seg").astype(jnp.float32),
        lax.psum(shares[3].astype(jnp.bfloat16), "seg").astype(jnp.float32),
        lax.psum(shares[4].astype(jnp.bfloat16), "seg").astype(jnp.float32),
    )
    return (
        activations,
        video_means,
        tokens_grad,
        big[0],
        big[1],
        big[2],
        big[3],
        big[4],
        unpacked[0],
        unpacked[1],
        unpacked[2],
        unpacked[3],
        unpacked[4],
        unpacked[5],
        unpacked[6],
    )


ROOT_TWO_OVER_PI = 0.7978845608
CUBIC = 0.044715


def smooth_pair(values):
    square = values * values
    bent = jnp.tanh(values * (ROOT_TWO_OVER_PI + ROOT_TWO_OVER_PI * CUBIC * square))
    half = 0.5 + 0.5 * bent
    slope = half * (
        1.0
        + values * (1.0 - bent) * (ROOT_TWO_OVER_PI + 3.0 * ROOT_TWO_OVER_PI * CUBIC * square)
    )
    return values * half, slope


def smooth_value(values):
    square = values * values
    bent = jnp.tanh(values * (ROOT_TWO_OVER_PI + ROOT_TWO_OVER_PI * CUBIC * square))
    return values * (0.5 + 0.5 * bent)


def rows_sum(values):
    return jnp.sum(values, axis=0, keepdims=True)


def flat(values):
    return values.reshape(-1, values.shape[-1])


def dot(left, right):
    return jnp.dot(left, right, preferred_element_type=jnp.float32)


def dot_back(left, right):
    return lax.dot_general(left, right, (((1,), (1,)), ((), ())), preferred_element_type=jnp.float32)


def dot_rows(left, right):
    return lax.dot_general(left, right, (((0,), (0,)), ((), ())), preferred_element_type=jnp.float32)


BF = jnp.bfloat16
F32 = jnp.float32
WIDE_TILE = 256
COLUMNS = 512


def near_taps():
    return [(a - 1, b - 1) for a in range(3) for b in range(3)]


def far_taps():
    return [(2 * (a - 1), 2 * (b - 1)) for a in range(3) for b in range(3)]


def block_kernel(segs, clips, amount, *refs):
    (
        tokens_hbm, cot_hbm, down_hbm, up_hbm, reduce_hbm, conv_hbm, expand_hbm,
        near, far, gate_bias, gains_mid, biases_mid, gains_wide, biases_wide, frames_at, crops_at,
        act_hbm, tokens_grad_hbm, down_grad, up_grad, reduce_grad, conv_grad, expand_grad, spill, frame_spill,
        video_means, near_grad, far_grad, gate_grad,
        gains_mid_grad, biases_mid_grad, gains_wide_grad, biases_wide_grad,
        tok, frame, outer, skip, cot, wide,
        inner, active, reduced, acts, change, gates, conv, conv_act, gated, back_pad, temp, back,
        halo_out, halo_in,
        down, up, reduce_w, conv_w, expand_w,
        slim_src, slim_land, wide_src, wide_mid, wide_seg, wide_clip,
        slim_norm, wide_norm, pool, video_src, depth, step_weight, past_weight, crop_id,
        load_sem, store_sem, halo_sem, slim_sem, wide_sem, ring_sem, video_sem,
    ) = refs
    seg = lax.axis_index("seg")
    clip = lax.axis_index("clip")
    devices = segs * clips
    me = seg * clips + clip
    scale = 1.0 / amount

    def peer_of(step):
        peer = lax.rem(me + step, devices)
        return (peer // clips, lax.rem(peer, clips))

    barrier = pltpu.get_barrier_semaphore()

    def greet(step, carry):
        pl.semaphore_signal(barrier, inc=1, device_id=peer_of(step), device_id_type=MESH)
        return carry

    lax.fori_loop(1, devices, greet, 0)

    def column_group(group):
        return pl.ds(group * COLUMNS, COLUMNS)

    class Loads:
        def __init__(self, at, pairs):
            self.copies = [
                pltpu.make_async_copy(source, target, load_sem.at[at + k])
                for k, (source, target) in enumerate(pairs)
            ]
            for copy in self.copies:
                copy.start()

        def wait(self):
            for copy in self.copies:
                copy.wait()

    def by_group(source, target):
        return [(source.at[:, :, :, column_group(g)], target.at[g]) for g in range(4)]

    loads = {
        "tok": Loads(0, [(tokens_hbm, tok)]),
        "down": Loads(1, [(down_hbm, down)]),
        "up": Loads(2, by_group(up_hbm, up)),
        "reduce": Loads(6, [(reduce_hbm, reduce_w)]),
        "conv": Loads(7, [(conv_hbm, conv_w)]),
        "expand": Loads(8, by_group(expand_hbm, expand_w)),
        "cot": Loads(
            12,
            [(cot_hbm.at[:, :, column_group(g)], cot.at[pl.ds(g * PIX, PIX)]) for g in range(4)],
        ),
    }

    segment = lax.broadcasted_iota(jnp.int32, (8, SEGS), 1)

    def frame_at(which):
        return jnp.sum(jnp.where(segment == which, frames_at[...].astype(F32), 0.0), axis=1, keepdims=True)

    def weight_at(which):
        inside_clip = jnp.logical_and(which >= 0, which < SEGS - 1)
        spacing = jnp.where(inside_clip, frame_at(which + 1) - frame_at(which), 1.0)
        return jnp.broadcast_to(jnp.where(inside_clip, 1.0 / spacing, 0.0), (8, COLUMNS))

    past_weight[...] = weight_at(seg * 2 - 1)
    step_weight[0:8] = weight_at(seg * 2)
    step_weight[8:16] = weight_at(seg * 2 + 1)
    names = jnp.broadcast_to(crops_at[...].astype(F32), (8, 8))
    diagonal = segment == lax.broadcasted_iota(jnp.int32, (8, SEGS), 0)
    crop_id[...] = jnp.broadcast_to(
        jnp.sum(jnp.where(diagonal, names, 0.0), axis=1, keepdims=True), (8, 128)
    )
    for k in range(9):
        depth[k] = jnp.broadcast_to(near[k : k + 1], (8, COLUMNS))
        depth[9 + k] = jnp.broadcast_to(far[k : k + 1], (8, COLUMNS))

    def slim_start(at):
        def one(step, carry):
            pltpu.make_async_remote_copy(
                slim_src.at[at], slim_land.at[at, me], slim_sem.at[0, at], slim_sem.at[1, at],
                device_id=peer_of(step), device_id_type=MESH,
            ).start()
            return carry

        lax.fori_loop(1, devices, one, 0)
        slim_land[at, pl.ds(me, 1)] = slim_src[at][None]

    def gather_wait(landing, count, sem):
        arrived = landing.at[pl.ds(0, count - 1)]
        pltpu.make_async_copy(arrived, arrived, sem).wait()

    def slot_total(landing, count):
        total = landing[0]
        for rank in range(1, count):
            total = total + landing[rank]
        return total

    def slim_finish(at):
        land = slim_land.at[at]
        gather_wait(land, devices, slim_sem.at[1, at])
        total = slot_total(land, devices)
        gather_wait(land, devices, slim_sem.at[0, at])
        return total

    def axis_start(source, landing, axis, count, send, recv):
        here = lax.axis_index(axis)
        for step in range(1, count):
            pltpu.make_async_remote_copy(
                source, landing.at[here], send, recv,
                device_id={axis: lax.rem(here + step, count)}, device_id_type=MESH,
            ).start()
        landing[pl.ds(here, 1)] = source[...][None]

    def wide_first(at):
        axis_start(wide_src.at[at], wide_seg.at[at], "seg", segs, wide_sem.at[0, at], wide_sem.at[1, at])

    def wide_second(at):
        gather_wait(wide_seg.at[at], segs, wide_sem.at[1, at])
        wide_mid[at] = slot_total(wide_seg.at[at], segs)
        gather_wait(wide_seg.at[at], segs, wide_sem.at[0, at])
        axis_start(wide_mid.at[at], wide_clip.at[at], "clip", clips, wide_sem.at[2, at], wide_sem.at[3, at])

    def wide_half(half):
        return pl.ds(half * 1024, 1024)

    def wide_finish(at):
        gather_wait(wide_clip.at[at], clips, wide_sem.at[3, at])
        total = slot_total(wide_clip.at[at], clips)
        gather_wait(wide_clip.at[at], clips, wide_sem.at[2, at])
        return total

    def keep_norm(total, kept):
        center = total[0:1] * scale
        spread = total[1:2] * scale - center * center
        kept[0:1] = center
        kept[1:2] = lax.rsqrt(spread + NORM_EPSILON)

    def pixels(body, start):
        def line(row, carry):
            for across in range(WIDTH):
                carry = body(row * WIDTH + across, row, across, carry)
            return carry

        return lax.fori_loop(0, HEIGHT, line, start)

    def halves(values):
        return values[0:8], values[8:16]

    def fold(values):
        return values[0:8] + values[8:16]

    slim_zero = jnp.zeros((8, COLUMNS), F32)

    def spread_row(row):
        return jnp.broadcast_to(row, (8, row.shape[-1]))

    def both(values):
        return jnp.concatenate([values, values], axis=0)

    def row16(row):
        return jnp.broadcast_to(row, (16, row.shape[-1]))

    def halo_start(source, target, at, ahead):
        copy = pltpu.make_async_remote_copy(
            source, target, halo_sem.at[0, at], halo_sem.at[1, at],
            device_id={"seg": jnp.clip(seg + ahead, 0, segs - 1)}, device_id_type=MESH,
        )
        can = seg < segs - 1 if ahead > 0 else seg > 0

        @pl.when(can)
        def _():
            copy.start()

    def halo_finish(source, target, at, ahead):
        copy = pltpu.make_async_remote_copy(
            source, target, halo_sem.at[0, at], halo_sem.at[1, at],
            device_id={"seg": jnp.clip(seg + ahead, 0, segs - 1)}, device_id_type=MESH,
        )
        sends = seg < segs - 1 if ahead > 0 else seg > 0
        takes = seg > 0 if ahead > 0 else seg < segs - 1

        @pl.when(takes)
        def _():
            copy.wait_recv()

        @pl.when(jnp.logical_not(takes))
        def _():
            target[...] = jnp.zeros_like(target)

        @pl.when(sends)
        def _():
            copy.wait_send()

    product, product_next = change, conv
    loads["tok"].wait()
    loads["down"].wait()
    for tile in range(2):
        at = pl.ds(tile * WIDE_TILE, WIDE_TILE)
        value = dot(flat(tok[...]), flat(down[:, :, :, :, at]))
        product[:, :, :, at] = value.reshape(PIX, 2, 8, WIDE_TILE)
        if tile == 0:
            pl.semaphore_wait(barrier, devices - 1)
        halo_start(product.at[:, 0, :, at], product_next.at[:, 0, :, at], tile, -1)
    for tile in range(2):
        at = pl.ds(tile * WIDE_TILE, WIDE_TILE)
        halo_finish(product.at[:, 0, :, at], product_next.at[:, 0, :, at], tile, -1)

    def inner_body(pixel, row, across, carry):
        first, second = carry
        zero, one, after = product[pixel, 0], product[pixel, 1], product_next[pixel, 0]
        early = (one - zero) * step_weight[0:8]
        late = (after - one) * step_weight[8:16]
        inner[pixel] = jnp.concatenate([early, late], axis=0)
        return first + early + late, second + early * early + late * late

    first, second = pixels(inner_body, (slim_zero, slim_zero))
    slim_src[0, 0:1] = rows_sum(first)
    slim_src[0, 1:2] = rows_sum(second)
    slim_start(0)

    token_out, token_in = wide.at[:, :, pl.ds(0, 1024)], wide.at[:, :, pl.ds(1024, 1024)]

    def token_pack(pixel, row, across, carry):
        value = tok[pixel].astype(F32)[0:8]
        wide[pixel, :, pl.ds(0, 1024)] = jnp.concatenate(
            [value[:, 0:1024], value[:, 1024:2048]], axis=0
        ).astype(BF)
        return carry

    pixels(token_pack, 0)
    halo_start(token_out, token_in, 2, -1)

    keep_norm(slim_finish(0), slim_norm.at[0])

    def activate(source, target, at):
        center, rate = row16(slim_norm[at, 0:1]), row16(slim_norm[at, 1:2] * gains_mid[at : at + 1])
        bias = row16(biases_mid[at : at + 1])

        def body(pixel, row, across, carry):
            target[pixel] = smooth_value((source[pixel] - center) * rate + bias).astype(BF)
            return carry

        pixels(body, 0)

    activate(inner, active, 0)

    loads["up"].wait()

    def widen(source, weight, sums):
        for half in range(2):

            def body(part, carry):
                tile = half * 4 + part
                at = pl.ds(pl.multiple_of(tile * WIDE_TILE, WIDE_TILE), WIDE_TILE)
                lanes = pl.ds(pl.multiple_of(lax.rem(part, 2) * WIDE_TILE, WIDE_TILE), WIDE_TILE)
                value = dot(flat(source[...]), flat(weight[half * 2 + part // 2, :, :, :, lanes]))
                outer[:, :, at] = value.reshape(PIX, 16, WIDE_TILE)
                here = pl.ds(pl.multiple_of(part * WIDE_TILE, WIDE_TILE), WIDE_TILE)
                wide_src[sums * 2 + half, 0:1, here] = rows_sum(value)
                wide_src[sums * 2 + half, 1:2, here] = rows_sum(value * value)
                return carry

            lax.fori_loop(0, 4, body, 0)
            wide_first(sums * 2 + half)

    widen(active, up, 0)
    wide_second(0)
    wide_second(1)

    def frame_start(pixel, row, across, carry):
        for part in range(4):
            at = pl.ds(part * COLUMNS, COLUMNS)
            zero, one = halves(tok[pixel, :, at].astype(F32))
            frame[part * PIX + pixel] = jnp.concatenate(
                [(one - zero) * step_weight[0:8], one], axis=0
            ).astype(BF)
        return carry

    pixels(frame_start, 0)

    def wide_pixels(body, half):
        def part(at, carry):
            columns = pl.ds(pl.multiple_of(at * COLUMNS, COLUMNS), COLUMNS)
            body(at, columns)
            return carry

        lax.fori_loop(half * 2, half * 2 + 2, part, 0)

    def input_part(group, columns):
        center = row16(wide_norm[0, 0:1, columns])
        rate = row16(wide_norm[0, 1:2, columns] * gains_wide[0:1, columns])
        bias = row16(biases_wide[0:1, columns])

        def body(pixel, row, across, carry):
            value = (outer[pixel, :, columns] - center) * rate + bias
            tok[pixel, :, columns] = (tok[pixel, :, columns].astype(F32) + value).astype(BF)
            return carry

        pixels(body, 0)

    for half in range(2):
        keep_norm(wide_finish(half), wide_norm.at[0, :, wide_half(half)])
        wide_pixels(input_part, half)
    block_input = tok
    spill_out = pltpu.make_async_copy(outer, spill, store_sem.at[0])
    spill_out.start()

    loads["reduce"].wait()
    for tile in range(2):
        at = pl.ds(tile * WIDE_TILE, WIDE_TILE)
        value = dot(flat(block_input[...]), flat(reduce_w[:, :, :, :, at]))
        reduced[:, :, at] = value.reshape(PIX, 16, WIDE_TILE)
        slim_src[1, 0:1, at] = rows_sum(value)
        slim_src[1, 1:2, at] = rows_sum(value * value)
    slim_start(1)
    halo_finish(token_out, token_in, 2, -1)

    def frame_finish(pixel, row, across, carry):
        ahead = wide[pixel, :, pl.ds(1024, 1024)].astype(F32)
        for part in range(4):
            zero, one = halves(frame[part * PIX + pixel].astype(F32))
            half, low = (0, part) if part < 2 else (8, part - 2)
            after = ahead[half : half + 8, low * COLUMNS : (low + 1) * COLUMNS]
            frame[part * PIX + pixel] = jnp.concatenate(
                [zero, (after - one) * step_weight[8:16]], axis=0
            ).astype(BF)
        return carry

    pixels(frame_finish, 0)
    frame_out = [
        pltpu.make_async_copy(
            frame.at[pl.ds(g * PIX, PIX)], frame_spill.at[:, :, column_group(g)], store_sem.at[2 + g]
        )
        for g in range(4)
    ]
    for copy in frame_out:
        copy.start()
    keep_norm(slim_finish(1), slim_norm.at[1])

    def act_parts():
        center, rate = row16(slim_norm[1, 0:1]), row16(slim_norm[1, 1:2] * gains_mid[1:2])
        bias = row16(biases_mid[1:2])

        def body(pixel, row, across, carry):
            value = smooth_value((reduced[pixel] - center) * rate + bias).astype(BF)
            acts[pixel] = value
            lead = value.astype(F32)[0:8]
            halo_out[pixel] = jnp.concatenate([lead[:, 0:256], lead[:, 256:512]], axis=0).astype(BF)
            return carry

        pixels(body, 0)

    act_parts()
    halo_start(halo_out, halo_in, 3, -1)

    def change_early(pixel, row, across, carry):
        zero, one = halves(acts[pixel].astype(F32))
        change[pixel, 0] = (one - zero) * step_weight[0:8]
        change[pixel, 1] = one
        return carry

    pixels(change_early, 0)

    def lanes_of(tile):
        return pl.ds(pl.multiple_of(tile * 128, 128), 128)

    def inside(row, column):
        return 0 <= row < HEIGHT and 0 <= column < WIDTH

    def gate_tile(which):
        def body(tile, carry):
            lanes = lanes_of(tile)
            kernels = [depth[k, :, lanes] for k in range(18)]
            middle = kernels[4] + kernels[13]
            offsets = jnp.broadcast_to(gate_bias[0:1, lanes], (8, 128))
            field = [change[p, which, :, lanes] for p in range(PIX)]
            for i in range(HEIGHT):
                for j in range(WIDTH):
                    mixed = offsets + middle * field[i * WIDTH + j]
                    for base, taps in ((0, near_taps()), (9, far_taps())):
                        for k, (di, dj) in enumerate(taps):
                            if (di or dj) and inside(i + di, j + dj):
                                mixed = mixed + kernels[base + k] * field[(i + di) * WIDTH + j + dj]
                    gates[i * WIDTH + j, which, :, lanes] = 0.5 + 0.5 * jnp.tanh(0.5 * mixed)
            return carry

        lax.fori_loop(0, 4, body, 0)

    gate_tile(0)
    halo_finish(halo_out, halo_in, 3, -1)

    def change_late(pixel, row, across, carry):
        ahead = halo_in[pixel].astype(F32)
        after = jnp.concatenate([ahead[0:8], ahead[8:16]], axis=1)
        change[pixel, 1] = (after - change[pixel, 1]) * step_weight[8:16]
        return carry

    pixels(change_late, 0)
    gate_tile(1)

    for side in range(9):
        edge = jnp.zeros((16, COLUMNS), BF)
        for pad in (gated, back_pad):
            pad[0, side] = edge
            pad[8, side] = edge
            pad[side, 0] = edge
            pad[side, 8] = edge

    def gated_body(pixel, row, across, carry):
        both_gates = jnp.concatenate([gates[pixel, 0], gates[pixel, 1]], axis=0)
        gated[row + 1, across + 1] = (acts[pixel].astype(F32) * (1.0 + both_gates)).astype(BF)
        return carry

    pixels(gated_body, 0)

    loads["conv"].wait()

    def window(pad, a, b):
        return flat(pad[a : a + HEIGHT, b : b + WIDTH])

    for tile in range(2):
        at = pl.ds(tile * WIDE_TILE, WIDE_TILE)
        value = dot(window(gated, 0, 0), flat(conv_w[0, :, :, :, at]))
        for tap in range(1, 9):
            value = value + dot(window(gated, tap // 3, tap % 3), flat(conv_w[tap, :, :, :, at]))
        conv[:, :, :, at] = value.reshape(PIX, 2, 8, WIDE_TILE)
        slim_src[2, 0:1, at] = rows_sum(value)
        slim_src[2, 1:2, at] = rows_sum(value * value)
    slim_start(2)
    spill_out.wait()
    loads["expand"].wait()
    loads["cot"].wait()
    keep_norm(slim_finish(2), slim_norm.at[2])

    def conv_rows(pixel):
        return conv[pixel].reshape(16, COLUMNS)

    def conv_act_part():
        center, rate = row16(slim_norm[2, 0:1]), row16(slim_norm[2, 1:2] * gains_mid[2:3])
        bias = row16(biases_mid[2:3])

        def body(pixel, row, across, carry):
            conv_act[pixel] = smooth_value((conv_rows(pixel) - center) * rate + bias).astype(BF)
            return carry

        pixels(body, 0)

    conv_act_part()
    widen(conv_act, expand_w, 1)
    wide_second(2)
    wide_second(3)

    def output_part(group, columns):
        center = row16(wide_norm[1, 0:1, columns])
        rate = row16(wide_norm[1, 1:2, columns])
        gain = row16(gains_wide[1:2, columns])
        bias = row16(biases_wide[1:2, columns])

        def body(pixel, row, across, carry):
            pool, shift, stretch = carry
            unit = (outer[pixel, :, columns] - center) * rate
            value, slope = smooth_pair(block_input[pixel, :, columns].astype(F32) + unit * gain + bias)
            incoming = cot[group * PIX + pixel].astype(F32) * slope
            cot[group * PIX + pixel] = value.astype(BF)
            skip[pixel, :, columns] = incoming
            return pool + fold(value), shift + fold(incoming), stretch + fold(incoming * unit)

        pool, shift, stretch = pixels(body, (slim_zero, slim_zero, slim_zero))
        video_src[group] = pool
        here = pl.ds(pl.multiple_of(lax.rem(group, 2) * COLUMNS, COLUMNS), COLUMNS)
        wide_src[4 + group // 2, 0:1, here] = rows_sum(shift)
        wide_src[4 + group // 2, 1:2, here] = rows_sum(stretch)

    for half in range(2):
        keep_norm(wide_finish(2 + half), wide_norm.at[1, :, wide_half(half)])
        wide_pixels(output_part, half)
        wide_first(4 + half)
    wide_second(4)
    wide_second(5)
    act_out = [
        pltpu.make_async_copy(
            cot.at[pl.ds(g * PIX, PIX)], act_hbm.at[:, :, column_group(g)], store_sem.at[6 + g]
        )
        for g in range(4)
    ]
    for copy in act_out:
        copy.start()

    def wide_grads(sums, at, half):
        total = wide_finish(sums * 2 + half)
        biases_wide_grad[at : at + 1, wide_half(half)] = total[0:1]
        gains_wide_grad[at : at + 1, wide_half(half)] = total[1:2]

    def wide_back(at, group, columns):
        center = row16(wide_norm[at, 0:1, columns])
        rate = row16(wide_norm[at, 1:2, columns])
        factor = rate * row16(gains_wide[at : at + 1, columns])
        shift = row16(biases_wide_grad[at : at + 1, columns] * scale)
        stretch = row16(gains_wide_grad[at : at + 1, columns] * scale) * rate

        def body(pixel, row, across, carry):
            value = skip[pixel, :, columns] - shift - (outer[pixel, :, columns] - center) * stretch
            wide[pixel, :, columns] = (value * factor).astype(BF)
            return carry

        pixels(body, 0)

    for half in range(2):
        wide_grads(2, 1, half)
        wide_pixels(functools.partial(wide_back, 1), half)
    spill_in = pltpu.make_async_copy(spill, outer, store_sem.at[0])
    spill_in.start()

    def narrow(weight):
        for tile in range(2):
            at = pl.ds(tile * WIDE_TILE, WIDE_TILE)
            value = dot_back(flat(wide[:, :, column_group(0)]), flat(weight[0, tile]))
            for g in range(1, 4):
                value = value + dot_back(flat(wide[:, :, column_group(g)]), flat(weight[g, tile]))
            temp[:, :, at] = value.reshape(PIX, 16, WIDE_TILE)

    narrow(expand_w)

    def slope_sums(source, norm, sums):
        center, rate = row16(slim_norm[norm, 0:1]), row16(slim_norm[norm, 1:2])
        gain, bias = row16(gains_mid[norm : norm + 1]), row16(biases_mid[norm : norm + 1])

        def body(pixel, row, across, carry):
            shift, stretch = carry
            unit = (source(pixel) - center) * rate
            unused, slope = smooth_pair(unit * gain + bias)
            value = temp[pixel] * slope
            temp[pixel] = value
            return shift + fold(value), stretch + fold(value * unit)

        shift, stretch = pixels(body, (slim_zero, slim_zero))
        slim_src[sums, 0:1] = rows_sum(shift)
        slim_src[sums, 1:2] = rows_sum(stretch)
        slim_start(sums)

    def slope_finish(source, norm, sums, store):
        total = slim_finish(sums)
        biases_mid_grad[norm : norm + 1] = total[0:1]
        gains_mid_grad[norm : norm + 1] = total[1:2]
        center, rate = row16(slim_norm[norm, 0:1]), row16(slim_norm[norm, 1:2])
        factor = rate * row16(gains_mid[norm : norm + 1])
        shift = row16(total[0:1] * scale)
        stretch = row16(total[1:2] * scale) * rate

        def body(pixel, row, across, carry):
            value = temp[pixel] - shift - (source(pixel) - center) * stretch
            store(pixel, row, across, (value * factor).astype(BF))
            return carry

        pixels(body, 0)

    for copy in act_out:
        copy.wait()
    for copy in frame_out:
        copy.wait()
    slope_sums(conv_rows, 2, 3)

    column, core = seg // 2, lax.rem(seg, 2)
    layer, line = clip // 2, lax.rem(clip, 2)
    to_core = {"seg": seg + 1 - 2 * core}
    to_column = {"seg": seg + 2 - 4 * column}
    to_corner = {"seg": 3 - seg}
    to_line = {"clip": clip + 1 - 2 * line}
    own = layer * 4 + line * 2

    class Ring:
        def __init__(self, at, slots, shared, single, places):
            self.at, self.slots, self.shared, self.single = at, slots, shared, single
            self.count = shared + 2 * single
            self.mine = shared + column * single
            self.other = shared + (1 - column) * single
            sizes = {
                "core": 16 * self.count, "line_a": 8 * shared, "layer_a": 8 * shared, "column_a": 2 * shared,
                "column_b": 16 * single, "line_b": 8 * single, "layer_b": 8 * single, "final": 4 * self.count,
            }
            self.land, self.kinds = {}, {}
            for number, (kind, size) in enumerate(sizes.items()):
                ref, base = places[kind]
                self.land[kind] = (ref, base)
                self.kinds[kind] = number

        def tiles(self, kind, start, size):
            ref, base = self.land[kind]
            return ref.at[pl.ds(base + start, size)]

        def send(self, kind, source, start, size, device):
            sems = [ring_sem.at[way, self.at, self.kinds[kind]] for way in range(2)]
            pltpu.make_async_remote_copy(
                source, self.tiles(kind, start, size), sems[0], sems[1],
                device_id=device, device_id_type=MESH,
            ).start()

        def wait(self, kind, size, sent=None):
            for way, amount in ((1, size), (0, size if sent is None else sent)):
                span = pool.at[pl.ds(0, amount)]
                pltpu.make_async_copy(span, span, ring_sem.at[way, self.at, self.kinds[kind]]).wait()

        def add_slots(self, kind, amount, slot_of):
            ref, base = self.land[kind]
            for item in range(amount):
                slot = slot_of(item)
                self.slots[slot, core] = self.slots[slot, core] + ref[pl.ds(base + item * 16, 16)]

        def add_lines(self, kind, amount, slot_of):
            ref, base = self.land[kind]
            for item in range(amount):
                for k in range(4):
                    here = pl.ds(k * 4 + line * 2, 2)
                    self.slots[slot_of(item), core, here] = (
                        self.slots[slot_of(item), core, here] + ref[pl.ds(base + (item * 4 + k) * 2, 2)]
                    )

        def gather(self, kind, amount, slot_of, store):
            ref, base = self.land[kind]
            for item in range(amount):
                ref[pl.ds(base + (item * 4 + layer) * 2, 2)] = self.slots[slot_of(item), core, pl.ds(own, 2)]
                value = ref[pl.ds(base + item * 8, 2)].astype(F32)
                for k in range(1, 4):
                    value = value + ref[pl.ds(base + (item * 4 + k) * 2, 2)].astype(F32)
                store(item, value.astype(BF))

        def stage0(self):
            for slot in range(self.count):
                self.send("core", self.slots.at[slot, 1 - core], slot * 16, 16, to_core)

        def send_line(self, kind, amount, slot_of):
            for item in range(amount):
                for k in range(4):
                    source = self.slots.at[slot_of(item), core, pl.ds(k * 4 + (1 - line) * 2, 2)]
                    self.send(kind, source, (item * 4 + k) * 2, 2, to_line)

        def send_layer(self, kind, amount, slot_of):
            for item in range(amount):
                for step in range(1, 4):
                    there = lax.rem(layer + step, 4)
                    source = self.slots.at[slot_of(item), core, pl.ds(there * 4 + line * 2, 2)]
                    self.send(kind, source, (item * 4 + layer) * 2, 2, {"clip": there * 2 + line})

        def stage1(self):
            self.wait("core", 16 * self.count)
            self.add_slots("core", self.count, lambda item: item)
            self.send_line("line_a", self.shared, lambda item: item)
            for item in range(self.single):
                self.send("column_b", self.slots.at[self.other + item, core], item * 16, 16, to_column)

        def stage2(self):
            self.wait("line_a", 8 * self.shared)
            self.add_lines("line_a", self.shared, lambda item: item)
            self.send_layer("layer_a", self.shared, lambda item: item)
            self.wait("column_b", 16 * self.single)
            self.add_slots("column_b", self.single, lambda item: self.mine + item)
            self.send_line("line_b", self.single, lambda item: self.mine + item)

        def stage3(self):
            self.wait("line_b", 8 * self.single)
            self.add_lines("line_b", self.single, lambda item: self.mine + item)
            self.send_layer("layer_b", self.single, lambda item: self.mine + item)
            self.wait("layer_a", 6 * self.shared)

            def store(item, value):
                self.slots[item, core, pl.ds(own, 2)] = value

            self.gather("layer_a", self.shared, lambda item: item, store)
            for item in range(self.shared):
                self.send("column_a", self.slots.at[item, core, pl.ds(own, 2)], item * 2, 2, to_column)

        def stage4(self):
            final, start = self.land["final"]
            here = start + core * self.count * 2
            self.wait("column_a", 2 * self.shared)
            ref, base = self.land["column_a"]
            for item in range(self.shared):
                final[pl.ds(here + item * 2, 2)] = (
                    self.slots[item, core, pl.ds(own, 2)] + ref[pl.ds(base + item * 2, 2)]
                )
                at = core * self.count * 2 + item * 2
                self.send("final", self.tiles("final", at, 2), at, 2, to_core)
            self.wait("layer_b", 6 * self.single)

            def store(item, value):
                final[pl.ds(here + (self.mine + item) * 2, 2)] = value

            self.gather("layer_b", self.single, lambda item: self.mine + item, store)
            for item in range(self.single):
                at = (core * self.count + self.mine + item) * 2
                for device in (to_core, to_column, to_corner):
                    self.send("final", self.tiles("final", at, 2), at, 2, device)

        def stage5(self):
            arrive = 2 * (self.shared + 3 * self.single)
            self.wait("final", arrive)

        def result(self, half, slot, part):
            final, start = self.land["final"]
            return final[start + (half * self.count + slot) * 2 + part].astype(F32)

    KINDS = ("core", "line_a", "layer_a", "column_a", "column_b", "line_b", "layer_b", "final")

    def places(spans):
        return {kind: span for kind, span in zip(KINDS, spans)}

    def packed(ref, start, shared, single):
        count = shared + 2 * single
        sizes = (16 * count, 8 * shared, 8 * shared, 2 * shared, 16 * single, 8 * single, 8 * single, 4 * count)
        spans = []
        for size in sizes:
            spans.append((ref, start))
            start = start + size
        return places(spans)

    ring_expand = Ring(0, expand_w, 2, 1, packed(cot, 0, 2, 1))
    ring_conv = Ring(1, conv_w.at[pl.ds(0, 4)], 2, 1, packed(pool, 0, 2, 1))
    ring_more = Ring(5, conv_w.at[pl.ds(4, 5)], 3, 1, packed(pool, 148, 3, 1))
    ring_reduce = Ring(2, reduce_w, 2, 1, packed(frame, 0, 2, 1))
    ring_down = Ring(4, expand_w, 2, 1, packed(cot, 0, 2, 1))
    ring_up = Ring(
        3, up, 2, 1,
        places(
            (
                (pool, 334), (frame, 148), (cot, 148), (cot, 164),
                (frame, 164), (cot, 168), (cot, 176), (frame, 180),
            )
        ),
    )

    def put_rows(slots, slot, value):
        parts = value.astype(BF).reshape(8, 2, 2, 16, COLUMNS)
        for half in range(2):
            slots[slot, half] = parts[:, half].reshape(16, 16, COLUMNS)

    def wide_weight_grad(left, slots):
        def body(slot, carry):
            columns = pl.ds(pl.multiple_of(slot * COLUMNS, COLUMNS), COLUMNS)
            put_rows(slots, slot, dot_rows(flat(left[...]), flat(wide[:, :, columns])))
            return carry

        lax.fori_loop(0, 4, body, 0)

    def tall_weight_grad(left, slots):
        def body(block, carry):
            columns = pl.ds(pl.multiple_of(block * WIDE_TILE, WIDE_TILE), WIDE_TILE)
            value = dot_rows(flat(left[:, :, columns]), flat(back[...])).astype(BF)
            parts = value.reshape(2, 4, 2, 16, COLUMNS)
            for half in range(2):
                for slot in range(4):
                    slots[slot, half, pl.ds(block * 2, 2)] = parts[half, slot]
            return carry

        lax.fori_loop(0, 8, body, 0)

    def conv_weight_grad(taps):
        for tap in taps:
            put_rows(conv_w, tap, dot_rows(window(gated, tap // 3, tap % 3), window(back_pad, 1, 1)))

    wide_weight_grad(conv_act, expand_w)

    def store_conv(pixel, row, across, value):
        back_pad[row + 1, across + 1] = value

    slope_finish(conv_rows, 2, 3, store_conv)
    ring_expand.stage0()

    grad_gated = conv_act
    for tile in range(2):
        at = pl.ds(tile * WIDE_TILE, WIDE_TILE)
        value = dot_back(window(back_pad, 2, 2), flat(conv_w[0, tile]))
        for tap in range(1, 9):
            value = value + dot_back(window(back_pad, 2 - tap // 3, 2 - tap % 3), flat(conv_w[tap, tile]))
        grad_gated[:, :, at] = value.astype(BF).reshape(PIX, 16, WIDE_TILE)
    ring_expand.stage1()
    conv_weight_grad(range(0, 4))
    ring_conv.stage0()

    grad_mixed = conv

    def mixed_body(pixel, row, across, carry):
        incoming = grad_gated[pixel].astype(F32)
        both_gates = jnp.concatenate([gates[pixel, 0], gates[pixel, 1]], axis=0)
        value = incoming * acts[pixel].astype(F32) * both_gates * (1.0 - both_gates)
        grad_mixed[pixel] = value.reshape(2, 8, COLUMNS)
        temp[pixel] = incoming * (1.0 + both_gates)
        return carry

    pixels(mixed_body, 0)
    weighted = gates

    def gate_back_tile(which):
        def body(tile, carry):
            lanes = lanes_of(tile)
            kernels = [depth[k, :, lanes] for k in range(18)]
            middle = kernels[4] + kernels[13]
            weight = step_weight[which * 8 : which * 8 + 8, 0:128]
            field = [grad_mixed[p, which, :, lanes] for p in range(PIX)]
            for i in range(HEIGHT):
                for j in range(WIDTH):
                    value = middle * field[i * WIDTH + j]
                    for base, taps in ((0, near_taps()), (9, far_taps())):
                        for k, (di, dj) in enumerate(taps):
                            if (di or dj) and inside(i - di, j - dj):
                                value = value + kernels[base + k] * field[(i - di) * WIDTH + j - dj]
                    weighted[i * WIDTH + j, which, :, lanes] = value * weight
            return carry

        lax.fori_loop(0, 4, body, 0)

    def depth_grad_tile():
        def body(tile, carry):
            lanes = lanes_of(tile)
            totals = [None] * 19
            for which in range(2):
                field = [grad_mixed[p, which, :, lanes] for p in range(PIX)]

                def grow(k, term):
                    totals[k] = term if totals[k] is None else totals[k] + term

                for p in range(PIX):
                    grow(18, field[p])
                for base, taps in ((0, near_taps()), (9, far_taps())):
                    for k, (di, dj) in enumerate(taps):
                        for i in range(HEIGHT):
                            for j in range(WIDTH):
                                if inside(i + di, j + dj):
                                    there = (i + di) * WIDTH + j + dj
                                    grow(base + k, field[i * WIDTH + j] * change[there, which, :, lanes])
            for k in range(19):
                video_src[4 + k // 8, k % 8 : k % 8 + 1, lanes] = rows_sum(totals[k])
            return carry

        lax.fori_loop(0, 4, body, 0)
        video_src[6, 3:8] = jnp.zeros((5, COLUMNS), F32)

    gate_back_tile(1)

    def weighted_pack(pixel, row, across, carry):
        last = weighted[pixel, 1]
        halo_out[pixel] = jnp.concatenate([last[:, 0:256], last[:, 256:512]], axis=0).astype(BF)
        return carry

    pixels(weighted_pack, 0)
    halo_start(halo_out, halo_in, 4, 1)
    gate_back_tile(0)
    ring_expand.stage2()
    ring_conv.stage1()
    halo_finish(halo_out, halo_in, 4, 1)

    def act_grad_body(pixel, row, across, carry):
        ahead = halo_in[pixel].astype(F32)
        before = jnp.concatenate([ahead[0:8], ahead[8:16]], axis=1)
        zero, one = weighted[pixel, 0], weighted[pixel, 1]
        value = temp[pixel] + jnp.concatenate([before - zero, zero - one], axis=0)
        temp[pixel] = value.astype(BF).astype(F32)
        return carry

    pixels(act_grad_body, 0)

    def reduced_rows(pixel):
        return reduced[pixel]

    slope_sums(reduced_rows, 1, 4)
    depth_grad_tile()
    conv_weight_grad(range(4, 9))
    ring_more.stage0()

    def store_back(pixel, row, across, value):
        back[pixel] = value

    slope_finish(reduced_rows, 1, 4, store_back)
    ring_expand.stage3()
    ring_conv.stage2()

    def video_span(way, at, ref):
        pltpu.make_async_copy(ref, ref, video_sem.at[way, at]).wait()

    def seg_spread(source, target, at):
        for step in range(1, segs):
            pltpu.make_async_remote_copy(
                source, target, video_sem.at[0, at], video_sem.at[1, at],
                device_id={"seg": lax.rem(seg + step, segs)}, device_id_type=MESH,
            ).start()

    def video_first():
        seg_spread(video_src, change.at[pl.ds(seg * 7, 7), 0], 0)
        change[pl.ds(seg * 7, 7), 0] = video_src[...]

    def video_second():
        for way in range(2):
            video_span(way, 0, change.at[pl.ds(0, 21), 0])

        def total(read):
            value = read(0)
            for rank in range(1, segs):
                value = value + read(rank * 7)
            return value

        quarter = pl.ds(pl.multiple_of(seg * 128, 128), 128)
        conv[clip, 0] = total(lambda base: change[base + seg, 0])
        for k in range(3):
            conv[clip, 1, :, pl.ds(k * 128, 128)] = total(lambda base: change[base + 4 + k, 0, :, quarter])
        conv[clip, 1, :, pl.ds(384, 128)] = crop_id[...]
        for step in range(1, clips):
            pltpu.make_async_remote_copy(
                conv.at[clip], conv.at[clip], video_sem.at[0, 1], video_sem.at[1, 1],
                device_id={"clip": lax.rem(clip + step, clips)}, device_id_type=MESH,
            ).start()

    def video_third():
        for way in range(2):
            video_span(way, 1, conv.at[pl.ds(0, clips - 1)])
        sums = jnp.concatenate([conv[k, 0] for k in range(clips)], axis=0)
        names = jnp.concatenate([conv[k, 1, :, pl.ds(384, 128)] for k in range(clips)], axis=0)
        lane = lax.broadcasted_iota(jnp.int32, names.shape, 1).astype(F32)
        member = (names == lane).astype(F32)

        def gather(values):
            return lax.dot_general(
                member, values, (((0,), (0,)), ((), ())),
                precision=lax.Precision.HIGHEST, preferred_element_type=F32,
            )[0:32]

        counts = gather(jnp.ones_like(names))
        means = gather(sums) / jnp.concatenate([counts * (SEGS * PIX)] * 4, axis=1)
        grads = conv[0, 1]
        for k in range(1, clips):
            grads = grads + conv[k, 1]
        gates[pl.ds(seg * 5, 4), 0] = means.reshape(4, 8, COLUMNS)
        gates[pl.ds(seg * 5 + 4, 1), 0] = grads[None]
        mine = gates.at[pl.ds(seg * 5, 5), 0]
        seg_spread(mine, mine, 2)

    def video_last():
        for way in range(2):
            video_span(way, 2, gates.at[pl.ds(0, 15), 0])
        for rank in range(segs):
            for k in range(4):
                video_means[k * 8 : k * 8 + 8, column_group(rank)] = gates[rank * 5 + k, 0]
            lanes = pl.ds(rank * 128, 128)
            parts = [gates[rank * 5 + 4, 0, :, pl.ds(k * 128, 128)] for k in range(3)]
            near_grad[0:8, lanes] = parts[0]
            near_grad[8:9, lanes] = parts[1][0:1]
            far_grad[0:7, lanes] = parts[1][1:8]
            far_grad[7:9, lanes] = parts[2][0:2]
            gate_grad[0:1, lanes] = parts[2][2:3]


    spill_in.wait()

    for half in range(2):

        def input_grad(part, carry):
            tile = half * 4 + part
            at = pl.ds(pl.multiple_of(tile * WIDE_TILE, WIDE_TILE), WIDE_TILE)
            weight = flat(reduce_w[half * 2 + part // 2, lax.rem(part, 2)])
            value = dot_back(flat(back[...]), weight) + flat(skip[:, :, at])
            skip[:, :, at] = value.reshape(PIX, 16, WIDE_TILE)
            unit = (flat(outer[:, :, at]) - wide_norm[0, 0:1, at]) * wide_norm[0, 1:2, at]
            here = pl.ds(pl.multiple_of(part * WIDE_TILE, WIDE_TILE), WIDE_TILE)
            wide_src[6 + half, 0:1, here] = rows_sum(value)
            wide_src[6 + half, 1:2, here] = rows_sum(value * unit)
            return carry

        lax.fori_loop(0, 4, input_grad, 0)
        wide_first(6 + half)
    wide_second(6)
    wide_second(7)
    ring_more.stage1()
    tall_weight_grad(block_input, reduce_w)
    ring_reduce.stage0()
    frame_in = pltpu.make_async_copy(frame_spill, tok, store_sem.at[1])
    frame_in.start()
    ring_expand.stage4()
    for half in range(2):
        wide_grads(3, 0, half)
        wide_pixels(functools.partial(wide_back, 0), half)
    ring_conv.stage3()
    narrow(up)

    def inner_rows(pixel):
        return inner[pixel]

    ring_expand.stage5()
    expand_kept = [
        [ring_expand.result(half, slot, part) for part in range(2)] for half in range(2) for slot in range(4)
    ]
    for index, pair in enumerate(expand_kept):
        for part in range(2):
            reduced[index * 2 + part] = pair[part]
    slope_sums(inner_rows, 0, 5)
    ring_reduce.stage1()
    ring_more.stage2()
    wide_weight_grad(active, up)
    ring_up.stage0()
    slope_finish(inner_rows, 0, 5, store_back)
    video_first()

    def last_pack(pixel, row, across, carry):
        last = back[pixel].astype(F32)[8:16]
        halo_out[pixel] = jnp.concatenate([last[:, 0:256], last[:, 256:512]], axis=0).astype(BF)
        return carry

    pixels(last_pack, 0)
    halo_start(halo_out, halo_in, 5, 1)
    ring_up.stage1()
    ring_conv.stage4()
    frame_in.wait()
    tall_weight_grad(tok, expand_w)
    ring_down.stage0()
    ring_reduce.stage2()
    ring_down.stage1()
    ring_more.stage3()
    halo_finish(halo_out, halo_in, 5, 1)

    def change_grad(pixel, row, across, carry):
        ahead = halo_in[pixel].astype(F32)
        before = jnp.concatenate([ahead[0:8], ahead[8:16]], axis=1) * past_weight[...]
        zero, one = halves(back[pixel].astype(F32) * step_weight[...])
        active[pixel] = jnp.concatenate([before - zero, zero - one], axis=0).astype(BF)
        return carry

    pixels(change_grad, 0)
    ring_up.stage2()

    def tokens_part(group):
        columns = column_group(group)
        return pltpu.make_async_copy(
            skip.at[:, :, columns], tokens_grad_hbm.at[:, :, columns], store_sem.at[11 + group]
        )

    for tile in range(8):
        at = pl.ds(tile * WIDE_TILE, WIDE_TILE)
        value = dot_back(flat(active[...]), flat(down[tile // 2, tile % 2])) + flat(skip[:, :, at])
        skip[:, :, at] = value.reshape(PIX, 16, WIDE_TILE)
        if tile % 2 == 1:
            tokens_part(tile // 2).start()
    video_second()

    ring_reduce.stage3()
    ring_more.stage4()
    ring_down.stage2()
    ring_up.stage3()
    ring_reduce.stage4()
    video_third()
    ring_conv.stage5()
    ring_more.stage5()

    def flush(index, source, target):
        copy = pltpu.make_async_copy(source, target, store_sem.at[20 + index])
        copy.start()
        return copy

    def tall_out(index, ring, target, first):
        for half in range(2):
            for slot in range(4):
                for part in range(2):
                    outer[first + half * 8 + slot * 2 + part, :, column_group(1)] = ring.result(half, slot, part)
        return flush(index, outer.at[pl.ds(first, 16), :, column_group(1)], target)

    def wide_out(index, read, target, first):
        for half in range(2):
            for slot in range(4):
                for part in range(2):
                    outer[first + half * 2 + part, :, column_group(slot)] = read(half, slot, part)
        return flush(index, outer.at[pl.ds(first, 4)], target)

    copies = [wide_out(0, lambda half, slot, part: reduced[(half * 4 + slot) * 2 + part], expand_grad, 40)]
    for tap in range(9):
        ring, slot = (ring_conv, tap) if tap < 4 else (ring_more, tap - 4)
        for half in range(2):
            for part in range(2):
                outer[tap * 4 + half * 2 + part, :, column_group(0)] = ring.result(half, slot, part)
    copies.append(flush(1, outer.at[pl.ds(0, 36), :, column_group(0)], conv_grad))
    ring_down.stage3()
    ring_up.stage4()
    ring_reduce.stage5()
    copies.append(tall_out(2, ring_reduce, reduce_grad, 16))
    ring_down.stage4()
    ring_up.stage5()
    copies.append(wide_out(3, ring_up.result, up_grad, 36))
    video_last()
    ring_down.stage5()
    copies.append(tall_out(4, ring_down, down_grad, 0))
    for group in range(4):
        tokens_part(group).wait()
    for copy in copies:
        copy.wait()


def hand_over(count, *refs):
    tokens_grad, *grads = refs[0:count]
    tokens_out, *outs = refs[count : 2 * count]
    held, *kept = refs[2 * count : 3 * count]
    sems = refs[3 * count]

    def load(group):
        columns = pl.ds(group * COLUMNS, COLUMNS)
        return pltpu.make_async_copy(
            tokens_grad.at[:, :, columns], held.at[:, :, columns], sems.at[0, group]
        )

    def store(group, part, clip_at):
        columns = pl.ds(group * COLUMNS, COLUMNS)
        return pltpu.make_async_copy(
            held.at[:, part * 8 + clip_at, columns], tokens_out.at[clip_at, :, part, columns], sems.at[1, group]
        )

    def move(way, at):
        source, target = (grads[at], kept[at]) if way == 0 else (kept[at], outs[at])
        return pltpu.make_async_copy(source, target, sems.at[way, 4 + at])

    for group in range(4):
        load(group).start()
    for at in range(count - 1):
        move(0, at).start()
    for group in range(4):
        load(group).wait()
        for part in range(2):
            for clip_at in range(8):
                store(group, part, clip_at).start()
    for at in range(count - 1):
        move(0, at).wait()
        move(1, at).start()
    for at in range(count - 1):
        move(1, at).wait()
    for group in range(4):
        span = held.at[:, :, pl.ds(group * COLUMNS, COLUMNS)]
        pltpu.make_async_copy(span, span, sems.at[1, group]).wait()


def fused_body(
    tokens, segment_index, crop_video, stem_down, stem_up, reduce_weight, conv_weight, expand_weight,
    depth_near, depth_far, gate_bias, gains_mid, biases_mid, gains_wide, biases_wide, cotangent,
):
    segs, clips = lax.axis_size("seg"), lax.axis_size("clip")
    amount = tokens.shape[0] * tokens.shape[1] * PIX * segs * clips
    def rows_first(field):
        return field.transpose(2, 1, 0, 3).reshape(PIX, 16, 2048)

    whole = pl.BlockSpec(memory_space=pl.ANY)
    near = pl.BlockSpec(memory_space=pltpu.VMEM)
    field = (PIX, 16, 2048)
    slim = (PIX, 16, COLUMNS)
    split = (PIX, 2, 8, COLUMNS)
    out_shapes = (
        (field, BF, whole), (field, F32, whole),
        ((16, 16, 512), F32, whole), ((4, 16, 2048), F32, whole), ((16, 16, 512), F32, whole),
        ((36, 16, 512), F32, whole), ((4, 16, 2048), F32, whole), (field, F32, whole), (field, BF, whole),
        ((32, 2048), F32, near), ((9, 512), F32, near), ((9, 512), F32, near), ((1, 512), F32, near),
        ((3, 512), F32, near), ((3, 512), F32, near), ((2, 2048), F32, near), ((2, 2048), F32, near),
    )
    tiles = (4 * PIX, 16, COLUMNS)
    weight = (4, 2, 16, 16, COLUMNS)
    scratch = [
        pltpu.VMEM(field, BF), pltpu.VMEM(tiles, BF), pltpu.VMEM(field, F32), pltpu.VMEM(field, F32),
        pltpu.VMEM(tiles, BF), pltpu.VMEM(field, BF),
        pltpu.VMEM(slim, F32), pltpu.VMEM(slim, BF), pltpu.VMEM(slim, F32), pltpu.VMEM(slim, BF),
        pltpu.VMEM(split, F32), pltpu.VMEM(split, F32), pltpu.VMEM(split, F32), pltpu.VMEM(slim, BF),
        pltpu.VMEM((9, 9, 16, 512), BF), pltpu.VMEM((9, 9, 16, 512), BF),
        pltpu.VMEM(slim, F32), pltpu.VMEM(slim, BF),
        pltpu.VMEM((PIX, 16, 256), BF), pltpu.VMEM((PIX, 16, 256), BF),
        pltpu.VMEM(weight, BF), pltpu.VMEM(weight, BF), pltpu.VMEM(weight, BF),
        pltpu.VMEM((9,) + weight[1:], BF), pltpu.VMEM(weight, BF),
        pltpu.VMEM((6, 2, 512), F32), pltpu.VMEM((6, segs * clips, 2, 512), F32),
        pltpu.VMEM((8, 2, 1024), F32), pltpu.VMEM((8, 2, 1024), F32),
        pltpu.VMEM((8, segs, 2, 1024), F32), pltpu.VMEM((8, clips, 2, 1024), F32),
        pltpu.VMEM((3, 2, 512), F32), pltpu.VMEM((2, 2, 2048), F32),
        pltpu.VMEM((POOL_TILES, 16, COLUMNS), BF), pltpu.VMEM((7, 8, COLUMNS), F32),
        pltpu.VMEM((18, 8, COLUMNS), F32), pltpu.VMEM((16, COLUMNS), F32), pltpu.VMEM((8, COLUMNS), F32),
        pltpu.VMEM((8, 128), F32),
        pltpu.SemaphoreType.DMA((16,)), pltpu.SemaphoreType.DMA((32,)), pltpu.SemaphoreType.DMA((2, 6)),
        pltpu.SemaphoreType.DMA((2, 6)), pltpu.SemaphoreType.DMA((4, 8)),
        pltpu.SemaphoreType.DMA((2, 6, 8)), pltpu.SemaphoreType.DMA((2, 3)),
    ]
    outs = pl.pallas_call(
        functools.partial(block_kernel, segs, clips, amount),
        out_shape=tuple(jax.ShapeDtypeStruct(s, d) for s, d, unused in out_shapes),
        in_specs=[whole] * 7 + [near] * 9,
        out_specs=tuple(m for unused, unused_too, m in out_shapes),
        scratch_shapes=scratch,
        compiler_params=pltpu.CompilerParams(
            collective_id=0, has_side_effects=True, vmem_limit_bytes=VMEM_BYTES
        ),
    )(
        rows_first(tokens), rows_first(cotangent), stem_down.reshape(weight),
        stem_up.reshape(2, 16, 16, 2048), reduce_weight.reshape(weight),
        conv_weight.reshape((9,) + weight[1:]), expand_weight.reshape(2, 16, 16, 2048),
        depth_near, depth_far, gate_bias[None], gains_mid, biases_mid, gains_wide, biases_wide,
        segment_index, crop_video[None],
    )
    act, *results = outs[0:7]
    results = results + list(outs[9:])
    handed = pl.pallas_call(
        functools.partial(hand_over, len(results)),
        out_shape=(jax.ShapeDtypeStruct((8, PIX, 2, 2048), F32),)
        + tuple(jax.ShapeDtypeStruct(x.shape, F32) for x in results[1:]),
        in_specs=[whole] * len(results),
        out_specs=(whole,) * len(results),
        scratch_shapes=[pltpu.VMEM(x.shape, F32) for x in results]
        + [pltpu.SemaphoreType.DMA((2, len(results) + 3))],
        compiler_params=pltpu.CompilerParams(vmem_limit_bytes=VMEM_BYTES),
    )(*results)
    (
        tokens_grad, down_grad, up_grad, reduce_grad, conv_grad, expand_grad,
        video_means, near_grad, far_grad, gate_grad,
        gains_mid_grad, biases_mid_grad, gains_wide_grad, biases_wide_grad,
    ) = handed

    def clips_first(value):
        return value.reshape(PIX, 2, 8, 2048).transpose(2, 1, 0, 3)

    return (
        clips_first(act),
        video_means,
        tokens_grad.transpose(0, 2, 1, 3),
        down_grad.reshape(256, 512),
        up_grad.reshape(64, 2048),
        reduce_grad.reshape(256, 512),
        conv_grad.reshape(9, 64, 512),
        expand_grad.reshape(64, 2048),
        near_grad,
        far_grad,
        gate_grad[0],
        gains_mid_grad,
        biases_mid_grad,
        gains_wide_grad,
        biases_wide_grad,
    )


POOL_TILES = 334 + 64
VMEM_BYTES = 63 << 20


def solution(mesh):
    def either(tokens, *others):
        devices = (lax.axis_size("seg"), lax.axis_size("clip"))
        fits = tokens.shape == (8, 2, PIX, 2048) and devices == (4, 8)
        return (fused_body if fits else body)(tokens, *others)

    return jax.shard_map(
        either,
        mesh=mesh,
        in_specs=(
            P("clip", "seg", None, None),
            P("clip", None),
            P("clip"),
            P(),
            P(),
            P(),
            P(),
            P(),
            P(),
            P(),
            P(),
            P(),
            P(),
            P(),
            P(),
            P("clip", "seg", None, None),
        ),
        out_specs=(
            P("clip", "seg", None, None),
            P(),
            P("clip", "seg", None, None),
            P("clip", None),
            P("clip", None),
            P("clip", None),
            P(None, "clip", None),
            P("clip", None),
            P(),
            P(),
            P(),
            P(),
            P(),
            P(),
            P(),
        ),
        check_vma=False,
    )
```
